32 devices in a mesh: canvas: 4 (over y, x), height: 8 (over z, core).
Axes of the slice: x: 2, y: 2, z: 4, core: 2. Of those that a mesh axis runs over, the one named last changes fastest.
Arguments:
- latents: bfloat16 [8, 64, 64, 512], P('canvas', 'height'), may hold values from -13 to 13
- crop_ids: int32 [8, 64, 64], P('canvas', 'height'), may hold values from 0 to 15, as said below
- params: float32 [11264, 512], P(('canvas', 'height')), may hold values from -0.53033009 to 0.53033009
- vectors: float32 [11, 512], replicated, may hold values from -1 to 2
- first_moment: float32 [11264, 512], P(('canvas', 'height')), may hold values from -320 to 320
- second_moment: float32 [11264, 512], P(('canvas', 'height')), may hold values from 1638.4 to 16384
- vector_first: float32 [11, 512], replicated, may hold values from -320 to 320
- vector_second: float32 [11, 512], replicated, may hold values from 1638.4 to 16384
- cotangent: bfloat16 [8, 64, 64, 512], P('canvas', 'height'), may hold values from -6 to 6
Outputs:
- first_hidden: float32 [8, 64, 64, 512], P('canvas', 'height')
- first_output: float32 [8, 64, 64, 512], P('canvas', 'height')
- second_output: float32 [8, 64, 64, 512], P('canvas', 'height')
- input_grad: float32 [8, 64, 64, 512], P('canvas', 'height')
- new_params: float32 [11264, 512], P(('canvas', 'height'))
- new_first: float32 [11264, 512], P(('canvas', 'height'))
- new_second: float32 [11264, 512], P(('canvas', 'height'))
- new_vectors: float32 [11, 512], replicated
- new_vector_first: float32 [11, 512], replicated
- new_vector_second: float32 [11, 512], replicated
The draws below stay inside these ranges and needn't reach their ends.
Inputs may be any that keep to these rules, and one draw needn't show every extreme that they name: `crop_ids`: in each canvas the pixels of one id form a rectangle whose columns are a run of aligned groups of 8 columns.
All inputs are finite; a program needn't handle non-finite values.
Results may differ from the reference program's by a relative error of at most 0.017.
The reference program's roundings to bfloat16 on the way count: a program that leaves them out, or rounds other values in their place, can miss the bound.
Values may be sent and summed in bfloat16 or wider, within the bound.
A program may use at most 256 MiB of HBM per device.

```python
import math
import jax
import jax.numpy as jnp
from jax import lax

C = 512
GROUPS = 32
H = 64
W = 64
STEP = 5
CANVASES = 8
CROPS = 16
PIXELS = 32768


def draw_crop_ids(key, part):
    key = jax.random.fold_in(key, 3)
    unit_count = W // 8
    cut_key, row_key, coin_key, pick_key = jax.random.split(key, 4)
    unit_index = jnp.arange(unit_count, dtype=jnp.int32)
    full_unit = jax.random.randint(pick_key, (CANVASES, 1), 0, unit_count)
    other_unit = (full_unit + 1) % unit_count
    band_cuts = jax.random.randint(cut_key, (CANVASES, unit_count), 0, 2)
    band_cuts = jnp.where((unit_index == unit_count - 1) | (unit_index == full_unit) | (unit_index + 1 == full_unit), 1, band_cuts)
    candidate = jnp.where(band_cuts[:, None, :] == 1, unit_index[None, None, :], unit_count)
    candidate = jnp.where(unit_index[None, None, :] >= unit_index[None, :, None], candidate, unit_count)
    band_end = jnp.min(candidate, axis=2).astype(jnp.int32)
    split_rows = jax.random.randint(row_key, (CANVASES, unit_count), 1, H)
    split_coins = jax.random.randint(coin_key, (CANVASES, unit_count), 0, 2)
    split_coins = jnp.where(unit_index == full_unit, 0, jnp.where(unit_index == other_unit, 1, split_coins))
    column_unit = jnp.arange(W, dtype=jnp.int32) // 8
    pixel_end = band_end[:, column_unit]
    pixel_split = jnp.take_along_axis(split_rows, pixel_end, axis=1)
    pixel_coin = jnp.take_along_axis(split_coins, pixel_end, axis=1)
    row_index = jnp.arange(H, dtype=jnp.int32)
    lower_part = (pixel_coin[:, None, :] == 1) & (row_index[None, :, None] >= pixel_split[:, None, :])
    return (2 * pixel_end[:, None, :] + lower_part.astype(jnp.int32)).astype(jnp.int32)


def draw_latents(key, part):
    key = jax.random.fold_in(key, 5)
    row_place = (jnp.arange(H, dtype=jnp.float32) / H)[None, :, None, None]
    random_part = jnp.clip(jax.random.normal(key, (CANVASES, H, W, C), jnp.float32), -4.0, 4.0)
    growth = 1.0 + 2.0 * row_place
    offset_part = 0.5 * row_place
    return (random_part * growth + offset_part).astype(jnp.bfloat16)


def draw_params(key, part):
    key = jax.random.fold_in(key, 7)
    row_index = jnp.arange(22 * C)[:, None]
    conv_scale = (9 * C) ** (-0.5)
    attn_scale = C ** (-0.5)
    row_scale = jnp.where(row_index < 9 * C, conv_scale, jnp.where(row_index < 18 * C, 1.5 * conv_scale, jnp.where(row_index < 20 * C, 1.4 * attn_scale, jnp.where(row_index < 21 * C, attn_scale, 4.0 * attn_scale))))
    random_part = jnp.clip(jax.random.normal(key, (22 * C, C), jnp.float32), -3.0, 3.0)
    return random_part * row_scale


def draw_vectors(key, part):
    key = jax.random.fold_in(key, 9)
    kind_index = jnp.arange(11)[:, None]
    is_gain = (kind_index == 0) | (kind_index == 3) | (kind_index == 6)
    random_part = jnp.clip(jax.random.normal(key, (11, C), jnp.float32), -3.0, 3.0)
    return jnp.where(is_gain, 1.0 + 0.25 * random_part, 0.3 * random_part)


def steps_of(own_key, shape, cuts, least, top_value):
    loudness = 1.0
    for position, shards_of in cuts:
        heights = jax.random.uniform(jax.random.fold_in(jax.random.fold_in(own_key, 6), position), (shards_of,), jnp.float32, least / len(cuts), top_value / len(cuts))
        loudness = loudness * jnp.repeat(jnp.exp(heights), shape[position] // shards_of).reshape((-1,) + (1,) * (len(shape) - 1 - position))
    return loudness


def bell_draw(rng, dims, scale, limit, cuts=(), kind=jnp.bfloat16):
    gain = steps_of(rng, dims, cuts, -0.22, 0.18) if cuts else 1.0
    values = jax.random.normal(rng, dims, jnp.float32) * scale * gain
    return jnp.minimum(jnp.maximum(values, -limit), limit).astype(kind)


def setup_inputs(seed: int = 0) -> dict:
    arg_keys = jax.random.split(jax.random.key(seed), 10)
    latents = draw_latents(jax.random.fold_in(arg_keys[9], 71), 0)
    crop_ids = draw_crop_ids(jax.random.fold_in(arg_keys[9], 71), 0)
    params = draw_params(jax.random.fold_in(arg_keys[9], 71), 0)
    vectors = draw_vectors(jax.random.fold_in(arg_keys[9], 71), 0)
    first_moment = bell_draw(arg_keys[4], (22 * C, C), (0.3 * PIXELS ** 0.5), 320.0, ((0, 32),), jnp.float32)
    second_moment = jnp.clip(jnp.exp(math.log(16384.0) - 2.3025851 * jax.random.uniform(arg_keys[5], (22 * C, C), jnp.float32) ** steps_of(arg_keys[5], (22 * C, C), ((0, 32),), -0.2, 0.2)), 1638.4, 16384.0)
    vector_first = bell_draw(arg_keys[6], (11, C), (0.3 * PIXELS ** 0.5), 320.0, (), jnp.float32)
    vector_second = jnp.clip(jnp.exp(jax.random.uniform(arg_keys[7], (11, C), jnp.float32, math.log(1638.4), math.log(16384.0))), 1638.4, 16384.0)
    cotangent = bell_draw(arg_keys[8], (CANVASES, H, W, C), 1.0, 6.0, ((0, 4), (1, 8)))
    return {"latents": latents, "crop_ids": crop_ids, "params": params, "vectors": vectors, "first_moment": first_moment, "second_moment": second_moment, "vector_first": vector_first, "vector_second": vector_second, "cotangent": cotangent}


@jax.custom_vjp
def low(v):
    return lax.optimization_barrier(v.astype(jnp.bfloat16)).astype(jnp.float32)

@jax.custom_vjp
def low_back(v):
    return v

def low_keep(v):
    return (low(v), None)

def low_pass(kept, grad):
    return (grad,)

def back_keep(v):
    return (v, None)

def back_low(kept, grad):
    return (low(grad),)
low.defvjp(low_keep, low_pass)
low_back.defvjp(back_keep, back_low)
norm_epsilon = 1e-06
adam_epsilon = 1e-08
matrix_rate = 0.015
vector_rate = 0.2
mask_fill = -1e+30
highest = lax.Precision.HIGHEST

def group_norm(hidden, norm_gain, norm_bias, onehot, divisor):
    grouped = hidden.reshape(hidden.shape[0], GROUPS, C // GROUPS)
    totals = jnp.einsum('pc,pgk->cg', onehot, grouped, precision=highest)
    centre = totals / divisor[:, None]
    centre_pix = jnp.einsum('pc,cg->pg', onehot, centre, precision=highest)
    centered = grouped - centre_pix[:, :, None]
    spread = jnp.einsum('pc,pgk->cg', onehot, centered * centered, precision=highest) / divisor[:, None]
    inverse_pix = jnp.einsum('pc,cg->pg', onehot, lax.rsqrt(spread + norm_epsilon), precision=highest)
    return (centered * inverse_pix[:, :, None]).reshape(hidden.shape) * norm_gain + norm_bias

def masked_conv(source, crop_map, weight, conv_bias):
    padded = jnp.pad(source, ((1, 1), (1, 1), (0, 0)))
    padded_ids = jnp.pad(crop_map, 1, constant_values=-1)
    pieces = []
    for row_step in range(3):
        for col_step in range(3):
            window = padded[row_step:row_step + H, col_step:col_step + W]
            same_crop = padded_ids[row_step:row_step + H, col_step:col_step + W] == crop_map
            pieces.append(window * same_crop[:, :, None].astype(jnp.float32))
    columns = jnp.stack(pieces, axis=2).reshape(H * W, 9 * C)
    return jnp.dot(columns, weight, precision=highest) + conv_bias

def attention_branch(normed, crop_flat, qkv_weight, proj_weight, vectors):
    inputs = low(normed)
    queries = low_back(low(jnp.dot(inputs, qkv_weight[0], precision=highest) + vectors[8]))
    keys_all = low_back(low(jnp.dot(inputs, qkv_weight[1], precision=highest)))
    values_all = low_back(low(jnp.dot(inputs, qkv_weight[2], precision=highest) + vectors[9]))
    block_rows = min(512, H * W)
    score_scale = C ** (-0.5)

    def one_block(block_pair):
        block_queries, block_crops = block_pair
        scores = low_back(jnp.dot(block_queries, keys_all.T, precision=highest) * score_scale)
        scores = jnp.where(block_crops[:, None] == crop_flat[None, :], scores, mask_fill)
        row_top = lax.optimization_barrier(jnp.max(scores, axis=1, keepdims=True))
        exponent = jnp.exp(scores - row_top)
        probabilities = exponent / lax.optimization_barrier(jnp.sum(exponent, axis=1, keepdims=True))
        return jnp.dot(low(probabilities), values_all, precision=highest)
    attended = lax.map(jax.checkpoint(one_block), (queries.reshape(-1, block_rows, C), crop_flat.reshape(-1, block_rows)))
    attended = low_back(low(attended.reshape(H * W, C)))
    return low_back(jnp.dot(attended, proj_weight, precision=highest) + vectors[10])

def canvas_forward(hidden, crop_map, weights, vectors):
    conv_one, conv_two, qkv_weight, proj_weight = weights
    crop_flat = crop_map.reshape(H * W)
    onehot = (crop_flat[:, None] == jnp.arange(CROPS, dtype=jnp.int32)[None, :]).astype(jnp.float32)
    divisor = jnp.maximum(lax.optimization_barrier(jnp.sum(onehot, axis=0)) * (C // GROUPS), 1.0)
    flattened = hidden.reshape(H * W, C)
    normed = group_norm(flattened, vectors[0], vectors[1], onehot, divisor)
    activated = low(jax.nn.silu(normed))
    conv_out = low_back(masked_conv(activated.reshape(H, W, C), crop_map, conv_one, vectors[2]))
    normed = group_norm(conv_out, vectors[3], vectors[4], onehot, divisor)
    activated = low(jax.nn.silu(normed))
    branch = low_back(masked_conv(activated.reshape(H, W, C), crop_map, conv_two, vectors[5]))
    first_hidden = flattened + branch
    normed = group_norm(first_hidden, vectors[6], vectors[7], onehot, divisor)
    output = first_hidden + attention_branch(normed, crop_flat, qkv_weight, proj_weight, vectors)
    return (first_hidden.reshape(H, W, C), output.reshape(H, W, C))

def network(hidden, params, vectors, crop_ids):
    rounded = low(params)
    vector_low = low(vectors)
    weights = (rounded[:9 * C], rounded[9 * C:18 * C], rounded[18 * C:21 * C].reshape(3, C, C), rounded[21 * C:])

    def per_canvas(canvas_pair):
        return canvas_forward(canvas_pair[0], canvas_pair[1], weights, vector_low)
    return lax.map(jax.checkpoint(per_canvas), (hidden, crop_ids))

def adam_update(current, gradient, moment_one, moment_two, learn_rate):
    first_new = 0.5 * moment_one + 0.5 * gradient
    second_new = 0.9 * moment_two + 0.1 * gradient * gradient
    first_hat = first_new / (1.0 - 0.5 ** STEP)
    second_hat = second_new / (1.0 - 0.9 ** STEP)
    return (current - learn_rate * first_hat / (jnp.sqrt(second_hat) + adam_epsilon), first_new, second_new)

def reference(latents, crop_ids, params, vectors, first_moment, second_moment, vector_first, vector_second, cotangent):
    hidden = latents.astype(jnp.float32)

    def forward_all(hidden_in, params_in, vectors_in):
        return network(hidden_in, params_in, vectors_in, crop_ids)
    (first_hidden, first_output), pullback = jax.vjp(forward_all, hidden, params, vectors)
    input_grad, params_grad, vectors_grad = pullback((jnp.zeros_like(first_hidden), cotangent.astype(jnp.float32)))
    new_params, new_first, new_second = adam_update(params, params_grad, first_moment, second_moment, matrix_rate)
    new_vectors, new_vector_first, new_vector_second = adam_update(vectors, vectors_grad, vector_first, vector_second, vector_rate)
    second_output = network(hidden, new_params, new_vectors, crop_ids)[1]
    return (first_hidden, first_output, second_output, input_grad, new_params, new_first, new_second, new_vectors, new_vector_first, new_vector_second)
```

```python
import functools

import jax
import jax.numpy as jnp
from jax import lax
from jax.experimental import pallas as pl
from jax.experimental.pallas import tpu as pltpu
from jax.sharding import PartitionSpec as P

C = 512
GROUPS = 32
STEP = 5
CROPS = 16
SPAN = C // GROUPS
LANES = 128
TILES = C // LANES
UNIT = 8

norm_epsilon = 1e-06
adam_epsilon = 1e-08
matrix_rate = 0.015
vector_rate = 0.2
mask_fill = -1e30

F32 = jnp.float32
B16 = jnp.bfloat16
MESH = pl.DeviceIdType.MESH
VMEM_LIMIT = 60 * 2**20

vmem = pl.BlockSpec(memory_space=pltpu.VMEM)
smem = pl.BlockSpec(memory_space=pltpu.SMEM)
anyw = pl.BlockSpec(memory_space=pl.ANY)


def params_of(cid=None):
    if cid is None:
        return pltpu.CompilerParams(vmem_limit_bytes=VMEM_LIMIT)
    return pltpu.CompilerParams(
        vmem_limit_bytes=VMEM_LIMIT, collective_id=cid, has_side_effects=True
    )


def sds(shape, dtype):
    return jax.ShapeDtypeStruct(shape, dtype)


def split_dot(pick, value):
    total = None
    rest = value
    for _ in range(3):
        part = rest.astype(B16)
        term = jnp.dot(pick, part, preferred_element_type=F32)
        total = term if total is None else total + term
        rest = rest - part.astype(F32)
    return total


def lane_group_sum(piece):
    lane = lax.broadcasted_iota(jnp.int32, piece.shape, 1)
    step = 1
    while step < SPAN:
        ahead = pltpu.roll(piece, LANES - step, 1)
        behind = pltpu.roll(piece, step, 1)
        piece = piece + jnp.where((lane & step) == 0, ahead, behind)
        step *= 2
    return piece


def tiles_of(value):
    return [value[:, j * LANES : (j + 1) * LANES] for j in range(TILES)]


def wide(piece, times=TILES):
    return jnp.concatenate([piece] * times, axis=1)


def pack(quantities):
    shape = quantities[0][0].shape
    sub = lax.broadcasted_iota(jnp.int32, shape, 1) & (SPAN - 1)
    out = jnp.zeros(shape, F32)
    for q, pieces in enumerate(quantities):
        for j, piece in enumerate(pieces):
            out = jnp.where(sub == TILES * q + j, piece, out)
    return out


def unpack(packed):
    sub = lax.broadcasted_iota(jnp.int32, packed.shape, 1) & (SPAN - 1)
    return jnp.concatenate(
        [lane_group_sum(jnp.where(sub == j, packed, 0.0)) for j in range(TILES)], axis=1
    )


def shift_down(packed, q):
    return pltpu.roll(packed, LANES - TILES * q, packed.ndim - 1)


def greet(n):
    me = lax.axis_index("height")
    barrier = pltpu.get_barrier_semaphore()
    for d in range(1, n):
        pl.semaphore_signal(
            barrier, inc=1, device_id={"height": lax.rem(me + d, n)}, device_id_type=MESH
        )
    pl.semaphore_wait(barrier, n - 1)


def spread_copies(n, buf, send, recv, rnd):
    me = lax.axis_index("height")
    return [
        pltpu.make_async_remote_copy(
            src_ref=buf.at[rnd, 0],
            dst_ref=buf.at[rnd, d],
            send_sem=send.at[rnd, d],
            recv_sem=recv.at[rnd, d],
            device_id={"height": lax.rem(me + d, n)},
            device_id_type=MESH,
        )
        for d in range(1, n)
    ]


def cell_totals(load, out_ref, cells):
    def body(i, _):
        out_ref[pl.ds(i * 16, 16), :] = jnp.sum(load(i).reshape(16, UNIT, C), axis=1)
        return 0

    lax.fori_loop(0, cells // 16, body, 0)


def over_cells(cell_ref, i):
    return jnp.broadcast_to(cell_ref[pl.ds(i * 16, 16), :][:, None, :], (16, UNIT, C)).reshape(
        16 * UNIT, C
    )


def group_totals(pick_ref, cell_value):
    return [lane_group_sum(t) for t in tiles_of(split_dot(pick_ref[...], cell_value))]


def stats_payload(load, pick_ref, spread_ref, count_ref, cells, tmp_a, tmp_b):
    cell_totals(load, tmp_a, cells)
    sums = group_totals(pick_ref, tmp_a[...])
    count = count_ref[...]
    inv_count = 1.0 / jnp.maximum(count, 1.0)
    mean = jnp.concatenate([s * inv_count for s in sums], axis=1)
    tmp_b[...] = split_dot(spread_ref[...], mean)

    def centred(i):
        delta = load(i) - over_cells(tmp_b, i)
        return delta * delta

    cell_totals(centred, tmp_a, cells)
    squares = group_totals(pick_ref, tmp_a[...])
    return pack([sums, squares, [count] * TILES])


def combine_stats(gathered):
    sums = gathered
    squares = shift_down(gathered, 1)
    counts = shift_down(gathered, 2)
    divisor = jnp.maximum(jnp.sum(counts, axis=0), 1.0)
    mean = jnp.sum(sums, axis=0) / divisor
    apart = sums / jnp.maximum(counts, 1.0) - mean[None]
    spread = jnp.sum(squares + counts * apart * apart, axis=0) / divisor
    return mean, lax.rsqrt(spread + norm_epsilon), divisor


def shift_columns(row, left_mask, right_mask):
    width = row.shape[0]
    left = pltpu.roll(row, 1, 0) * wide(left_mask)
    right = pltpu.roll(row, width - 1, 0) * wide(right_mask)
    return jnp.concatenate([left, row, right], axis=1).astype(B16)


def logistic(a):
    return 1.0 / (1.0 + jnp.exp(-a))


def silu(a):
    return a * logistic(a)


def silu_slope(a):
    s = logistic(a)
    return s * (1.0 + a * (1.0 - s))


def layout_kernel(n, dims, x, pick, spread, ids_px, ids_lane, ids_all, mean_c, inv_c, div, cnt,
                  col_l, col_r, row_u, row_d, buf, idbuf, halo, tmp_a, tmp_b, send, recv, isend, irecv,
                  hsend, hrecv):
    canvases, rows, width = dims
    cells = canvases * rows * width // UNIT
    me = lax.axis_index("height")
    greet(n)
    id_copies = []
    idbuf[0] = ids_lane[...]
    for d in range(1, n):
        cp = pltpu.make_async_remote_copy(
            src_ref=idbuf.at[0], dst_ref=idbuf.at[d], send_sem=isend.at[d], recv_sem=irecv.at[d],
            device_id={"height": lax.rem(me + d, n)}, device_id_type=MESH)
        cp.start()
        id_copies.append(cp)
    up, down = halo_copies(n, ids_px.at[:, 0], ids_px.at[:, rows - 1], halo, hsend, hrecv)
    start_halo(n, up, down)

    def load(i):
        return x[pl.ds(i * 16 * UNIT, 16 * UNIT), :].astype(F32)

    ones = jnp.sum(pick[...].astype(F32), axis=1, keepdims=True) * float(UNIT * SPAN)
    cnt[...] = jnp.broadcast_to(ones, cnt.shape)
    buf[0, 0] = stats_payload(load, pick, spread, cnt, cells, tmp_a, tmp_b)
    copies = spread_copies(n, buf, send, recv, 0)
    for cp in copies:
        cp.start()
    wait_halo(n, up, down, halo, -1.0)
    column = lax.broadcasted_iota(jnp.int32, (width, LANES), 0)
    first, last = column == 0, column == width - 1
    for v in range(canvases):
        for r in range(rows + 2):
            here = halo[0, v] if r == 0 else halo[1, v] if r == rows + 1 else ids_px[v, r - 1]
            same_l = (pltpu.roll(here, 1, 0) == here) & jnp.logical_not(first)
            same_r = (pltpu.roll(here, width - 1, 0) == here) & jnp.logical_not(last)
            col_l[v, r] = same_l.astype(F32)
            col_r[v, r] = same_r.astype(F32)
            if 1 <= r <= rows:
                above = halo[0, v] if r == 1 else ids_px[v, r - 2]
                below = halo[1, v] if r == rows else ids_px[v, r]
                at = pl.ds((v * rows + r - 1) * width, width)
                row_u[at, :] = (above == here).astype(F32)
                row_d[at, :] = (below == here).astype(F32)
    for cp in copies:
        cp.wait_recv()
    mean, inv, divisor = combine_stats(buf[0])
    mean_c[...] = split_dot(spread[...], unpack(mean))
    inv_c[...] = split_dot(spread[...], unpack(inv))
    div[...] = unpack(divisor)[:, :LANES]
    for cp in id_copies:
        cp.wait_recv()
    ids_all[me] = idbuf[0]
    for d in range(1, n):
        ids_all[lax.rem(me - d + n, n)] = idbuf[d]
    for cp in copies + id_copies:
        cp.wait_send()


def halo_copies(n, first_row, last_row, halo, hsend, hrecv):
    me = lax.axis_index("height")
    up = pltpu.make_async_remote_copy(
        src_ref=first_row, dst_ref=halo.at[1], send_sem=hsend.at[0], recv_sem=hrecv.at[1],
        device_id={"height": lax.rem(me + n - 1, n)}, device_id_type=MESH)
    down = pltpu.make_async_remote_copy(
        src_ref=last_row, dst_ref=halo.at[0], send_sem=hsend.at[1], recv_sem=hrecv.at[0],
        device_id={"height": lax.rem(me + 1, n)}, device_id_type=MESH)
    return up, down


def start_halo(n, up, down):
    me = lax.axis_index("height")

    @pl.when(me > 0)
    def _():
        up.start()

    @pl.when(me < n - 1)
    def _():
        down.start()


def wait_halo(n, up, down, halo, edge):
    me = lax.axis_index("height")

    @pl.when(me > 0)
    def _():
        up.wait_send()
        down.wait_recv()

    @pl.when(me < n - 1)
    def _():
        down.wait_send()
        up.wait_recv()

    @pl.when(me == 0)
    def _():
        halo[0] = jnp.full(halo.shape[1:], edge, halo.dtype)

    @pl.when(me == n - 1)
    def _():
        halo[1] = jnp.full(halo.shape[1:], edge, halo.dtype)


def layout_call(n, dims, x, pick, spread, ids_px, ids_lane):
    canvases, rows, width = dims
    px = canvases * rows * width
    cells = px // UNIT
    stats = canvases * CROPS
    return pl.pallas_call(
        functools.partial(layout_kernel, n, dims),
        out_shape=[
            sds((n,) + ids_lane.shape, F32),
            sds((cells, C), F32),
            sds((cells, C), F32),
            sds((stats, LANES), F32),
            sds((stats, LANES), F32),
            sds((canvases, rows + 2, width, LANES), F32),
            sds((canvases, rows + 2, width, LANES), F32),
            sds((px, LANES), F32),
            sds((px, LANES), F32),
        ],
        in_specs=[vmem] * 5,
        out_specs=[vmem] * 9,
        scratch_shapes=[
            pltpu.VMEM((1, n, stats, LANES), F32),
            pltpu.VMEM((n,) + ids_lane.shape, F32),
            pltpu.VMEM((2, canvases, width, LANES), F32),
            pltpu.VMEM((cells, C), F32),
            pltpu.VMEM((cells, C), F32),
            pltpu.SemaphoreType.DMA((1, n)),
            pltpu.SemaphoreType.DMA((1, n)),
            pltpu.SemaphoreType.DMA((n,)),
            pltpu.SemaphoreType.DMA((n,)),
            pltpu.SemaphoreType.DMA((2,)),
            pltpu.SemaphoreType.DMA((2,)),
        ],
        compiler_params=params_of(1),
        name="layout",
    )(x, pick, spread, ids_px, ids_lane)


def resnet_forward_kernel(n, dims, keep, x, pick, spread, cnt, mean1, inv1, col_l, col_r, row_u, row_d,
                          vec, whole, *refs):
    canvases, rows, width = dims
    px = canvases * rows * width
    cells = px // UNIT
    plane = rows * width
    if keep:
        hid, u, y1, s1, s2, mean2, inv2, mean3, inv3 = refs[:9]
        refs = refs[9:]
    else:
        hid, u = refs[:2]
        y1, s1, s2, mean2, inv2, mean3, inv3 = refs[2:9]
        refs = refs[9:]
    k1, k2, halo, buf, tmp_a, tmp_b, ksem, send, recv, hsend, hrecv = refs
    load1 = pltpu.make_async_copy(whole.at[pl.ds(0, 9 * C)], k1, ksem.at[0])
    load2 = pltpu.make_async_copy(whole.at[pl.ds(9 * C, 9 * C)], k2, ksem.at[1])
    load1.start()
    load2.start()
    greet(n)
    row_cells = width // UNIT

    def activate(source, mean, inv, gain, bias, dest, rnd):
        def one(v, r):
            at = pl.ds(pl.multiple_of((v * rows + r) * width, width), width)
            cell = pl.ds(pl.multiple_of((v * rows + r) * row_cells, row_cells), row_cells)
            value = source[at, :].astype(F32)
            m = jnp.broadcast_to(mean[cell, :][:, None, :], (row_cells, UNIT, C)).reshape(width, C)
            s = jnp.broadcast_to(inv[cell, :][:, None, :], (row_cells, UNIT, C)).reshape(width, C)
            a = (value - m) * s * gain + bias
            dest[v, r + 1] = shift_columns(silu(a), col_l[v, r + 1], col_r[v, r + 1])

        def edges(v, _):
            one(v, 0)
            if rows > 1:
                one(v, rows - 1)
            return 0

        lax.fori_loop(0, canvases, edges, 0)
        mid = pl.ds(C, C)
        up, down = halo_copies(n, dest.at[:, 1, :, mid], dest.at[:, rows, :, mid], halo.at[rnd],
                               hsend.at[rnd], hrecv.at[rnd])
        start_halo(n, up, down)

        def inner(i, _):
            one(i // (rows - 2), 1 + lax.rem(i, rows - 2))
            return 0

        if rows > 2:
            lax.fori_loop(0, canvases * (rows - 2), inner, 0)
        wait_halo(n, up, down, halo.at[rnd], 0.0)
        for v in range(canvases):
            for side, r in ((0, 0), (1, rows + 1)):
                dest[v, r] = shift_columns(halo[rnd, side, v].astype(F32), col_l[v, r], col_r[v, r])

    def convolve(source, weight, emit):
        def body(v, _):
            at = pl.ds(pl.multiple_of(v * plane, plane), plane)
            total = None
            for dr in (1, 0, 2):
                lhs = source[v, dr : dr + rows].reshape(plane, 3 * C)
                part = jnp.dot(lhs, weight[3 * C * dr : 3 * C * (dr + 1), :],
                               preferred_element_type=F32)
                if dr == 0:
                    part = part * wide(row_u[at, :])
                if dr == 2:
                    part = part * wide(row_d[at, :])
                total = part if total is None else total + part
            emit(at, total)
            return 0

        lax.fori_loop(0, canvases, body, 0)

    def statistics(source, mean, inv, rnd):
        def load(i):
            return source[pl.ds(i * 16 * UNIT, 16 * UNIT), :]

        buf[rnd, 0] = stats_payload(load, pick, spread, cnt, cells, tmp_a, tmp_b)
        copies = spread_copies(n, buf, send, recv, rnd)
        for cp in copies:
            cp.start()
        for cp in copies:
            cp.wait_recv()
        m, s, _ = combine_stats(buf[rnd])
        mean[...] = split_dot(spread[...], unpack(m))
        inv[...] = split_dot(spread[...], unpack(s))
        return copies

    activate(x, mean1, inv1, vec[0:1, :], vec[1:2, :], s1, 0)
    load1.wait()

    def emit_first(at, total):
        y1[at, :] = total + vec[2:3, :]

    convolve(s1, k1, emit_first)
    sent = statistics(y1, mean2, inv2, 0)
    activate(y1, mean2, inv2, vec[3:4, :], vec[4:5, :], s2, 1)
    load2.wait()

    def emit_second(at, total):
        hid[at, :] = total + vec[5:6, :] + x[at, :].astype(F32)

    convolve(s2, k2, emit_second)
    sent = sent + statistics(hid, mean3, inv3, 1)
    gain3, bias3 = vec[6:7, :], vec[7:8, :]

    def last(i, _):
        at = pl.ds(i * 16 * UNIT, 16 * UNIT)
        value = (hid[at, :] - over_cells(mean3, i)) * over_cells(inv3, i)
        u[at, :] = (value * gain3 + bias3).astype(B16)
        return 0

    lax.fori_loop(0, cells // 16, last, 0)
    for cp in sent:
        cp.wait_send()


def resnet_forward_call(n, dims, keep, x, pick, spread, cnt, mean1, inv1, masks, vec, whole):
    canvases, rows, width = dims
    px = canvases * rows * width
    cells = px // UNIT
    stats = canvases * CROPS
    saved = [
        ((px, C), F32),
        ((canvases, rows + 2, width, 3 * C), B16),
        ((canvases, rows + 2, width, 3 * C), B16),
        ((cells, C), F32),
        ((cells, C), F32),
        ((cells, C), F32),
        ((cells, C), F32),
    ]
    main = [((px, C), F32), ((px, C), B16)]
    outs = main + (saved if keep else [])
    scratch = [] if keep else [pltpu.VMEM(*s) for s in saved]
    return pl.pallas_call(
        functools.partial(resnet_forward_kernel, n, dims, keep),
        out_shape=[sds(*s) for s in outs],
        in_specs=[vmem] * 11 + [anyw],
        out_specs=[vmem] * len(outs),
        scratch_shapes=scratch
        + [
            pltpu.VMEM((9 * C, C), B16),
            pltpu.VMEM((9 * C, C), B16),
            pltpu.VMEM((2, 2, canvases, width, C), B16),
            pltpu.VMEM((2, n, stats, LANES), F32),
            pltpu.VMEM((cells, C), F32),
            pltpu.VMEM((cells, C), F32),
            pltpu.SemaphoreType.DMA((2,)),
            pltpu.SemaphoreType.DMA((2, n)),
            pltpu.SemaphoreType.DMA((2, n)),
            pltpu.SemaphoreType.DMA((2, 2)),
            pltpu.SemaphoreType.DMA((2, 2)),
        ],
        compiler_params=params_of(2 if keep else 3),
        name="resnet_forward" if keep else "resnet_again",
    )(x, pick, spread, cnt, mean1, inv1, *masks, vec, whole)


def attention_kernel(keep, chunk, block, ua, key_ids, query_ids, offsets, dz, vec, whole, *refs):
    total = ua.shape[0] * ua.shape[1]
    queries = query_ids.shape[0]
    segment = ua.shape[1]
    scale = C ** (-0.5)
    if keep:
        out, dup, dw, dvec = refs[:4]
        u, w, k, v, pbuf, sbuf, q, dout, dq, usem, wsem = refs[4:]
    else:
        out = refs[0]
        u, w, k, v, usem, wsem = refs[1:]
    load_w = pltpu.make_async_copy(whole.at[pl.ds(18 * C, 4 * C)], w, wsem.at[0])
    load_w.start()
    blocks = ua.shape[0]
    loads = [
        pltpu.make_async_copy(ua.at[i], u.at[pl.ds(i * segment, segment)], usem.at[i])
        for i in range(blocks)
    ]
    for cp in loads:
        cp.start()
    load_w.wait()
    for cp in loads:
        cp.wait()
    nt = (((1,), (1,)), ((), ()))
    tn = (((0,), (0,)), ((), ()))

    def project(i, _):
        at = pl.ds(pl.multiple_of(i * chunk, chunk), chunk)
        piece = u[at, :]
        k[at, :] = jnp.dot(piece, w[C : 2 * C, :], preferred_element_type=F32).astype(B16)
        v[at, :] = (
            jnp.dot(piece, w[2 * C : 3 * C, :], preferred_element_type=F32) + vec[9:10, :]
        ).astype(B16)
        return 0

    lax.fori_loop(0, total // chunk, project, 0)
    per = segment // block

    def place(i):
        return pl.multiple_of(offsets[i // per] + lax.rem(i, per) * block, block)

    def attend(i, _):
        at = pl.ds(pl.multiple_of(i * block, block), block)
        uq = u[pl.ds(place(i), block), :]
        qb = (
            jnp.dot(uq, w[0:C, :], preferred_element_type=F32) + vec[8:9, :]
        ).astype(B16)
        s = lax.dot_general(qb, k[...], nt, preferred_element_type=F32) * scale
        s = jnp.where(query_ids[at, :][:, :1] == key_ids[...], s, mask_fill)
        e = jnp.exp(s - jnp.max(s, axis=1, keepdims=True))
        p = e * (1.0 / jnp.sum(e, axis=1, keepdims=True))
        pb = p.astype(B16)
        ob = jnp.dot(pb, v[...], preferred_element_type=F32).astype(B16)
        out[at, :] = ob
        if keep:
            pbuf[at, :] = pb
            q[at, :] = qb
            do = lax.dot_general(
                dz[at, :], w[3 * C : 4 * C, :], nt, preferred_element_type=F32
            ).astype(B16)
            dout[at, :] = do
            dp = lax.dot_general(do, v[...], nt, preferred_element_type=F32)
            delta = jnp.sum(p * dp, axis=1, keepdims=True)
            ds = (p * (dp - delta)).astype(B16)
            sbuf[at, :] = ds
            dq[at, :] = (jnp.dot(ds, k[...], preferred_element_type=F32) * scale).astype(B16)
        return 0

    lax.fori_loop(0, queries // block, attend, 0)
    if not keep:
        return
    zero = jnp.zeros((C, C), F32)

    def back(i, carry):
        dwk, dwv, dbv = carry
        at = pl.ds(pl.multiple_of(i * chunk, chunk), chunk)
        dk = (
            lax.dot_general(sbuf[:, at], q[...], tn, preferred_element_type=F32) * scale
        ).astype(B16)
        dvf = lax.dot_general(pbuf[:, at], dout[...], tn, preferred_element_type=F32)
        dv = dvf.astype(B16)
        du = lax.dot_general(dk, w[C : 2 * C, :], nt, preferred_element_type=F32)
        du = du + lax.dot_general(dv, w[2 * C : 3 * C, :], nt, preferred_element_type=F32)
        dup[at, :] = du.astype(B16)
        piece = u[at, :]
        dwk = dwk + lax.dot_general(piece, dk, tn, preferred_element_type=F32)
        dwv = dwv + lax.dot_general(piece, dv, tn, preferred_element_type=F32)
        return dwk, dwv, dbv + jnp.sum(dvf, axis=0, keepdims=True)

    dwk, dwv, dbv = lax.fori_loop(0, total // chunk, back, (zero, zero, jnp.zeros((1, C), F32)))
    dw[C : 2 * C, :] = dwk.astype(B16)
    dw[2 * C : 3 * C, :] = dwv.astype(B16)
    dw[3 * C : 4 * C, :] = lax.dot_general(
        out[...], dz[...], tn, preferred_element_type=F32
    ).astype(B16)
    dwq = zero
    for s in range(2):
        where = pl.ds(pl.multiple_of(offsets[s], segment), segment)
        at = pl.ds(s * segment, segment)
        dwq = dwq + lax.dot_general(u[where, :], dq[at, :], tn, preferred_element_type=F32)
        du = lax.dot_general(dq[at, :], w[0:C, :], nt, preferred_element_type=F32)
        dup[where, :] = (dup[where, :].astype(F32) + du).astype(B16)
    dw[0:C, :] = dwq.astype(B16)
    dvec[...] = jnp.concatenate(
        [
            jnp.sum(dq[...].astype(F32), axis=0, keepdims=True),
            dbv,
            jnp.sum(dz[...].astype(F32), axis=0, keepdims=True),
            jnp.zeros((5, C), F32),
        ],
        axis=0,
    )


def attention_call(keep, ua, key_ids, query_ids, offsets, dz, vec, whole):
    blocks, segment, _ = ua.shape
    total = blocks * segment
    queries = query_ids.shape[0]
    block = min(256, segment)
    chunk = 512
    outs = [sds((queries, C), B16)]
    scratch = [
        pltpu.VMEM((total, C), B16),
        pltpu.VMEM((4 * C, C), B16),
        pltpu.VMEM((total, C), B16),
        pltpu.VMEM((total, C), B16),
    ]
    if keep:
        outs += [sds((total, C), B16), sds((4 * C, C), B16), sds((8, C), F32)]
        scratch += [
            pltpu.VMEM((queries, total), B16),
            pltpu.VMEM((queries, total), B16),
            pltpu.VMEM((queries, C), B16),
            pltpu.VMEM((queries, C), B16),
            pltpu.VMEM((queries, C), B16),
        ]
    return pl.pallas_call(
        functools.partial(attention_kernel, keep, chunk, block),
        out_shape=outs,
        in_specs=[anyw, vmem, vmem, smem, vmem, vmem, anyw],
        out_specs=[vmem] * len(outs),
        scratch_shapes=scratch
        + [pltpu.SemaphoreType.DMA((blocks,)), pltpu.SemaphoreType.DMA((1,))],
        compiler_params=params_of(),
        name="attention" if keep else "attention_again",
    )(ua, key_ids, query_ids, offsets, dz, vec, whole)


def other_core(h):
    return h + 1 - 2 * lax.rem(h, 2)


def gather_kernel(n, u, ua, lsem, send, recv):
    me = lax.axis_index("height")
    half = n // 2
    mine = me // half
    base = mine * half
    core = lax.rem(me, 2)
    partner = lax.rem(me + half, n)
    sibling = other_core(me)
    mates = half // 2
    seat = (me - base) // 2

    def mate(j):
        return base + core + 2 * lax.rem(seat + j, mates)

    barrier = pltpu.get_barrier_semaphore()
    peers = [partner, sibling] + [mate(j) for j in range(1, mates)]
    for p in peers:
        pl.semaphore_signal(barrier, inc=1, device_id={"height": p}, device_id_type=MESH)
    pl.semaphore_wait(barrier, len(peers))
    count = [0]
    started = []

    def push(src, slot, to):
        cp = pltpu.make_async_remote_copy(
            src_ref=src, dst_ref=ua.at[slot], send_sem=send.at[count[0]], recv_sem=recv.at[slot],
            device_id={"height": to}, device_id_type=MESH)
        count[0] += 1
        cp.start()
        started.append(cp)

    def arrived(slot):
        pltpu.make_async_remote_copy(
            src_ref=u.at[0], dst_ref=ua.at[slot], send_sem=send.at[0], recv_sem=recv.at[slot],
            device_id={"height": partner}, device_id_type=MESH).wait_recv()

    own = pltpu.make_async_copy(u.at[mine], ua.at[me], lsem.at[0])
    own.start()
    push(u.at[1 - mine], me, partner)
    for j in range(1, mates):
        push(u.at[mine], me, mate(j))
    push(u.at[mine], me, sibling)
    arrived(partner)
    for j in range(1, mates):
        push(ua.at[partner], partner, mate(j))
    push(ua.at[partner], partner, sibling)
    for j in range(1, mates):
        friend = base + core + 2 * lax.rem(seat + mates - j, mates)
        far = lax.rem(friend + half, n)
        arrived(friend)
        push(ua.at[friend], friend, sibling)
        arrived(far)
        push(ua.at[far], far, sibling)
    arrived(sibling)
    arrived(lax.rem(sibling + half, n))
    for j in range(1, mates):
        friend = base + (1 - core) + 2 * lax.rem(seat + mates - j, mates)
        arrived(friend)
        arrived(lax.rem(friend + half, n))
    own.wait()
    for cp in started:
        cp.wait_send()


def gather_call(n, cid, u):
    half = n // 2
    sends = 2 * (half // 2) + 1 + 2 * (half // 2 - 1) + 1
    return pl.pallas_call(
        functools.partial(gather_kernel, n),
        out_shape=sds((n,) + u.shape[1:], B16),
        in_specs=[anyw],
        out_specs=anyw,
        scratch_shapes=[
            pltpu.SemaphoreType.DMA((1,)),
            pltpu.SemaphoreType.DMA((sends,)),
            pltpu.SemaphoreType.DMA((n,)),
        ],
        compiler_params=params_of(cid),
        name="gather_u",
    )(u)


def scatter_kernel(n, dup, out, from_sib, from_mate, mine_sum, from_partner, lsem, send, recv):
    me = lax.axis_index("height")
    half = n // 2
    mine = me // half
    base = mine * half
    core = lax.rem(me, 2)
    partner = lax.rem(me + half, n)
    sibling = other_core(me)
    mates = half // 2
    seat = (me - base) // 2
    barrier = pltpu.get_barrier_semaphore()

    def mate(j, c=core):
        return base + c + 2 * lax.rem(seat + j, mates)

    peers = [partner, sibling] + [mate(j) for j in range(1, mates)]
    for p in peers:
        pl.semaphore_signal(barrier, inc=1, device_id={"height": p}, device_id_type=MESH)
    pl.semaphore_wait(barrier, len(peers))
    order = [(j, far) for j in range(1, mates) for far in (1, 0)] + [(0, 1), (0, 0)]

    def rows_of(j, far, c):
        owner = mate(j, c)
        return lax.rem(owner + half, n) if far else owner

    sib = []
    for t, (j, far) in enumerate(order):
        cp = pltpu.make_async_remote_copy(
            src_ref=dup.at[rows_of(j, far, 1 - core)], dst_ref=from_sib.at[t],
            send_sem=send.at[t], recv_sem=recv.at[t],
            device_id={"height": sibling}, device_id_type=MESH)
        cp.start()
        sib.append(cp)
    base_sem = len(order)
    out_copies = []
    for t, (j, far) in enumerate(order):
        sib[t].wait_recv()
        block = rows_of(j, far, core)
        if j > 0:
            mine_sum[t] = (dup[block].astype(F32) + from_sib[t].astype(F32)).astype(B16)
            at = (j - 1) * 2 + far
            cp = pltpu.make_async_remote_copy(
                src_ref=mine_sum.at[t], dst_ref=from_mate.at[at],
                send_sem=send.at[base_sem + at], recv_sem=recv.at[base_sem + at],
                device_id={"height": mate(j)}, device_id_type=MESH)
            cp.start()
            out_copies.append(cp)
    t_far, t_own = len(order) - 2, len(order) - 1
    total = dup[partner].astype(F32) + from_sib[t_far].astype(F32)
    for j in range(1, mates):
        at = (j - 1) * 2 + 1
        pltpu.make_async_remote_copy(
            src_ref=mine_sum.at[0], dst_ref=from_mate.at[at], send_sem=send.at[0],
            recv_sem=recv.at[base_sem + at], device_id={"height": sibling},
            device_id_type=MESH).wait_recv()
        total = total + from_mate[at].astype(F32)
    mine_sum[t_far] = total.astype(B16)
    last = base_sem + 2 * (mates - 1)
    home = pltpu.make_async_remote_copy(
        src_ref=mine_sum.at[t_far], dst_ref=from_partner, send_sem=send.at[last],
        recv_sem=recv.at[last], device_id={"height": partner}, device_id_type=MESH)
    home.start()
    total = dup[me].astype(F32) + from_sib[t_own].astype(F32)
    for j in range(1, mates):
        at = (j - 1) * 2
        pltpu.make_async_remote_copy(
            src_ref=mine_sum.at[0], dst_ref=from_mate.at[at], send_sem=send.at[0],
            recv_sem=recv.at[base_sem + at], device_id={"height": sibling},
            device_id_type=MESH).wait_recv()
        total = total + from_mate[at].astype(F32)
    out[mine] = total
    home.wait_recv()
    out[1 - mine] = from_partner[...].astype(F32)
    for cp in sib + out_copies + [home]:
        cp.wait_send()


def scatter_call(n, cid, dup):
    half = n // 2
    mates = half // 2
    copies = 2 * mates + 2 * (mates - 1) + 1
    seg = dup.shape[1:]
    return pl.pallas_call(
        functools.partial(scatter_kernel, n),
        out_shape=sds((2,) + seg, F32),
        in_specs=[vmem],
        out_specs=vmem,
        scratch_shapes=[
            pltpu.VMEM((2 * mates,) + seg, B16),
            pltpu.VMEM((max(2 * (mates - 1), 1),) + seg, B16),
            pltpu.VMEM((2 * mates,) + seg, B16),
            pltpu.VMEM(seg, B16),
            pltpu.SemaphoreType.DMA((1,)),
            pltpu.SemaphoreType.DMA((copies,)),
            pltpu.SemaphoreType.DMA((copies,)),
        ],
        compiler_params=params_of(cid),
        name="scatter_du",
    )(dup)


def resnet_backward_kernel(n, dims, cot, du, hid, y1, x, mean1, inv1, mean2, inv2, mean3, inv3, s1, s2, pick,
                           spread, div, col_l, col_r, row_u, row_d, vec, whole, datt, igrad, grads, dvec,
                           dw1, dw2, k, dh, d3, low, low_u, low_d, part, norm, halo, buf, tmp_a, tmp_b, ksem, send,
                           recv, hsend, hrecv):
    canvases, rows, width = dims
    px = canvases * rows * width
    cells = px // UNIT
    plane = rows * width
    nt = (((1,), (1,)), ((), ()))
    tn = (((0,), (0,)), ((), ()))
    load2 = pltpu.make_async_copy(whole.at[pl.ds(9 * C, 9 * C)], k, ksem.at[0])
    load1 = pltpu.make_async_copy(whole.at[pl.ds(0, 9 * C)], k, ksem.at[1])
    load2.start()
    out_att = pltpu.make_async_copy(datt, grads.at[pl.ds(18 * C, 4 * C)], ksem.at[2])
    out_two = pltpu.make_async_copy(dw2, grads.at[pl.ds(9 * C, 9 * C)], ksem.at[3])
    out_one = pltpu.make_async_copy(dw1, grads.at[pl.ds(0, 9 * C)], ksem.at[4])
    out_att.start()
    greet(n)
    zero_row = jnp.zeros((1, C), F32)

    def pixels(i):
        return pl.ds(i * 16 * UNIT, 16 * UNIT)

    def norm_sums(grad_of, source, mean, inv, gain):
        def body(i, carry):
            dg, db = carry
            at = pixels(i)
            unit = (source[at, :].astype(F32) - over_cells(mean, i)) * over_cells(inv, i)
            d = grad_of(i, unit)
            norm[at, :] = unit
            e = d * gain
            part[at, :] = e
            cross = d * unit
            here = pl.ds(i * 16, 16)
            tmp_a[here, :] = jnp.sum(e.reshape(16, UNIT, C), axis=1)
            tmp_b[here, :] = jnp.sum((cross * gain).reshape(16, UNIT, C), axis=1)
            return (dg + jnp.sum(cross, axis=0, keepdims=True), db + jnp.sum(d, axis=0, keepdims=True))

        dg, db = lax.fori_loop(0, cells // 16, body, (zero_row, zero_row))
        packed = pack([group_totals(pick, tmp_a[...]), group_totals(pick, tmp_b[...])])
        return packed, dg, db

    def send_sums(packed, rnd):
        buf[rnd, 0] = packed
        copies = spread_copies(n, buf, send, recv, rnd)
        for cp in copies:
            cp.start()
        return copies

    def norm_finish(copies, rnd, inv, emit):
        for cp in copies:
            cp.wait_recv()
        gathered = jnp.sum(buf[rnd], axis=0) / div[...]
        tmp_a[...] = split_dot(spread[...], unpack(gathered))
        tmp_b[...] = split_dot(spread[...], unpack(shift_down(gathered, 1)))

        def body(i, _):
            at = pixels(i)
            emit(i, over_cells(inv, i) * (part[at, :] - over_cells(tmp_a, i) - norm[at, :] * over_cells(tmp_b, i)))
            return 0

        lax.fori_loop(0, cells // 16, body, 0)

    def spread_rows(rnd):
        def row_at(v, r):
            return pl.ds(pl.multiple_of((v * rows + r) * width, width), width)

        def one(i, _):
            v, r = i // rows, lax.rem(i, rows)
            d3[v, r + 1] = shift_columns(low[row_at(v, r), :].astype(F32), col_l[v, r + 1], col_r[v, r + 1])
            return 0

        lax.fori_loop(0, canvases * rows, one, 0)
        mid = pl.ds(C, C)
        up, down = halo_copies(n, d3.at[:, 1, :, mid], d3.at[:, rows, :, mid], halo.at[rnd],
                               hsend.at[rnd], hrecv.at[rnd])
        start_halo(n, up, down)
        return up, down

    def finish_rows(up, down, rnd):
        wait_halo(n, up, down, halo.at[rnd], 0.0)
        for v in range(canvases):
            for side, r in ((0, 0), (1, rows + 1)):
                d3[v, r] = shift_columns(halo[rnd, side, v].astype(F32), col_l[v, r], col_r[v, r])

    def convolve_back(emit):
        def body(v, _):
            at = pl.ds(pl.multiple_of(v * plane, plane), plane)
            total = None
            for dr in (1, 0, 2):
                acc = None
                for dc in range(3):
                    tap = 3 * (2 - dr) + (2 - dc)
                    lhs = d3[v, dr : dr + rows, :, dc * C : (dc + 1) * C].reshape(plane, C)
                    term = lax.dot_general(lhs, k[tap * C : (tap + 1) * C, :], nt, preferred_element_type=F32)
                    acc = term if acc is None else acc + term
                if dr == 0:
                    acc = acc * wide(row_u[at, :])
                if dr == 2:
                    acc = acc * wide(row_d[at, :])
                total = acc if total is None else total + acc
            emit(at, total)
            return 0

        lax.fori_loop(0, canvases, body, 0)

    def mask_rows():
        def body(i, _):
            at = pixels(i)
            value = low[at, :].astype(F32)
            low_u[at, :] = (value * wide(row_u[at, :])).astype(B16)
            low_d[at, :] = (value * wide(row_d[at, :])).astype(B16)
            return 0

        lax.fori_loop(0, cells // 16, body, 0)

    def weight_grad(source, dest):
        for dr, grad in ((0, low_u), (1, low), (2, low_d)):
            def body(dc, _):
                acc = None
                for v in range(canvases):
                    lhs = source[v, dr : dr + rows, :, pl.ds(pl.multiple_of(dc * C, C), C)].reshape(plane, C)
                    term = lax.dot_general(
                        lhs, grad[v * plane : (v + 1) * plane, :], tn, preferred_element_type=F32)
                    acc = term if acc is None else acc + term
                dest[pl.ds(pl.multiple_of((3 * dr + dc) * C, C), C), :] = acc.astype(B16)
                return 0

            lax.fori_loop(0, 3, body, 0)

    packed, dg3, db3 = norm_sums(lambda i, unit: du[pixels(i), :], hid, mean3, inv3, vec[6:7, :])
    sent = send_sums(packed, 0)

    def emit_hidden(i, value):
        at = pixels(i)
        total = cot[at, :].astype(F32) + value
        dh[at, :] = total
        low[at, :] = total.astype(B16)

    norm_finish(sent, 0, inv3, emit_hidden)
    up, down = spread_rows(0)
    mask_rows()
    dc2 = jnp.sum(low[...].astype(F32), axis=0, keepdims=True)
    finish_rows(up, down, 0)
    load2.wait()

    def emit_part(at, total):
        part[at, :] = total

    convolve_back(emit_part)
    load1.start()
    gain2, bias2 = vec[3:4, :], vec[4:5, :]

    def grad_two(i, unit):
        return part[pixels(i), :] * silu_slope(unit * gain2 + bias2)

    packed, dg2, db2 = norm_sums(grad_two, y1, mean2, inv2, gain2)
    more = send_sums(packed, 1)
    weight_grad(s2, dw2)
    out_two.start()

    def emit_low(i, value):
        low[pixels(i), :] = value.astype(B16)

    norm_finish(more, 1, inv2, emit_low)
    sent = sent + more
    up, down = spread_rows(1)
    mask_rows()
    dc1 = jnp.sum(low[...].astype(F32), axis=0, keepdims=True)
    weight_grad(s1, dw1)
    out_one.start()
    finish_rows(up, down, 1)
    load1.wait()
    convolve_back(emit_part)
    gain1, bias1 = vec[0:1, :], vec[1:2, :]

    def grad_one(i, unit):
        return part[pixels(i), :] * silu_slope(unit * gain1 + bias1)

    packed, dg1, db1 = norm_sums(grad_one, x, mean1, inv1, gain1)
    more = send_sums(packed, 2)
    dvec[...] = jnp.concatenate([dg1, db1, dc1, dg2, db2, dc2, dg3, db3], axis=0)

    def emit_input(i, value):
        igrad[pixels(i), :] = dh[pixels(i), :] + value

    norm_finish(more, 2, inv1, emit_input)
    sent = sent + more
    out_att.wait()
    out_two.wait()
    out_one.wait()
    for cp in sent:
        cp.wait_send()


def resnet_backward_call(n, dims, cid, cot, du, hid, y1, x, norms, s1, s2, pick, spread, div, masks, vec, whole,
                         datt):
    canvases, rows, width = dims
    px = canvases * rows * width
    cells = px // UNIT
    stats = canvases * CROPS
    return pl.pallas_call(
        functools.partial(resnet_backward_kernel, n, dims),
        out_shape=[sds((px, C), F32), sds((22 * C, C), B16), sds((8, C), F32)],
        in_specs=[vmem] * 21 + [anyw, anyw],
        out_specs=[vmem, anyw, vmem],
        scratch_shapes=[
            pltpu.VMEM((9 * C, C), B16),
            pltpu.VMEM((9 * C, C), B16),
            pltpu.VMEM((9 * C, C), B16),
            pltpu.VMEM((px, C), F32),
            pltpu.VMEM((canvases, rows + 2, width, 3 * C), B16),
            pltpu.VMEM((px, C), B16),
            pltpu.VMEM((px, C), B16),
            pltpu.VMEM((px, C), B16),
            pltpu.VMEM((px, C), F32),
            pltpu.VMEM((px, C), F32),
            pltpu.VMEM((2, 2, canvases, width, C), B16),
            pltpu.VMEM((3, n, stats, LANES), F32),
            pltpu.VMEM((cells, C), F32),
            pltpu.VMEM((cells, C), F32),
            pltpu.SemaphoreType.DMA((5,)),
            pltpu.SemaphoreType.DMA((3, n)),
            pltpu.SemaphoreType.DMA((3, n)),
            pltpu.SemaphoreType.DMA((2, 2)),
            pltpu.SemaphoreType.DMA((2, 2)),
        ],
        compiler_params=params_of(cid),
        name="resnet_backward",
    )(cot, du, hid, y1, x, *norms, s1, s2, pick, spread, div, *masks, vec, whole, datt)


class Grid:
    def __init__(self, columns, n):
        self.columns, self.n, self.seats = columns, n, n // 2
        self.phases = columns.bit_length() - 1
        self.c = lax.axis_index("canvas")
        self.h = lax.axis_index("height")
        self.seat, self.core = self.h // 2, lax.rem(self.h, 2)
        flips = [
            (1 - 2 * lax.rem(self.c // 2**t, 2)) * 2**t for t in range(self.phases)
        ]
        last = self.phases - 1
        self.flips = [
            (1 - self.core) * flips[last - k] + self.core * flips[k] for k in range(self.phases)
        ]
        self.other_flips = [
            self.core * flips[last - k] + (1 - self.core) * flips[k] for k in range(self.phases)
        ]

    def column(self, e, flips=None):
        flips = self.flips if flips is None else flips
        col = self.c
        for k in range(self.phases):
            if (e >> k) & 1:
                col = col + flips[k]
        return col

    def mate(self, k):
        return {"canvas": self.c + self.flips[k], "height": self.h}

    def sibling(self):
        return {"canvas": self.c, "height": 2 * self.seat + 1 - self.core}

    def beside(self, step):
        return {"canvas": self.c, "height": self.h + 2 * step}

    def greet(self):
        barrier = pltpu.get_barrier_semaphore()
        for d in range(1, self.n):
            pl.semaphore_signal(
                barrier, inc=1, device_id={"canvas": self.c, "height": lax.rem(self.h + d, self.n)},
                device_id_type=MESH)
        for k in range(self.phases):
            pl.semaphore_signal(barrier, inc=1, device_id=self.mate(k), device_id_type=MESH)
        pl.semaphore_wait(barrier, self.n - 1 + self.phases)


def remote(src, dst, send, recv, to):
    return pltpu.make_async_remote_copy(
        src_ref=src, dst_ref=dst, send_sem=send, recv_sem=recv, device_id=to, device_id_type=MESH)


def lowest_bit(e):
    return (e & -e).bit_length() - 1


def spread_blocks(grid, fresh, whole, own_sem, zsend, msend, ssend, recv, srecv):
    g = grid
    seats, phases = g.seats, g.phases
    own = pltpu.make_async_copy(fresh, whole.at[g.c, g.seat, g.core], own_sem)
    own.start()

    def slot(e, seat):
        return whole.at[g.column(e), seat, g.core]

    def forward(e, seat, src, start):
        k_top = phases if e == 0 else lowest_bit(e)
        for k in range(k_top - 1, -1, -1):
            cp = remote(src, slot(e, seat), msend.at[k, e, seat], recv.at[e | (1 << k), seat], g.mate(k))
            cp.start() if start else cp.wait_send()
        cp = remote(src, slot(e, seat), ssend.at[e, seat], srecv.at[e, seat], g.sibling())
        cp.start() if start else cp.wait_send()

    def along(seat, step, src, start):
        cp = remote(src, slot(0, seat), zsend.at[(step + 1) // 2, seat], recv.at[0, seat], g.beside(step))
        cp.start() if start else cp.wait_send()

    def line(seat, src, start):
        @pl.when((seat <= g.seat) & (g.seat < seats - 1))
        def _():
            along(seat, 1, src, start)

        @pl.when((seat >= g.seat) & (g.seat > 0))
        def _():
            along(seat, -1, src, start)

    def arrive(e, seat):
        remote(fresh, slot(e, seat), ssend.at[0, 0], recv.at[e, seat], g.sibling()).wait_recv()

    early = [e for e in range(1, 2**phases) if lowest_bit(e) > 0]
    early.sort(key=lambda e: -lowest_bit(e))
    late = [e for e in range(1, 2**phases) if lowest_bit(e) == 0]

    def handle(e, seat):
        arrive(e, seat)
        if e == 0:
            line(seat, slot(0, seat), True)
        forward(e, seat, slot(e, seat), True)

    def both_sides(d, todo):
        for side in (-1, 1):
            seat = g.seat + side * d

            @pl.when((seat >= 0) & (seat < seats))
            def _():
                for e in todo:
                    handle(e, seat)

    line(g.seat, fresh, True)
    forward(0, g.seat, fresh, True)
    for e in early:
        handle(e, g.seat)

    def further(d, _):
        both_sides(d, [0] + early)
        return 0

    lax.fori_loop(1, seats, further, 0)
    for e in late:
        handle(e, g.seat)

    def finish(d, _):
        both_sides(d, late)
        return 0

    lax.fori_loop(1, seats, finish, 0)

    def drain(seat, _):
        for e in range(2**phases):
            remote(fresh, whole.at[g.column(e, g.other_flips), seat, 1 - g.core], ssend.at[0, 0],
                   srecv.at[e, seat], g.sibling()).wait_recv()
            forward(e, seat, slot(e, seat), False)
        line(seat, slot(0, seat), False)
        return 0

    lax.fori_loop(0, seats, drain, 0)
    own.wait()


def spread_scratch(columns, n):
    seats, phases = n // 2, columns.bit_length() - 1
    dma = pltpu.SemaphoreType.DMA
    return [
        dma((1,)),
        dma((2, seats)),
        dma((phases, columns, seats)),
        dma((columns, seats)),
        dma((columns, seats)),
        dma((columns, seats)),
    ]


def spread_kernel(columns, n, block, whole, fresh, own, zsend, msend, ssend, recv, srecv):
    grid = Grid(columns, n)
    fresh[...] = block[...].astype(B16)
    grid.greet()
    spread_blocks(grid, fresh, whole, own.at[0], zsend, msend, ssend, recv, srecv)


def spread_call(columns, n, cid, block):
    return pl.pallas_call(
        functools.partial(spread_kernel, columns, n),
        out_shape=sds((columns, n // 2, 2) + block.shape, B16),
        in_specs=[vmem],
        out_specs=anyw,
        scratch_shapes=[pltpu.VMEM(block.shape, B16)] + spread_scratch(columns, n),
        compiler_params=params_of(cid),
        name="spread_weights",
    )(block)


def adam_update(current, gradient, moment_one, moment_two, learn_rate):
    first_new = 0.5 * moment_one + 0.5 * gradient
    second_new = 0.9 * moment_two + 0.1 * gradient * gradient
    first_hat = first_new / (1.0 - 0.5**STEP)
    second_hat = second_new / (1.0 - 0.9**STEP)
    return (
        current - learn_rate * first_hat / (jnp.sqrt(second_hat) + adam_epsilon),
        first_new,
        second_new,
    )


def step_kernel(columns, n, grads, w, m, s, dvec, vw, vm, vs, new_w, new_m, new_s, new_vw, new_vm, new_vs, whole,
                acc, sib, got, up, down, fresh, vbuf, vtrade, lsem, gsend, grecv, psend, precv, usend, urecv,
                vsend, vrecv, tsend, trecv, own, zsend, msend, ssend, recv, srecv):
    g = Grid(columns, n)
    seats, phases = g.seats, g.phases
    slots = 2**phases
    order = sorted(range(slots), key=lambda e: (lowest_bit(e) if e else phases, e == (e & -e)))
    loads = []
    for e in order:
        cp = pltpu.make_async_copy(grads.at[g.column(e), :, g.core], acc.at[e], lsem.at[e])
        cp.start()
        loads.append(cp)

    @pl.when(g.seat == 0)
    def _():
        up[...] = jnp.zeros(up.shape, B16)

    @pl.when(g.seat == seats - 1)
    def _():
        down[...] = jnp.zeros(down.shape, B16)

    vbuf[g.h] = dvec[...]
    g.greet()
    sib_copies = []
    for e in order:
        cp = remote(grads.at[g.column(e, g.other_flips), :, 1 - g.core], sib.at[e], gsend.at[e], grecv.at[e],
                    g.sibling())
        cp.start()
        sib_copies.append(cp)

    def vector_copy(d):
        src = lax.rem(g.h + d, n)
        return remote(vbuf.at[g.h], vbuf.at[g.h], vsend.at[d], vrecv.at[g.h],
                      {"canvas": g.c, "height": src})

    def vector_arrival(d):
        src = lax.rem(g.h + d, n)
        return remote(vbuf.at[src], vbuf.at[src], vsend.at[d], vrecv.at[src],
                      {"canvas": g.c, "height": src})

    for d in range(1, n):
        vector_copy(d).start()

    def local(e, seat, below):
        total = acc[e, seat].astype(F32) + sib[e, seat].astype(F32)
        for k in range(below):
            total = total + got[k, e >> (k + 1), seat].astype(F32)
        return total

    def in_turn(i):
        even = 1 - lax.rem(i, 2)
        return (i // 2) * even + (1 - even) * (seats - 1 - i // 2)

    def phase_copy(k, e, seat):
        return remote(acc.at[e, seat], got.at[k, e >> (k + 1), seat], psend.at[k, e >> (k + 1), seat],
                      precv.at[k, e >> (k + 1), seat], g.mate(k))

    ready = 0
    for e in order:
        loads[ready].wait()
        sib_copies[ready].wait_recv()
        ready += 1
        if e == 0:
            break
        k = lowest_bit(e)

        def one(i, _):
            seat = in_turn(i)
            for q in range(k):
                phase_copy(q, e | (1 << q), seat).wait_recv()
            acc[e, seat] = local(e, seat, k).astype(B16)
            phase_copy(k, e, seat).start()
            return 0

        lax.fori_loop(0, seats, one, 0)

    for d in range(1, n):
        vector_arrival(d).wait_recv()
    vtrade[0, 0] = jnp.sum(vbuf[...], axis=0)
    for k in range(phases):
        cp = remote(vtrade.at[k, 0], vtrade.at[k, 1], tsend.at[k], trecv.at[k], g.mate(k))
        cp.start()
        cp.wait_recv()
        vtrade[k + 1, 0] = vtrade[k, 0] + vtrade[k, 1]
    new_vw[...], new_vm[...], new_vs[...] = adam_update(vw[...], vtrade[phases, 0], vm[...], vs[...], vector_rate)

    def line_copy(step, seat):
        box = up if step > 0 else down
        at = (step + 1) // 2
        return remote(acc.at[0, seat], box.at[seat], usend.at[at, seat], urecv.at[at, seat], g.beside(step))

    def own_column(i, _):
        seat = in_turn(i)
        for q in range(phases):
            phase_copy(q, 1 << q, seat).wait_recv()

        @pl.when(seat > g.seat)
        def _():
            @pl.when(g.seat > 0)
            def _():
                line_copy(1, seat).wait_recv()

            acc[0, seat] = (local(0, seat, phases) + up[seat].astype(F32)).astype(B16)
            line_copy(1, seat).start()

        @pl.when(seat < g.seat)
        def _():
            @pl.when(g.seat < seats - 1)
            def _():
                line_copy(-1, seat).wait_recv()

            acc[0, seat] = (local(0, seat, phases) + down[seat].astype(F32)).astype(B16)
            line_copy(-1, seat).start()

        return 0

    lax.fori_loop(0, seats, own_column, 0)

    @pl.when(g.seat > 0)
    def _():
        line_copy(1, g.seat).wait_recv()

    @pl.when(g.seat < seats - 1)
    def _():
        line_copy(-1, g.seat).wait_recv()

    total = local(0, g.seat, phases) + up[g.seat].astype(F32) + down[g.seat].astype(F32)
    next_w, new_m[...], new_s[...] = adam_update(w[...], total, m[...], s[...], matrix_rate)
    new_w[...] = next_w
    fresh[...] = next_w.astype(B16)
    spread_blocks(g, fresh, whole, own.at[0], zsend, msend, ssend, recv, srecv)
    for cp in sib_copies:
        cp.wait_send()
    for d in range(1, n):
        vector_copy(d).wait_send()
    for k in range(phases):
        remote(vtrade.at[k, 0], vtrade.at[k, 1], tsend.at[k], trecv.at[k], g.mate(k)).wait_send()

    def drain(seat, _):
        for e in range(1, slots):
            phase_copy(lowest_bit(e), e, seat).wait_send()

        @pl.when(seat > g.seat)
        def _():
            line_copy(1, seat).wait_send()

        @pl.when(seat < g.seat)
        def _():
            line_copy(-1, seat).wait_send()

        return 0

    lax.fori_loop(0, seats, drain, 0)


def step_call(columns, n, cid, grads, w, m, s, dvec, vw, vm, vs):
    seats, phases = n // 2, columns.bit_length() - 1
    block = w.shape
    half = max(columns // 2, 1)
    dma = pltpu.SemaphoreType.DMA
    return pl.pallas_call(
        functools.partial(step_kernel, columns, n),
        out_shape=[sds(block, F32)] * 3 + [sds(vw.shape, F32)] * 3 + [sds((columns, seats, 2) + block, B16)],
        in_specs=[anyw] + [vmem] * 7,
        out_specs=[vmem] * 6 + [anyw],
        scratch_shapes=[
            pltpu.VMEM((columns, seats) + block, B16),
            pltpu.VMEM((columns, seats) + block, B16),
            pltpu.VMEM((phases, half, seats) + block, B16),
            pltpu.VMEM((seats,) + block, B16),
            pltpu.VMEM((seats,) + block, B16),
            pltpu.VMEM(block, B16),
            pltpu.VMEM((n,) + vw.shape, F32),
            pltpu.VMEM((phases + 1, 2) + vw.shape, F32),
            dma((columns,)),
            dma((columns,)),
            dma((columns,)),
            dma((phases, half, seats)),
            dma((phases, half, seats)),
            dma((2, seats)),
            dma((2, seats)),
            dma((n,)),
            dma((n,)),
            dma((phases,)),
            dma((phases,)),
        ]
        + spread_scratch(columns, n),
        compiler_params=params_of(cid),
        name="step_weights",
    )(grads, w, m, s, dvec, vw, vm, vs)


def rounded_vectors(vectors):
    return lax.reduce_precision(vectors, exponent_bits=8, mantissa_bits=7)


def body(columns, n, latents, crop_ids, params, vectors, first_moment, second_moment, vector_first, vector_second,
         cotangent):
    canvases, rows, width, channels = latents.shape
    dims = (canvases, rows, width)
    px = canvases * rows * width
    plane = rows * width
    half = n // 2
    me = lax.axis_index("height")
    mine = me // half
    partner = lax.rem(me + half, n)
    swap = [(i, (i + half) % n) for i in range(n)]

    count = vectors.shape[0]

    def padded(value):
        return jnp.pad(value, ((0, 16 - count), (0, 0)))

    whole = spread_call(columns, n, 8, params).reshape(-1, channels)
    wide_vectors = padded(vectors)
    vec = rounded_vectors(wide_vectors)
    cell_ids = crop_ids[:, :, ::UNIT] + CROPS * jnp.arange(canvases, dtype=jnp.int32)[:, None, None]
    cell_ids = cell_ids.reshape(1, -1)
    stat = jnp.arange(canvases * CROPS, dtype=jnp.int32)[:, None]
    pick = (cell_ids == stat).astype(B16)
    spread = (cell_ids.reshape(-1, 1) == stat.reshape(1, -1)).astype(B16)
    ids = crop_ids.astype(F32)
    ids_px = jnp.broadcast_to(ids[..., None], (canvases, rows, width, LANES))
    ids_lane = jnp.pad(ids.reshape(canvases, plane), ((0, 8 - canvases), (0, 0)))
    x = latents.reshape(px, channels)
    cot = cotangent.reshape(px, channels)
    ids_all, mean1, inv1, div, cnt, *masks = layout_call(n, dims, x, pick, spread, ids_px, ids_lane)
    canvas_ids = lax.dynamic_index_in_dim(ids_all, mine, axis=1, keepdims=False)
    key_ids = canvas_ids.reshape(1, n * plane)
    query_ids = jnp.stack([canvas_ids[me], canvas_ids[partner]]).reshape(2 * plane, 1)
    query_ids = jnp.broadcast_to(query_ids, (2 * plane, LANES))
    offsets = jnp.stack([me, partner]) * plane
    cot3 = cotangent.reshape(canvases, plane, channels)
    own_cot = lax.dynamic_index_in_dim(cot3, mine, axis=0, keepdims=False)
    far_cot = lax.ppermute(
        lax.dynamic_index_in_dim(cot3, 1 - mine, axis=0, keepdims=False), "height", swap)
    dz = jnp.concatenate([own_cot, far_cot], axis=0)

    def attention_output(o, hid, weight, bias):
        o = o.reshape(2, plane, channels)
        back = lax.ppermute(o[1], "height", swap)
        ordered = jnp.where(mine == 0, jnp.stack([o[0], back]), jnp.stack([back, o[0]]))
        product = jnp.dot(ordered.reshape(px, channels), weight, preferred_element_type=F32)
        return hid + product + bias

    hid, u, y1, s1, s2, mean2, inv2, mean3, inv3 = resnet_forward_call(
        n, dims, True, x, pick, spread, cnt, mean1, inv1, masks, vec, whole)
    ua = gather_call(n, 4, u.reshape(canvases, plane, channels))
    o, dup, dw_att, dvec_att = attention_call(True, ua, key_ids, query_ids, offsets, dz, vec, whole)
    first_output = attention_output(o, hid, whole[21 * C :], vec[10])
    du = scatter_call(n, 6, dup.reshape(n, plane, channels)).reshape(px, channels)
    norms = (mean1, inv1, mean2, inv2, mean3, inv3)
    input_grad, matrix_grad, dvec = resnet_backward_call(
        n, dims, 7, cot, du, hid, y1, x, norms, s1, s2, pick, spread, div, masks, vec, whole, dw_att)
    vector_grad = jnp.concatenate([dvec, dvec_att], axis=0)
    new_params, new_first, new_second, *new_small, new_whole = step_call(
        columns, n, 9, matrix_grad.reshape((columns, half, 2) + params.shape), params, first_moment, second_moment,
        vector_grad, wide_vectors, padded(vector_first), padded(vector_second))
    new_vectors, new_vector_first, new_vector_second = [a[:count] for a in new_small]
    new_whole = new_whole.reshape(-1, channels)
    new_vec = rounded_vectors(new_small[0])
    hid2, u2 = resnet_forward_call(
        n, dims, False, x, pick, spread, cnt, mean1, inv1, masks, new_vec, new_whole)
    ua2 = gather_call(n, 5, u2.reshape(canvases, plane, channels))
    (o2,) = attention_call(False, ua2, key_ids, query_ids, offsets, dz, new_vec, new_whole)
    second_output = attention_output(o2, hid2, new_whole[21 * C :], new_vec[10])
    shape = latents.shape
    return (
        hid.reshape(shape),
        first_output.reshape(shape),
        second_output.reshape(shape),
        input_grad.reshape(shape),
        new_params,
        new_first,
        new_second,
        new_vectors,
        new_vector_first,
        new_vector_second,
    )


def solution(mesh):
    spatial = P("canvas", "height", None, None)
    owned = P(("canvas", "height"), None)
    return jax.shard_map(
        functools.partial(body, mesh.shape["canvas"], mesh.shape["height"]),
        mesh=mesh,
        in_specs=(spatial, P("canvas", "height", None), owned, P(), owned, owned, P(), P(), spatial),
        out_specs=(spatial, spatial, spatial, spatial, owned, owned, owned, P(), P(), P()),
        check_vma=False,
    )
```

```python
import functools

import jax
import jax.numpy as jnp
from jax import lax
from jax.experimental import pallas as pl
from jax.experimental.pallas import tpu as pltpu
from jax.sharding import PartitionSpec as P

C = 512
GROUPS = 32
STEP = 5
CROPS = 16
SPAN = C // GROUPS
LANES = 128
TILES = C // LANES
UNIT = 8

norm_epsilon = 1e-06
adam_epsilon = 1e-08
matrix_rate = 0.015
vector_rate = 0.2
mask_fill = -1e30

F32 = jnp.float32
B16 = jnp.bfloat16
MESH = pl.DeviceIdType.MESH
VMEM_LIMIT = 60 * 2**20

vmem = pl.BlockSpec(memory_space=pltpu.VMEM)
smem = pl.BlockSpec(memory_space=pltpu.SMEM)
anyw = pl.BlockSpec(memory_space=pl.ANY)


def params_of(cid=None):
    if cid is None:
        return pltpu.CompilerParams(vmem_limit_bytes=VMEM_LIMIT)
    return pltpu.CompilerParams(
        vmem_limit_bytes=VMEM_LIMIT, collective_id=cid, has_side_effects=True
    )


def sds(shape, dtype):
    return jax.ShapeDtypeStruct(shape, dtype)


def split_dot(pick, value):
    total = None
    rest = value
    for _ in range(3):
        part = rest.astype(B16)
        term = jnp.dot(pick, part, preferred_element_type=F32)
        total = term if total is None else total + term
        rest = rest - part.astype(F32)
    return total


def lane_group_sum(piece):
    lane = lax.broadcasted_iota(jnp.int32, piece.shape, 1)
    step = 1
    while step < SPAN:
        ahead = pltpu.roll(piece, LANES - step, 1)
        behind = pltpu.roll(piece, step, 1)
        piece = piece + jnp.where((lane & step) == 0, ahead, behind)
        step *= 2
    return piece


def tiles_of(value):
    return [value[:, j * LANES : (j + 1) * LANES] for j in range(TILES)]


def wide(piece, times=TILES):
    return jnp.concatenate([piece] * times, axis=1)


def pack(quantities):
    shape = quantities[0][0].shape
    sub = lax.broadcasted_iota(jnp.int32, shape, 1) & (SPAN - 1)
    out = jnp.zeros(shape, F32)
    for q, pieces in enumerate(quantities):
        for j, piece in enumerate(pieces):
            out = jnp.where(sub == TILES * q + j, piece, out)
    return out


def unpack(packed):
    sub = lax.broadcasted_iota(jnp.int32, packed.shape, 1) & (SPAN - 1)
    return jnp.concatenate(
        [lane_group_sum(jnp.where(sub == j, packed, 0.0)) for j in range(TILES)], axis=1
    )


def shift_down(packed, q):
    return pltpu.roll(packed, LANES - TILES * q, packed.ndim - 1)


def no_pump():
    return None


def greet(n):
    me = lax.axis_index("height")
    barrier = pltpu.get_barrier_semaphore()
    for d in range(1, n):
        pl.semaphore_signal(
            barrier, inc=1, device_id={"height": lax.rem(me + d, n)}, device_id_type=MESH
        )
    pl.semaphore_wait(barrier, n - 1)


def spread_copies(n, buf, send, recv, rnd):
    me = lax.axis_index("height")
    return [
        pltpu.make_async_remote_copy(
            src_ref=buf.at[rnd, 0],
            dst_ref=buf.at[rnd, d],
            send_sem=send.at[rnd, d],
            recv_sem=recv.at[rnd, d],
            device_id={"height": lax.rem(me + d, n)},
            device_id_type=MESH,
        )
        for d in range(1, n)
    ]


def cell_totals(load, out_ref, cells):
    def body(i, _):
        out_ref[pl.ds(i * 16, 16), :] = jnp.sum(load(i).reshape(16, UNIT, C), axis=1)
        return 0

    lax.fori_loop(0, cells // 16, body, 0)


def over_cells(cell_ref, i):
    return jnp.broadcast_to(cell_ref[pl.ds(i * 16, 16), :][:, None, :], (16, UNIT, C)).reshape(
        16 * UNIT, C
    )


def group_totals(pick_ref, cell_value):
    return [lane_group_sum(t) for t in tiles_of(split_dot(pick_ref[...], cell_value))]


def stats_payload(load, pick_ref, spread_ref, count_ref, cells, tmp_a, tmp_b):
    cell_totals(load, tmp_a, cells)
    sums = group_totals(pick_ref, tmp_a[...])
    count = count_ref[...]
    inv_count = 1.0 / jnp.maximum(count, 1.0)
    mean = jnp.concatenate([s * inv_count for s in sums], axis=1)
    tmp_b[...] = split_dot(spread_ref[...], mean)

    def centred(i):
        delta = load(i) - over_cells(tmp_b, i)
        return delta * delta

    cell_totals(centred, tmp_a, cells)
    squares = group_totals(pick_ref, tmp_a[...])
    return pack([sums, squares, [count] * TILES])


def combine_stats(gathered):
    sums = gathered
    squares = shift_down(gathered, 1)
    counts = shift_down(gathered, 2)
    divisor = jnp.maximum(jnp.sum(counts, axis=0), 1.0)
    mean = jnp.sum(sums, axis=0) / divisor
    apart = sums / jnp.maximum(counts, 1.0) - mean[None]
    spread = jnp.sum(squares + counts * apart * apart, axis=0) / divisor
    return mean, lax.rsqrt(spread + norm_epsilon), divisor


def shift_columns(row, left_mask, right_mask):
    width = row.shape[0]
    left = pltpu.roll(row, 1, 0) * wide(left_mask)
    right = pltpu.roll(row, width - 1, 0) * wide(right_mask)
    return jnp.concatenate([left, row, right], axis=1).astype(B16)


def logistic(a):
    return 1.0 / (1.0 + jnp.exp(-a))


def silu(a):
    return a * logistic(a)


def silu_slope(a):
    s = logistic(a)
    return s * (1.0 + a * (1.0 - s))


def layout_kernel(n, dims, x, pick, spread, ids_px, ids_lane, ids_all, mean_c, inv_c, div, cnt,
                  col_l, col_r, row_u, row_d, *scratch):
    greet(n)
    layout_body(n, dims, x, pick, spread, ids_px, ids_lane, ids_all, mean_c, inv_c, div, cnt,
                col_l, col_r, row_u, row_d, *scratch)


def layout_body(n, dims, x, pick, spread, ids_px, ids_lane, ids_all, mean_c, inv_c, div, cnt,
                col_l, col_r, row_u, row_d, buf, idbuf, halo, tmp_a, tmp_b, send, recv, isend, irecv,
                hsend, hrecv, pump=no_pump):
    canvases, rows, width = dims
    cells = canvases * rows * width // UNIT
    me = lax.axis_index("height")
    id_copies = []
    idbuf[0] = ids_lane[...]
    for d in range(1, n):
        cp = pltpu.make_async_remote_copy(
            src_ref=idbuf.at[0], dst_ref=idbuf.at[d], send_sem=isend.at[d], recv_sem=irecv.at[d],
            device_id={"height": lax.rem(me + d, n)}, device_id_type=MESH)
        cp.start()
        id_copies.append(cp)
    up, down = halo_copies(n, ids_px.at[:, 0], ids_px.at[:, rows - 1], halo, hsend, hrecv)
    start_halo(n, up, down)

    def load(i):
        return x[pl.ds(i * 16 * UNIT, 16 * UNIT), :].astype(F32)

    ones = jnp.sum(pick[...].astype(F32), axis=1, keepdims=True) * float(UNIT * SPAN)
    cnt[...] = jnp.broadcast_to(ones, cnt.shape)
    buf[0, 0] = stats_payload(load, pick, spread, cnt, cells, tmp_a, tmp_b)
    copies = spread_copies(n, buf, send, recv, 0)
    for cp in copies:
        cp.start()
    pump()
    wait_halo(n, up, down, halo, -1.0)
    column = lax.broadcasted_iota(jnp.int32, (width, LANES), 0)
    first, last = column == 0, column == width - 1
    for v in range(canvases):
        for r in range(rows + 2):
            here = halo[0, v] if r == 0 else halo[1, v] if r == rows + 1 else ids_px[v, r - 1]
            same_l = (pltpu.roll(here, 1, 0) == here) & jnp.logical_not(first)
            same_r = (pltpu.roll(here, width - 1, 0) == here) & jnp.logical_not(last)
            col_l[v, r] = same_l.astype(F32)
            col_r[v, r] = same_r.astype(F32)
            if 1 <= r <= rows:
                above = halo[0, v] if r == 1 else ids_px[v, r - 2]
                below = halo[1, v] if r == rows else ids_px[v, r]
                at = pl.ds((v * rows + r - 1) * width, width)
                row_u[at, :] = (above == here).astype(F32)
                row_d[at, :] = (below == here).astype(F32)
    pump()
    for cp in copies:
        cp.wait_recv()
    mean, inv, divisor = combine_stats(buf[0])
    mean_c[...] = split_dot(spread[...], unpack(mean))
    inv_c[...] = split_dot(spread[...], unpack(inv))
    div[...] = unpack(divisor)[:, :LANES]
    for cp in id_copies:
        cp.wait_recv()
    ids_all[me] = idbuf[0]
    for d in range(1, n):
        ids_all[lax.rem(me - d + n, n)] = idbuf[d]
    for cp in copies + id_copies:
        cp.wait_send()


def halo_copies(n, first_row, last_row, halo, hsend, hrecv):
    me = lax.axis_index("height")
    up = pltpu.make_async_remote_copy(
        src_ref=first_row, dst_ref=halo.at[1], send_sem=hsend.at[0], recv_sem=hrecv.at[1],
        device_id={"height": lax.rem(me + n - 1, n)}, device_id_type=MESH)
    down = pltpu.make_async_remote_copy(
        src_ref=last_row, dst_ref=halo.at[0], send_sem=hsend.at[1], recv_sem=hrecv.at[0],
        device_id={"height": lax.rem(me + 1, n)}, device_id_type=MESH)
    return up, down


def start_halo(n, up, down):
    me = lax.axis_index("height")

    @pl.when(me > 0)
    def _():
        up.start()

    @pl.when(me < n - 1)
    def _():
        down.start()


def wait_halo(n, up, down, halo, edge):
    me = lax.axis_index("height")

    @pl.when(me > 0)
    def _():
        up.wait_send()
        down.wait_recv()

    @pl.when(me < n - 1)
    def _():
        down.wait_send()
        up.wait_recv()

    @pl.when(me == 0)
    def _():
        halo[0] = jnp.full(halo.shape[1:], edge, halo.dtype)

    @pl.when(me == n - 1)
    def _():
        halo[1] = jnp.full(halo.shape[1:], edge, halo.dtype)


def layout_scratch(n, dims, ids_lane):
    canvases, rows, width = dims
    cells = canvases * rows * width // UNIT
    return [
        pltpu.VMEM((1, n, canvases * CROPS, LANES), F32),
        pltpu.VMEM((n,) + ids_lane.shape, F32),
        pltpu.VMEM((2, canvases, width, LANES), F32),
        pltpu.VMEM((cells, C), F32),
        pltpu.VMEM((cells, C), F32),
        pltpu.SemaphoreType.DMA((1, n)),
        pltpu.SemaphoreType.DMA((1, n)),
        pltpu.SemaphoreType.DMA((n,)),
        pltpu.SemaphoreType.DMA((n,)),
        pltpu.SemaphoreType.DMA((2,)),
        pltpu.SemaphoreType.DMA((2,)),
    ]


def layout_call(n, dims, x, pick, spread, ids_px, ids_lane):
    canvases, rows, width = dims
    px = canvases * rows * width
    cells = px // UNIT
    stats = canvases * CROPS
    return pl.pallas_call(
        functools.partial(layout_kernel, n, dims),
        out_shape=[
            sds((n,) + ids_lane.shape, F32),
            sds((cells, C), F32),
            sds((cells, C), F32),
            sds((stats, LANES), F32),
            sds((stats, LANES), F32),
            sds((canvases, rows + 2, width, LANES), F32),
            sds((canvases, rows + 2, width, LANES), F32),
            sds((px, LANES), F32),
            sds((px, LANES), F32),
        ],
        in_specs=[vmem] * 5,
        out_specs=[vmem] * 9,
        scratch_shapes=layout_scratch(n, dims, ids_lane),
        compiler_params=params_of(1),
        name="layout",
    )(x, pick, spread, ids_px, ids_lane)


def second_matrix(top, low, dest, sem):
    return [
        pltpu.make_async_copy(top.at[pl.ds(9 * C, 2 * C)], dest.at[pl.ds(0, 2 * C)], sem.at[1]),
        pltpu.make_async_copy(low.at[pl.ds(0, 7 * C)], dest.at[pl.ds(2 * C, 7 * C)], sem.at[2]),
    ]


class Convolver:
    def __init__(self, n, dims, x, pick, spread, cnt, col_l, col_r, row_u, row_d, halo, buf, tmp_a, tmp_b, send,
                 recv, hsend, hrecv):
        self.n, self.dims = n, dims
        self.x, self.pick, self.spread, self.cnt = x, pick, spread, cnt
        self.col_l, self.col_r, self.row_u, self.row_d = col_l, col_r, row_u, row_d
        self.halo, self.buf, self.tmp_a, self.tmp_b = halo, buf, tmp_a, tmp_b
        self.send, self.recv, self.hsend, self.hrecv = send, recv, hsend, hrecv
        self.px = dims[0] * dims[1] * dims[2]
        self.cells = self.px // UNIT
        self.sent = []

    def activate(self, source, mean, inv, gain, bias, dest, rnd, pump=no_pump):
        canvases, rows, width = self.dims
        row_cells = width // UNIT
        col_l, col_r, halo = self.col_l, self.col_r, self.halo

        def one(v, r):
            at = pl.ds(pl.multiple_of((v * rows + r) * width, width), width)
            cell = pl.ds(pl.multiple_of((v * rows + r) * row_cells, row_cells), row_cells)
            value = source[at, :].astype(F32)
            m = jnp.broadcast_to(mean[cell, :][:, None, :], (row_cells, UNIT, C)).reshape(width, C)
            s = jnp.broadcast_to(inv[cell, :][:, None, :], (row_cells, UNIT, C)).reshape(width, C)
            a = (value - m) * s * gain + bias
            dest[v, r + 1] = shift_columns(silu(a), col_l[v, r + 1], col_r[v, r + 1])

        def edges(v, _):
            one(v, 0)
            if rows > 1:
                one(v, rows - 1)
            return 0

        lax.fori_loop(0, canvases, edges, 0)
        mid = pl.ds(C, C)
        up, down = halo_copies(self.n, dest.at[:, 1, :, mid], dest.at[:, rows, :, mid], halo.at[rnd],
                               self.hsend.at[rnd], self.hrecv.at[rnd])
        start_halo(self.n, up, down)
        pump()

        def inner(i, _):
            one(i // (rows - 2), 1 + lax.rem(i, rows - 2))
            return 0

        if rows > 2:
            lax.fori_loop(0, canvases * (rows - 2), inner, 0)
        pump()
        wait_halo(self.n, up, down, halo.at[rnd], 0.0)
        for v in range(canvases):
            for side, r in ((0, 0), (1, rows + 1)):
                dest[v, r] = shift_columns(halo[rnd, side, v].astype(F32), col_l[v, r], col_r[v, r])

    def convolve(self, source, weights, emit, pump=no_pump):
        canvases, rows, width = self.dims
        plane = rows * width
        for v in range(canvases):
            at = pl.ds(v * plane, plane)
            total = None
            for dr in (1, 0, 2):
                part = None
                for lo, hi, ref, row in weights(dr):
                    lhs = source[v, dr : dr + rows, :, lo:hi].reshape(plane, hi - lo)
                    term = jnp.dot(lhs, ref[row : row + hi - lo, :], preferred_element_type=F32)
                    part = term if part is None else part + term
                if dr == 0:
                    part = part * wide(self.row_u[at, :])
                if dr == 2:
                    part = part * wide(self.row_d[at, :])
                total = part if total is None else total + part
            emit(at, total)
            pump()

    def statistics(self, source, mean, inv, rnd, pump=no_pump):
        def load(i):
            return source[pl.ds(i * 16 * UNIT, 16 * UNIT), :]

        self.buf[rnd, 0] = stats_payload(load, self.pick, self.spread, self.cnt, self.cells, self.tmp_a, self.tmp_b)
        copies = spread_copies(self.n, self.buf, self.send, self.recv, rnd)
        for cp in copies:
            cp.start()
        pump()
        for cp in copies:
            cp.wait_recv()
        m, s, _ = combine_stats(self.buf[rnd])
        mean[...] = split_dot(self.spread[...], unpack(m))
        inv[...] = split_dot(self.spread[...], unpack(s))
        self.sent = self.sent + copies

    def normalise(self, source, mean, inv, gain, bias, dest):
        def last(i, _):
            at = pl.ds(i * 16 * UNIT, 16 * UNIT)
            value = (source[at, :] - over_cells(mean, i)) * over_cells(inv, i)
            dest[at, :] = (value * gain + bias).astype(B16)
            return 0

        lax.fori_loop(0, self.cells // 16, last, 0)


def resnet_forward_kernel(n, dims, keep, x, pick, spread, cnt, mean1, inv1, col_l, col_r, row_u, row_d,
                          vec, top, low, *refs):
    canvases, rows, width = dims
    px = canvases * rows * width
    cells = px // UNIT
    plane = rows * width
    if keep:
        hid, u, y1, s1, s2, mean2, inv2, mean3, inv3 = refs[:9]
        refs = refs[9:]
    else:
        hid, u = refs[:2]
        y1, s1, s2, mean2, inv2, mean3, inv3 = refs[2:9]
        refs = refs[9:]
    k1, k2, halo, buf, tmp_a, tmp_b, ksem, send, recv, hsend, hrecv = refs
    load1 = [pltpu.make_async_copy(top.at[pl.ds(0, 9 * C)], k1, ksem.at[0])]
    load2 = second_matrix(top, low, k2, ksem)
    for cp in load1 + load2:
        cp.start()
    greet(n)
    for_conv = Convolver(n, dims, x, pick, spread, cnt, col_l, col_r, row_u, row_d, halo, buf, tmp_a, tmp_b,
                         send, recv, hsend, hrecv)

    def wait_all(copies):
        for cp in copies:
            cp.wait()

    for_conv.activate(x, mean1, inv1, vec[0:1, :], vec[1:2, :], s1, 0)
    wait_all(load1)

    def emit_first(at, total):
        y1[at, :] = total + vec[2:3, :]

    for_conv.convolve(s1, lambda dr: [(0, 3 * C, k1, 3 * C * dr)], emit_first)
    for_conv.statistics(y1, mean2, inv2, 0)
    for_conv.activate(y1, mean2, inv2, vec[3:4, :], vec[4:5, :], s2, 1)
    wait_all(load2)

    def emit_second(at, total):
        hid[at, :] = total + vec[5:6, :] + x[at, :].astype(F32)

    for_conv.convolve(s2, lambda dr: [(0, 3 * C, k2, 3 * C * dr)], emit_second)
    for_conv.statistics(hid, mean3, inv3, 1)
    for_conv.normalise(hid, mean3, inv3, vec[6:7, :], vec[7:8, :], u)
    for cp in for_conv.sent:
        cp.wait_send()


def resnet_forward_call(n, dims, keep, x, pick, spread, cnt, mean1, inv1, masks, vec, top, low):
    canvases, rows, width = dims
    px = canvases * rows * width
    cells = px // UNIT
    stats = canvases * CROPS
    saved = [
        ((px, C), F32),
        ((canvases, rows + 2, width, 3 * C), B16),
        ((canvases, rows + 2, width, 3 * C), B16),
        ((cells, C), F32),
        ((cells, C), F32),
        ((cells, C), F32),
        ((cells, C), F32),
    ]
    main = [((px, C), F32), ((px, C), B16)]
    outs = main + (saved if keep else [])
    scratch = [] if keep else [pltpu.VMEM(*s) for s in saved]
    return pl.pallas_call(
        functools.partial(resnet_forward_kernel, n, dims, keep),
        out_shape=[sds(*s) for s in outs],
        in_specs=[vmem] * 11 + [anyw] * 2,
        out_specs=[vmem] * len(outs),
        scratch_shapes=scratch
        + [
            pltpu.VMEM((9 * C, C), B16),
            pltpu.VMEM((9 * C, C), B16),
            pltpu.VMEM((2, 2, canvases, width, C), B16),
            pltpu.VMEM((2, n, stats, LANES), F32),
            pltpu.VMEM((cells, C), F32),
            pltpu.VMEM((cells, C), F32),
            pltpu.SemaphoreType.DMA((3,)),
            pltpu.SemaphoreType.DMA((2, n)),
            pltpu.SemaphoreType.DMA((2, n)),
            pltpu.SemaphoreType.DMA((2, 2)),
            pltpu.SemaphoreType.DMA((2, 2)),
        ],
        compiler_params=params_of(2 if keep else 3),
        name="resnet_forward" if keep else "resnet_again",
    )(x, pick, spread, cnt, mean1, inv1, *masks, vec, top, low)


def attention_kernel(keep, chunk, block, ua, key_ids, query_ids, offsets, dz, vec, low, *refs):
    total = ua.shape[0] * ua.shape[1]
    queries = query_ids.shape[0]
    segment = ua.shape[1]
    scale = C ** (-0.5)
    if keep:
        out, dup, dw, dvec = refs[:4]
        u, w, k, v, pbuf, sbuf, q, dout, dq, usem, wsem = refs[4:]
    else:
        out = refs[0]
        u, w, k, v, usem, wsem = refs[1:]
    load_w = pltpu.make_async_copy(low.at[pl.ds(7 * C, 4 * C)], w, wsem.at[0])
    load_w.start()
    blocks = ua.shape[0]
    loads = [
        pltpu.make_async_copy(ua.at[i], u.at[pl.ds(i * segment, segment)], usem.at[i])
        for i in range(blocks)
    ]
    for cp in loads:
        cp.start()
    load_w.wait()
    for cp in loads:
        cp.wait()
    nt = (((1,), (1,)), ((), ()))
    tn = (((0,), (0,)), ((), ()))

    def project(i, _):
        at = pl.ds(pl.multiple_of(i * chunk, chunk), chunk)
        piece = u[at, :]
        k[at, :] = jnp.dot(piece, w[C : 2 * C, :], preferred_element_type=F32).astype(B16)
        v[at, :] = (
            jnp.dot(piece, w[2 * C : 3 * C, :], preferred_element_type=F32) + vec[9:10, :]
        ).astype(B16)
        return 0

    lax.fori_loop(0, total // chunk, project, 0)
    per = segment // block

    def place(i):
        return pl.multiple_of(offsets[i // per] + lax.rem(i, per) * block, block)

    def attend(i, _):
        at = pl.ds(pl.multiple_of(i * block, block), block)
        uq = u[pl.ds(place(i), block), :]
        qb = (
            jnp.dot(uq, w[0:C, :], preferred_element_type=F32) + vec[8:9, :]
        ).astype(B16)
        s = lax.dot_general(qb, k[...], nt, preferred_element_type=F32) * scale
        s = jnp.where(query_ids[at, :][:, :1] == key_ids[...], s, mask_fill)
        e = jnp.exp(s - jnp.max(s, axis=1, keepdims=True))
        p = e * (1.0 / jnp.sum(e, axis=1, keepdims=True))
        pb = p.astype(B16)
        ob = jnp.dot(pb, v[...], preferred_element_type=F32).astype(B16)
        out[at, :] = ob
        if keep:
            pbuf[at, :] = pb
            q[at, :] = qb
            do = lax.dot_general(
                dz[at, :], w[3 * C : 4 * C, :], nt, preferred_element_type=F32
            ).astype(B16)
            dout[at, :] = do
            dp = lax.dot_general(do, v[...], nt, preferred_element_type=F32)
            delta = jnp.sum(p * dp, axis=1, keepdims=True)
            ds = (p * (dp - delta)).astype(B16)
            sbuf[at, :] = ds
            dq[at, :] = (jnp.dot(ds, k[...], preferred_element_type=F32) * scale).astype(B16)
        return 0

    lax.fori_loop(0, queries // block, attend, 0)
    if not keep:
        return
    zero = jnp.zeros((C, C), F32)

    def back(i, carry):
        dwk, dwv, dbv = carry
        at = pl.ds(pl.multiple_of(i * chunk, chunk), chunk)
        dk = (
            lax.dot_general(sbuf[:, at], q[...], tn, preferred_element_type=F32) * scale
        ).astype(B16)
        dvf = lax.dot_general(pbuf[:, at], dout[...], tn, preferred_element_type=F32)
        dv = dvf.astype(B16)
        du = lax.dot_general(dk, w[C : 2 * C, :], nt, preferred_element_type=F32)
        du = du + lax.dot_general(dv, w[2 * C : 3 * C, :], nt, preferred_element_type=F32)
        dup[at, :] = du.astype(B16)
        piece = u[at, :]
        dwk = dwk + lax.dot_general(piece, dk, tn, preferred_element_type=F32)
        dwv = dwv + lax.dot_general(piece, dv, tn, preferred_element_type=F32)
        return dwk, dwv, dbv + jnp.sum(dvf, axis=0, keepdims=True)

    dwk, dwv, dbv = lax.fori_loop(0, total // chunk, back, (zero, zero, jnp.zeros((1, C), F32)))
    dw[C : 2 * C, :] = dwk.astype(B16)
    dw[2 * C : 3 * C, :] = dwv.astype(B16)
    dw[3 * C : 4 * C, :] = lax.dot_general(
        out[...], dz[...], tn, preferred_element_type=F32
    ).astype(B16)
    dwq = zero
    for s in range(2):
        where = pl.ds(pl.multiple_of(offsets[s], segment), segment)
        at = pl.ds(s * segment, segment)
        dwq = dwq + lax.dot_general(u[where, :], dq[at, :], tn, preferred_element_type=F32)
        du = lax.dot_general(dq[at, :], w[0:C, :], nt, preferred_element_type=F32)
        dup[where, :] = (dup[where, :].astype(F32) + du).astype(B16)
    dw[0:C, :] = dwq.astype(B16)
    dvec[...] = jnp.concatenate(
        [
            jnp.sum(dq[...].astype(F32), axis=0, keepdims=True),
            dbv,
            jnp.sum(dz[...].astype(F32), axis=0, keepdims=True),
            jnp.zeros((5, C), F32),
        ],
        axis=0,
    )


def attention_call(keep, ua, key_ids, query_ids, offsets, dz, vec, low):
    blocks, segment, _ = ua.shape
    total = blocks * segment
    queries = query_ids.shape[0]
    block = min(256, segment)
    chunk = 512
    outs = [sds((queries, C), B16)]
    scratch = [
        pltpu.VMEM((total, C), B16),
        pltpu.VMEM((4 * C, C), B16),
        pltpu.VMEM((total, C), B16),
        pltpu.VMEM((total, C), B16),
    ]
    if keep:
        outs += [sds((total, C), B16), sds((4 * C, C), B16), sds((8, C), F32)]
        scratch += [
            pltpu.VMEM((queries, total), B16),
            pltpu.VMEM((queries, total), B16),
            pltpu.VMEM((queries, C), B16),
            pltpu.VMEM((queries, C), B16),
            pltpu.VMEM((queries, C), B16),
        ]
    return pl.pallas_call(
        functools.partial(attention_kernel, keep, chunk, block),
        out_shape=outs,
        in_specs=[anyw, vmem, vmem, smem, vmem, vmem, anyw],
        out_specs=[vmem] * len(outs),
        scratch_shapes=scratch
        + [pltpu.SemaphoreType.DMA((blocks,)), pltpu.SemaphoreType.DMA((1,))],
        compiler_params=params_of(),
        name="attention" if keep else "attention_again",
    )(ua, key_ids, query_ids, offsets, dz, vec, low)


def other_core(h):
    return h + 1 - 2 * lax.rem(h, 2)


def gather_kernel(n, u, ua, lsem, send, recv):
    me = lax.axis_index("height")
    half = n // 2
    mine = me // half
    base = mine * half
    core = lax.rem(me, 2)
    partner = lax.rem(me + half, n)
    sibling = other_core(me)
    mates = half // 2
    seat = (me - base) // 2

    def mate(j):
        return base + core + 2 * lax.rem(seat + j, mates)

    barrier = pltpu.get_barrier_semaphore()
    peers = [partner, sibling] + [mate(j) for j in range(1, mates)]
    for p in peers:
        pl.semaphore_signal(barrier, inc=1, device_id={"height": p}, device_id_type=MESH)
    pl.semaphore_wait(barrier, len(peers))
    count = [0]
    started = []

    def push(src, slot, to):
        cp = pltpu.make_async_remote_copy(
            src_ref=src, dst_ref=ua.at[slot], send_sem=send.at[count[0]], recv_sem=recv.at[slot],
            device_id={"height": to}, device_id_type=MESH)
        count[0] += 1
        cp.start()
        started.append(cp)

    def arrived(slot):
        pltpu.make_async_remote_copy(
            src_ref=u.at[0], dst_ref=ua.at[slot], send_sem=send.at[0], recv_sem=recv.at[slot],
            device_id={"height": partner}, device_id_type=MESH).wait_recv()

    own = pltpu.make_async_copy(u.at[mine], ua.at[me], lsem.at[0])
    own.start()
    push(u.at[1 - mine], me, partner)
    for j in range(1, mates):
        push(u.at[mine], me, mate(j))
    push(u.at[mine], me, sibling)
    arrived(partner)
    for j in range(1, mates):
        push(ua.at[partner], partner, mate(j))
    push(ua.at[partner], partner, sibling)
    for j in range(1, mates):
        friend = base + core + 2 * lax.rem(seat + mates - j, mates)
        far = lax.rem(friend + half, n)
        arrived(friend)
        push(ua.at[friend], friend, sibling)
        arrived(far)
        push(ua.at[far], far, sibling)
    arrived(sibling)
    arrived(lax.rem(sibling + half, n))
    for j in range(1, mates):
        friend = base + (1 - core) + 2 * lax.rem(seat + mates - j, mates)
        arrived(friend)
        arrived(lax.rem(friend + half, n))
    own.wait()
    for cp in started:
        cp.wait_send()


def gather_call(n, cid, u):
    half = n // 2
    sends = 2 * (half // 2) + 1 + 2 * (half // 2 - 1) + 1
    return pl.pallas_call(
        functools.partial(gather_kernel, n),
        out_shape=sds((n,) + u.shape[1:], B16),
        in_specs=[anyw],
        out_specs=anyw,
        scratch_shapes=[
            pltpu.SemaphoreType.DMA((1,)),
            pltpu.SemaphoreType.DMA((sends,)),
            pltpu.SemaphoreType.DMA((n,)),
        ],
        compiler_params=params_of(cid),
        name="gather_u",
    )(u)


def scatter_kernel(n, dup, out, from_sib, from_mate, mine_sum, from_partner, lsem, send, recv):
    me = lax.axis_index("height")
    half = n // 2
    mine = me // half
    base = mine * half
    core = lax.rem(me, 2)
    partner = lax.rem(me + half, n)
    sibling = other_core(me)
    mates = half // 2
    seat = (me - base) // 2
    barrier = pltpu.get_barrier_semaphore()

    def mate(j, c=core):
        return base + c + 2 * lax.rem(seat + j, mates)

    peers = [partner, sibling] + [mate(j) for j in range(1, mates)]
    for p in peers:
        pl.semaphore_signal(barrier, inc=1, device_id={"height": p}, device_id_type=MESH)
    pl.semaphore_wait(barrier, len(peers))
    order = [(j, far) for j in range(1, mates) for far in (1, 0)] + [(0, 1), (0, 0)]

    def rows_of(j, far, c):
        owner = mate(j, c)
        return lax.rem(owner + half, n) if far else owner

    sib = []
    for t, (j, far) in enumerate(order):
        cp = pltpu.make_async_remote_copy(
            src_ref=dup.at[rows_of(j, far, 1 - core)], dst_ref=from_sib.at[t],
            send_sem=send.at[t], recv_sem=recv.at[t],
            device_id={"height": sibling}, device_id_type=MESH)
        cp.start()
        sib.append(cp)
    base_sem = len(order)
    out_copies = []
    for t, (j, far) in enumerate(order):
        sib[t].wait_recv()
        block = rows_of(j, far, core)
        if j > 0:
            mine_sum[t] = (dup[block].astype(F32) + from_sib[t].astype(F32)).astype(B16)
            at = (j - 1) * 2 + far
            cp = pltpu.make_async_remote_copy(
                src_ref=mine_sum.at[t], dst_ref=from_mate.at[at],
                send_sem=send.at[base_sem + at], recv_sem=recv.at[base_sem + at],
                device_id={"height": mate(j)}, device_id_type=MESH)
            cp.start()
            out_copies.append(cp)
    t_far, t_own = len(order) - 2, len(order) - 1
    total = dup[partner].astype(F32) + from_sib[t_far].astype(F32)
    for j in range(1, mates):
        at = (j - 1) * 2 + 1
        pltpu.make_async_remote_copy(
            src_ref=mine_sum.at[0], dst_ref=from_mate.at[at], send_sem=send.at[0],
            recv_sem=recv.at[base_sem + at], device_id={"height": sibling},
            device_id_type=MESH).wait_recv()
        total = total + from_mate[at].astype(F32)
    mine_sum[t_far] = total.astype(B16)
    last = base_sem + 2 * (mates - 1)
    home = pltpu.make_async_remote_copy(
        src_ref=mine_sum.at[t_far], dst_ref=from_partner, send_sem=send.at[last],
        recv_sem=recv.at[last], device_id={"height": partner}, device_id_type=MESH)
    home.start()
    total = dup[me].astype(F32) + from_sib[t_own].astype(F32)
    for j in range(1, mates):
        at = (j - 1) * 2
        pltpu.make_async_remote_copy(
            src_ref=mine_sum.at[0], dst_ref=from_mate.at[at], send_sem=send.at[0],
            recv_sem=recv.at[base_sem + at], device_id={"height": sibling},
            device_id_type=MESH).wait_recv()
        total = total + from_mate[at].astype(F32)
    out[mine] = total
    home.wait_recv()
    out[1 - mine] = from_partner[...].astype(F32)
    for cp in sib + out_copies + [home]:
        cp.wait_send()


def scatter_call(n, cid, dup):
    half = n // 2
    mates = half // 2
    copies = 2 * mates + 2 * (mates - 1) + 1
    seg = dup.shape[1:]
    return pl.pallas_call(
        functools.partial(scatter_kernel, n),
        out_shape=sds((2,) + seg, F32),
        in_specs=[vmem],
        out_specs=vmem,
        scratch_shapes=[
            pltpu.VMEM((2 * mates,) + seg, B16),
            pltpu.VMEM((max(2 * (mates - 1), 1),) + seg, B16),
            pltpu.VMEM((2 * mates,) + seg, B16),
            pltpu.VMEM(seg, B16),
            pltpu.SemaphoreType.DMA((1,)),
            pltpu.SemaphoreType.DMA((copies,)),
            pltpu.SemaphoreType.DMA((copies,)),
        ],
        compiler_params=params_of(cid),
        name="scatter_du",
    )(dup)


def resnet_backward_kernel(n, dims, cot, du, hid, y1, x, mean1, inv1, mean2, inv2, mean3, inv3, s1, s2, pick,
                           spread, div, col_l, col_r, row_u, row_d, vec, top, bottom, datt, igrad, grads, dvec,
                           dw1, dw2, k, dh, d3, low, low_u, low_d, part, norm, halo, buf, tmp_a, tmp_b, ksem, wsem, send,
                           recv, hsend, hrecv):
    canvases, rows, width = dims
    px = canvases * rows * width
    cells = px // UNIT
    plane = rows * width
    nt = (((1,), (1,)), ((), ()))
    tn = (((0,), (0,)), ((), ()))
    load2 = second_matrix(top, bottom, k, wsem)
    load1 = pltpu.make_async_copy(top.at[pl.ds(0, 9 * C)], k, wsem.at[0])
    for cp in load2:
        cp.start()
    out_att = pltpu.make_async_copy(datt, grads.at[pl.ds(18 * C, 4 * C)], ksem.at[2])
    out_two = pltpu.make_async_copy(dw2, grads.at[pl.ds(9 * C, 9 * C)], ksem.at[3])
    out_one = pltpu.make_async_copy(dw1, grads.at[pl.ds(0, 9 * C)], ksem.at[4])
    out_att.start()
    greet(n)
    zero_row = jnp.zeros((1, C), F32)

    def pixels(i):
        return pl.ds(i * 16 * UNIT, 16 * UNIT)

    def norm_sums(grad_of, source, mean, inv, gain):
        def body(i, carry):
            dg, db = carry
            at = pixels(i)
            unit = (source[at, :].astype(F32) - over_cells(mean, i)) * over_cells(inv, i)
            d = grad_of(i, unit)
            norm[at, :] = unit
            e = d * gain
            part[at, :] = e
            cross = d * unit
            here = pl.ds(i * 16, 16)
            tmp_a[here, :] = jnp.sum(e.reshape(16, UNIT, C), axis=1)
            tmp_b[here, :] = jnp.sum((cross * gain).reshape(16, UNIT, C), axis=1)
            return (dg + jnp.sum(cross, axis=0, keepdims=True), db + jnp.sum(d, axis=0, keepdims=True))

        dg, db = lax.fori_loop(0, cells // 16, body, (zero_row, zero_row))
        packed = pack([group_totals(pick, tmp_a[...]), group_totals(pick, tmp_b[...])])
        return packed, dg, db

    def send_sums(packed, rnd):
        buf[rnd, 0] = packed
        copies = spread_copies(n, buf, send, recv, rnd)
        for cp in copies:
            cp.start()
        return copies

    def norm_finish(copies, rnd, inv, emit):
        for cp in copies:
            cp.wait_recv()
        gathered = jnp.sum(buf[rnd], axis=0) / div[...]
        tmp_a[...] = split_dot(spread[...], unpack(gathered))
        tmp_b[...] = split_dot(spread[...], unpack(shift_down(gathered, 1)))

        def body(i, _):
            at = pixels(i)
            emit(i, over_cells(inv, i) * (part[at, :] - over_cells(tmp_a, i) - norm[at, :] * over_cells(tmp_b, i)))
            return 0

        lax.fori_loop(0, cells // 16, body, 0)

    def spread_rows(rnd):
        def row_at(v, r):
            return pl.ds(pl.multiple_of((v * rows + r) * width, width), width)

        def one(i, _):
            v, r = i // rows, lax.rem(i, rows)
            d3[v, r + 1] = shift_columns(low[row_at(v, r), :].astype(F32), col_l[v, r + 1], col_r[v, r + 1])
            return 0

        lax.fori_loop(0, canvases * rows, one, 0)
        mid = pl.ds(C, C)
        up, down = halo_copies(n, d3.at[:, 1, :, mid], d3.at[:, rows, :, mid], halo.at[rnd],
                               hsend.at[rnd], hrecv.at[rnd])
        start_halo(n, up, down)
        return up, down

    def finish_rows(up, down, rnd):
        wait_halo(n, up, down, halo.at[rnd], 0.0)
        for v in range(canvases):
            for side, r in ((0, 0), (1, rows + 1)):
                d3[v, r] = shift_columns(halo[rnd, side, v].astype(F32), col_l[v, r], col_r[v, r])

    def convolve_back(emit):
        def body(v, _):
            at = pl.ds(pl.multiple_of(v * plane, plane), plane)
            total = None
            for dr in (1, 0, 2):
                acc = None
                for dc in range(3):
                    tap = 3 * (2 - dr) + (2 - dc)
                    lhs = d3[v, dr : dr + rows, :, dc * C : (dc + 1) * C].reshape(plane, C)
                    term = lax.dot_general(lhs, k[tap * C : (tap + 1) * C, :], nt, preferred_element_type=F32)
                    acc = term if acc is None else acc + term
                if dr == 0:
                    acc = acc * wide(row_u[at, :])
                if dr == 2:
                    acc = acc * wide(row_d[at, :])
                total = acc if total is None else total + acc
            emit(at, total)
            return 0

        lax.fori_loop(0, canvases, body, 0)

    def mask_rows():
        def body(i, _):
            at = pixels(i)
            value = low[at, :].astype(F32)
            low_u[at, :] = (value * wide(row_u[at, :])).astype(B16)
            low_d[at, :] = (value * wide(row_d[at, :])).astype(B16)
            return 0

        lax.fori_loop(0, cells // 16, body, 0)

    def weight_grad(source, dest):
        for dr, grad in ((0, low_u), (1, low), (2, low_d)):
            def body(dc, _):
                acc = None
                for v in range(canvases):
                    lhs = source[v, dr : dr + rows, :, pl.ds(pl.multiple_of(dc * C, C), C)].reshape(plane, C)
                    term = lax.dot_general(
                        lhs, grad[v * plane : (v + 1) * plane, :], tn, preferred_element_type=F32)
                    acc = term if acc is None else acc + term
                dest[pl.ds(pl.multiple_of((3 * dr + dc) * C, C), C), :] = acc.astype(B16)
                return 0

            lax.fori_loop(0, 3, body, 0)

    packed, dg3, db3 = norm_sums(lambda i, unit: du[pixels(i), :], hid, mean3, inv3, vec[6:7, :])
    sent = send_sums(packed, 0)

    def emit_hidden(i, value):
        at = pixels(i)
        total = cot[at, :].astype(F32) + value
        dh[at, :] = total
        low[at, :] = total.astype(B16)

    norm_finish(sent, 0, inv3, emit_hidden)
    up, down = spread_rows(0)
    mask_rows()
    dc2 = jnp.sum(low[...].astype(F32), axis=0, keepdims=True)
    finish_rows(up, down, 0)
    for cp in load2:
        cp.wait()

    def emit_part(at, total):
        part[at, :] = total

    convolve_back(emit_part)
    load1.start()
    gain2, bias2 = vec[3:4, :], vec[4:5, :]

    def grad_two(i, unit):
        return part[pixels(i), :] * silu_slope(unit * gain2 + bias2)

    packed, dg2, db2 = norm_sums(grad_two, y1, mean2, inv2, gain2)
    more = send_sums(packed, 1)
    weight_grad(s2, dw2)
    out_two.start()

    def emit_low(i, value):
        low[pixels(i), :] = value.astype(B16)

    norm_finish(more, 1, inv2, emit_low)
    sent = sent + more
    up, down = spread_rows(1)
    mask_rows()
    dc1 = jnp.sum(low[...].astype(F32), axis=0, keepdims=True)
    weight_grad(s1, dw1)
    out_one.start()
    finish_rows(up, down, 1)
    load1.wait()
    convolve_back(emit_part)
    gain1, bias1 = vec[0:1, :], vec[1:2, :]

    def grad_one(i, unit):
        return part[pixels(i), :] * silu_slope(unit * gain1 + bias1)

    packed, dg1, db1 = norm_sums(grad_one, x, mean1, inv1, gain1)
    more = send_sums(packed, 2)
    dvec[...] = jnp.concatenate([dg1, db1, dc1, dg2, db2, dc2, dg3, db3], axis=0)

    def emit_input(i, value):
        igrad[pixels(i), :] = dh[pixels(i), :] + value

    norm_finish(more, 2, inv1, emit_input)
    sent = sent + more
    out_att.wait()
    out_two.wait()
    out_one.wait()
    for cp in sent:
        cp.wait_send()


def resnet_backward_call(n, dims, cid, cot, du, hid, y1, x, norms, s1, s2, pick, spread, div, masks, vec, top,
                         bottom, datt):
    canvases, rows, width = dims
    px = canvases * rows * width
    cells = px // UNIT
    stats = canvases * CROPS
    return pl.pallas_call(
        functools.partial(resnet_backward_kernel, n, dims),
        out_shape=[sds((px, C), F32), sds((22 * C, C), B16), sds((8, C), F32)],
        in_specs=[vmem] * 21 + [anyw] * 3,
        out_specs=[vmem, anyw, vmem],
        scratch_shapes=[
            pltpu.VMEM((9 * C, C), B16),
            pltpu.VMEM((9 * C, C), B16),
            pltpu.VMEM((9 * C, C), B16),
            pltpu.VMEM((px, C), F32),
            pltpu.VMEM((canvases, rows + 2, width, 3 * C), B16),
            pltpu.VMEM((px, C), B16),
            pltpu.VMEM((px, C), B16),
            pltpu.VMEM((px, C), B16),
            pltpu.VMEM((px, C), F32),
            pltpu.VMEM((px, C), F32),
            pltpu.VMEM((2, 2, canvases, width, C), B16),
            pltpu.VMEM((3, n, stats, LANES), F32),
            pltpu.VMEM((cells, C), F32),
            pltpu.VMEM((cells, C), F32),
            pltpu.SemaphoreType.DMA((5,)),
            pltpu.SemaphoreType.DMA((3,)),
            pltpu.SemaphoreType.DMA((3, n)),
            pltpu.SemaphoreType.DMA((3, n)),
            pltpu.SemaphoreType.DMA((2, 2)),
            pltpu.SemaphoreType.DMA((2, 2)),
        ],
        compiler_params=params_of(cid),
        name="resnet_backward",
    )(cot, du, hid, y1, x, *norms, s1, s2, pick, spread, div, *masks, vec, top, bottom, datt)


class Grid:
    def __init__(self, columns, n):
        self.columns, self.n, self.seats = columns, n, n // 2
        self.phases = columns.bit_length() - 1
        self.c = lax.axis_index("canvas")
        self.h = lax.axis_index("height")
        self.seat, self.core = self.h // 2, lax.rem(self.h, 2)
        flips = [
            (1 - 2 * lax.rem(self.c // 2**t, 2)) * 2**t for t in range(self.phases)
        ]
        last = self.phases - 1
        self.flips = [
            (1 - self.core) * flips[last - k] + self.core * flips[k] for k in range(self.phases)
        ]
        self.other_flips = [
            self.core * flips[last - k] + (1 - self.core) * flips[k] for k in range(self.phases)
        ]

    def column(self, e, flips=None):
        flips = self.flips if flips is None else flips
        col = self.c
        for k in range(self.phases):
            if (e >> k) & 1:
                col = col + flips[k]
        return col

    def mate(self, k):
        return {"canvas": self.c + self.flips[k], "height": self.h}

    def sibling(self):
        return {"canvas": self.c, "height": 2 * self.seat + 1 - self.core}

    def beside(self, step):
        return {"canvas": self.c, "height": self.h + 2 * step}

    def greet(self):
        barrier = pltpu.get_barrier_semaphore()
        for d in range(1, self.n):
            pl.semaphore_signal(
                barrier, inc=1, device_id={"canvas": self.c, "height": lax.rem(self.h + d, self.n)},
                device_id_type=MESH)
        for k in range(self.phases):
            pl.semaphore_signal(barrier, inc=1, device_id=self.mate(k), device_id_type=MESH)
        pl.semaphore_wait(barrier, self.n - 1 + self.phases)


def remote(src, dst, send, recv, to):
    return pltpu.make_async_remote_copy(
        src_ref=src, dst_ref=dst, send_sem=send, recv_sem=recv, device_id=to, device_id_type=MESH)


def lowest_bit(e):
    return (e & -e).bit_length() - 1


def spread_blocks(grid, fresh, whole, own_sem, zsend, msend, ssend, recv, srecv):
    g = grid
    seats, phases = g.seats, g.phases
    own = pltpu.make_async_copy(fresh, whole.at[g.c, g.seat, g.core], own_sem)
    own.start()

    def slot(e, seat):
        return whole.at[g.column(e), seat, g.core]

    def forward(e, seat, src, start):
        k_top = phases if e == 0 else lowest_bit(e)
        for k in range(k_top - 1, -1, -1):
            cp = remote(src, slot(e, seat), msend.at[k, e, seat], recv.at[e | (1 << k), seat], g.mate(k))
            cp.start() if start else cp.wait_send()
        cp = remote(src, slot(e, seat), ssend.at[e, seat], srecv.at[e, seat], g.sibling())
        cp.start() if start else cp.wait_send()

    def along(seat, step, src, start):
        cp = remote(src, slot(0, seat), zsend.at[(step + 1) // 2, seat], recv.at[0, seat], g.beside(step))
        cp.start() if start else cp.wait_send()

    def line(seat, src, start):
        @pl.when((seat <= g.seat) & (g.seat < seats - 1))
        def _():
            along(seat, 1, src, start)

        @pl.when((seat >= g.seat) & (g.seat > 0))
        def _():
            along(seat, -1, src, start)

    def arrive(e, seat):
        remote(fresh, slot(e, seat), ssend.at[0, 0], recv.at[e, seat], g.sibling()).wait_recv()

    early = [e for e in range(1, 2**phases) if lowest_bit(e) > 0]
    early.sort(key=lambda e: -lowest_bit(e))
    late = [e for e in range(1, 2**phases) if lowest_bit(e) == 0]

    def handle(e, seat):
        arrive(e, seat)
        if e == 0:
            line(seat, slot(0, seat), True)
        forward(e, seat, slot(e, seat), True)

    def both_sides(d, todo):
        for side in (-1, 1):
            seat = g.seat + side * d

            @pl.when((seat >= 0) & (seat < seats))
            def _():
                for e in todo:
                    handle(e, seat)

    line(g.seat, fresh, True)
    forward(0, g.seat, fresh, True)
    for e in early:
        handle(e, g.seat)

    def further(d, _):
        both_sides(d, [0] + early)
        return 0

    lax.fori_loop(1, seats, further, 0)
    for e in late:
        handle(e, g.seat)

    def finish(d, _):
        both_sides(d, late)
        return 0

    lax.fori_loop(1, seats, finish, 0)

    def drain(seat, _):
        for e in range(2**phases):
            remote(fresh, whole.at[g.column(e, g.other_flips), seat, 1 - g.core], ssend.at[0, 0],
                   srecv.at[e, seat], g.sibling()).wait_recv()
            forward(e, seat, slot(e, seat), False)
        line(seat, slot(0, seat), False)
        return 0

    lax.fori_loop(0, seats, drain, 0)
    own.wait()


def spread_scratch(columns, n):
    seats, phases = n // 2, columns.bit_length() - 1
    dma = pltpu.SemaphoreType.DMA
    return [
        dma((1,)),
        dma((2, seats)),
        dma((phases, columns, seats)),
        dma((columns, seats)),
        dma((columns, seats)),
        dma((columns, seats)),
    ]


def spread_kernel(columns, n, block, whole, fresh, own, zsend, msend, ssend, recv, srecv):
    grid = Grid(columns, n)
    fresh[...] = block[...].astype(B16)
    grid.greet()
    spread_blocks(grid, fresh, whole, own.at[0], zsend, msend, ssend, recv, srecv)


def spread_call(columns, n, cid, block):
    return pl.pallas_call(
        functools.partial(spread_kernel, columns, n),
        out_shape=sds((columns, n // 2, 2) + block.shape, B16),
        in_specs=[vmem],
        out_specs=anyw,
        scratch_shapes=[pltpu.VMEM(block.shape, B16)] + spread_scratch(columns, n),
        compiler_params=params_of(cid),
        name="spread_weights",
    )(block)


def adam_update(current, gradient, moment_one, moment_two, learn_rate):
    first_new = 0.5 * moment_one + 0.5 * gradient
    second_new = 0.9 * moment_two + 0.1 * gradient * gradient
    first_hat = first_new / (1.0 - 0.5**STEP)
    second_hat = second_new / (1.0 - 0.9**STEP)
    return (
        current - learn_rate * first_hat / (jnp.sqrt(second_hat) + adam_epsilon),
        first_new,
        second_new,
    )


def step_kernel(columns, n, grads, w, m, s, dvec, vw, vm, vs, new_w, new_m, new_s, new_vw, new_vm, new_vs, whole,
                acc, sib, got, up, down, fresh, vbuf, vtrade, lsem, gsend, grecv, psend, precv, usend, urecv,
                vsend, vrecv, tsend, trecv, own, zsend, msend, ssend, recv, srecv):
    g = Grid(columns, n)
    seats, phases = g.seats, g.phases
    slots = 2**phases
    order = sorted(range(slots), key=lambda e: (lowest_bit(e) if e else phases, e == (e & -e)))
    loads = []
    for e in order:
        cp = pltpu.make_async_copy(grads.at[g.column(e), :, g.core], acc.at[e], lsem.at[e])
        cp.start()
        loads.append(cp)

    @pl.when(g.seat == 0)
    def _():
        up[...] = jnp.zeros(up.shape, B16)

    @pl.when(g.seat == seats - 1)
    def _():
        down[...] = jnp.zeros(down.shape, B16)

    vbuf[g.h] = dvec[...]
    g.greet()
    sib_copies = []
    for e in order:
        cp = remote(grads.at[g.column(e, g.other_flips), :, 1 - g.core], sib.at[e], gsend.at[e], grecv.at[e],
                    g.sibling())
        cp.start()
        sib_copies.append(cp)

    def vector_copy(d):
        src = lax.rem(g.h + d, n)
        return remote(vbuf.at[g.h], vbuf.at[g.h], vsend.at[d], vrecv.at[g.h],
                      {"canvas": g.c, "height": src})

    def vector_arrival(d):
        src = lax.rem(g.h + d, n)
        return remote(vbuf.at[src], vbuf.at[src], vsend.at[d], vrecv.at[src],
                      {"canvas": g.c, "height": src})

    for d in range(1, n):
        vector_copy(d).start()

    def local(e, seat, below):
        total = acc[e, seat].astype(F32) + sib[e, seat].astype(F32)
        for k in range(below):
            total = total + got[k, e >> (k + 1), seat].astype(F32)
        return total

    def in_turn(i):
        even = 1 - lax.rem(i, 2)
        return (i // 2) * even + (1 - even) * (seats - 1 - i // 2)

    def phase_copy(k, e, seat):
        return remote(acc.at[e, seat], got.at[k, e >> (k + 1), seat], psend.at[k, e >> (k + 1), seat],
                      precv.at[k, e >> (k + 1), seat], g.mate(k))

    ready = 0
    for e in order:
        loads[ready].wait()
        sib_copies[ready].wait_recv()
        ready += 1
        if e == 0:
            break
        k = lowest_bit(e)

        def one(i, _):
            seat = in_turn(i)
            for q in range(k):
                phase_copy(q, e | (1 << q), seat).wait_recv()
            acc[e, seat] = local(e, seat, k).astype(B16)
            phase_copy(k, e, seat).start()
            return 0

        lax.fori_loop(0, seats, one, 0)

    for d in range(1, n):
        vector_arrival(d).wait_recv()
    vtrade[0, 0] = jnp.sum(vbuf[...], axis=0)
    for k in range(phases):
        cp = remote(vtrade.at[k, 0], vtrade.at[k, 1], tsend.at[k], trecv.at[k], g.mate(k))
        cp.start()
        cp.wait_recv()
        vtrade[k + 1, 0] = vtrade[k, 0] + vtrade[k, 1]
    new_vw[...], new_vm[...], new_vs[...] = adam_update(vw[...], vtrade[phases, 0], vm[...], vs[...], vector_rate)

    def line_copy(step, seat):
        box = up if step > 0 else down
        at = (step + 1) // 2
        return remote(acc.at[0, seat], box.at[seat], usend.at[at, seat], urecv.at[at, seat], g.beside(step))

    def own_column(i, _):
        seat = in_turn(i)
        for q in range(phases):
            phase_copy(q, 1 << q, seat).wait_recv()

        @pl.when(seat > g.seat)
        def _():
            @pl.when(g.seat > 0)
            def _():
                line_copy(1, seat).wait_recv()

            acc[0, seat] = (local(0, seat, phases) + up[seat].astype(F32)).astype(B16)
            line_copy(1, seat).start()

        @pl.when(seat < g.seat)
        def _():
            @pl.when(g.seat < seats - 1)
            def _():
                line_copy(-1, seat).wait_recv()

            acc[0, seat] = (local(0, seat, phases) + down[seat].astype(F32)).astype(B16)
            line_copy(-1, seat).start()

        return 0

    lax.fori_loop(0, seats, own_column, 0)

    @pl.when(g.seat > 0)
    def _():
        line_copy(1, g.seat).wait_recv()

    @pl.when(g.seat < seats - 1)
    def _():
        line_copy(-1, g.seat).wait_recv()

    total = local(0, g.seat, phases) + up[g.seat].astype(F32) + down[g.seat].astype(F32)
    next_w, new_m[...], new_s[...] = adam_update(w[...], total, m[...], s[...], matrix_rate)
    new_w[...] = next_w
    fresh[...] = next_w.astype(B16)
    spread_blocks(g, fresh, whole, own.at[0], zsend, msend, ssend, recv, srecv)
    for cp in sib_copies:
        cp.wait_send()
    for d in range(1, n):
        vector_copy(d).wait_send()
    for k in range(phases):
        remote(vtrade.at[k, 0], vtrade.at[k, 1], tsend.at[k], trecv.at[k], g.mate(k)).wait_send()

    def drain(seat, _):
        for e in range(1, slots):
            phase_copy(lowest_bit(e), e, seat).wait_send()

        @pl.when(seat > g.seat)
        def _():
            line_copy(1, seat).wait_send()

        @pl.when(seat < g.seat)
        def _():
            line_copy(-1, seat).wait_send()

        return 0

    lax.fori_loop(0, seats, drain, 0)


def step_call(columns, n, cid, grads, w, m, s, dvec, vw, vm, vs):
    seats, phases = n // 2, columns.bit_length() - 1
    block = w.shape
    half = max(columns // 2, 1)
    dma = pltpu.SemaphoreType.DMA
    return pl.pallas_call(
        functools.partial(step_kernel, columns, n),
        out_shape=[sds(block, F32)] * 3 + [sds(vw.shape, F32)] * 3 + [sds((columns, seats, 2) + block, B16)],
        in_specs=[anyw] + [vmem] * 7,
        out_specs=[vmem] * 6 + [anyw],
        scratch_shapes=[
            pltpu.VMEM((columns, seats) + block, B16),
            pltpu.VMEM((columns, seats) + block, B16),
            pltpu.VMEM((phases, half, seats) + block, B16),
            pltpu.VMEM((seats,) + block, B16),
            pltpu.VMEM((seats,) + block, B16),
            pltpu.VMEM(block, B16),
            pltpu.VMEM((n,) + vw.shape, F32),
            pltpu.VMEM((phases + 1, 2) + vw.shape, F32),
            dma((columns,)),
            dma((columns,)),
            dma((columns,)),
            dma((phases, half, seats)),
            dma((phases, half, seats)),
            dma((2, seats)),
            dma((2, seats)),
            dma((n,)),
            dma((n,)),
            dma((phases,)),
            dma((phases,)),
        ]
        + spread_scratch(columns, n),
        compiler_params=params_of(cid),
        name="step_weights",
    )(grads, w, m, s, dvec, vw, vm, vs)


class Engine:
    def __init__(self, steps):
        self.steps = steps

    def pump(self, count=1):
        for _ in range(count):
            next(self.steps, None)

    def finish(self):
        for _ in self.steps:
            pass


class Group:
    def __init__(self, grid, number, half_rows, first=0, size=None):
        self.g, self.number, self.half = grid, number, half_rows
        self.first, self.size = first, half_rows if size is None else size
        self.owner = 2 * number + grid.c // 2
        self.is_owner = grid.c // 2 == number

    def row(self, q, seat, core):
        block = (q // 2) * self.g.n + 2 * seat + core
        return pl.multiple_of((2 * block + lax.rem(q, 2)) * self.half + self.first, 16)

    def rows(self, q, seat, core):
        return pl.ds(self.row(q, seat, core), self.size)

    def at_column(self, col):
        return {"canvas": col, "height": self.g.h}

    def halves(self):
        first = 2 * lax.rem(self.g.c, 2)
        return [(0, first), (1, first + 1)]

    def part(self, ref, half):
        return ref.at[pl.ds(half * self.half, self.half)]

    def to_pieces(self, block, piece, send, recv, start):
        g = self.g

        @pl.when(self.is_owner)
        def _():
            for half, col in self.halves():
                @pl.when(col != g.c)
                def _():
                    cp = remote(self.part(block, half), piece, send.at[half], recv.at[0], self.at_column(col))
                    cp.start() if start else cp.wait_send()

                if start:
                    @pl.when(col == g.c)
                    def _():
                        piece[...] = block[half * self.half : (half + 1) * self.half, :]

    def piece_arrived(self, block, piece, send, recv):
        @pl.when(self.owner != self.g.c)
        def _():
            remote(self.part(block, 0), piece, send.at[0], recv.at[0], self.at_column(self.owner)).wait_recv()

    def to_owner(self, piece, block, send, recv, start):
        g = self.g
        half = lax.rem(g.c, 2)
        where = pl.ds(pl.multiple_of(half * self.half, 16), self.half)

        @pl.when(self.owner != g.c)
        def _():
            cp = remote(piece, block.at[where], send.at[0], recv.at[half], self.at_column(self.owner))
            cp.start() if start else cp.wait_send()

        if start:
            @pl.when(self.owner == g.c)
            def _():
                block[where, :] = piece[...]

    def block_arrived(self, piece, block, send, recv):
        g = self.g

        @pl.when(self.is_owner)
        def _():
            for half, col in self.halves():
                @pl.when(col != g.c)
                def _():
                    remote(piece, self.part(block, half), send.at[0], recv.at[half], self.at_column(col)).wait_recv()


def gather_pieces(group, piece, dest, own, zsend, msend, ssend, recv, srecv):
    g = group.g
    seats, phases = g.seats, g.phases
    local = pltpu.make_async_copy(piece, dest.at[group.rows(g.c, g.seat, g.core)], own.at[0])
    local.start()

    def slot(e, seat):
        return dest.at[group.rows(g.column(e), seat, g.core)]

    def forward(e, seat, src, start):
        k_top = phases if e == 0 else lowest_bit(e)
        for k in range(k_top - 1, -1, -1):
            cp = remote(src, slot(e, seat), msend.at[k, e, seat], recv.at[e | (1 << k), seat], g.mate(k))
            cp.start() if start else cp.wait_send()
        cp = remote(src, slot(e, seat), ssend.at[e, seat], srecv.at[e, seat], g.sibling())
        cp.start() if start else cp.wait_send()

    def along(seat, step, src, start):
        cp = remote(src, slot(0, seat), zsend.at[(step + 1) // 2, seat], recv.at[0, seat], g.beside(step))
        cp.start() if start else cp.wait_send()

    def line(seat, src, start):
        @pl.when((seat <= g.seat) & (g.seat < seats - 1))
        def _():
            along(seat, 1, src, start)

        @pl.when((seat >= g.seat) & (g.seat > 0))
        def _():
            along(seat, -1, src, start)

    def handle(e, seat):
        remote(piece, slot(e, seat), ssend.at[0, 0], recv.at[e, seat], g.sibling()).wait_recv()
        if e == 0:
            line(seat, slot(0, seat), True)
        forward(e, seat, slot(e, seat), True)

    early = sorted((e for e in range(1, 2**phases) if lowest_bit(e) > 0), key=lambda e: -lowest_bit(e))
    late = [e for e in range(1, 2**phases) if lowest_bit(e) == 0]

    def both_sides(d, todo):
        for side in (-1, 1):
            seat = g.seat + side * d

            @pl.when((seat >= 0) & (seat < seats))
            def _():
                for e in todo:
                    handle(e, seat)

    line(g.seat, piece, True)
    forward(0, g.seat, piece, True)
    yield
    for e in early:
        handle(e, g.seat)
    yield
    for d in range(1, seats):
        both_sides(d, [0] + early)
        yield
    for e in late:
        handle(e, g.seat)
    yield
    for d in range(1, seats):
        both_sides(d, late)
        yield

    def drain(seat, _):
        for e in range(2**phases):
            remote(piece, dest.at[group.rows(g.column(e, g.other_flips), seat, 1 - g.core)], ssend.at[0, 0],
                   srecv.at[e, seat], g.sibling()).wait_recv()
            forward(e, seat, slot(e, seat), False)
        line(seat, slot(0, seat), False)
        return 0

    lax.fori_loop(0, seats, drain, 0)
    local.wait()


def gather_pieces_scratch(columns, n):
    seats, phases = n // 2, columns.bit_length() - 1
    dma = pltpu.SemaphoreType.DMA
    return [
        dma((1,)),
        dma((2, seats)),
        dma((phases, columns, seats)),
        dma((columns, seats)),
        dma((columns, seats)),
        dma((columns, seats)),
    ]


def reduce_pieces(group, src, piece, sib, got, box, gsend, grecv, psend, precv, usend, urecv):
    g = group.g
    seats, phases = g.seats, g.phases
    slots = 2**phases
    order = sorted(range(slots), key=lambda e: (lowest_bit(e) if e else phases, e == (e & -e)))
    turns = [i // 2 if i % 2 == 0 else seats - 1 - i // 2 for i in range(seats)]

    def mine(e, seat):
        return group.rows(g.column(e), seat, g.core)

    def sibling_copy(e, seat):
        return remote(src.at[group.rows(g.column(e, g.other_flips), seat, 1 - g.core)], sib.at[e, seat],
                      gsend.at[e, seat], grecv.at[e, seat], g.sibling())

    def phase_copy(k, e, seat):
        at = (k, e >> (k + 1), seat)
        return remote(src.at[mine(e, seat), :], got.at[at], psend.at[at], precv.at[at], g.mate(k))

    def line_copy(seat):
        return remote(src.at[mine(0, seat), :], box.at[g.seat], usend.at[seat], urecv.at[g.seat],
                      {"canvas": g.c, "height": 2 * seat + g.core})

    def line_arrival(seat):
        return remote(src.at[mine(0, seat), :], box.at[seat], usend.at[seat], urecv.at[seat],
                      {"canvas": g.c, "height": 2 * seat + g.core})

    def local(e, seat, below):
        total = src[mine(e, seat), :].astype(F32) + sib[e, seat].astype(F32)
        for k in range(below):
            total = total + got[k, e >> (k + 1), seat].astype(F32)
        return total

    for e in order:
        for seat in turns:
            sibling_copy(e, seat).start()
    yield
    for e in order:
        if e == 0:
            break
        k = lowest_bit(e)
        for seat in turns:
            sibling_copy(e, seat).wait_recv()
            for q in range(k):
                phase_copy(q, e | (1 << q), seat).wait_recv()
            src[mine(e, seat), :] = local(e, seat, k).astype(B16)
            phase_copy(k, e, seat).start()
            yield
    for seat in turns:
        sibling_copy(0, seat).wait_recv()
        for q in range(phases):
            phase_copy(q, 1 << q, seat).wait_recv()

        @pl.when(seat != g.seat)
        def _():
            src[mine(0, seat), :] = local(0, seat, phases).astype(B16)
            line_copy(seat).start()

        yield
    total = local(0, g.seat, phases)
    for seat in turns:
        @pl.when(seat != g.seat)
        def _():
            line_arrival(seat).wait_recv()

        total = total + jnp.where(seat == g.seat, 0.0, box[seat].astype(F32))
    piece[...] = total.astype(B16)
    yield

    def drain(seat, _):
        for e in range(slots):
            sibling_copy(e, seat).wait_send()
            if e > 0:
                phase_copy(lowest_bit(e), e, seat).wait_send()

        @pl.when(seat != g.seat)
        def _():
            line_copy(seat).wait_send()

        return 0

    lax.fori_loop(0, seats, drain, 0)


def reduce_pieces_scratch(columns, n, half_rows):
    seats, phases = n // 2, columns.bit_length() - 1
    half = columns // 2
    dma = pltpu.SemaphoreType.DMA
    block = (half_rows, C)
    return [
        pltpu.VMEM((columns, seats) + block, B16),
        pltpu.VMEM((phases, half, seats) + block, B16),
        pltpu.VMEM((seats,) + block, B16),
        dma((columns, seats)),
        dma((columns, seats)),
        dma((phases, half, seats)),
        dma((phases, half, seats)),
        dma((seats,)),
        dma((seats,)),
    ]


class Named:
    def __init__(self, shapes, refs):
        refs = list(refs)
        for name, shape in shapes.items():
            if isinstance(shape, list):
                setattr(self, name, [refs.pop(0) for _ in shape])
            else:
                setattr(self, name, refs.pop(0))


def named_call(kernel, name, cid, inputs, outputs, scratch):
    shapes = {**inputs, **outputs, **scratch}
    flat = []
    for value in scratch.values():
        flat += value if isinstance(value, list) else [value]
    results = pl.pallas_call(
        lambda *refs: kernel(Named(shapes, refs)),
        out_shape=[sds(shape, kind) for shape, kind, _ in outputs.values()],
        in_specs=[spec for _, spec in inputs.values()],
        out_specs=[spec for _, _, spec in outputs.values()],
        scratch_shapes=flat,
        compiler_params=params_of(cid),
        name=name,
    )(*[array for array, _ in inputs.values()])
    return dict(zip(outputs, results))


def greet_all(grid):
    barrier = pltpu.get_barrier_semaphore()
    for d in range(1, grid.n):
        pl.semaphore_signal(
            barrier, inc=1, device_id={"canvas": grid.c, "height": lax.rem(grid.h + d, grid.n)}, device_id_type=MESH)
    for d in range(1, grid.columns):
        pl.semaphore_signal(
            barrier, inc=1, device_id={"canvas": lax.rem(grid.c + d, grid.columns), "height": grid.h},
            device_id_type=MESH)
    pl.semaphore_wait(barrier, grid.n - 1 + grid.columns - 1)


def first_kernel(columns, n, dims, R):
    g = Grid(columns, n)
    half = R.block.shape[0] // 2
    groups = [Group(g, i, half) for i in range(2)]
    R.low[...] = R.block[...].astype(B16)
    greet_all(g)
    for i, group in enumerate(groups):
        group.to_pieces(R.low, R.pieces.at[i], R.tsend.at[i], R.trecv.at[i], True)
    weights = [R.w_top, R.w_low]
    engines = [
        Engine(gather_pieces(group, R.pieces.at[i], weights[i], *(R.gather0 if i == 0 else R.gather1)))
        for i, group in enumerate(groups)
    ]
    turn = [0]
    mine = g.h // (n // 2)
    cot_copy = remote(R.cot.at[1 - mine], R.far_cot, R.csem.at[0], R.csem.at[1],
                      {"canvas": g.c, "height": lax.rem(g.h + n // 2, n)})

    def pump():
        if turn[0] == 0:
            groups[0].piece_arrived(R.low, R.pieces.at[0], R.tsend.at[0], R.trecv.at[0])
        engines[0].pump()
        if turn[0] == g.seats:
            cot_copy.start()
        turn[0] += 1

    layout_body(n, dims, R.x, R.pick, R.spread, R.ids_px, R.ids_lane, R.ids_all, R.mean1, R.inv1, R.div, R.cnt,
                R.col_l, R.col_r, R.row_u, R.row_d, *R.layout, pump=pump)
    pump()
    conv = Convolver(n, dims, R.x, R.pick, R.spread, R.cnt, R.col_l, R.col_r, R.row_u, R.row_d, R.halo, R.buf,
                     R.tmp_a, R.tmp_b, R.send, R.recv, R.hsend, R.hrecv)
    vec = R.vec
    conv.activate(R.x, R.mean1, R.inv1, vec[0:1, :], vec[1:2, :], R.s1, 0, pump)
    out_s1 = pltpu.make_async_copy(R.s1, R.s1_out, R.osem.at[0])
    out_s1.start()
    while turn[0] <= g.seats:
        pump()
    engines[0].finish()
    out_top = pltpu.make_async_copy(R.w_top, R.top, R.osem.at[1])
    out_top.start()
    groups[1].piece_arrived(R.low, R.pieces.at[1], R.tsend.at[1], R.trecv.at[1])
    pump_low = engines[1].pump
    pump_low()

    def emit_first(at, total):
        R.y1[at, :] = total + vec[2:3, :]

    conv.convolve(R.s1, lambda dr: [(0, 3 * C, R.w_top, 3 * C * dr)], emit_first, pump_low)
    out_y1 = pltpu.make_async_copy(R.y1, R.y1_out, R.osem.at[2])
    out_y1.start()
    conv.statistics(R.y1, R.mean2, R.inv2, 0, pump_low)
    conv.activate(R.y1, R.mean2, R.inv2, vec[3:4, :], vec[4:5, :], R.s2, 1, pump_low)
    out_s2 = pltpu.make_async_copy(R.s2, R.s2_out, R.osem.at[3])
    out_s2.start()
    engines[1].finish()
    out_low = pltpu.make_async_copy(R.w_low, R.bottom, R.osem.at[4])
    out_low.start()

    def emit_second(at, total):
        R.hid[at, :] = total + vec[5:6, :] + R.x[at, :].astype(F32)

    def second(dr):
        if dr == 0:
            return [(0, 2 * C, R.w_top, 9 * C), (2 * C, 3 * C, R.w_low, 0)]
        return [(0, 3 * C, R.w_low, 3 * C * dr - 2 * C)]

    conv.convolve(R.s2, second, emit_second)
    conv.statistics(R.hid, R.mean3, R.inv3, 1)
    conv.normalise(R.hid, R.mean3, R.inv3, vec[6:7, :], vec[7:8, :], R.u)
    for cp in conv.sent:
        cp.wait_send()
    for i, group in enumerate(groups):
        group.to_pieces(R.low, R.pieces.at[i], R.tsend.at[i], R.trecv.at[i], False)
    for cp in (out_s1, out_top, out_y1, out_s2, out_low, cot_copy):
        cp.wait()


def first_call(columns, n, dims, x, pick, spread, ids_px, ids_lane, vec, block, cot):
    canvases, rows, width = dims
    px = canvases * rows * width
    cells = px // UNIT
    stats = canvases * CROPS
    tall = (canvases, rows + 2, width)
    half = block.shape[0] // 2
    dma = pltpu.SemaphoreType.DMA
    inputs = dict(x=(x, vmem), pick=(pick, vmem), spread=(spread, vmem), ids_px=(ids_px, vmem),
                  ids_lane=(ids_lane, vmem), vec=(vec, vmem), block=(block, vmem),
                  cot=(cot, anyw))
    cell = ((cells, C), F32, vmem)
    outputs = dict(
        ids_all=((n,) + ids_lane.shape, F32, vmem), mean1=cell, inv1=cell, div=((stats, LANES), F32, vmem),
        cnt=((stats, LANES), F32, vmem), col_l=(tall + (LANES,), F32, vmem), col_r=(tall + (LANES,), F32, vmem),
        row_u=((px, LANES), F32, vmem), row_d=((px, LANES), F32, vmem), hid=((px, C), F32, vmem),
        u=((px, C), B16, vmem), mean2=cell, inv2=cell, mean3=cell, inv3=cell, y1_out=((px, C), F32, anyw),
        s1_out=(tall + (3 * C,), B16, anyw), s2_out=(tall + (3 * C,), B16, anyw),
        top=((11 * C, C), B16, anyw), bottom=((11 * C, C), B16, anyw), far_cot=(cot.shape[1:], B16, anyw))
    scratch = dict(
        csem=dma((2,)), y1=pltpu.VMEM((px, C), F32), s1=pltpu.VMEM(tall + (3 * C,), B16), s2=pltpu.VMEM(tall + (3 * C,), B16),
        w_top=pltpu.VMEM((11 * C, C), B16), w_low=pltpu.VMEM((11 * C, C), B16), low=pltpu.VMEM(block.shape, B16),
        pieces=pltpu.VMEM((2, half, C), B16), tsend=dma((2, 2)), trecv=dma((2, 1)),
        gather0=gather_pieces_scratch(columns, n), gather1=gather_pieces_scratch(columns, n),
        layout=layout_scratch(n, dims, ids_lane), halo=pltpu.VMEM((2, 2, canvases, width, C), B16),
        buf=pltpu.VMEM((2, n, stats, LANES), F32), tmp_a=pltpu.VMEM((cells, C), F32),
        tmp_b=pltpu.VMEM((cells, C), F32), send=dma((2, n)), recv=dma((2, n)), hsend=dma((2, 2)),
        hrecv=dma((2, 2)), osem=dma((5,)))
    return named_call(functools.partial(first_kernel, columns, n, dims), "first_forward", 1, inputs, outputs, scratch)


class Backer:
    def __init__(self, n, dims, R):
        self.n, self.dims, self.R = n, dims, R
        self.px = dims[0] * dims[1] * dims[2]
        self.cells = self.px // UNIT
        self.sent = []

    @staticmethod
    def pixels(i):
        return pl.ds(i * 16 * UNIT, 16 * UNIT)

    def norm_sums(self, grad_of, source, mean, inv, gain, rnd):
        R = self.R

        def body(i, carry):
            dg, db = carry
            at = self.pixels(i)
            unit = (source[at, :].astype(F32) - over_cells(mean, i)) * over_cells(inv, i)
            d = grad_of(i, unit)
            R.norm[at, :] = unit
            e = d * gain
            R.part[at, :] = e
            cross = d * unit
            here = pl.ds(i * 16, 16)
            R.tmp_a[here, :] = jnp.sum(e.reshape(16, UNIT, C), axis=1)
            R.tmp_b[here, :] = jnp.sum((cross * gain).reshape(16, UNIT, C), axis=1)
            return (dg + jnp.sum(cross, axis=0, keepdims=True), db + jnp.sum(d, axis=0, keepdims=True))

        zero = jnp.zeros((1, C), F32)
        dg, db = lax.fori_loop(0, self.cells // 16, body, (zero, zero))
        R.buf[rnd, 0] = pack([group_totals(R.pick, R.tmp_a[...]), group_totals(R.pick, R.tmp_b[...])])
        copies = spread_copies(self.n, R.buf, R.send, R.recv, rnd)
        for cp in copies:
            cp.start()
        self.sent = self.sent + copies
        return copies, dg, db

    def norm_finish(self, copies, rnd, inv, emit):
        R = self.R
        for cp in copies:
            cp.wait_recv()
        gathered = jnp.sum(R.buf[rnd], axis=0) / R.div[...]
        R.tmp_a[...] = split_dot(R.spread[...], unpack(gathered))
        R.tmp_b[...] = split_dot(R.spread[...], unpack(shift_down(gathered, 1)))

        def body(i, _):
            at = self.pixels(i)
            emit(i, over_cells(inv, i) * (
                R.part[at, :] - over_cells(R.tmp_a, i) - R.norm[at, :] * over_cells(R.tmp_b, i)))
            return 0

        lax.fori_loop(0, self.cells // 16, body, 0)

    def send_rows(self, source, rnd):
        R = self.R
        canvases, rows, width = self.dims

        def one(v, r):
            at = pl.ds(pl.multiple_of((v * rows + r) * width, width), width)
            R.d3[v, r + 1] = shift_columns(source[at, :].astype(F32), R.col_l[v, r + 1], R.col_r[v, r + 1])

        def edges(v, _):
            one(v, 0)
            one(v, rows - 1)
            return 0

        lax.fori_loop(0, canvases, edges, 0)
        mid = pl.ds(C, C)
        up, down = halo_copies(self.n, R.d3.at[:, 1, :, mid], R.d3.at[:, rows, :, mid], R.halo.at[rnd],
                               R.hsend.at[rnd], R.hrecv.at[rnd])
        start_halo(self.n, up, down)

        def inner(i, _):
            one(i // (rows - 2), 1 + lax.rem(i, rows - 2))
            return 0

        if rows > 2:
            lax.fori_loop(0, canvases * (rows - 2), inner, 0)
        return up, down

    def finish_rows(self, up, down, rnd):
        R = self.R
        canvases, rows, _ = self.dims
        wait_halo(self.n, up, down, R.halo.at[rnd], 0.0)
        for v in range(canvases):
            for side, r in ((0, 0), (1, rows + 1)):
                R.d3[v, r] = shift_columns(R.halo[rnd, side, v].astype(F32), R.col_l[v, r], R.col_r[v, r])

    def convolve_back(self, weights, pump=no_pump):
        R = self.R
        canvases, rows, width = self.dims
        plane = rows * width
        nt = (((1,), (1,)), ((), ()))
        for v in range(canvases):
            at = pl.ds(v * plane, plane)
            total = None
            for dr in (1, 0, 2):
                acc = None
                for dc in range(3):
                    ref, row = weights(3 * (2 - dr) + (2 - dc))
                    lhs = R.d3[v, dr : dr + rows, :, dc * C : (dc + 1) * C].reshape(plane, C)
                    term = lax.dot_general(lhs, ref[row : row + C, :], nt, preferred_element_type=F32)
                    acc = term if acc is None else acc + term
                if dr == 0:
                    acc = acc * wide(R.row_u[at, :])
                if dr == 2:
                    acc = acc * wide(R.row_d[at, :])
                total = acc if total is None else total + acc
                pump()
            R.part[at, :] = total

    def mask_rows(self, source):
        R = self.R

        def body(i, _):
            at = self.pixels(i)
            value = source[at, :].astype(F32)
            R.low_u[at, :] = (value * wide(R.row_u[at, :])).astype(B16)
            R.low_d[at, :] = (value * wide(R.row_d[at, :])).astype(B16)
            return 0

        lax.fori_loop(0, self.cells // 16, body, 0)

    def weight_grad(self, s, grad, dest, pump=no_pump):
        R = self.R
        canvases, rows, width = self.dims
        plane = rows * width
        tn = (((0,), (0,)), ((), ()))
        for dr, source in ((0, R.low_u), (1, grad), (2, R.low_d)):
            for dc in range(3):
                acc = None
                for v in range(canvases):
                    lhs = s[v, dr : dr + rows, :, dc * C : (dc + 1) * C].reshape(plane, C)
                    term = lax.dot_general(
                        lhs, source[v * plane : (v + 1) * plane, :], tn, preferred_element_type=F32)
                    acc = term if acc is None else acc + term
                ref, row = dest(3 * dr + dc)
                ref[row : row + C, :] = acc.astype(B16)
                pump()


def back_kernel(columns, n, dims, R):
    g = Grid(columns, n)
    half = R.sum_low.shape[0]
    group = Group(g, 1, half)
    load_s = pltpu.make_async_copy(R.s2, R.s, R.lsem.at[0])
    load_s.start()
    load_k = second_matrix(R.top, R.bottom, R.k, R.ksem)
    load_att = pltpu.make_async_copy(R.datt, R.g_low.at[pl.ds(7 * C, 4 * C)], R.lsem.at[1])
    for cp in load_k + [load_att]:
        cp.start()
    greet_all(g)
    vec = R.vec
    back = Backer(n, dims, R)
    copies, dg3, db3 = back.norm_sums(lambda i, unit: R.du[back.pixels(i), :], R.hid, R.mean3, R.inv3, vec[6:7, :], 0)

    def emit_hidden(i, value):
        at = back.pixels(i)
        total = R.cot[at, :].astype(F32) + value
        R.dh[at, :] = total
        R.grad[at, :] = total.astype(B16)

    back.norm_finish(copies, 0, R.inv3, emit_hidden)
    up, down = back.send_rows(R.grad, 0)
    back.mask_rows(R.grad)
    load_s.wait()

    def dest_two(tap):
        return (R.g_top, (9 + tap) * C) if tap < 2 else (R.g_low, (tap - 2) * C)

    back.weight_grad(R.s, R.grad, dest_two)
    load_s = pltpu.make_async_copy(R.s1, R.s, R.lsem.at[0])
    load_s.start()
    load_att.wait()
    engine = Engine(reduce_pieces(group, R.g_low, R.sum_low, *R.reduce))
    engine.pump()
    dc2 = jnp.sum(R.grad[...].astype(F32), axis=0, keepdims=True)
    back.finish_rows(up, down, 0)
    for cp in load_k:
        cp.wait()
    back.convolve_back(lambda tap: (R.k, tap * C), engine.pump)
    gain2, bias2 = vec[3:4, :], vec[4:5, :]

    def grad_two(i, unit):
        return R.part[back.pixels(i), :] * silu_slope(unit * gain2 + bias2)

    copies, dg2, db2 = back.norm_sums(grad_two, R.y1, R.mean2, R.inv2, gain2, 1)
    engine.pump(2)

    def emit_grad(i, value):
        R.grad[back.pixels(i), :] = value.astype(B16)

    back.norm_finish(copies, 1, R.inv2, emit_grad)
    engine.pump(2)
    back.mask_rows(R.grad)
    dc1 = jnp.sum(R.grad[...].astype(F32), axis=0, keepdims=True)
    load_s.wait()
    back.weight_grad(R.s, R.grad, lambda tap: (R.g_top, tap * C), engine.pump)
    R.dvec[...] = jnp.concatenate([dc1, dg2, db2, dc2, dg3, db3, jnp.zeros((2, C), F32)], axis=0)
    engine.finish()
    for cp in back.sent:
        cp.wait_send()


def back_call(columns, n, dims, cot, du, hid, y1, norms, s1, s2, pick, spread, div, masks, vec, top, bottom, datt,
              block_rows):
    canvases, rows, width = dims
    px = canvases * rows * width
    cells = px // UNIT
    stats = canvases * CROPS
    dma = pltpu.SemaphoreType.DMA
    names = ("mean2", "inv2", "mean3", "inv3")
    inputs = dict(cot=(cot, vmem), du=(du, vmem), hid=(hid, vmem), y1=(y1, vmem), s1=(s1, anyw), s2=(s2, anyw),
                  pick=(pick, vmem), spread=(spread, vmem), div=(div, vmem), vec=(vec, vmem), top=(top, anyw),
                  bottom=(bottom, anyw), datt=(datt, anyw),
                  **{k: (v, vmem) for k, v in zip(names, norms)},
                  **{k: (v, vmem) for k, v in zip(("col_l", "col_r", "row_u", "row_d"), masks)})
    outputs = dict(dh=((px, C), F32, vmem), grad=((px, C), B16, vmem), g_top=((11 * C, C), B16, vmem),
                   dvec=((8, C), F32, vmem), sum_low=((block_rows // 2, C), B16, vmem))
    scratch = dict(
        g_low=pltpu.VMEM((11 * C, C), B16), s=pltpu.VMEM(s1.shape, B16), k=pltpu.VMEM((9 * C, C), B16),
        d3=pltpu.VMEM(s1.shape, B16), low_u=pltpu.VMEM((px, C), B16), low_d=pltpu.VMEM((px, C), B16),
        part=pltpu.VMEM((px, C), F32), norm=pltpu.VMEM((px, C), F32),
        halo=pltpu.VMEM((1, 2, canvases, width, C), B16), buf=pltpu.VMEM((2, n, stats, LANES), F32),
        tmp_a=pltpu.VMEM((cells, C), F32), tmp_b=pltpu.VMEM((cells, C), F32),
        reduce=reduce_pieces_scratch(columns, n, block_rows // 2), lsem=dma((5,)), ksem=dma((3,)),
        send=dma((2, n)), recv=dma((2, n)), hsend=dma((1, 2)), hrecv=dma((1, 2)))
    return named_call(functools.partial(back_kernel, columns, n, dims), "back", 7, inputs, outputs, scratch)


def update_kernel(columns, n, dims, R):
    g = Grid(columns, n)
    half = R.w.shape[0] // 2
    upper, lower = Group(g, 0, half), Group(g, 1, half)
    load_k = pltpu.make_async_copy(R.top.at[pl.ds(0, 9 * C)], R.k, R.ksem.at[0])
    load_k.start()
    load_g = pltpu.make_async_copy(R.g_in, R.g_top, R.ksem.at[1])
    load_g.start()
    load_p = pltpu.make_async_copy(R.bottom.at[pl.ds(10 * C, C)], R.wp, R.ksem.at[2])
    load_p.start()
    greet_all(g)
    vec = R.vec
    lower.to_owner(R.sum_low, R.totals.at[1], R.asend.at[1], R.arecv.at[1], True)
    load_g.wait()
    reducer = Engine(reduce_pieces(upper, R.g_top, R.sum_top, *R.reduce))
    reducer.pump()
    back = Backer(n, dims, R)
    up, down = back.send_rows(R.grad, 0)
    reducer.pump(2)

    def adam(group, totals):
        @pl.when(group.is_owner)
        def _():
            total = totals[...].astype(F32)
            next_w, R.new_m[...], R.new_s[...] = adam_update(R.w[...], total, R.m[...], R.v[...], matrix_rate)
            R.new_w[...] = next_w
            R.fresh[...] = next_w.astype(B16)

    load_p.wait()
    for v in range(dims[0]):
        at = pl.ds(v * dims[1] * dims[2], dims[1] * dims[2])
        R.output[at, :] = (
            R.hid[at, :] + jnp.dot(R.o[at, :], R.wp[...], preferred_element_type=F32) + vec[10:11, :])
    lower.block_arrived(R.sum_low, R.totals.at[1], R.asend.at[1], R.arecv.at[1])
    adam(lower, R.totals.at[1])
    lower.to_pieces(R.fresh, R.pieces.at[1], R.tsend.at[1], R.trecv.at[1], True)
    reducer.pump(2)
    back.finish_rows(up, down, 0)
    load_k.wait()
    back.convolve_back(lambda tap: (R.k, tap * C), reducer.pump)
    lower.piece_arrived(R.fresh, R.pieces.at[1], R.tsend.at[1], R.trecv.at[1])
    gather_low = Engine(gather_pieces(lower, R.pieces.at[1], R.new_low, *R.gather1))
    gain1, bias1 = vec[0:1, :], vec[1:2, :]

    def grad_one(i, unit):
        return R.part[back.pixels(i), :] * silu_slope(unit * gain1 + bias1)

    copies, dg1, db1 = back.norm_sums(grad_one, R.x, R.mean1, R.inv1, gain1, 0)
    reducer.pump(2)
    R.vbuf[g.h] = jnp.concatenate([dg1, db1, R.dvec[0:6, :], R.dvec_att[...]], axis=0)
    vector_sends = [
        remote(R.vbuf.at[g.h], R.vbuf.at[g.h], R.vsend.at[d], R.vrecv.at[g.h],
               {"canvas": g.c, "height": lax.rem(g.h + d, n)})
        for d in range(1, n)
    ]
    for cp in vector_sends:
        cp.start()

    def emit_input(i, value):
        at = back.pixels(i)
        R.igrad[at, :] = R.dh[at, :] + value

    back.norm_finish(copies, 0, R.inv1, emit_input)
    reducer.pump(2)
    for d in range(1, n):
        src = lax.rem(g.h + d, n)
        remote(R.vbuf.at[src], R.vbuf.at[src], R.vsend.at[d], R.vrecv.at[src],
               {"canvas": g.c, "height": src}).wait_recv()
    R.vtrade[0, 0] = jnp.sum(R.vbuf[...], axis=0)

    def trade(k):
        return remote(R.vtrade.at[k, 0], R.vtrade.at[k, 1], R.qsend.at[k], R.qrecv.at[k], g.mate(k))

    trade(0).start()
    reducer.finish()
    upper.to_owner(R.sum_top, R.totals.at[0], R.asend.at[0], R.arecv.at[0], True)
    gather_low.pump()
    for k in range(g.phases):
        trade(k).wait_recv()
        R.vtrade[k + 1, 0] = R.vtrade[k, 0] + R.vtrade[k, 1]
        if k + 1 < g.phases:
            trade(k + 1).start()
    R.new_vw[...], R.new_vm[...], R.new_vs[...] = adam_update(
        R.vw[...], R.vtrade[g.phases, 0], R.vm[...], R.vs[...], vector_rate)
    upper.block_arrived(R.sum_top, R.totals.at[0], R.asend.at[0], R.arecv.at[0])
    adam(upper, R.totals.at[0])
    upper.to_pieces(R.fresh, R.pieces.at[0], R.tsend.at[0], R.trecv.at[0], True)
    gather_low.pump()
    upper.piece_arrived(R.fresh, R.pieces.at[0], R.tsend.at[0], R.trecv.at[0])
    gather_top = Engine(gather_pieces(upper, R.pieces.at[0], R.new_top, *R.gather0))
    gather_top.pump()
    for _ in range(2 * g.seats + 2):
        gather_low.pump()
        gather_top.pump()
    gather_low.finish()
    gather_top.finish()
    for cp in back.sent + vector_sends:
        cp.wait_send()
    for k in range(g.phases):
        trade(k).wait_send()
    for i, group in enumerate((upper, lower)):
        group.to_owner((R.sum_top, R.sum_low)[i], R.totals.at[i], R.asend.at[i], R.arecv.at[i], False)
        group.to_pieces(R.fresh, R.pieces.at[i], R.tsend.at[i], R.trecv.at[i], False)


def update_call(columns, n, dims, grad, dh, x, mean1, inv1, pick, spread, div, masks, vec, top, bottom, g_top, sum_low, dvec,
                dvec_att, w, m, v, vw, vm, vs, hid, o):
    canvases, rows, width = dims
    px = canvases * rows * width
    cells = px // UNIT
    stats = canvases * CROPS
    block = w.shape
    half = block[0] // 2
    seats, phases = n // 2, columns.bit_length() - 1
    dma = pltpu.SemaphoreType.DMA
    tall = (canvases, rows + 2, width, 3 * C)
    arrays = dict(grad=grad, dh=dh, x=x, mean1=mean1, inv1=inv1, pick=pick, spread=spread, div=div, vec=vec,
                  g_in=g_top, sum_low=sum_low, dvec=dvec, dvec_att=dvec_att, w=w, m=m, v=v, vw=vw, vm=vm, vs=vs, hid=hid, o=o)
    inputs = dict(top=(top, anyw), bottom=(bottom, anyw), **{k: (a, vmem) for k, a in arrays.items()},
                  **{k: (a, vmem) for k, a in zip(("col_l", "col_r", "row_u", "row_d"), masks)})
    inputs["g_in"] = (g_top, anyw)
    outputs = dict(igrad=((px, C), F32, vmem), output=((px, C), F32, vmem), new_w=(block, F32, vmem), new_m=(block, F32, vmem),
                   new_s=(block, F32, vmem), new_vw=(vw.shape, F32, vmem), new_vm=(vw.shape, F32, vmem),
                   new_vs=(vw.shape, F32, vmem), new_top=((11 * C, C), B16, anyw), new_low=((11 * C, C), B16, anyw))
    scratch = dict(
        g_top=pltpu.VMEM((11 * C, C), B16), sum_top=pltpu.VMEM((half, C), B16), totals=pltpu.VMEM((2,) + block, B16),
        fresh=pltpu.VMEM(block, B16), pieces=pltpu.VMEM((2, half, C), B16), k=pltpu.VMEM((9 * C, C), B16),
        d3=pltpu.VMEM(tall, B16), part=pltpu.VMEM((px, C), F32), norm=pltpu.VMEM((px, C), F32),
        halo=pltpu.VMEM((1, 2, canvases, width, C), B16), buf=pltpu.VMEM((1, n, stats, LANES), F32),
        tmp_a=pltpu.VMEM((cells, C), F32), tmp_b=pltpu.VMEM((cells, C), F32),
        vbuf=pltpu.VMEM((n,) + vw.shape, F32), vtrade=pltpu.VMEM((phases + 1, 2) + vw.shape, F32),
        reduce=reduce_pieces_scratch(columns, n, half), gather0=gather_pieces_scratch(columns, n),
        gather1=gather_pieces_scratch(columns, n), wp=pltpu.VMEM((C, C), B16), ksem=dma((3,)), asend=dma((2, 1)), arecv=dma((2, 2)),
        tsend=dma((2, 2)), trecv=dma((2, 1)), vsend=dma((n,)), vrecv=dma((n,)), qsend=dma((phases,)),
        qrecv=dma((phases,)), send=dma((1, n)), recv=dma((1, n)), hsend=dma((1, 2)), hrecv=dma((1, 2)))
    return named_call(functools.partial(update_kernel, columns, n, dims), "update", 9, inputs, outputs, scratch)


def attend_kernel(n, keep, R):
    me = lax.axis_index("height")
    half = n // 2
    mine = me // half
    base = mine * half
    core = lax.rem(me, 2)
    partner = lax.rem(me + half, n)
    sibling = other_core(me)
    mates = half // 2
    seat = (me - base) // 2
    seg = R.u.shape[1]
    total = n * seg
    scale = C ** (-0.5)
    nt = (((1,), (1,)), ((), ()))
    tn = (((0,), (0,)), ((), ()))
    vec = R.vec

    def mate(j, c=core):
        return base + c + 2 * lax.rem(seat + j, mates)

    def far_of(b):
        return lax.rem(b + half, n)

    def to(h):
        return {"canvas": lax.axis_index("canvas"), "height": h}

    loads = [pltpu.make_async_copy(R.low.at[pl.ds(7 * C, 4 * C)], R.w, R.lsem.at[0])]
    if keep:
        loads += [
            pltpu.make_async_copy(R.far_cot, R.dz.at[pl.ds(0, seg)], R.lsem.at[1]),
            pltpu.make_async_copy(R.cot.at[mine], R.dz.at[pl.ds(seg, seg)], R.lsem.at[2]),
        ]
    for cp in loads:
        cp.start()
    own = pltpu.make_async_copy(R.u_in.at[mine], R.u.at[me], R.lsem.at[3])
    own.start()
    barrier = pltpu.get_barrier_semaphore()
    peers = [partner, sibling] + [mate(j) for j in range(1, mates)]
    for p in peers:
        pl.semaphore_signal(barrier, inc=1, device_id=to(p), device_id_type=MESH)
    pl.semaphore_wait(barrier, len(peers))
    started = []

    def push(src, slot, dest):
        cp = remote(src, R.u.at[slot], R.gsend.at[len(started)], R.grecv.at[slot], to(dest))
        cp.start()
        started.append(cp)

    def block(b):
        return pl.ds(pl.multiple_of(b * seg, seg), seg)

    def project(b):
        piece = R.u[b]
        R.k[block(b), :] = jnp.dot(piece, R.w[C : 2 * C, :], preferred_element_type=F32).astype(B16)
        R.v[block(b), :] = (
            jnp.dot(piece, R.w[2 * C : 3 * C, :], preferred_element_type=F32) + vec[9:10, :]
        ).astype(B16)

    def arrived(slot):
        remote(R.u_in.at[0], R.u.at[slot], R.gsend.at[0], R.grecv.at[slot], to(partner)).wait_recv()

    push(R.u_in.at[1 - mine], me, partner)
    for j in range(1, mates):
        push(R.u_in.at[mine], me, mate(j))
    push(R.u_in.at[mine], me, sibling)
    for cp in loads:
        cp.wait()
    own.wait()
    project(me)
    arrived(sibling)
    project(sibling)
    key_ids = jnp.concatenate([R.ids_all[b, pl.ds(mine, 1), :] for b in range(n)], axis=1)
    for i, b in enumerate((partner, me)):
        turned = jnp.transpose(R.ids_all[b])
        picked = jnp.where(mine == 0, turned[:, 0:1], turned[:, 1:2])
        R.qid[i * seg : (i + 1) * seg, :] = jnp.broadcast_to(picked, (seg, LANES))
    if keep:
        R.dout[...] = lax.dot_general(
            R.dz[...], R.w[3 * C : 4 * C, :], nt, preferred_element_type=F32).astype(B16)
    arrived(partner)
    for j in range(1, mates):
        push(R.u.at[partner], partner, mate(j))
    push(R.u.at[partner], partner, sibling)
    project(partner)
    for j in range(1, mates):
        friend = mate(mates - j)
        arrived(friend)
        push(R.u.at[friend], friend, sibling)
        project(friend)
    arrived(far_of(sibling))
    project(far_of(sibling))
    for j in range(1, mates):
        friend = far_of(mate(mates - j))
        arrived(friend)
        push(R.u.at[friend], friend, sibling)
        project(friend)
    for j in range(1, mates):
        friend = mate(mates - j, 1 - core)
        arrived(friend)
        project(friend)
        arrived(far_of(friend))
        project(far_of(friend))

    rows = R.rows
    per = seg // rows
    o_home = R.o_home
    far_out = remote(R.out.at[pl.ds(0, seg)], o_home.at[mine], R.osem.at[0], R.osem.at[1], to(partner))

    def attend(i, _):
        at = pl.ds(pl.multiple_of(i * rows, rows), rows)
        b = jnp.where(i < per, partner, me)
        uq = R.u[b, pl.ds(pl.multiple_of(lax.rem(i, per) * rows, rows), rows), :]
        qb = (jnp.dot(uq, R.w[0:C, :], preferred_element_type=F32) + vec[8:9, :]).astype(B16)
        s = lax.dot_general(qb, R.k[...], nt, preferred_element_type=F32) * scale
        s = jnp.where(R.qid[at, :][:, :1] == key_ids, s, mask_fill)
        e = jnp.exp(s - jnp.max(s, axis=1, keepdims=True))
        p = e * (1.0 / jnp.sum(e, axis=1, keepdims=True))
        pb = p.astype(B16)
        R.out[at, :] = jnp.dot(pb, R.v[...], preferred_element_type=F32).astype(B16)
        if keep:
            R.pbuf[at, :] = pb
            R.q[at, :] = qb
            dp = lax.dot_general(R.dout[at, :], R.v[...], nt, preferred_element_type=F32)
            delta = jnp.sum(p * dp, axis=1, keepdims=True)
            ds = (p * (dp - delta)).astype(B16)
            R.sbuf[at, :] = ds
            R.dq[at, :] = (jnp.dot(ds, R.k[...], preferred_element_type=F32) * scale).astype(B16)

        @pl.when(i == per - 1)
        def _():
            far_out.start()

        return 0

    lax.fori_loop(0, 2 * per, attend, 0)
    own_out = pltpu.make_async_copy(R.out.at[pl.ds(seg, seg)], o_home.at[mine], R.lsem.at[4])
    own_out.start()
    if not keep:
        own_out.wait()
        far_out.wait_recv()
        bias = vec[10:11, :]
        for v in range(2):
            at = pl.ds(v * seg, seg)
            R.final[at, :] = (
                R.hid[at, :] + jnp.dot(o_home[v], R.w[3 * C : 4 * C, :], preferred_element_type=F32) + bias)
        far_out.wait_send()
        for cp in started:
            cp.wait_send()
        return
    zero = jnp.zeros((C, C), F32)
    pairs = 2 * mates

    def share(b, carry):
        dwk, dwv, dbv = carry
        at = block(b)
        dk = (lax.dot_general(R.sbuf[:, at], R.q[...], tn, preferred_element_type=F32) * scale).astype(B16)
        dvf = lax.dot_general(R.pbuf[:, at], R.dout[...], tn, preferred_element_type=F32)
        dv = dvf.astype(B16)
        du = lax.dot_general(dk, R.w[C : 2 * C, :], nt, preferred_element_type=F32)
        du = du + lax.dot_general(dv, R.w[2 * C : 3 * C, :], nt, preferred_element_type=F32)
        piece = R.u[b]
        dwk = dwk + lax.dot_general(piece, dk, tn, preferred_element_type=F32)
        dwv = dwv + lax.dot_general(piece, dv, tn, preferred_element_type=F32)
        return du, (dwk, dwv, dbv + jnp.sum(dvf, axis=0, keepdims=True))

    def place(t):
        other = t < pairs - 2
        return jnp.where(other, t // 2 + 1, 0), 1 - lax.rem(t, 2)

    def sib_copy(t):
        return remote(R.for_sib.at[t], R.from_sib.at[t], R.ssend.at[t], R.srecv.at[t], to(sibling))

    def mate_copy(t):
        j, _ = place(t)
        return remote(R.sums.at[t], R.from_mate.at[t], R.msend.at[t], R.mrecv.at[t], to(mate(j)))

    def back(t, carry):
        j, far = place(t)
        theirs, ours = mate(j, 1 - core), mate(j)
        du, carry = share(lax.rem(theirs + far * half, n), carry)
        R.for_sib[t] = du.astype(B16)
        sib_copy(t).start()
        du, carry = share(lax.rem(ours + far * half, n), carry)
        sib_copy(t).wait_recv()
        R.sums[t] = (du + R.from_sib[t].astype(F32)).astype(B16)

        @pl.when(t < pairs - 2)
        def _():
            mate_copy(t).start()

        return carry

    dwk, dwv, dbv = lax.fori_loop(0, pairs, back, (zero, zero, jnp.zeros((1, C), F32)))

    def gathered(far):
        at = pl.ds(0, seg) if far else pl.ds(seg, seg)
        value = lax.dot_general(R.dq[at, :], R.w[0:C, :], nt, preferred_element_type=F32)
        value = value + R.sums[pairs - 1 - far].astype(F32)
        for j in range(1, mates):
            t = 2 * (j - 1) + 1 - far
            mate_copy(t).wait_recv()
            value = value + R.from_mate[t].astype(F32)
        return value

    R.for_home[...] = gathered(1).astype(B16)
    home = remote(R.for_home, R.from_partner, R.hsem.at[0], R.hsem.at[1], to(partner))
    home.start()
    R.du[mine] = gathered(0)
    R.dw[C : 2 * C, :] = dwk.astype(B16)
    R.dw[2 * C : 3 * C, :] = dwv.astype(B16)
    R.dw[3 * C : 4 * C, :] = lax.dot_general(
        R.out[...], R.dz[...], tn, preferred_element_type=F32).astype(B16)
    dwq = lax.dot_general(R.u[partner], R.dq[0:seg, :], tn, preferred_element_type=F32)
    dwq = dwq + lax.dot_general(R.u[me], R.dq[seg : 2 * seg, :], tn, preferred_element_type=F32)
    R.dw[0:C, :] = dwq.astype(B16)
    R.dvec[...] = jnp.concatenate(
        [
            jnp.sum(R.dq[...].astype(F32), axis=0, keepdims=True),
            dbv,
            jnp.sum(R.dz[...].astype(F32), axis=0, keepdims=True),
            jnp.zeros((5, C), F32),
        ],
        axis=0,
    )
    home.wait_recv()
    R.du[1 - mine] = R.from_partner[...].astype(F32)
    home.wait_send()
    own_out.wait()
    far_out.wait()
    for cp in started:
        cp.wait_send()

    def drain(t, _):
        sib_copy(t).wait_send()

        @pl.when(t < pairs - 2)
        def _():
            mate_copy(t).wait_send()

        return 0

    lax.fori_loop(0, pairs, drain, 0)


def attend_call(n, keep, cid, u, ids_all, vec, low, cot=None, far_cot=None, hid=None):
    seg = u.shape[1]
    half = n // 2
    mates = half // 2
    pairs = 2 * mates
    total = n * seg
    dma = pltpu.SemaphoreType.DMA
    inputs = dict(u_in=(u, anyw), ids_all=(ids_all, vmem), vec=(vec, vmem), low=(low, anyw))
    piece = (seg, C)
    home = (2,) + piece
    scratch = dict(
        u=pltpu.VMEM((n,) + piece, B16), w=pltpu.VMEM((4 * C, C), B16), k=pltpu.VMEM((total, C), B16),
        v=pltpu.VMEM((total, C), B16), qid=pltpu.VMEM((2 * seg, LANES), F32), out=pltpu.VMEM((2 * seg, C), B16),
        lsem=dma((5,)), gsend=dma((4 * mates,)), grecv=dma((n,)), osem=dma((2,)))
    if keep:
        inputs.update(cot=(cot, anyw), far_cot=(far_cot, anyw))
        outputs = dict(o_home=(home, B16, anyw), dw=((4 * C, C), B16, vmem), dvec=((8, C), F32, vmem),
                       du=(home, F32, vmem))
        scratch.update(
            dz=pltpu.VMEM((2 * seg, C), B16), dout=pltpu.VMEM((2 * seg, C), B16), q=pltpu.VMEM((2 * seg, C), B16),
            dq=pltpu.VMEM((2 * seg, C), B16), pbuf=pltpu.VMEM((2 * seg, total), B16),
            sbuf=pltpu.VMEM((2 * seg, total), B16), for_sib=pltpu.VMEM((pairs,) + piece, B16),
            from_sib=pltpu.VMEM((pairs,) + piece, B16), sums=pltpu.VMEM((pairs,) + piece, B16),
            from_mate=pltpu.VMEM((pairs - 2,) + piece, B16), for_home=pltpu.VMEM(piece, B16),
            from_partner=pltpu.VMEM(piece, B16), ssend=dma((pairs,)), srecv=dma((pairs,)), msend=dma((pairs,)),
            mrecv=dma((pairs,)), hsem=dma((2,)))
    else:
        inputs.update(hid=(hid, vmem))
        outputs = dict(final=((2 * seg, C), F32, vmem))
        scratch.update(o_home=pltpu.VMEM(home, B16))

    def kernel(R):
        R.rows = min(256, seg)
        attend_kernel(n, keep, R)

    return named_call(kernel, "attend" if keep else "attend_again", cid, inputs, outputs, scratch)


def rounded_vectors(vectors):
    return lax.reduce_precision(vectors, exponent_bits=8, mantissa_bits=7)


def body(columns, n, latents, crop_ids, params, vectors, first_moment, second_moment, vector_first, vector_second,
         cotangent):
    canvases, rows, width, channels = latents.shape
    dims = (canvases, rows, width)
    px = canvases * rows * width
    plane = rows * width
    half = n // 2
    me = lax.axis_index("height")
    mine = me // half
    partner = lax.rem(me + half, n)
    swap = [(i, (i + half) % n) for i in range(n)]
    count = vectors.shape[0]
    joined = columns == 4 and params.shape[0] % 32 == 0 and rows > 2

    def padded(value):
        return jnp.pad(value, ((0, 16 - count), (0, 0)))

    wide_vectors = padded(vectors)
    vec = rounded_vectors(wide_vectors)
    cell_ids = crop_ids[:, :, ::UNIT] + CROPS * jnp.arange(canvases, dtype=jnp.int32)[:, None, None]
    cell_ids = cell_ids.reshape(1, -1)
    stat = jnp.arange(canvases * CROPS, dtype=jnp.int32)[:, None]
    pick = (cell_ids == stat).astype(B16)
    spread = (cell_ids.reshape(-1, 1) == stat.reshape(1, -1)).astype(B16)
    ids = crop_ids.astype(F32)
    ids_px = jnp.broadcast_to(ids[..., None], (canvases, rows, width, LANES))
    ids_lane = jnp.pad(ids.reshape(canvases, plane), ((0, 8 - canvases), (0, 0)))
    x = latents.reshape(px, channels)
    cot = cotangent.reshape(px, channels)
    cot3 = cotangent.reshape(canvases, plane, channels)

    if joined:
        first = first_call(columns, n, dims, x, pick, spread, ids_px, ids_lane, vec, params, cot3)
        ids_all, mean1, inv1, div, cnt = (first[k] for k in ("ids_all", "mean1", "inv1", "div", "cnt"))
        masks = [first[k] for k in ("col_l", "col_r", "row_u", "row_d")]
        hid, u, y1, s1, s2 = (first[k] for k in ("hid", "u", "y1_out", "s1_out", "s2_out"))
        mean2, inv2, mean3, inv3 = (first[k] for k in ("mean2", "inv2", "mean3", "inv3"))
        top, low = first["top"], first["bottom"]
    else:
        whole = spread_call(columns, n, 8, params).reshape(-1, channels)
        top, low = whole[: 11 * C], whole[11 * C :]
        ids_all, mean1, inv1, div, cnt, *masks = layout_call(n, dims, x, pick, spread, ids_px, ids_lane)
        hid, u, y1, s1, s2, mean2, inv2, mean3, inv3 = resnet_forward_call(
            n, dims, True, x, pick, spread, cnt, mean1, inv1, masks, vec, top, low)
    small = (wide_vectors, padded(vector_first), padded(vector_second))
    u = u.reshape(canvases, plane, channels)
    if joined:
        att = attend_call(n, True, 4, u, ids_all, vec, low, cot3, first["far_cot"])
        du = att["du"].reshape(px, channels)
        back = back_call(columns, n, dims, cot, du, hid, y1, (mean2, inv2, mean3, inv3), s1, s2, pick, spread, div,
                         masks, vec, top, low, att["dw"], params.shape[0])
        new = update_call(columns, n, dims, back["grad"], back["dh"], x, mean1, inv1, pick, spread, div, masks, vec,
                          top, low, back["g_top"], back["sum_low"], back["dvec"], att["dvec"], params, first_moment,
                          second_moment, *small, hid, att["o_home"].reshape(px, channels))
        first_output = new["output"]
        input_grad, new_params, new_first, new_second = (new[k] for k in ("igrad", "new_w", "new_m", "new_s"))
        new_small = [new[k] for k in ("new_vw", "new_vm", "new_vs")]
        new_vec = rounded_vectors(new_small[0])
        hid2, u2 = resnet_forward_call(
            n, dims, False, x, pick, spread, cnt, mean1, inv1, masks, new_vec, new["new_top"], new["new_low"])
        second_output = attend_call(
            n, False, 5, u2.reshape(canvases, plane, channels), ids_all, new_vec, new["new_low"], hid=hid2)["final"]
    else:
        own_cot = lax.dynamic_index_in_dim(cot3, mine, axis=0, keepdims=False)
        far_cot = lax.ppermute(
            lax.dynamic_index_in_dim(cot3, 1 - mine, axis=0, keepdims=False), "height", swap)
        dz = jnp.concatenate([own_cot, far_cot], axis=0)
        canvas_ids = lax.dynamic_index_in_dim(ids_all, mine, axis=1, keepdims=False)
        key_ids = canvas_ids.reshape(1, n * plane)
        query_ids = jnp.stack([canvas_ids[me], canvas_ids[partner]]).reshape(2 * plane, 1)
        query_ids = jnp.broadcast_to(query_ids, (2 * plane, LANES))
        offsets = jnp.stack([me, partner]) * plane

        def attention_output(o, hid, low, bias):
            back = lax.ppermute(o[plane:], "height", swap)
            ordered = jnp.where(mine == 0, jnp.stack([o[:plane], back]), jnp.stack([back, o[:plane]]))
            product = jnp.dot(ordered.reshape(px, channels), low[10 * C :], preferred_element_type=F32)
            return hid + product + bias

        ua = gather_call(n, 4, u)
        o, dup, dw_att, dvec_att = attention_call(True, ua, key_ids, query_ids, offsets, dz, vec, low)
        first_output = attention_output(o, hid, low, vec[10])
        du = scatter_call(n, 6, dup.reshape(n, plane, channels)).reshape(px, channels)
        norms = (mean1, inv1, mean2, inv2, mean3, inv3)
        input_grad, matrix_grad, dvec = resnet_backward_call(
            n, dims, 7, cot, du, hid, y1, x, norms, s1, s2, pick, spread, div, masks, vec, top, low, dw_att)
        vector_grad = jnp.concatenate([dvec, dvec_att], axis=0)
        new_params, new_first, new_second, *new_small, new_whole = step_call(
            columns, n, 9, matrix_grad.reshape((columns, half, 2) + params.shape), params, first_moment,
            second_moment, vector_grad, *small)
        new_whole = new_whole.reshape(-1, channels)
        new_top, new_low = new_whole[: 11 * C], new_whole[11 * C :]
        new_vec = rounded_vectors(new_small[0])
        hid2, u2 = resnet_forward_call(
            n, dims, False, x, pick, spread, cnt, mean1, inv1, masks, new_vec, new_top, new_low)
        ua2 = gather_call(n, 5, u2.reshape(canvases, plane, channels))
        (o2,) = attention_call(False, ua2, key_ids, query_ids, offsets, dz, new_vec, new_low)
        second_output = attention_output(o2, hid2, new_low, new_vec[10])
    new_vectors, new_vector_first, new_vector_second = [a[:count] for a in new_small]
    shape = latents.shape
    return (
        hid.reshape(shape),
        first_output.reshape(shape),
        second_output.reshape(shape),
        input_grad.reshape(shape),
        new_params,
        new_first,
        new_second,
        new_vectors,
        new_vector_first,
        new_vector_second,
    )


def solution(mesh):
    spatial = P("canvas", "height", None, None)
    owned = P(("canvas", "height"), None)
    return jax.shard_map(
        functools.partial(body, mesh.shape["canvas"], mesh.shape["height"]),
        mesh=mesh,
        in_specs=(spatial, P("canvas", "height", None), owned, P(), owned, owned, P(), P(), spatial),
        out_specs=(spatial, spatial, spatial, spatial, owned, owned, owned, P(), P(), P()),
        check_vma=False,
    )
```

```python
import functools

import jax
import jax.numpy as jnp
from jax import lax
from jax.experimental import pallas as pl
from jax.experimental.pallas import tpu as pltpu
from jax.sharding import PartitionSpec as P

C = 512
GROUPS = 32
STEP = 5
CROPS = 16
SPAN = C // GROUPS
LANES = 128
TILES = C // LANES
UNIT = 8

norm_epsilon = 1e-06
adam_epsilon = 1e-08
matrix_rate = 0.015
vector_rate = 0.2
mask_fill = -1e30

F32 = jnp.float32
B16 = jnp.bfloat16
MESH = pl.DeviceIdType.MESH
VMEM_LIMIT = 60 * 2**20

vmem = pl.BlockSpec(memory_space=pltpu.VMEM)
smem = pl.BlockSpec(memory_space=pltpu.SMEM)
anyw = pl.BlockSpec(memory_space=pl.ANY)


def params_of(cid=None):
    if cid is None:
        return pltpu.CompilerParams(vmem_limit_bytes=VMEM_LIMIT)
    return pltpu.CompilerParams(
        vmem_limit_bytes=VMEM_LIMIT, collective_id=cid, has_side_effects=True
    )


def sds(shape, dtype):
    return jax.ShapeDtypeStruct(shape, dtype)


def split_dot(pick, value):
    total = None
    rest = value
    for _ in range(3):
        part = rest.astype(B16)
        term = jnp.dot(pick, part, preferred_element_type=F32)
        total = term if total is None else total + term
        rest = rest - part.astype(F32)
    return total


def lane_group_sum(piece):
    lane = lax.broadcasted_iota(jnp.int32, piece.shape, 1)
    step = 1
    while step < SPAN:
        ahead = pltpu.roll(piece, LANES - step, 1)
        behind = pltpu.roll(piece, step, 1)
        piece = piece + jnp.where((lane & step) == 0, ahead, behind)
        step *= 2
    return piece


def tiles_of(value):
    return [value[:, j * LANES : (j + 1) * LANES] for j in range(TILES)]


def wide(piece, times=TILES):
    return jnp.concatenate([piece] * times, axis=1)


def pack(quantities):
    shape = quantities[0][0].shape
    sub = lax.broadcasted_iota(jnp.int32, shape, 1) & (SPAN - 1)
    out = jnp.zeros(shape, F32)
    for q, pieces in enumerate(quantities):
        for j, piece in enumerate(pieces):
            out = jnp.where(sub == TILES * q + j, piece, out)
    return out


def unpack(packed):
    sub = lax.broadcasted_iota(jnp.int32, packed.shape, 1) & (SPAN - 1)
    return jnp.concatenate(
        [lane_group_sum(jnp.where(sub == j, packed, 0.0)) for j in range(TILES)], axis=1
    )


def shift_down(packed, q):
    return pltpu.roll(packed, LANES - TILES * q, packed.ndim - 1)


def no_pump():
    return None


def greet(n):
    me = lax.axis_index("height")
    barrier = pltpu.get_barrier_semaphore()
    for d in range(1, n):
        pl.semaphore_signal(
            barrier, inc=1, device_id={"height": lax.rem(me + d, n)}, device_id_type=MESH
        )
    pl.semaphore_wait(barrier, n - 1)


def spread_copies(n, buf, send, recv, rnd):
    me = lax.axis_index("height")
    return [
        pltpu.make_async_remote_copy(
            src_ref=buf.at[rnd, 0],
            dst_ref=buf.at[rnd, d],
            send_sem=send.at[rnd, d],
            recv_sem=recv.at[rnd, d],
            device_id={"height": lax.rem(me + d, n)},
            device_id_type=MESH,
        )
        for d in range(1, n)
    ]


def cell_totals(load, out_ref, cells):
    def body(i, _):
        out_ref[pl.ds(i * 16, 16), :] = jnp.sum(load(i).reshape(16, UNIT, C), axis=1)
        return 0

    lax.fori_loop(0, cells // 16, body, 0)


def over_cells(cell_ref, i):
    return jnp.broadcast_to(cell_ref[pl.ds(i * 16, 16), :][:, None, :], (16, UNIT, C)).reshape(
        16 * UNIT, C
    )


def group_totals(pick_ref, cell_value):
    return [lane_group_sum(t) for t in tiles_of(split_dot(pick_ref[...], cell_value))]


def stats_payload(load, pick_ref, spread_ref, count_ref, cells, tmp_a, tmp_b):
    cell_totals(load, tmp_a, cells)
    sums = group_totals(pick_ref, tmp_a[...])
    count = count_ref[...]
    inv_count = 1.0 / jnp.maximum(count, 1.0)
    mean = jnp.concatenate([s * inv_count for s in sums], axis=1)
    tmp_b[...] = split_dot(spread_ref[...], mean)

    def centred(i):
        delta = load(i) - over_cells(tmp_b, i)
        return delta * delta

    cell_totals(centred, tmp_a, cells)
    squares = group_totals(pick_ref, tmp_a[...])
    return pack([sums, squares, [count] * TILES])


def combine_stats(gathered):
    sums = gathered
    squares = shift_down(gathered, 1)
    counts = shift_down(gathered, 2)
    divisor = jnp.maximum(jnp.sum(counts, axis=0), 1.0)
    mean = jnp.sum(sums, axis=0) / divisor
    apart = sums / jnp.maximum(counts, 1.0) - mean[None]
    spread = jnp.sum(squares + counts * apart * apart, axis=0) / divisor
    return mean, lax.rsqrt(spread + norm_epsilon), divisor


def shift_columns(row, left_mask, right_mask):
    width = row.shape[0]
    left = pltpu.roll(row, 1, 0) * wide(left_mask)
    right = pltpu.roll(row, width - 1, 0) * wide(right_mask)
    return jnp.concatenate([left, row, right], axis=1).astype(B16)


def logistic(a):
    return 1.0 / (1.0 + jnp.exp(-a))


def silu(a):
    return a * logistic(a)


def silu_slope(a):
    s = logistic(a)
    return s * (1.0 + a * (1.0 - s))


def layout_kernel(n, dims, x, pick, spread, ids_px, ids_lane, ids_all, mean_c, inv_c, div, cnt,
                  col_l, col_r, row_u, row_d, *scratch):
    greet(n)
    layout_body(n, dims, x, pick, spread, ids_px, ids_lane, ids_all, mean_c, inv_c, div, cnt,
                col_l, col_r, row_u, row_d, *scratch)


def layout_body(n, dims, x, pick, spread, ids_px, ids_lane, ids_all, mean_c, inv_c, div, cnt,
                col_l, col_r, row_u, row_d, buf, idbuf, halo, tmp_a, tmp_b, send, recv, isend, irecv,
                hsend, hrecv, pump=no_pump):
    canvases, rows, width = dims
    cells = canvases * rows * width // UNIT
    me = lax.axis_index("height")
    id_copies = []
    idbuf[0] = ids_lane[...]
    for d in range(1, n):
        cp = pltpu.make_async_remote_copy(
            src_ref=idbuf.at[0], dst_ref=idbuf.at[d], send_sem=isend.at[d], recv_sem=irecv.at[d],
            device_id={"height": lax.rem(me + d, n)}, device_id_type=MESH)
        cp.start()
        id_copies.append(cp)
    up, down = halo_copies(n, ids_px.at[:, 0], ids_px.at[:, rows - 1], halo, hsend, hrecv)
    start_halo(n, up, down)

    def load(i):
        return x[pl.ds(i * 16 * UNIT, 16 * UNIT), :].astype(F32)

    ones = jnp.sum(pick[...].astype(F32), axis=1, keepdims=True) * float(UNIT * SPAN)
    cnt[...] = jnp.broadcast_to(ones, cnt.shape)
    buf[0, 0] = stats_payload(load, pick, spread, cnt, cells, tmp_a, tmp_b)
    copies = spread_copies(n, buf, send, recv, 0)
    for cp in copies:
        cp.start()
    pump()
    wait_halo(n, up, down, halo, -1.0)
    column = lax.broadcasted_iota(jnp.int32, (width, LANES), 0)
    first, last = column == 0, column == width - 1
    for v in range(canvases):
        for r in range(rows + 2):
            here = halo[0, v] if r == 0 else halo[1, v] if r == rows + 1 else ids_px[v, r - 1]
            same_l = (pltpu.roll(here, 1, 0) == here) & jnp.logical_not(first)
            same_r = (pltpu.roll(here, width - 1, 0) == here) & jnp.logical_not(last)
            col_l[v, r] = same_l.astype(F32)
            col_r[v, r] = same_r.astype(F32)
            if 1 <= r <= rows:
                above = halo[0, v] if r == 1 else ids_px[v, r - 2]
                below = halo[1, v] if r == rows else ids_px[v, r]
                at = pl.ds((v * rows + r - 1) * width, width)
                row_u[at, :] = (above == here).astype(F32)
                row_d[at, :] = (below == here).astype(F32)
    pump()
    for cp in copies:
        cp.wait_recv()
    mean, inv, divisor = combine_stats(buf[0])
    mean_c[...] = split_dot(spread[...], unpack(mean))
    inv_c[...] = split_dot(spread[...], unpack(inv))
    div[...] = unpack(divisor)[:, :LANES]
    for cp in id_copies:
        cp.wait_recv()
    ids_all[me] = idbuf[0]
    for d in range(1, n):
        ids_all[lax.rem(me - d + n, n)] = idbuf[d]
    for cp in copies + id_copies:
        cp.wait_send()


def halo_copies(n, first_row, last_row, halo, hsend, hrecv):
    me = lax.axis_index("height")
    up = pltpu.make_async_remote_copy(
        src_ref=first_row, dst_ref=halo.at[1], send_sem=hsend.at[0], recv_sem=hrecv.at[1],
        device_id={"height": lax.rem(me + n - 1, n)}, device_id_type=MESH)
    down = pltpu.make_async_remote_copy(
        src_ref=last_row, dst_ref=halo.at[0], send_sem=hsend.at[1], recv_sem=hrecv.at[0],
        device_id={"height": lax.rem(me + 1, n)}, device_id_type=MESH)
    return up, down


def start_halo(n, up, down):
    me = lax.axis_index("height")

    @pl.when(me > 0)
    def _():
        up.start()

    @pl.when(me < n - 1)
    def _():
        down.start()


def wait_halo(n, up, down, halo, edge):
    me = lax.axis_index("height")

    @pl.when(me > 0)
    def _():
        up.wait_send()
        down.wait_recv()

    @pl.when(me < n - 1)
    def _():
        down.wait_send()
        up.wait_recv()

    @pl.when(me == 0)
    def _():
        halo[0] = jnp.full(halo.shape[1:], edge, halo.dtype)

    @pl.when(me == n - 1)
    def _():
        halo[1] = jnp.full(halo.shape[1:], edge, halo.dtype)


def layout_scratch(n, dims, ids_lane):
    canvases, rows, width = dims
    cells = canvases * rows * width // UNIT
    return [
        pltpu.VMEM((1, n, canvases * CROPS, LANES), F32),
        pltpu.VMEM((n,) + ids_lane.shape, F32),
        pltpu.VMEM((2, canvases, width, LANES), F32),
        pltpu.VMEM((cells, C), F32),
        pltpu.VMEM((cells, C), F32),
        pltpu.SemaphoreType.DMA((1, n)),
        pltpu.SemaphoreType.DMA((1, n)),
        pltpu.SemaphoreType.DMA((n,)),
        pltpu.SemaphoreType.DMA((n,)),
        pltpu.SemaphoreType.DMA((2,)),
        pltpu.SemaphoreType.DMA((2,)),
    ]


def layout_call(n, dims, x, pick, spread, ids_px, ids_lane):
    canvases, rows, width = dims
    px = canvases * rows * width
    cells = px // UNIT
    stats = canvases * CROPS
    return pl.pallas_call(
        functools.partial(layout_kernel, n, dims),
        out_shape=[
            sds((n,) + ids_lane.shape, F32),
            sds((cells, C), F32),
            sds((cells, C), F32),
            sds((stats, LANES), F32),
            sds((stats, LANES), F32),
            sds((canvases, rows + 2, width, LANES), F32),
            sds((canvases, rows + 2, width, LANES), F32),
            sds((px, LANES), F32),
            sds((px, LANES), F32),
        ],
        in_specs=[vmem] * 5,
        out_specs=[vmem] * 9,
        scratch_shapes=layout_scratch(n, dims, ids_lane),
        compiler_params=params_of(1),
        name="layout",
    )(x, pick, spread, ids_px, ids_lane)


def second_matrix(top, low, dest, sem):
    return [
        pltpu.make_async_copy(top.at[pl.ds(9 * C, 2 * C)], dest.at[pl.ds(0, 2 * C)], sem.at[1]),
        pltpu.make_async_copy(low.at[pl.ds(0, 7 * C)], dest.at[pl.ds(2 * C, 7 * C)], sem.at[2]),
    ]


class Convolver:
    def __init__(self, n, dims, x, pick, spread, cnt, col_l, col_r, row_u, row_d, halo, buf, tmp_a, tmp_b, send,
                 recv, hsend, hrecv):
        self.n, self.dims = n, dims
        self.x, self.pick, self.spread, self.cnt = x, pick, spread, cnt
        self.col_l, self.col_r, self.row_u, self.row_d = col_l, col_r, row_u, row_d
        self.halo, self.buf, self.tmp_a, self.tmp_b = halo, buf, tmp_a, tmp_b
        self.send, self.recv, self.hsend, self.hrecv = send, recv, hsend, hrecv
        self.px = dims[0] * dims[1] * dims[2]
        self.cells = self.px // UNIT
        self.sent = []

    def activate(self, source, mean, inv, gain, bias, dest, rnd, pump=no_pump):
        canvases, rows, width = self.dims
        row_cells = width // UNIT
        col_l, col_r, halo = self.col_l, self.col_r, self.halo

        def one(v, r):
            at = pl.ds(pl.multiple_of((v * rows + r) * width, width), width)
            cell = pl.ds(pl.multiple_of((v * rows + r) * row_cells, row_cells), row_cells)
            value = source[at, :].astype(F32)
            m = jnp.broadcast_to(mean[cell, :][:, None, :], (row_cells, UNIT, C)).reshape(width, C)
            s = jnp.broadcast_to(inv[cell, :][:, None, :], (row_cells, UNIT, C)).reshape(width, C)
            a = (value - m) * s * gain + bias
            dest[v, r + 1] = shift_columns(silu(a), col_l[v, r + 1], col_r[v, r + 1])

        def edges(v, _):
            one(v, 0)
            if rows > 1:
                one(v, rows - 1)
            return 0

        lax.fori_loop(0, canvases, edges, 0)
        mid = pl.ds(C, C)
        up, down = halo_copies(self.n, dest.at[:, 1, :, mid], dest.at[:, rows, :, mid], halo.at[rnd],
                               self.hsend.at[rnd], self.hrecv.at[rnd])
        start_halo(self.n, up, down)
        pump()

        def inner(i, _):
            one(i // (rows - 2), 1 + lax.rem(i, rows - 2))
            return 0

        if rows > 2:
            lax.fori_loop(0, canvases * (rows - 2), inner, 0)
        pump()
        wait_halo(self.n, up, down, halo.at[rnd], 0.0)
        for v in range(canvases):
            for side, r in ((0, 0), (1, rows + 1)):
                dest[v, r] = shift_columns(halo[rnd, side, v].astype(F32), col_l[v, r], col_r[v, r])

    def convolve(self, source, weights, emit, pump=no_pump):
        canvases, rows, width = self.dims
        plane = rows * width
        for v in range(canvases):
            at = pl.ds(v * plane, plane)
            total = None
            for dr in (1, 0, 2):
                part = None
                for lo, hi, ref, row in weights(dr):
                    lhs = source[v, dr : dr + rows, :, lo:hi].reshape(plane, hi - lo)
                    term = jnp.dot(lhs, ref[row : row + hi - lo, :], preferred_element_type=F32)
                    part = term if part is None else part + term
                if dr == 0:
                    part = part * wide(self.row_u[at, :])
                if dr == 2:
                    part = part * wide(self.row_d[at, :])
                total = part if total is None else total + part
            emit(at, total)
            pump()

    def statistics(self, source, mean, inv, rnd, pump=no_pump):
        def load(i):
            return source[pl.ds(i * 16 * UNIT, 16 * UNIT), :]

        self.buf[rnd, 0] = stats_payload(load, self.pick, self.spread, self.cnt, self.cells, self.tmp_a, self.tmp_b)
        copies = spread_copies(self.n, self.buf, self.send, self.recv, rnd)
        for cp in copies:
            cp.start()
        pump()
        for cp in copies:
            cp.wait_recv()
        m, s, _ = combine_stats(self.buf[rnd])
        mean[...] = split_dot(self.spread[...], unpack(m))
        inv[...] = split_dot(self.spread[...], unpack(s))
        self.sent = self.sent + copies

    def normalise(self, source, mean, inv, gain, bias, dest):
        def last(i, _):
            at = pl.ds(i * 16 * UNIT, 16 * UNIT)
            value = (source[at, :] - over_cells(mean, i)) * over_cells(inv, i)
            dest[at, :] = (value * gain + bias).astype(B16)
            return 0

        lax.fori_loop(0, self.cells // 16, last, 0)


def resnet_forward_kernel(n, dims, keep, x, pick, spread, cnt, mean1, inv1, col_l, col_r, row_u, row_d,
                          vec, top, low, *refs):
    canvases, rows, width = dims
    px = canvases * rows * width
    cells = px // UNIT
    plane = rows * width
    if keep:
        hid, u, y1, s1, s2, mean2, inv2, mean3, inv3 = refs[:9]
        refs = refs[9:]
    else:
        hid, u = refs[:2]
        y1, s1, s2, mean2, inv2, mean3, inv3 = refs[2:9]
        refs = refs[9:]
    k1, k2, halo, buf, tmp_a, tmp_b, ksem, send, recv, hsend, hrecv = refs
    load1 = [pltpu.make_async_copy(top.at[pl.ds(0, 9 * C)], k1, ksem.at[0])]
    load2 = second_matrix(top, low, k2, ksem)
    for cp in load1 + load2:
        cp.start()
    greet(n)
    for_conv = Convolver(n, dims, x, pick, spread, cnt, col_l, col_r, row_u, row_d, halo, buf, tmp_a, tmp_b,
                         send, recv, hsend, hrecv)

    def wait_all(copies):
        for cp in copies:
            cp.wait()

    for_conv.activate(x, mean1, inv1, vec[0:1, :], vec[1:2, :], s1, 0)
    wait_all(load1)

    def emit_first(at, total):
        y1[at, :] = total + vec[2:3, :]

    for_conv.convolve(s1, lambda dr: [(0, 3 * C, k1, 3 * C * dr)], emit_first)
    for_conv.statistics(y1, mean2, inv2, 0)
    for_conv.activate(y1, mean2, inv2, vec[3:4, :], vec[4:5, :], s2, 1)
    wait_all(load2)

    def emit_second(at, total):
        hid[at, :] = total + vec[5:6, :] + x[at, :].astype(F32)

    for_conv.convolve(s2, lambda dr: [(0, 3 * C, k2, 3 * C * dr)], emit_second)
    for_conv.statistics(hid, mean3, inv3, 1)
    for_conv.normalise(hid, mean3, inv3, vec[6:7, :], vec[7:8, :], u)
    for cp in for_conv.sent:
        cp.wait_send()


def resnet_forward_call(n, dims, keep, x, pick, spread, cnt, mean1, inv1, masks, vec, top, low):
    canvases, rows, width = dims
    px = canvases * rows * width
    cells = px // UNIT
    stats = canvases * CROPS
    saved = [
        ((px, C), F32),
        ((canvases, rows + 2, width, 3 * C), B16),
        ((canvases, rows + 2, width, 3 * C), B16),
        ((cells, C), F32),
        ((cells, C), F32),
        ((cells, C), F32),
        ((cells, C), F32),
    ]
    main = [((px, C), F32), ((px, C), B16)]
    outs = main + (saved if keep else [])
    scratch = [] if keep else [pltpu.VMEM(*s) for s in saved]
    return pl.pallas_call(
        functools.partial(resnet_forward_kernel, n, dims, keep),
        out_shape=[sds(*s) for s in outs],
        in_specs=[vmem] * 11 + [anyw] * 2,
        out_specs=[vmem] * len(outs),
        scratch_shapes=scratch
        + [
            pltpu.VMEM((9 * C, C), B16),
            pltpu.VMEM((9 * C, C), B16),
            pltpu.VMEM((2, 2, canvases, width, C), B16),
            pltpu.VMEM((2, n, stats, LANES), F32),
            pltpu.VMEM((cells, C), F32),
            pltpu.VMEM((cells, C), F32),
            pltpu.SemaphoreType.DMA((3,)),
            pltpu.SemaphoreType.DMA((2, n)),
            pltpu.SemaphoreType.DMA((2, n)),
            pltpu.SemaphoreType.DMA((2, 2)),
            pltpu.SemaphoreType.DMA((2, 2)),
        ],
        compiler_params=params_of(2 if keep else 3),
        name="resnet_forward" if keep else "resnet_again",
    )(x, pick, spread, cnt, mean1, inv1, *masks, vec, top, low)


def attention_kernel(keep, chunk, block, ua, key_ids, query_ids, offsets, dz, vec, low, *refs):
    total = ua.shape[0] * ua.shape[1]
    queries = query_ids.shape[0]
    segment = ua.shape[1]
    scale = C ** (-0.5)
    if keep:
        out, dup, dw, dvec = refs[:4]
        u, w, k, v, pbuf, sbuf, q, dout, dq, usem, wsem = refs[4:]
    else:
        out = refs[0]
        u, w, k, v, usem, wsem = refs[1:]
    load_w = pltpu.make_async_copy(low.at[pl.ds(7 * C, 4 * C)], w, wsem.at[0])
    load_w.start()
    blocks = ua.shape[0]
    loads = [
        pltpu.make_async_copy(ua.at[i], u.at[pl.ds(i * segment, segment)], usem.at[i])
        for i in range(blocks)
    ]
    for cp in loads:
        cp.start()
    load_w.wait()
    for cp in loads:
        cp.wait()
    nt = (((1,), (1,)), ((), ()))
    tn = (((0,), (0,)), ((), ()))

    def project(i, _):
        at = pl.ds(pl.multiple_of(i * chunk, chunk), chunk)
        piece = u[at, :]
        k[at, :] = jnp.dot(piece, w[C : 2 * C, :], preferred_element_type=F32).astype(B16)
        v[at, :] = (
            jnp.dot(piece, w[2 * C : 3 * C, :], preferred_element_type=F32) + vec[9:10, :]
        ).astype(B16)
        return 0

    lax.fori_loop(0, total // chunk, project, 0)
    per = segment // block

    def place(i):
        return pl.multiple_of(offsets[i // per] + lax.rem(i, per) * block, block)

    def attend(i, _):
        at = pl.ds(pl.multiple_of(i * block, block), block)
        uq = u[pl.ds(place(i), block), :]
        qb = (
            jnp.dot(uq, w[0:C, :], preferred_element_type=F32) + vec[8:9, :]
        ).astype(B16)
        s = lax.dot_general(qb, k[...], nt, preferred_element_type=F32) * scale
        s = jnp.where(query_ids[at, :][:, :1] == key_ids[...], s, mask_fill)
        e = jnp.exp(s - jnp.max(s, axis=1, keepdims=True))
        p = e * (1.0 / jnp.sum(e, axis=1, keepdims=True))
        pb = p.astype(B16)
        ob = jnp.dot(pb, v[...], preferred_element_type=F32).astype(B16)
        out[at, :] = ob
        if keep:
            pbuf[at, :] = pb
            q[at, :] = qb
            do = lax.dot_general(
                dz[at, :], w[3 * C : 4 * C, :], nt, preferred_element_type=F32
            ).astype(B16)
            dout[at, :] = do
            dp = lax.dot_general(do, v[...], nt, preferred_element_type=F32)
            delta = jnp.sum(p * dp, axis=1, keepdims=True)
            ds = (p * (dp - delta)).astype(B16)
            sbuf[at, :] = ds
            dq[at, :] = (jnp.dot(ds, k[...], preferred_element_type=F32) * scale).astype(B16)
        return 0

    lax.fori_loop(0, queries // block, attend, 0)
    if not keep:
        return
    zero = jnp.zeros((C, C), F32)

    def back(i, carry):
        dwk, dwv, dbv = carry
        at = pl.ds(pl.multiple_of(i * chunk, chunk), chunk)
        dk = (
            lax.dot_general(sbuf[:, at], q[...], tn, preferred_element_type=F32) * scale
        ).astype(B16)
        dvf = lax.dot_general(pbuf[:, at], dout[...], tn, preferred_element_type=F32)
        dv = dvf.astype(B16)
        du = lax.dot_general(dk, w[C : 2 * C, :], nt, preferred_element_type=F32)
        du = du + lax.dot_general(dv, w[2 * C : 3 * C, :], nt, preferred_element_type=F32)
        dup[at, :] = du.astype(B16)
        piece = u[at, :]
        dwk = dwk + lax.dot_general(piece, dk, tn, preferred_element_type=F32)
        dwv = dwv + lax.dot_general(piece, dv, tn, preferred_element_type=F32)
        return dwk, dwv, dbv + jnp.sum(dvf, axis=0, keepdims=True)

    dwk, dwv, dbv = lax.fori_loop(0, total // chunk, back, (zero, zero, jnp.zeros((1, C), F32)))
    dw[C : 2 * C, :] = dwk.astype(B16)
    dw[2 * C : 3 * C, :] = dwv.astype(B16)
    dw[3 * C : 4 * C, :] = lax.dot_general(
        out[...], dz[...], tn, preferred_element_type=F32
    ).astype(B16)
    dwq = zero
    for s in range(2):
        where = pl.ds(pl.multiple_of(offsets[s], segment), segment)
        at = pl.ds(s * segment, segment)
        dwq = dwq + lax.dot_general(u[where, :], dq[at, :], tn, preferred_element_type=F32)
        du = lax.dot_general(dq[at, :], w[0:C, :], nt, preferred_element_type=F32)
        dup[where, :] = (dup[where, :].astype(F32) + du).astype(B16)
    dw[0:C, :] = dwq.astype(B16)
    dvec[...] = jnp.concatenate(
        [
            jnp.sum(dq[...].astype(F32), axis=0, keepdims=True),
            dbv,
            jnp.sum(dz[...].astype(F32), axis=0, keepdims=True),
            jnp.zeros((5, C), F32),
        ],
        axis=0,
    )


def attention_call(keep, ua, key_ids, query_ids, offsets, dz, vec, low):
    blocks, segment, _ = ua.shape
    total = blocks * segment
    queries = query_ids.shape[0]
    block = min(256, segment)
    chunk = 512
    outs = [sds((queries, C), B16)]
    scratch = [
        pltpu.VMEM((total, C), B16),
        pltpu.VMEM((4 * C, C), B16),
        pltpu.VMEM((total, C), B16),
        pltpu.VMEM((total, C), B16),
    ]
    if keep:
        outs += [sds((total, C), B16), sds((4 * C, C), B16), sds((8, C), F32)]
        scratch += [
            pltpu.VMEM((queries, total), B16),
            pltpu.VMEM((queries, total), B16),
            pltpu.VMEM((queries, C), B16),
            pltpu.VMEM((queries, C), B16),
            pltpu.VMEM((queries, C), B16),
        ]
    return pl.pallas_call(
        functools.partial(attention_kernel, keep, chunk, block),
        out_shape=outs,
        in_specs=[anyw, vmem, vmem, smem, vmem, vmem, anyw],
        out_specs=[vmem] * len(outs),
        scratch_shapes=scratch
        + [pltpu.SemaphoreType.DMA((blocks,)), pltpu.SemaphoreType.DMA((1,))],
        compiler_params=params_of(),
        name="attention" if keep else "attention_again",
    )(ua, key_ids, query_ids, offsets, dz, vec, low)


def other_core(h):
    return h + 1 - 2 * lax.rem(h, 2)


def gather_kernel(n, u, ua, lsem, send, recv):
    me = lax.axis_index("height")
    half = n // 2
    mine = me // half
    base = mine * half
    core = lax.rem(me, 2)
    partner = lax.rem(me + half, n)
    sibling = other_core(me)
    mates = half // 2
    seat = (me - base) // 2

    def mate(j):
        return base + core + 2 * lax.rem(seat + j, mates)

    barrier = pltpu.get_barrier_semaphore()
    peers = [partner, sibling] + [mate(j) for j in range(1, mates)]
    for p in peers:
        pl.semaphore_signal(barrier, inc=1, device_id={"height": p}, device_id_type=MESH)
    pl.semaphore_wait(barrier, len(peers))
    count = [0]
    started = []

    def push(src, slot, to):
        cp = pltpu.make_async_remote_copy(
            src_ref=src, dst_ref=ua.at[slot], send_sem=send.at[count[0]], recv_sem=recv.at[slot],
            device_id={"height": to}, device_id_type=MESH)
        count[0] += 1
        cp.start()
        started.append(cp)

    def arrived(slot):
        pltpu.make_async_remote_copy(
            src_ref=u.at[0], dst_ref=ua.at[slot], send_sem=send.at[0], recv_sem=recv.at[slot],
            device_id={"height": partner}, device_id_type=MESH).wait_recv()

    own = pltpu.make_async_copy(u.at[mine], ua.at[me], lsem.at[0])
    own.start()
    push(u.at[1 - mine], me, partner)
    for j in range(1, mates):
        push(u.at[mine], me, mate(j))
    push(u.at[mine], me, sibling)
    arrived(partner)
    for j in range(1, mates):
        push(ua.at[partner], partner, mate(j))
    push(ua.at[partner], partner, sibling)
    for j in range(1, mates):
        friend = base + core + 2 * lax.rem(seat + mates - j, mates)
        far = lax.rem(friend + half, n)
        arrived(friend)
        push(ua.at[friend], friend, sibling)
        arrived(far)
        push(ua.at[far], far, sibling)
    arrived(sibling)
    arrived(lax.rem(sibling + half, n))
    for j in range(1, mates):
        friend = base + (1 - core) + 2 * lax.rem(seat + mates - j, mates)
        arrived(friend)
        arrived(lax.rem(friend + half, n))
    own.wait()
    for cp in started:
        cp.wait_send()


def gather_call(n, cid, u):
    half = n // 2
    sends = 2 * (half // 2) + 1 + 2 * (half // 2 - 1) + 1
    return pl.pallas_call(
        functools.partial(gather_kernel, n),
        out_shape=sds((n,) + u.shape[1:], B16),
        in_specs=[anyw],
        out_specs=anyw,
        scratch_shapes=[
            pltpu.SemaphoreType.DMA((1,)),
            pltpu.SemaphoreType.DMA((sends,)),
            pltpu.SemaphoreType.DMA((n,)),
        ],
        compiler_params=params_of(cid),
        name="gather_u",
    )(u)


def scatter_kernel(n, dup, out, from_sib, from_mate, mine_sum, from_partner, lsem, send, recv):
    me = lax.axis_index("height")
    half = n // 2
    mine = me // half
    base = mine * half
    core = lax.rem(me, 2)
    partner = lax.rem(me + half, n)
    sibling = other_core(me)
    mates = half // 2
    seat = (me - base) // 2
    barrier = pltpu.get_barrier_semaphore()

    def mate(j, c=core):
        return base + c + 2 * lax.rem(seat + j, mates)

    peers = [partner, sibling] + [mate(j) for j in range(1, mates)]
    for p in peers:
        pl.semaphore_signal(barrier, inc=1, device_id={"height": p}, device_id_type=MESH)
    pl.semaphore_wait(barrier, len(peers))
    order = [(j, far) for j in range(1, mates) for far in (1, 0)] + [(0, 1), (0, 0)]

    def rows_of(j, far, c):
        owner = mate(j, c)
        return lax.rem(owner + half, n) if far else owner

    sib = []
    for t, (j, far) in enumerate(order):
        cp = pltpu.make_async_remote_copy(
            src_ref=dup.at[rows_of(j, far, 1 - core)], dst_ref=from_sib.at[t],
            send_sem=send.at[t], recv_sem=recv.at[t],
            device_id={"height": sibling}, device_id_type=MESH)
        cp.start()
        sib.append(cp)
    base_sem = len(order)
    out_copies = []
    for t, (j, far) in enumerate(order):
        sib[t].wait_recv()
        block = rows_of(j, far, core)
        if j > 0:
            mine_sum[t] = (dup[block].astype(F32) + from_sib[t].astype(F32)).astype(B16)
            at = (j - 1) * 2 + far
            cp = pltpu.make_async_remote_copy(
                src_ref=mine_sum.at[t], dst_ref=from_mate.at[at],
                send_sem=send.at[base_sem + at], recv_sem=recv.at[base_sem + at],
                device_id={"height": mate(j)}, device_id_type=MESH)
            cp.start()
            out_copies.append(cp)
    t_far, t_own = len(order) - 2, len(order) - 1
    total = dup[partner].astype(F32) + from_sib[t_far].astype(F32)
    for j in range(1, mates):
        at = (j - 1) * 2 + 1
        pltpu.make_async_remote_copy(
            src_ref=mine_sum.at[0], dst_ref=from_mate.at[at], send_sem=send.at[0],
            recv_sem=recv.at[base_sem + at], device_id={"height": sibling},
            device_id_type=MESH).wait_recv()
        total = total + from_mate[at].astype(F32)
    mine_sum[t_far] = total.astype(B16)
    last = base_sem + 2 * (mates - 1)
    home = pltpu.make_async_remote_copy(
        src_ref=mine_sum.at[t_far], dst_ref=from_partner, send_sem=send.at[last],
        recv_sem=recv.at[last], device_id={"height": partner}, device_id_type=MESH)
    home.start()
    total = dup[me].astype(F32) + from_sib[t_own].astype(F32)
    for j in range(1, mates):
        at = (j - 1) * 2
        pltpu.make_async_remote_copy(
            src_ref=mine_sum.at[0], dst_ref=from_mate.at[at], send_sem=send.at[0],
            recv_sem=recv.at[base_sem + at], device_id={"height": sibling},
            device_id_type=MESH).wait_recv()
        total = total + from_mate[at].astype(F32)
    out[mine] = total
    home.wait_recv()
    out[1 - mine] = from_partner[...].astype(F32)
    for cp in sib + out_copies + [home]:
        cp.wait_send()


def scatter_call(n, cid, dup):
    half = n // 2
    mates = half // 2
    copies = 2 * mates + 2 * (mates - 1) + 1
    seg = dup.shape[1:]
    return pl.pallas_call(
        functools.partial(scatter_kernel, n),
        out_shape=sds((2,) + seg, F32),
        in_specs=[vmem],
        out_specs=vmem,
        scratch_shapes=[
            pltpu.VMEM((2 * mates,) + seg, B16),
            pltpu.VMEM((max(2 * (mates - 1), 1),) + seg, B16),
            pltpu.VMEM((2 * mates,) + seg, B16),
            pltpu.VMEM(seg, B16),
            pltpu.SemaphoreType.DMA((1,)),
            pltpu.SemaphoreType.DMA((copies,)),
            pltpu.SemaphoreType.DMA((copies,)),
        ],
        compiler_params=params_of(cid),
        name="scatter_du",
    )(dup)


def resnet_backward_kernel(n, dims, cot, du, hid, y1, x, mean1, inv1, mean2, inv2, mean3, inv3, s1, s2, pick,
                           spread, div, col_l, col_r, row_u, row_d, vec, top, bottom, datt, igrad, grads, dvec,
                           dw1, dw2, k, dh, d3, low, low_u, low_d, part, norm, halo, buf, tmp_a, tmp_b, ksem, wsem, send,
                           recv, hsend, hrecv):
    canvases, rows, width = dims
    px = canvases * rows * width
    cells = px // UNIT
    plane = rows * width
    nt = (((1,), (1,)), ((), ()))
    tn = (((0,), (0,)), ((), ()))
    load2 = second_matrix(top, bottom, k, wsem)
    load1 = pltpu.make_async_copy(top.at[pl.ds(0, 9 * C)], k, wsem.at[0])
    for cp in load2:
        cp.start()
    out_att = pltpu.make_async_copy(datt, grads.at[pl.ds(18 * C, 4 * C)], ksem.at[2])
    out_two = pltpu.make_async_copy(dw2, grads.at[pl.ds(9 * C, 9 * C)], ksem.at[3])
    out_one = pltpu.make_async_copy(dw1, grads.at[pl.ds(0, 9 * C)], ksem.at[4])
    out_att.start()
    greet(n)
    zero_row = jnp.zeros((1, C), F32)

    def pixels(i):
        return pl.ds(i * 16 * UNIT, 16 * UNIT)

    def norm_sums(grad_of, source, mean, inv, gain):
        def body(i, carry):
            dg, db = carry
            at = pixels(i)
            unit = (source[at, :].astype(F32) - over_cells(mean, i)) * over_cells(inv, i)
            d = grad_of(i, unit)
            norm[at, :] = unit
            e = d * gain
            part[at, :] = e
            cross = d * unit
            here = pl.ds(i * 16, 16)
            tmp_a[here, :] = jnp.sum(e.reshape(16, UNIT, C), axis=1)
            tmp_b[here, :] = jnp.sum((cross * gain).reshape(16, UNIT, C), axis=1)
            return (dg + jnp.sum(cross, axis=0, keepdims=True), db + jnp.sum(d, axis=0, keepdims=True))

        dg, db = lax.fori_loop(0, cells // 16, body, (zero_row, zero_row))
        packed = pack([group_totals(pick, tmp_a[...]), group_totals(pick, tmp_b[...])])
        return packed, dg, db

    def send_sums(packed, rnd):
        buf[rnd, 0] = packed
        copies = spread_copies(n, buf, send, recv, rnd)
        for cp in copies:
            cp.start()
        return copies

    def norm_finish(copies, rnd, inv, emit):
        for cp in copies:
            cp.wait_recv()
        gathered = jnp.sum(buf[rnd], axis=0) / div[...]
        tmp_a[...] = split_dot(spread[...], unpack(gathered))
        tmp_b[...] = split_dot(spread[...], unpack(shift_down(gathered, 1)))

        def body(i, _):
            at = pixels(i)
            emit(i, over_cells(inv, i) * (part[at, :] - over_cells(tmp_a, i) - norm[at, :] * over_cells(tmp_b, i)))
            return 0

        lax.fori_loop(0, cells // 16, body, 0)

    def spread_rows(rnd):
        def row_at(v, r):
            return pl.ds(pl.multiple_of((v * rows + r) * width, width), width)

        def one(i, _):
            v, r = i // rows, lax.rem(i, rows)
            d3[v, r + 1] = shift_columns(low[row_at(v, r), :].astype(F32), col_l[v, r + 1], col_r[v, r + 1])
            return 0

        lax.fori_loop(0, canvases * rows, one, 0)
        mid = pl.ds(C, C)
        up, down = halo_copies(n, d3.at[:, 1, :, mid], d3.at[:, rows, :, mid], halo.at[rnd],
                               hsend.at[rnd], hrecv.at[rnd])
        start_halo(n, up, down)
        return up, down

    def finish_rows(up, down, rnd):
        wait_halo(n, up, down, halo.at[rnd], 0.0)
        for v in range(canvases):
            for side, r in ((0, 0), (1, rows + 1)):
                d3[v, r] = shift_columns(halo[rnd, side, v].astype(F32), col_l[v, r], col_r[v, r])

    def convolve_back(emit):
        def body(v, _):
            at = pl.ds(pl.multiple_of(v * plane, plane), plane)
            total = None
            for dr in (1, 0, 2):
                acc = None
                for dc in range(3):
                    tap = 3 * (2 - dr) + (2 - dc)
                    lhs = d3[v, dr : dr + rows, :, dc * C : (dc + 1) * C].reshape(plane, C)
                    term = lax.dot_general(lhs, k[tap * C : (tap + 1) * C, :], nt, preferred_element_type=F32)
                    acc = term if acc is None else acc + term
                if dr == 0:
                    acc = acc * wide(row_u[at, :])
                if dr == 2:
                    acc = acc * wide(row_d[at, :])
                total = acc if total is None else total + acc
            emit(at, total)
            return 0

        lax.fori_loop(0, canvases, body, 0)

    def mask_rows():
        def body(i, _):
            at = pixels(i)
            value = low[at, :].astype(F32)
            low_u[at, :] = (value * wide(row_u[at, :])).astype(B16)
            low_d[at, :] = (value * wide(row_d[at, :])).astype(B16)
            return 0

        lax.fori_loop(0, cells // 16, body, 0)

    def weight_grad(source, dest):
        for dr, grad in ((0, low_u), (1, low), (2, low_d)):
            def body(dc, _):
                acc = None
                for v in range(canvases):
                    lhs = source[v, dr : dr + rows, :, pl.ds(pl.multiple_of(dc * C, C), C)].reshape(plane, C)
                    term = lax.dot_general(
                        lhs, grad[v * plane : (v + 1) * plane, :], tn, preferred_element_type=F32)
                    acc = term if acc is None else acc + term
                dest[pl.ds(pl.multiple_of((3 * dr + dc) * C, C), C), :] = acc.astype(B16)
                return 0

            lax.fori_loop(0, 3, body, 0)

    packed, dg3, db3 = norm_sums(lambda i, unit: du[pixels(i), :], hid, mean3, inv3, vec[6:7, :])
    sent = send_sums(packed, 0)

    def emit_hidden(i, value):
        at = pixels(i)
        total = cot[at, :].astype(F32) + value
        dh[at, :] = total
        low[at, :] = total.astype(B16)

    norm_finish(sent, 0, inv3, emit_hidden)
    up, down = spread_rows(0)
    mask_rows()
    dc2 = jnp.sum(low[...].astype(F32), axis=0, keepdims=True)
    finish_rows(up, down, 0)
    for cp in load2:
        cp.wait()

    def emit_part(at, total):
        part[at, :] = total

    convolve_back(emit_part)
    load1.start()
    gain2, bias2 = vec[3:4, :], vec[4:5, :]

    def grad_two(i, unit):
        return part[pixels(i), :] * silu_slope(unit * gain2 + bias2)

    packed, dg2, db2 = norm_sums(grad_two, y1, mean2, inv2, gain2)
    more = send_sums(packed, 1)
    weight_grad(s2, dw2)
    out_two.start()

    def emit_low(i, value):
        low[pixels(i), :] = value.astype(B16)

    norm_finish(more, 1, inv2, emit_low)
    sent = sent + more
    up, down = spread_rows(1)
    mask_rows()
    dc1 = jnp.sum(low[...].astype(F32), axis=0, keepdims=True)
    weight_grad(s1, dw1)
    out_one.start()
    finish_rows(up, down, 1)
    load1.wait()
    convolve_back(emit_part)
    gain1, bias1 = vec[0:1, :], vec[1:2, :]

    def grad_one(i, unit):
        return part[pixels(i), :] * silu_slope(unit * gain1 + bias1)

    packed, dg1, db1 = norm_sums(grad_one, x, mean1, inv1, gain1)
    more = send_sums(packed, 2)
    dvec[...] = jnp.concatenate([dg1, db1, dc1, dg2, db2, dc2, dg3, db3], axis=0)

    def emit_input(i, value):
        igrad[pixels(i), :] = dh[pixels(i), :] + value

    norm_finish(more, 2, inv1, emit_input)
    sent = sent + more
    out_att.wait()
    out_two.wait()
    out_one.wait()
    for cp in sent:
        cp.wait_send()


def resnet_backward_call(n, dims, cid, cot, du, hid, y1, x, norms, s1, s2, pick, spread, div, masks, vec, top,
                         bottom, datt):
    canvases, rows, width = dims
    px = canvases * rows * width
    cells = px // UNIT
    stats = canvases * CROPS
    return pl.pallas_call(
        functools.partial(resnet_backward_kernel, n, dims),
        out_shape=[sds((px, C), F32), sds((22 * C, C), B16), sds((8, C), F32)],
        in_specs=[vmem] * 21 + [anyw] * 3,
        out_specs=[vmem, anyw, vmem],
        scratch_shapes=[
            pltpu.VMEM((9 * C, C), B16),
            pltpu.VMEM((9 * C, C), B16),
            pltpu.VMEM((9 * C, C), B16),
            pltpu.VMEM((px, C), F32),
            pltpu.VMEM((canvases, rows + 2, width, 3 * C), B16),
            pltpu.VMEM((px, C), B16),
            pltpu.VMEM((px, C), B16),
            pltpu.VMEM((px, C), B16),
            pltpu.VMEM((px, C), F32),
            pltpu.VMEM((px, C), F32),
            pltpu.VMEM((2, 2, canvases, width, C), B16),
            pltpu.VMEM((3, n, stats, LANES), F32),
            pltpu.VMEM((cells, C), F32),
            pltpu.VMEM((cells, C), F32),
            pltpu.SemaphoreType.DMA((5,)),
            pltpu.SemaphoreType.DMA((3,)),
            pltpu.SemaphoreType.DMA((3, n)),
            pltpu.SemaphoreType.DMA((3, n)),
            pltpu.SemaphoreType.DMA((2, 2)),
            pltpu.SemaphoreType.DMA((2, 2)),
        ],
        compiler_params=params_of(cid),
        name="resnet_backward",
    )(cot, du, hid, y1, x, *norms, s1, s2, pick, spread, div, *masks, vec, top, bottom, datt)


class Grid:
    def __init__(self, columns, n):
        self.columns, self.n, self.seats = columns, n, n // 2
        self.phases = columns.bit_length() - 1
        self.c = lax.axis_index("canvas")
        self.h = lax.axis_index("height")
        self.seat, self.core = self.h // 2, lax.rem(self.h, 2)
        flips = [
            (1 - 2 * lax.rem(self.c // 2**t, 2)) * 2**t for t in range(self.phases)
        ]
        last = self.phases - 1
        self.flips = [
            (1 - self.core) * flips[last - k] + self.core * flips[k] for k in range(self.phases)
        ]
        self.other_flips = [
            self.core * flips[last - k] + (1 - self.core) * flips[k] for k in range(self.phases)
        ]

    def column(self, e, flips=None):
        flips = self.flips if flips is None else flips
        col = self.c
        for k in range(self.phases):
            if (e >> k) & 1:
                col = col + flips[k]
        return col

    def mate(self, k):
        return {"canvas": self.c + self.flips[k], "height": self.h}

    def sibling(self):
        return {"canvas": self.c, "height": 2 * self.seat + 1 - self.core}

    def beside(self, step):
        return {"canvas": self.c, "height": self.h + 2 * step}

    def greet(self):
        barrier = pltpu.get_barrier_semaphore()
        for d in range(1, self.n):
            pl.semaphore_signal(
                barrier, inc=1, device_id={"canvas": self.c, "height": lax.rem(self.h + d, self.n)},
                device_id_type=MESH)
        for k in range(self.phases):
            pl.semaphore_signal(barrier, inc=1, device_id=self.mate(k), device_id_type=MESH)
        pl.semaphore_wait(barrier, self.n - 1 + self.phases)


def remote(src, dst, send, recv, to):
    return pltpu.make_async_remote_copy(
        src_ref=src, dst_ref=dst, send_sem=send, recv_sem=recv, device_id=to, device_id_type=MESH)


def lowest_bit(e):
    return (e & -e).bit_length() - 1


def spread_blocks(grid, fresh, whole, own_sem, zsend, msend, ssend, recv, srecv):
    g = grid
    seats, phases = g.seats, g.phases
    own = pltpu.make_async_copy(fresh, whole.at[g.c, g.seat, g.core], own_sem)
    own.start()

    def slot(e, seat):
        return whole.at[g.column(e), seat, g.core]

    def forward(e, seat, src, start):
        k_top = phases if e == 0 else lowest_bit(e)
        for k in range(k_top - 1, -1, -1):
            cp = remote(src, slot(e, seat), msend.at[k, e, seat], recv.at[e | (1 << k), seat], g.mate(k))
            cp.start() if start else cp.wait_send()
        cp = remote(src, slot(e, seat), ssend.at[e, seat], srecv.at[e, seat], g.sibling())
        cp.start() if start else cp.wait_send()

    def along(seat, step, src, start):
        cp = remote(src, slot(0, seat), zsend.at[(step + 1) // 2, seat], recv.at[0, seat], g.beside(step))
        cp.start() if start else cp.wait_send()

    def line(seat, src, start):
        @pl.when((seat <= g.seat) & (g.seat < seats - 1))
        def _():
            along(seat, 1, src, start)

        @pl.when((seat >= g.seat) & (g.seat > 0))
        def _():
            along(seat, -1, src, start)

    def arrive(e, seat):
        remote(fresh, slot(e, seat), ssend.at[0, 0], recv.at[e, seat], g.sibling()).wait_recv()

    early = [e for e in range(1, 2**phases) if lowest_bit(e) > 0]
    early.sort(key=lambda e: -lowest_bit(e))
    late = [e for e in range(1, 2**phases) if lowest_bit(e) == 0]

    def handle(e, seat):
        arrive(e, seat)
        if e == 0:
            line(seat, slot(0, seat), True)
        forward(e, seat, slot(e, seat), True)

    def both_sides(d, todo):
        for side in (-1, 1):
            seat = g.seat + side * d

            @pl.when((seat >= 0) & (seat < seats))
            def _():
                for e in todo:
                    handle(e, seat)

    line(g.seat, fresh, True)
    forward(0, g.seat, fresh, True)
    for e in early:
        handle(e, g.seat)

    def further(d, _):
        both_sides(d, [0] + early)
        return 0

    lax.fori_loop(1, seats, further, 0)
    for e in late:
        handle(e, g.seat)

    def finish(d, _):
        both_sides(d, late)
        return 0

    lax.fori_loop(1, seats, finish, 0)

    def drain(seat, _):
        for e in range(2**phases):
            remote(fresh, whole.at[g.column(e, g.other_flips), seat, 1 - g.core], ssend.at[0, 0],
                   srecv.at[e, seat], g.sibling()).wait_recv()
            forward(e, seat, slot(e, seat), False)
        line(seat, slot(0, seat), False)
        return 0

    lax.fori_loop(0, seats, drain, 0)
    own.wait()


def spread_scratch(columns, n):
    seats, phases = n // 2, columns.bit_length() - 1
    dma = pltpu.SemaphoreType.DMA
    return [
        dma((1,)),
        dma((2, seats)),
        dma((phases, columns, seats)),
        dma((columns, seats)),
        dma((columns, seats)),
        dma((columns, seats)),
    ]


def spread_kernel(columns, n, block, whole, fresh, own, zsend, msend, ssend, recv, srecv):
    grid = Grid(columns, n)
    fresh[...] = block[...].astype(B16)
    grid.greet()
    spread_blocks(grid, fresh, whole, own.at[0], zsend, msend, ssend, recv, srecv)


def spread_call(columns, n, cid, block):
    return pl.pallas_call(
        functools.partial(spread_kernel, columns, n),
        out_shape=sds((columns, n // 2, 2) + block.shape, B16),
        in_specs=[vmem],
        out_specs=anyw,
        scratch_shapes=[pltpu.VMEM(block.shape, B16)] + spread_scratch(columns, n),
        compiler_params=params_of(cid),
        name="spread_weights",
    )(block)


def adam_update(current, gradient, moment_one, moment_two, learn_rate):
    first_new = 0.5 * moment_one + 0.5 * gradient
    second_new = 0.9 * moment_two + 0.1 * gradient * gradient
    first_hat = first_new / (1.0 - 0.5**STEP)
    second_hat = second_new / (1.0 - 0.9**STEP)
    return (
        current - learn_rate * first_hat / (jnp.sqrt(second_hat) + adam_epsilon),
        first_new,
        second_new,
    )


def step_kernel(columns, n, grads, w, m, s, dvec, vw, vm, vs, new_w, new_m, new_s, new_vw, new_vm, new_vs, whole,
                acc, sib, got, up, down, fresh, vbuf, vtrade, lsem, gsend, grecv, psend, precv, usend, urecv,
                vsend, vrecv, tsend, trecv, own, zsend, msend, ssend, recv, srecv):
    g = Grid(columns, n)
    seats, phases = g.seats, g.phases
    slots = 2**phases
    order = sorted(range(slots), key=lambda e: (lowest_bit(e) if e else phases, e == (e & -e)))
    loads = []
    for e in order:
        cp = pltpu.make_async_copy(grads.at[g.column(e), :, g.core], acc.at[e], lsem.at[e])
        cp.start()
        loads.append(cp)

    @pl.when(g.seat == 0)
    def _():
        up[...] = jnp.zeros(up.shape, B16)

    @pl.when(g.seat == seats - 1)
    def _():
        down[...] = jnp.zeros(down.shape, B16)

    vbuf[g.h] = dvec[...]
    g.greet()
    sib_copies = []
    for e in order:
        cp = remote(grads.at[g.column(e, g.other_flips), :, 1 - g.core], sib.at[e], gsend.at[e], grecv.at[e],
                    g.sibling())
        cp.start()
        sib_copies.append(cp)

    def vector_copy(d):
        src = lax.rem(g.h + d, n)
        return remote(vbuf.at[g.h], vbuf.at[g.h], vsend.at[d], vrecv.at[g.h],
                      {"canvas": g.c, "height": src})

    def vector_arrival(d):
        src = lax.rem(g.h + d, n)
        return remote(vbuf.at[src], vbuf.at[src], vsend.at[d], vrecv.at[src],
                      {"canvas": g.c, "height": src})

    for d in range(1, n):
        vector_copy(d).start()

    def local(e, seat, below):
        total = acc[e, seat].astype(F32) + sib[e, seat].astype(F32)
        for k in range(below):
            total = total + got[k, e >> (k + 1), seat].astype(F32)
        return total

    def in_turn(i):
        even = 1 - lax.rem(i, 2)
        return (i // 2) * even + (1 - even) * (seats - 1 - i // 2)

    def phase_copy(k, e, seat):
        return remote(acc.at[e, seat], got.at[k, e >> (k + 1), seat], psend.at[k, e >> (k + 1), seat],
                      precv.at[k, e >> (k + 1), seat], g.mate(k))

    ready = 0
    for e in order:
        loads[ready].wait()
        sib_copies[ready].wait_recv()
        ready += 1
        if e == 0:
            break
        k = lowest_bit(e)

        def one(i, _):
            seat = in_turn(i)
            for q in range(k):
                phase_copy(q, e | (1 << q), seat).wait_recv()
            acc[e, seat] = local(e, seat, k).astype(B16)
            phase_copy(k, e, seat).start()
            return 0

        lax.fori_loop(0, seats, one, 0)

    for d in range(1, n):
        vector_arrival(d).wait_recv()
    vtrade[0, 0] = jnp.sum(vbuf[...], axis=0)
    for k in range(phases):
        cp = remote(vtrade.at[k, 0], vtrade.at[k, 1], tsend.at[k], trecv.at[k], g.mate(k))
        cp.start()
        cp.wait_recv()
        vtrade[k + 1, 0] = vtrade[k, 0] + vtrade[k, 1]
    new_vw[...], new_vm[...], new_vs[...] = adam_update(vw[...], vtrade[phases, 0], vm[...], vs[...], vector_rate)

    def line_copy(step, seat):
        box = up if step > 0 else down
        at = (step + 1) // 2
        return remote(acc.at[0, seat], box.at[seat], usend.at[at, seat], urecv.at[at, seat], g.beside(step))

    def own_column(i, _):
        seat = in_turn(i)
        for q in range(phases):
            phase_copy(q, 1 << q, seat).wait_recv()

        @pl.when(seat > g.seat)
        def _():
            @pl.when(g.seat > 0)
            def _():
                line_copy(1, seat).wait_recv()

            acc[0, seat] = (local(0, seat, phases) + up[seat].astype(F32)).astype(B16)
            line_copy(1, seat).start()

        @pl.when(seat < g.seat)
        def _():
            @pl.when(g.seat < seats - 1)
            def _():
                line_copy(-1, seat).wait_recv()

            acc[0, seat] = (local(0, seat, phases) + down[seat].astype(F32)).astype(B16)
            line_copy(-1, seat).start()

        return 0

    lax.fori_loop(0, seats, own_column, 0)

    @pl.when(g.seat > 0)
    def _():
        line_copy(1, g.seat).wait_recv()

    @pl.when(g.seat < seats - 1)
    def _():
        line_copy(-1, g.seat).wait_recv()

    total = local(0, g.seat, phases) + up[g.seat].astype(F32) + down[g.seat].astype(F32)
    next_w, new_m[...], new_s[...] = adam_update(w[...], total, m[...], s[...], matrix_rate)
    new_w[...] = next_w
    fresh[...] = next_w.astype(B16)
    spread_blocks(g, fresh, whole, own.at[0], zsend, msend, ssend, recv, srecv)
    for cp in sib_copies:
        cp.wait_send()
    for d in range(1, n):
        vector_copy(d).wait_send()
    for k in range(phases):
        remote(vtrade.at[k, 0], vtrade.at[k, 1], tsend.at[k], trecv.at[k], g.mate(k)).wait_send()

    def drain(seat, _):
        for e in range(1, slots):
            phase_copy(lowest_bit(e), e, seat).wait_send()

        @pl.when(seat > g.seat)
        def _():
            line_copy(1, seat).wait_send()

        @pl.when(seat < g.seat)
        def _():
            line_copy(-1, seat).wait_send()

        return 0

    lax.fori_loop(0, seats, drain, 0)


def step_call(columns, n, cid, grads, w, m, s, dvec, vw, vm, vs):
    seats, phases = n // 2, columns.bit_length() - 1
    block = w.shape
    half = max(columns // 2, 1)
    dma = pltpu.SemaphoreType.DMA
    return pl.pallas_call(
        functools.partial(step_kernel, columns, n),
        out_shape=[sds(block, F32)] * 3 + [sds(vw.shape, F32)] * 3 + [sds((columns, seats, 2) + block, B16)],
        in_specs=[anyw] + [vmem] * 7,
        out_specs=[vmem] * 6 + [anyw],
        scratch_shapes=[
            pltpu.VMEM((columns, seats) + block, B16),
            pltpu.VMEM((columns, seats) + block, B16),
            pltpu.VMEM((phases, half, seats) + block, B16),
            pltpu.VMEM((seats,) + block, B16),
            pltpu.VMEM((seats,) + block, B16),
            pltpu.VMEM(block, B16),
            pltpu.VMEM((n,) + vw.shape, F32),
            pltpu.VMEM((phases + 1, 2) + vw.shape, F32),
            dma((columns,)),
            dma((columns,)),
            dma((columns,)),
            dma((phases, half, seats)),
            dma((phases, half, seats)),
            dma((2, seats)),
            dma((2, seats)),
            dma((n,)),
            dma((n,)),
            dma((phases,)),
            dma((phases,)),
        ]
        + spread_scratch(columns, n),
        compiler_params=params_of(cid),
        name="step_weights",
    )(grads, w, m, s, dvec, vw, vm, vs)


class Engine:
    def __init__(self, steps):
        self.steps = steps

    def pump(self, count=1):
        for _ in range(count):
            next(self.steps, None)

    def ready(self):
        for done in self.steps:
            if done:
                return

    def finish(self):
        for _ in self.steps:
            pass


class Group:
    def __init__(self, grid, number, half_rows, first=0, size=None):
        self.g, self.number, self.half = grid, number, half_rows
        self.first, self.size = first, half_rows if size is None else size
        self.owner = 2 * number + grid.c // 2
        self.is_owner = grid.c // 2 == number

    def row(self, q, seat, core):
        block = (q // 2) * self.g.n + 2 * seat + core
        return pl.multiple_of((2 * block + lax.rem(q, 2)) * self.half + self.first, 16)

    def rows(self, q, seat, core):
        return pl.ds(self.row(q, seat, core), self.size)

    def at_column(self, col):
        return {"canvas": col, "height": self.g.h}

    def halves(self):
        first = 2 * lax.rem(self.g.c, 2)
        return [(0, first), (1, first + 1)]

    def part(self, ref, half):
        return ref.at[pl.ds(half * self.half, self.half)]

    def to_pieces(self, block, piece, send, recv, start):
        g = self.g

        @pl.when(self.is_owner)
        def _():
            for half, col in self.halves():
                @pl.when(col != g.c)
                def _():
                    cp = remote(self.part(block, half), piece, send.at[half], recv.at[0], self.at_column(col))
                    cp.start() if start else cp.wait_send()

                if start:
                    @pl.when(col == g.c)
                    def _():
                        piece[...] = block[half * self.half : (half + 1) * self.half, :]

    def piece_arrived(self, block, piece, send, recv):
        @pl.when(self.owner != self.g.c)
        def _():
            remote(self.part(block, 0), piece, send.at[0], recv.at[0], self.at_column(self.owner)).wait_recv()

    def to_owner(self, piece, block, send, recv, start):
        g = self.g
        half = lax.rem(g.c, 2)
        where = pl.ds(pl.multiple_of(half * self.half, 16), self.half)

        @pl.when(self.owner != g.c)
        def _():
            cp = remote(piece, block.at[where], send.at[0], recv.at[half], self.at_column(self.owner))
            cp.start() if start else cp.wait_send()

        if start:
            @pl.when(self.owner == g.c)
            def _():
                block[where, :] = piece[...]

    def block_arrived(self, piece, block, send, recv):
        g = self.g

        @pl.when(self.is_owner)
        def _():
            for half, col in self.halves():
                @pl.when(col != g.c)
                def _():
                    remote(piece, self.part(block, half), send.at[0], recv.at[half], self.at_column(col)).wait_recv()


def gate(only, q, seat, core, do):
    if only is None:
        do()
    else:
        pl.when(only(q, seat, core))(do)


def gather_pieces(group, piece, dest, own, zsend, msend, ssend, recv, srecv, only=None):
    g = group.g
    seats, phases = g.seats, g.phases
    local = pltpu.make_async_copy(piece, dest.at[group.rows(g.c, g.seat, g.core)], own.at[0])

    def gated(e, seat, do):
        gate(only, g.column(e), seat, g.core, do)

    gated(0, g.seat, local.start)

    def slot(e, seat):
        return dest.at[group.rows(g.column(e), seat, g.core)]

    def forward(e, seat, src, start):
        k_top = phases if e == 0 else lowest_bit(e)
        for k in range(k_top - 1, -1, -1):
            cp = remote(src, slot(e, seat), msend.at[k, e, seat], recv.at[e | (1 << k), seat], g.mate(k))
            cp.start() if start else cp.wait_send()
        cp = remote(src, slot(e, seat), ssend.at[e, seat], srecv.at[e, seat], g.sibling())
        cp.start() if start else cp.wait_send()

    def along(seat, step, src, start):
        cp = remote(src, slot(0, seat), zsend.at[(step + 1) // 2, seat], recv.at[0, seat], g.beside(step))
        cp.start() if start else cp.wait_send()

    def line(seat, src, start):
        @pl.when((seat <= g.seat) & (g.seat < seats - 1))
        def _():
            along(seat, 1, src, start)

        @pl.when((seat >= g.seat) & (g.seat > 0))
        def _():
            along(seat, -1, src, start)

    def handle(e, seat):
        def do():
            remote(piece, slot(e, seat), ssend.at[0, 0], recv.at[e, seat], g.sibling()).wait_recv()
            if e == 0:
                line(seat, slot(0, seat), True)
            forward(e, seat, slot(e, seat), True)

        gated(e, seat, do)

    early = sorted((e for e in range(1, 2**phases) if lowest_bit(e) > 0), key=lambda e: -lowest_bit(e))
    late = [e for e in range(1, 2**phases) if lowest_bit(e) == 0]

    def both_sides(d, todo):
        for side in (-1, 1):
            seat = g.seat + side * d

            @pl.when((seat >= 0) & (seat < seats))
            def _():
                for e in todo:
                    handle(e, seat)

    def first():
        line(g.seat, piece, True)
        forward(0, g.seat, piece, True)

    gated(0, g.seat, first)
    yield
    for e in early:
        handle(e, g.seat)
    yield
    for d in range(1, seats):
        both_sides(d, [0] + early)
        yield
    for e in late:
        handle(e, g.seat)
    yield
    for d in range(1, seats):
        both_sides(d, late)
        yield

    def siblings(seat, _):
        for e in range(2**phases):
            q = g.column(e, g.other_flips)
            cp = remote(piece, dest.at[group.rows(q, seat, 1 - g.core)], ssend.at[0, 0], srecv.at[e, seat],
                        g.sibling())
            gate(only, q, seat, 1 - g.core, cp.wait_recv)
        return 0

    lax.fori_loop(0, seats, siblings, 0)
    gated(0, g.seat, local.wait)
    yield True

    def drain(seat, _):
        def sent(e):
            forward(e, seat, slot(e, seat), False)
            if e == 0:
                line(seat, slot(0, seat), False)

        for e in range(2**phases):
            gated(e, seat, functools.partial(sent, e))
        return 0

    lax.fori_loop(0, seats, drain, 0)


def gather_pieces_scratch(columns, n):
    seats, phases = n // 2, columns.bit_length() - 1
    dma = pltpu.SemaphoreType.DMA
    return [
        dma((1,)),
        dma((2, seats)),
        dma((phases, columns, seats)),
        dma((columns, seats)),
        dma((columns, seats)),
        dma((columns, seats)),
    ]


def reduce_pieces(group, src, piece, sib, got, box, gsend, grecv, psend, precv, usend, urecv, only=None):
    g = group.g
    seats, phases = g.seats, g.phases
    slots = 2**phases
    order = sorted(range(slots), key=lambda e: (lowest_bit(e) if e else phases, e == (e & -e)))
    turns = [i // 2 if i % 2 == 0 else seats - 1 - i // 2 for i in range(seats)]

    def mine(e, seat):
        return group.rows(g.column(e), seat, g.core)

    def sibling_copy(e, seat):
        return remote(src.at[group.rows(g.column(e, g.other_flips), seat, 1 - g.core)], sib.at[e, seat],
                      gsend.at[e, seat], grecv.at[e, seat], g.sibling())

    def phase_copy(k, e, seat):
        at = (k, e >> (k + 1), seat)
        return remote(src.at[mine(e, seat), :], got.at[at], psend.at[at], precv.at[at], g.mate(k))

    def line_copy(seat):
        return remote(src.at[mine(0, seat), :], box.at[g.seat], usend.at[seat], urecv.at[g.seat],
                      {"canvas": g.c, "height": 2 * seat + g.core})

    def line_arrival(seat):
        return remote(src.at[mine(0, seat), :], box.at[seat], usend.at[seat], urecv.at[seat],
                      {"canvas": g.c, "height": 2 * seat + g.core})

    def local(e, seat, below):
        total = src[mine(e, seat), :].astype(F32) + sib[e, seat].astype(F32)
        for k in range(below):
            total = total + got[k, e >> (k + 1), seat].astype(F32)
        return total

    def gated(e, seat, do):
        gate(only, g.column(e), seat, g.core, do)

    def gated_sibling(e, seat, do):
        gate(only, g.column(e, g.other_flips), seat, 1 - g.core, do)

    for e in order:
        for seat in turns:
            gated_sibling(e, seat, sibling_copy(e, seat).start)
    yield

    def pass_on(e, k, seat):
        sibling_copy(e, seat).wait_recv()
        for q in range(k):
            phase_copy(q, e | (1 << q), seat).wait_recv()
        src[mine(e, seat), :] = local(e, seat, k).astype(B16)
        phase_copy(k, e, seat).start()

    for e in order:
        if e == 0:
            break
        for seat in turns:
            gated(e, seat, functools.partial(pass_on, e, lowest_bit(e), seat))
            yield

    def own_column(seat):
        sibling_copy(0, seat).wait_recv()
        for q in range(phases):
            phase_copy(q, 1 << q, seat).wait_recv()

        @pl.when(seat != g.seat)
        def _():
            src[mine(0, seat), :] = local(0, seat, phases).astype(B16)
            line_copy(seat).start()

    for seat in turns:
        gated(0, seat, functools.partial(own_column, seat))
        yield

    def last():
        total = local(0, g.seat, phases)
        for seat in turns:
            @pl.when(seat != g.seat)
            def _():
                line_arrival(seat).wait_recv()

            total = total + jnp.where(seat == g.seat, 0.0, box[seat].astype(F32))
        piece[...] = total.astype(B16)

    gated(0, g.seat, last)
    yield True

    def drain(seat, _):
        def sent(e):
            if e > 0:
                phase_copy(lowest_bit(e), e, seat).wait_send()
            else:
                @pl.when(seat != g.seat)
                def _():
                    line_copy(seat).wait_send()

        for e in range(slots):
            gated_sibling(e, seat, sibling_copy(e, seat).wait_send)
            gated(e, seat, functools.partial(sent, e))
        return 0

    lax.fori_loop(0, seats, drain, 0)


def reduce_pieces_scratch(columns, n, half_rows):
    seats, phases = n // 2, columns.bit_length() - 1
    half = columns // 2
    dma = pltpu.SemaphoreType.DMA
    block = (half_rows, C)
    return [
        pltpu.VMEM((columns, seats) + block, B16),
        pltpu.VMEM((phases, half, seats) + block, B16),
        pltpu.VMEM((seats,) + block, B16),
        dma((columns, seats)),
        dma((columns, seats)),
        dma((phases, half, seats)),
        dma((phases, half, seats)),
        dma((seats,)),
        dma((seats,)),
    ]


class Named:
    def __init__(self, shapes, refs):
        refs = list(refs)
        for name, shape in shapes.items():
            if isinstance(shape, list):
                setattr(self, name, [refs.pop(0) for _ in shape])
            else:
                setattr(self, name, refs.pop(0))


def named_call(kernel, name, cid, inputs, outputs, scratch):
    shapes = {**inputs, **outputs, **scratch}
    flat = []
    for value in scratch.values():
        flat += value if isinstance(value, list) else [value]
    results = pl.pallas_call(
        lambda *refs: kernel(Named(shapes, refs)),
        out_shape=[sds(shape, kind) for shape, kind, _ in outputs.values()],
        in_specs=[spec for _, spec in inputs.values()],
        out_specs=[spec for _, _, spec in outputs.values()],
        scratch_shapes=flat,
        compiler_params=params_of(cid),
        name=name,
    )(*[array for array, _ in inputs.values()])
    return dict(zip(outputs, results))


def greet_all(grid):
    barrier = pltpu.get_barrier_semaphore()
    for d in range(1, grid.n):
        pl.semaphore_signal(
            barrier, inc=1, device_id={"canvas": grid.c, "height": lax.rem(grid.h + d, grid.n)}, device_id_type=MESH)
    for d in range(1, grid.columns):
        pl.semaphore_signal(
            barrier, inc=1, device_id={"canvas": lax.rem(grid.c + d, grid.columns), "height": grid.h},
            device_id_type=MESH)
    pl.semaphore_wait(barrier, grid.n - 1 + grid.columns - 1)


def across(top, low):
    def taps(dr):
        if dr == 0:
            return [(0, 2 * C, top, 9 * C), (2 * C, 3 * C, low, 0)]
        return [(0, 3 * C, low, 3 * C * dr - 2 * C)]

    return taps


def first_kernel(columns, n, dims, R):
    g = Grid(columns, n)
    half = R.block.shape[0] // 2
    groups = [Group(g, i, half) for i in range(2)]
    R.low[...] = R.block[...].astype(B16)
    count = R.vectors.shape[0]
    R.vec[...] = jnp.zeros(R.vec.shape, F32)
    R.vec[0:count, :] = R.vectors[...].astype(B16).astype(F32)
    canvases, rows, width = dims
    turned = jnp.transpose(R.ids_lane[...])
    for v in range(canvases):
        R.ids_px[v] = jnp.broadcast_to(turned[:, v : v + 1], (rows * width, LANES)).reshape(rows, width, LANES)
    greet_all(g)
    for i, group in enumerate(groups):
        group.to_pieces(R.low, R.pieces.at[i], R.tsend.at[i], R.trecv.at[i], True)
    engines = [
        Engine(gather_pieces(groups[0], R.pieces.at[0], R.w_top, *R.gather0)),
        Engine(gather_pieces(groups[1], R.pieces.at[1], R.w_low, *R.gather1)),
    ]
    each = rows * width // UNIT
    for v in range(canvases):
        cell_ids = R.ids_px[v].reshape(each, UNIT, LANES)[:, 0, :] + float(CROPS * v)
        lane = lax.broadcasted_iota(jnp.int32, (each, LANES), 1).astype(F32)
        R.hot[v * each : (v + 1) * each, :] = (cell_ids == lane).astype(F32)
    stats = canvases * CROPS
    R.spread[...] = R.hot[:, :stats].astype(B16)
    R.pick[...] = jnp.transpose(R.hot[...])[:stats, :].astype(B16)
    turn = [0]
    lag = 2 * g.seats - 3

    def pump():
        if turn[0] == 0:
            groups[0].piece_arrived(R.low, R.pieces.at[0], R.tsend.at[0], R.trecv.at[0])
        if turn[0] < 2 * g.seats + 1:
            engines[0].pump()
        if turn[0] == lag:
            groups[1].piece_arrived(R.low, R.pieces.at[1], R.tsend.at[1], R.trecv.at[1])
        if turn[0] >= lag:
            engines[1].pump()
        turn[0] += 1

    layout_body(n, dims, R.x, R.pick, R.spread, R.ids_px, R.ids_lane, R.ids_all, R.mean1, R.inv1, R.div, R.cnt,
                R.col_l, R.col_r, R.row_u, R.row_d, *R.layout, pump=pump)
    pump()
    conv = Convolver(n, dims, R.x, R.pick, R.spread, R.cnt, R.col_l, R.col_r, R.row_u, R.row_d, R.halo, R.buf,
                     R.tmp_a, R.tmp_b, R.send, R.recv, R.hsend, R.hrecv)
    vec = R.vec
    conv.activate(R.x, R.mean1, R.inv1, vec[0:1, :], vec[1:2, :], R.s1, 0, pump)
    out_s1 = pltpu.make_async_copy(R.s1, R.s1_out, R.osem.at[0])
    out_s1.start()
    while turn[0] < 2 * g.seats + 1:
        pump()
    engines[0].ready()
    out_top = pltpu.make_async_copy(R.w_top, R.top, R.osem.at[1])
    out_top.start()
    pump_low = engines[1].pump
    if turn[0] <= lag:
        groups[1].piece_arrived(R.low, R.pieces.at[1], R.tsend.at[1], R.trecv.at[1])
        pump_low()

    def emit_first(at, total):
        R.y1[at, :] = total + vec[2:3, :]

    conv.convolve(R.s1, lambda dr: [(0, 3 * C, R.w_top, 3 * C * dr)], emit_first, pump_low)
    out_y1 = pltpu.make_async_copy(R.y1, R.y1_out, R.osem.at[2])
    out_y1.start()
    conv.statistics(R.y1, R.mean2, R.inv2, 0, pump_low)
    conv.activate(R.y1, R.mean2, R.inv2, vec[3:4, :], vec[4:5, :], R.s2, 1, pump_low)
    out_s2 = pltpu.make_async_copy(R.s2, R.s2_out, R.osem.at[3])
    out_s2.start()
    engines[1].ready()
    out_low = pltpu.make_async_copy(R.w_low, R.bottom, R.osem.at[4])
    out_low.start()

    def emit_second(at, total):
        R.hid[at, :] = total + vec[5:6, :] + R.x[at, :].astype(F32)

    conv.convolve(R.s2, across(R.w_top, R.w_low), emit_second)
    conv.statistics(R.hid, R.mean3, R.inv3, 1)
    conv.normalise(R.hid, R.mean3, R.inv3, vec[6:7, :], vec[7:8, :], R.u)
    for cp in conv.sent:
        cp.wait_send()
    for i, group in enumerate(groups):
        group.to_pieces(R.low, R.pieces.at[i], R.tsend.at[i], R.trecv.at[i], False)
    for cp in (out_s1, out_top, out_y1, out_s2, out_low):
        cp.wait()
    for engine in engines:
        engine.finish()


def first_call(columns, n, dims, x, ids_lane, vectors, block):
    canvases, rows, width = dims
    px = canvases * rows * width
    cells = px // UNIT
    stats = canvases * CROPS
    tall = (canvases, rows + 2, width)
    half = block.shape[0] // 2
    dma = pltpu.SemaphoreType.DMA
    inputs = dict(x=(x, vmem), ids_lane=(ids_lane, vmem), vectors=(vectors, vmem), block=(block, vmem))
    cell = ((cells, C), F32, vmem)
    outputs = dict(
        vec=((16, C), F32, vmem), pick=((stats, cells), B16, vmem), spread=((cells, stats), B16, vmem),
        ids_all=((n,) + ids_lane.shape, F32, vmem), mean1=cell, inv1=cell, div=((stats, LANES), F32, vmem),
        cnt=((stats, LANES), F32, vmem), col_l=(tall + (LANES,), F32, vmem), col_r=(tall + (LANES,), F32, vmem),
        row_u=((px, LANES), F32, vmem), row_d=((px, LANES), F32, vmem), hid=((px, C), F32, vmem),
        u=((px, C), B16, vmem), mean2=cell, inv2=cell, mean3=cell, inv3=cell, y1_out=((px, C), F32, anyw),
        s1_out=(tall + (3 * C,), B16, anyw), s2_out=(tall + (3 * C,), B16, anyw),
        top=((11 * C, C), B16, anyw), bottom=((11 * C, C), B16, anyw))
    scratch = dict(
        ids_px=pltpu.VMEM(dims + (LANES,), F32), hot=pltpu.VMEM((cells, LANES), F32),
        y1=pltpu.VMEM((px, C), F32), s1=pltpu.VMEM(tall + (3 * C,), B16), s2=pltpu.VMEM(tall + (3 * C,), B16),
        w_top=pltpu.VMEM((11 * C, C), B16), w_low=pltpu.VMEM((11 * C, C), B16), low=pltpu.VMEM(block.shape, B16),
        pieces=pltpu.VMEM((2, half, C), B16), tsend=dma((2, 2)), trecv=dma((2, 1)),
        gather0=gather_pieces_scratch(columns, n), gather1=gather_pieces_scratch(columns, n),
        layout=layout_scratch(n, dims, ids_lane), halo=pltpu.VMEM((2, 2, canvases, width, C), B16),
        buf=pltpu.VMEM((2, n, stats, LANES), F32), tmp_a=pltpu.VMEM((cells, C), F32),
        tmp_b=pltpu.VMEM((cells, C), F32), send=dma((2, n)), recv=dma((2, n)), hsend=dma((2, 2)),
        hrecv=dma((2, 2)), osem=dma((5,)))
    return named_call(functools.partial(first_kernel, columns, n, dims), "first_forward", 1, inputs, outputs, scratch)


class Backer:
    def __init__(self, n, dims, R):
        self.n, self.dims, self.R = n, dims, R
        self.px = dims[0] * dims[1] * dims[2]
        self.cells = self.px // UNIT
        self.sent = []

    @staticmethod
    def pixels(i):
        return pl.ds(i * 16 * UNIT, 16 * UNIT)

    def norm_sums(self, grad_of, source, mean, inv, gain, rnd):
        R = self.R

        def body(i, carry):
            dg, db = carry
            at = self.pixels(i)
            unit = (source[at, :].astype(F32) - over_cells(mean, i)) * over_cells(inv, i)
            d = grad_of(i, unit)
            R.norm[at, :] = unit
            e = d * gain
            R.part[at, :] = e
            cross = d * unit
            here = pl.ds(i * 16, 16)
            R.tmp_a[here, :] = jnp.sum(e.reshape(16, UNIT, C), axis=1)
            R.tmp_b[here, :] = jnp.sum((cross * gain).reshape(16, UNIT, C), axis=1)
            return (dg + jnp.sum(cross, axis=0, keepdims=True), db + jnp.sum(d, axis=0, keepdims=True))

        zero = jnp.zeros((1, C), F32)
        dg, db = lax.fori_loop(0, self.cells // 16, body, (zero, zero))
        R.buf[rnd, 0] = pack([group_totals(R.pick, R.tmp_a[...]), group_totals(R.pick, R.tmp_b[...])])
        copies = spread_copies(self.n, R.buf, R.send, R.recv, rnd)
        for cp in copies:
            cp.start()
        self.sent = self.sent + copies
        return copies, dg, db

    def norm_finish(self, copies, rnd, inv, emit):
        R = self.R
        for cp in copies:
            cp.wait_recv()
        gathered = jnp.sum(R.buf[rnd], axis=0) / R.div[...]
        R.tmp_a[...] = split_dot(R.spread[...], unpack(gathered))
        R.tmp_b[...] = split_dot(R.spread[...], unpack(shift_down(gathered, 1)))

        def body(i, _):
            at = self.pixels(i)
            emit(i, over_cells(inv, i) * (
                R.part[at, :] - over_cells(R.tmp_a, i) - R.norm[at, :] * over_cells(R.tmp_b, i)))
            return 0

        lax.fori_loop(0, self.cells // 16, body, 0)

    def send_rows(self, source, rnd):
        R = self.R
        canvases, rows, width = self.dims

        def one(v, r):
            at = pl.ds(pl.multiple_of((v * rows + r) * width, width), width)
            R.d3[v, r + 1] = shift_columns(source[at, :].astype(F32), R.col_l[v, r + 1], R.col_r[v, r + 1])

        def edges(v, _):
            one(v, 0)
            one(v, rows - 1)
            return 0

        lax.fori_loop(0, canvases, edges, 0)
        mid = pl.ds(C, C)
        up, down = halo_copies(self.n, R.d3.at[:, 1, :, mid], R.d3.at[:, rows, :, mid], R.halo.at[rnd],
                               R.hsend.at[rnd], R.hrecv.at[rnd])
        start_halo(self.n, up, down)

        def inner(i, _):
            one(i // (rows - 2), 1 + lax.rem(i, rows - 2))
            return 0

        if rows > 2:
            lax.fori_loop(0, canvases * (rows - 2), inner, 0)
        return up, down

    def finish_rows(self, up, down, rnd):
        R = self.R
        canvases, rows, _ = self.dims
        wait_halo(self.n, up, down, R.halo.at[rnd], 0.0)
        for v in range(canvases):
            for side, r in ((0, 0), (1, rows + 1)):
                R.d3[v, r] = shift_columns(R.halo[rnd, side, v].astype(F32), R.col_l[v, r], R.col_r[v, r])

    def convolve_back(self, weights, pump=no_pump):
        R = self.R
        canvases, rows, width = self.dims
        plane = rows * width
        nt = (((1,), (1,)), ((), ()))
        for v in range(canvases):
            at = pl.ds(v * plane, plane)
            total = None
            for dr in (1, 0, 2):
                acc = None
                for dc in range(3):
                    ref, row = weights(3 * (2 - dr) + (2 - dc))
                    lhs = R.d3[v, dr : dr + rows, :, dc * C : (dc + 1) * C].reshape(plane, C)
                    term = lax.dot_general(lhs, ref[row : row + C, :], nt, preferred_element_type=F32)
                    acc = term if acc is None else acc + term
                if dr == 0:
                    acc = acc * wide(R.row_u[at, :])
                if dr == 2:
                    acc = acc * wide(R.row_d[at, :])
                total = acc if total is None else total + acc
                pump()
            R.part[at, :] = total

    def mask_rows(self, source):
        R = self.R

        def body(i, _):
            at = self.pixels(i)
            value = source[at, :].astype(F32)
            R.low_u[at, :] = (value * wide(R.row_u[at, :])).astype(B16)
            R.low_d[at, :] = (value * wide(R.row_d[at, :])).astype(B16)
            return 0

        lax.fori_loop(0, self.cells // 16, body, 0)

    def weight_grad(self, s, grad, dest, pump=no_pump):
        R = self.R
        canvases, rows, width = self.dims
        plane = rows * width
        tn = (((0,), (0,)), ((), ()))
        for dr, source in ((0, R.low_u), (1, grad), (2, R.low_d)):
            for dc in range(3):
                acc = None
                for v in range(canvases):
                    lhs = s[v, dr : dr + rows, :, dc * C : (dc + 1) * C].reshape(plane, C)
                    term = lax.dot_general(
                        lhs, source[v * plane : (v + 1) * plane, :], tn, preferred_element_type=F32)
                    acc = term if acc is None else acc + term
                ref, row = dest(3 * dr + dc)
                ref[row : row + C, :] = acc.astype(B16)
                pump()


def back_kernel(columns, n, dims, R):
    g = Grid(columns, n)
    half = R.sum_low.shape[0]
    group = Group(g, 1, half)
    load_s = pltpu.make_async_copy(R.s2, R.s, R.lsem.at[0])
    load_s.start()
    load_k = second_matrix(R.top, R.bottom, R.k, R.ksem)
    load_att = pltpu.make_async_copy(R.datt, R.g_low.at[pl.ds(7 * C, 4 * C)], R.lsem.at[1])
    for cp in load_k + [load_att]:
        cp.start()
    greet_all(g)
    vec = R.vec
    back = Backer(n, dims, R)
    copies, dg3, db3 = back.norm_sums(lambda i, unit: R.du[back.pixels(i), :], R.hid, R.mean3, R.inv3, vec[6:7, :], 0)

    def emit_hidden(i, value):
        at = back.pixels(i)
        total = R.cot[at, :].astype(F32) + value
        R.dh[at, :] = total
        R.grad[at, :] = total.astype(B16)

    back.norm_finish(copies, 0, R.inv3, emit_hidden)
    up, down = back.send_rows(R.grad, 0)
    plane = dims[1] * dims[2]
    o_back = remote(R.o.at[pl.ds(plane, plane)], R.o_back, R.lsem.at[2], R.lsem.at[3],
                    {"canvas": g.c, "height": lax.rem(g.h + n // 2, n)})
    o_back.start()
    back.mask_rows(R.grad)
    load_s.wait()

    def dest_two(tap):
        return (R.g_top, (9 + tap) * C) if tap < 2 else (R.g_low, (tap - 2) * C)

    back.weight_grad(R.s, R.grad, dest_two)
    load_att.wait()
    load_s = pltpu.make_async_copy(R.s1, R.s, R.lsem.at[0])
    load_s.start()
    engine = Engine(reduce_pieces(group, R.g_low, R.sum_low, *R.reduce))
    engine.pump()
    dc2 = jnp.sum(R.grad[...].astype(F32), axis=0, keepdims=True)
    back.finish_rows(up, down, 0)
    for cp in load_k:
        cp.wait()
    back.convolve_back(lambda tap: (R.k, tap * C), engine.pump)
    gain2, bias2 = vec[3:4, :], vec[4:5, :]

    def grad_two(i, unit):
        return R.part[back.pixels(i), :] * silu_slope(unit * gain2 + bias2)

    copies, dg2, db2 = back.norm_sums(grad_two, R.y1, R.mean2, R.inv2, gain2, 1)
    engine.pump(2)

    def emit_grad(i, value):
        R.grad[back.pixels(i), :] = value.astype(B16)

    back.norm_finish(copies, 1, R.inv2, emit_grad)
    engine.pump(2)
    back.mask_rows(R.grad)
    dc1 = jnp.sum(R.grad[...].astype(F32), axis=0, keepdims=True)
    load_s.wait()
    back.weight_grad(R.s, R.grad, lambda tap: (R.g_top, tap * C), engine.pump)
    R.dvec[...] = jnp.concatenate([dc1, dg2, db2, dc2, dg3, db3, jnp.zeros((2, C), F32)], axis=0)
    engine.ready()
    engine.finish()
    for cp in back.sent:
        cp.wait_send()
    o_back.wait()


def back_call(columns, n, dims, cot, du, hid, y1, norms, s1, s2, pick, spread, div, masks, vec, top, bottom, datt, o,
              block_rows):
    canvases, rows, width = dims
    px = canvases * rows * width
    cells = px // UNIT
    stats = canvases * CROPS
    dma = pltpu.SemaphoreType.DMA
    names = ("mean2", "inv2", "mean3", "inv3")
    inputs = dict(cot=(cot, vmem), du=(du, vmem), hid=(hid, vmem), y1=(y1, vmem), s1=(s1, anyw), s2=(s2, anyw),
                  pick=(pick, vmem), spread=(spread, vmem), div=(div, vmem), vec=(vec, vmem), top=(top, anyw),
                  bottom=(bottom, anyw), datt=(datt, anyw), o=(o, anyw),
                  **{k: (v, vmem) for k, v in zip(names, norms)},
                  **{k: (v, vmem) for k, v in zip(("col_l", "col_r", "row_u", "row_d"), masks)})
    outputs = dict(dh=((px, C), F32, vmem), grad=((px, C), B16, vmem), g_top=((11 * C, C), B16, vmem),
                   dvec=((8, C), F32, vmem), sum_low=((block_rows // 2, C), B16, vmem),
                   o_back=((px // canvases, C), B16, anyw))
    scratch = dict(
        g_low=pltpu.VMEM((11 * C, C), B16), s=pltpu.VMEM(s1.shape, B16), k=pltpu.VMEM((9 * C, C), B16),
        d3=pltpu.VMEM(s1.shape, B16), low_u=pltpu.VMEM((px, C), B16), low_d=pltpu.VMEM((px, C), B16),
        part=pltpu.VMEM((px, C), F32), norm=pltpu.VMEM((px, C), F32),
        halo=pltpu.VMEM((1, 2, canvases, width, C), B16), buf=pltpu.VMEM((2, n, stats, LANES), F32),
        tmp_a=pltpu.VMEM((cells, C), F32), tmp_b=pltpu.VMEM((cells, C), F32),
        reduce=reduce_pieces_scratch(columns, n, block_rows // 2),
        lsem=dma((5,)), ksem=dma((3,)),
        send=dma((2, n)), recv=dma((2, n)), hsend=dma((1, 2)), hrecv=dma((1, 2)))
    return named_call(functools.partial(back_kernel, columns, n, dims), "back", 7, inputs, outputs, scratch)


def renew_kernel(columns, n, dims, R):
    g = Grid(columns, n)
    half = R.fresh.shape[0] // 2
    upper, lower = Group(g, 0, half), Group(g, 1, half)
    load_g = pltpu.make_async_copy(R.g_in, R.g_top, R.ksem.at[1])
    load_g.start()
    load_k = pltpu.make_async_copy(R.top.at[pl.ds(0, 9 * C)], R.k, R.ksem.at[0])
    load_k.start()
    loads = [
        pltpu.make_async_copy(src, dst, R.ksem.at[2 + i])
        for i, (src, dst) in enumerate(((R.w, R.new_w), (R.m, R.new_m), (R.v, R.new_s), (R.dh, R.igrad)))
    ]
    for cp in loads:
        cp.start()
    piece_loads = []
    for i, src in enumerate((R.w, R.m, R.v)):
        here = pltpu.make_async_copy(src.at[pl.ds(0, half)], R.piece_in.at[i], R.psem.at[i])
        there = pltpu.make_async_copy(R.shares.at[i], R.piece_in.at[i], R.psem.at[i])
        pl.when(g.c == 0)(here.start)
        pl.when(g.c != 0)(there.start)
        piece_loads.append(there)
    greet_all(g)
    vec = R.vec
    lower.to_owner(R.sum_low, R.totals.at[1], R.asend.at[1], R.arecv.at[1], True)
    load_g.wait()
    reducer = Engine(reduce_pieces(upper, R.g_top, R.sum_top, *R.reduce))
    reducer.pump()
    back = Backer(n, dims, R)
    up, down = back.send_rows(R.grad, 0)
    reducer.pump(2)
    for cp in loads:
        cp.wait()

    def adam(group, totals):
        @pl.when(group.is_owner)
        def _():
            total = totals[...].astype(F32)
            next_w, R.new_m[...], R.new_s[...] = adam_update(
                R.new_w[...], total, R.new_m[...], R.new_s[...], matrix_rate)
            R.new_w[...] = next_w
            R.fresh[...] = next_w.astype(B16)

    lower.block_arrived(R.sum_low, R.totals.at[1], R.asend.at[1], R.arecv.at[1])
    adam(lower, R.totals.at[1])
    lower.to_pieces(R.fresh, R.pieces.at[1], R.tsend.at[1], R.trecv.at[1], True)
    reducer.pump(2)
    back.finish_rows(up, down, 0)
    load_k.wait()
    back.convolve_back(lambda tap: (R.k, tap * C), reducer.pump)
    gain1, bias1 = vec[0:1, :], vec[1:2, :]

    def grad_one(i, unit):
        return R.part[back.pixels(i), :] * silu_slope(unit * gain1 + bias1)

    copies, dg1, db1 = back.norm_sums(grad_one, R.x, R.mean1, R.inv1, gain1, 0)
    reducer.pump(2)
    R.vbuf[g.h] = jnp.concatenate([dg1, db1, R.dvec[0:6, :], R.dvec_att[...]], axis=0)
    vector_sends = [
        remote(R.vbuf.at[g.h], R.vbuf.at[g.h], R.vsend.at[d], R.vrecv.at[g.h],
               {"canvas": g.c, "height": lax.rem(g.h + d, n)})
        for d in range(1, n)
    ]
    for cp in vector_sends:
        cp.start()
    lower.piece_arrived(R.fresh, R.pieces.at[1], R.tsend.at[1], R.trecv.at[1])
    gather_low = Engine(gather_pieces(lower, R.pieces.at[1], R.new_low, *R.gather1))
    gather_low.pump()
    reducer.ready()
    for cp in piece_loads:
        cp.wait()
    next_piece, _, _ = adam_update(
        R.piece_in[0], R.sum_top[...].astype(F32), R.piece_in[1], R.piece_in[2], matrix_rate)
    R.pieces[0] = next_piece.astype(B16)
    gather_top = Engine(gather_pieces(upper, R.pieces.at[0], R.new_top, *R.gather0))
    gather_top.pump()
    upper.to_owner(R.sum_top, R.totals.at[0], R.asend.at[0], R.arecv.at[0], True)

    def emit_input(i, value):
        at = back.pixels(i)
        R.igrad[at, :] = R.igrad[at, :] + value

    back.norm_finish(copies, 0, R.inv1, emit_input)
    gather_top.pump()
    for d in range(1, n):
        src = lax.rem(g.h + d, n)
        remote(R.vbuf.at[src], R.vbuf.at[src], R.vsend.at[d], R.vrecv.at[src],
               {"canvas": g.c, "height": src}).wait_recv()
    R.vtrade[0, 0] = jnp.sum(R.vbuf[...], axis=0)

    def trade(k):
        return remote(R.vtrade.at[k, 0], R.vtrade.at[k, 1], R.qsend.at[k], R.qrecv.at[k], g.mate(k))

    trade(0).start()
    gather_top.pump()
    for k in range(g.phases):
        trade(k).wait_recv()
        R.vtrade[k + 1, 0] = R.vtrade[k, 0] + R.vtrade[k, 1]
        if k + 1 < g.phases:
            trade(k + 1).start()
        gather_top.pump()
    count = R.vw.shape[0]
    R.new_vw[...], R.new_vm[...], R.new_vs[...] = adam_update(
        R.vw[...], R.vtrade[g.phases, 0][0:count, :], R.vm[...], R.vs[...], vector_rate)
    R.new_vec[...] = jnp.zeros(R.new_vec.shape, F32)
    R.new_vec[0:count, :] = R.new_vw[...].astype(B16).astype(F32)
    new_vec, s1, y1 = R.new_vec, R.d3, R.part
    conv = Convolver(n, dims, R.x, R.pick, R.spread, R.cnt, R.col_l, R.col_r, R.row_u, R.row_d, R.chalo, R.cbuf,
                     R.tmp_a, R.tmp_b, R.csend, R.crecv, R.chsend, R.chrecv)
    conv.activate(R.x, R.mean1, R.inv1, new_vec[0:1, :], new_vec[1:2, :], s1, 0, gather_top.pump)
    gather_top.ready()
    pump = gather_low.pump
    pump()

    def emit_first(at, total):
        y1[at, :] = total + new_vec[2:3, :]

    conv.convolve(s1, lambda dr: [(0, 3 * C, R.new_top, 3 * C * dr)], emit_first, pump)
    conv.statistics(y1, R.mean2, R.inv2, 0, pump)
    conv.activate(y1, R.mean2, R.inv2, new_vec[3:4, :], new_vec[4:5, :], R.s2, 1, pump)
    gather_low.ready()
    out_att = pltpu.make_async_copy(R.new_low.at[pl.ds(7 * C, 4 * C)], R.new_att, R.ksem.at[0])
    out_att.start()

    def emit_second(at, total):
        R.hid[at, :] = total + new_vec[5:6, :] + R.x[at, :].astype(F32)

    conv.convolve(R.s2, across(R.new_top, R.new_low), emit_second)
    conv.statistics(R.hid, R.mean2, R.inv2, 1)
    upper.block_arrived(R.sum_top, R.totals.at[0], R.asend.at[0], R.arecv.at[0])
    adam(upper, R.totals.at[0])
    conv.normalise(R.hid, R.mean2, R.inv2, new_vec[6:7, :], new_vec[7:8, :], R.u)
    for engine in (gather_low, gather_top, reducer):
        engine.finish()
    for cp in back.sent + conv.sent + vector_sends:
        cp.wait_send()
    for k in range(g.phases):
        trade(k).wait_send()
    for i, group in enumerate((upper, lower)):
        group.to_owner((R.sum_top, R.sum_low)[i], R.totals.at[i], R.asend.at[i], R.arecv.at[i], False)
    lower.to_pieces(R.fresh, R.pieces.at[1], R.tsend.at[1], R.trecv.at[1], False)
    out_att.wait()


def renew_call(columns, n, dims, grad, dh, x, mean1, inv1, pick, spread, div, cnt, masks, vec, top, g_top, sum_low,
               dvec, dvec_att, w, m, v, shares, vw, vm, vs):
    canvases, rows, width = dims
    px = canvases * rows * width
    cells = px // UNIT
    stats = canvases * CROPS
    block = w.shape
    half = block[0] // 2
    seats, phases = n // 2, columns.bit_length() - 1
    dma = pltpu.SemaphoreType.DMA
    tall = (canvases, rows + 2, width, 3 * C)
    arrays = dict(grad=grad, x=x, mean1=mean1, inv1=inv1, pick=pick, spread=spread, div=div, cnt=cnt, vec=vec,
                  sum_low=sum_low, dvec=dvec, dvec_att=dvec_att, vw=vw, vm=vm, vs=vs)
    inputs = dict(top=(top, anyw), g_in=(g_top, anyw), w=(w, anyw), m=(m, anyw), v=(v, anyw), shares=(shares, anyw), dh=(dh, anyw),
                  **{k: (a, vmem) for k, a in arrays.items()},
                  **{k: (a, vmem) for k, a in zip(("col_l", "col_r", "row_u", "row_d"), masks)})
    outputs = dict(igrad=((px, C), F32, vmem), new_w=(block, F32, vmem), new_m=(block, F32, vmem),
                   new_s=(block, F32, vmem), new_vw=(vw.shape, F32, vmem), new_vm=(vw.shape, F32, vmem),
                   new_vs=(vw.shape, F32, vmem), new_vec=((16, C), F32, vmem), hid=((px, C), F32, vmem),
                   u=((px, C), B16, vmem), new_att=((4 * C, C), B16, anyw))
    scratch = dict(
        g_top=pltpu.VMEM((11 * C, C), B16), sum_top=pltpu.VMEM((half, C), B16), totals=pltpu.VMEM((2,) + block, B16),
        new_top=pltpu.VMEM((11 * C, C), B16), new_low=pltpu.VMEM((11 * C, C), B16),
        fresh=pltpu.VMEM(block, B16), pieces=pltpu.VMEM((2, half, C), B16), k=pltpu.VMEM((9 * C, C), B16),
        d3=pltpu.VMEM(tall, B16), s2=pltpu.VMEM(tall, B16), part=pltpu.VMEM((px, C), F32),
        norm=pltpu.VMEM((px, C), F32), mean2=pltpu.VMEM((cells, C), F32), inv2=pltpu.VMEM((cells, C), F32),
        halo=pltpu.VMEM((1, 2, canvases, width, C), B16), chalo=pltpu.VMEM((2, 2, canvases, width, C), B16),
        buf=pltpu.VMEM((1, n, stats, LANES), F32), cbuf=pltpu.VMEM((2, n, stats, LANES), F32),
        tmp_a=pltpu.VMEM((cells, C), F32), tmp_b=pltpu.VMEM((cells, C), F32),
        vbuf=pltpu.VMEM((n, 16, C), F32), vtrade=pltpu.VMEM((phases + 1, 2, 16, C), F32),
        reduce=reduce_pieces_scratch(columns, n, half), gather0=gather_pieces_scratch(columns, n),
        gather1=gather_pieces_scratch(columns, n),
        piece_in=pltpu.VMEM((3, half, C), F32), psem=dma((3,)), ksem=dma((6,)), asend=dma((2, 1)), arecv=dma((2, 2)),
        tsend=dma((2, 2)), trecv=dma((2, 1)), vsend=dma((n,)), vrecv=dma((n,)), qsend=dma((phases,)),
        qrecv=dma((phases,)), send=dma((1, n)), recv=dma((1, n)), hsend=dma((1, 2)), hrecv=dma((1, 2)),
        csend=dma((2, n)), crecv=dma((2, n)), chsend=dma((2, 2)), chrecv=dma((2, 2)))
    return named_call(functools.partial(renew_kernel, columns, n, dims), "renew", 9, inputs, outputs, scratch)


def attend_kernel(n, keep, R):
    me = lax.axis_index("height")
    half = n // 2
    mine = me // half
    base = mine * half
    core = lax.rem(me, 2)
    partner = lax.rem(me + half, n)
    sibling = other_core(me)
    mates = half // 2
    seat = (me - base) // 2
    seg = R.u.shape[1]
    total = n * seg
    scale = C ** (-0.5)
    nt = (((1,), (1,)), ((), ()))
    tn = (((0,), (0,)), ((), ()))
    vec = R.vec

    def mate(j, c=core):
        return base + c + 2 * lax.rem(seat + j, mates)

    def far_of(b):
        return lax.rem(b + half, n)

    def to(h):
        return {"canvas": lax.axis_index("canvas"), "height": h}

    loads = [pltpu.make_async_copy(R.low.at[pl.ds(R.low.shape[0] - 4 * C, 4 * C)], R.w, R.lsem.at[0])]
    if keep:
        loads.append(pltpu.make_async_copy(R.cot.at[mine], R.dz.at[pl.ds(0, seg)], R.lsem.at[1]))
    for cp in loads:
        cp.start()
    own = pltpu.make_async_copy(R.u_in.at[mine], R.u.at[me], R.lsem.at[3])
    own.start()
    barrier = pltpu.get_barrier_semaphore()
    peers = [to(p) for p in [partner, sibling] + [mate(j) for j in range(1, mates)]]
    column = lax.axis_index("canvas")
    if keep:
        peers += [{"canvas": lax.rem(column + d, 4), "height": me} for d in range(1, 4)]
    for p in peers:
        pl.semaphore_signal(barrier, inc=1, device_id=p, device_id_type=MESH)
    pl.semaphore_wait(barrier, len(peers))
    started = []

    def share(from_column, half_number, to_column, begin):
        rows = R.shares.shape[1]
        for i, src in enumerate((R.params, R.first, R.second)):
            cp = remote(src.at[pl.ds(half_number * rows, rows)], R.shares.at[i], R.wsend.at[half_number, i],
                        R.wrecv.at[i], {"canvas": to_column, "height": me})
            if begin:
                pl.when(column == from_column)(cp.start)
            else:
                pl.when(column == from_column)(cp.wait_send)
                pl.when(column == to_column)(cp.wait_recv)

    moves = ((0, 1, 1), (1, 0, 2), (1, 1, 3))
    if keep:
        for move in moves:
            share(*move, True)

    def push(src, slot, dest):
        cp = remote(src, R.u.at[slot], R.gsend.at[len(started)], R.grecv.at[slot], to(dest))
        cp.start()
        started.append(cp)

    def block(b):
        return pl.ds(pl.multiple_of(b * seg, seg), seg)

    def project(b):
        piece = R.u[b]
        R.k[block(b), :] = jnp.dot(piece, R.w[C : 2 * C, :], preferred_element_type=F32).astype(B16)
        R.v[block(b), :] = (
            jnp.dot(piece, R.w[2 * C : 3 * C, :], preferred_element_type=F32) + vec[9:10, :]
        ).astype(B16)

    def arrived(slot):
        remote(R.u_in.at[0], R.u.at[slot], R.gsend.at[0], R.grecv.at[slot], to(partner)).wait_recv()

    push(R.u_in.at[1 - mine], me, partner)
    for j in range(1, mates):
        push(R.u_in.at[mine], me, mate(j))
    push(R.u_in.at[mine], me, sibling)
    for cp in loads:
        cp.wait()
    own.wait()
    project(me)
    arrived(sibling)
    project(sibling)
    key_ids = jnp.concatenate([R.ids_all[b, pl.ds(mine, 1), :] for b in range(n)], axis=1)
    order = (me, partner) if keep else (partner, me)
    first_far = 1 if keep else 0
    far_rows, own_rows = pl.ds(first_far * seg, seg), pl.ds((1 - first_far) * seg, seg)
    for i, b in enumerate(order):
        turned = jnp.transpose(R.ids_all[b])
        picked = jnp.where(mine == 0, turned[:, 0:1], turned[:, 1:2])
        R.qid[i * seg : (i + 1) * seg, :] = jnp.broadcast_to(picked, (seg, LANES))
    arrived(partner)
    for j in range(1, mates):
        push(R.u.at[partner], partner, mate(j))
    push(R.u.at[partner], partner, sibling)
    project(partner)
    for j in range(1, mates):
        friend = mate(mates - j)
        arrived(friend)
        push(R.u.at[friend], friend, sibling)
        project(friend)
    arrived(far_of(sibling))
    project(far_of(sibling))
    for j in range(1, mates):
        friend = far_of(mate(mates - j))
        arrived(friend)
        push(R.u.at[friend], friend, sibling)
        project(friend)
    for j in range(1, mates):
        friend = mate(mates - j, 1 - core)
        arrived(friend)
        project(friend)
        arrived(far_of(friend))
        project(far_of(friend))

    rows = R.rows
    per = seg // rows

    def swap_cot(i):
        here = pl.ds(pl.multiple_of(i * rows, rows), rows)
        there = pl.ds(pl.multiple_of(seg + i * rows, rows), rows)
        return remote(R.cot.at[1 - mine, here], R.dz.at[there], R.csend.at[i], R.crecv.at[i], to(partner))

    if keep:
        for i in range(per):
            swap_cot(i).start()
    o_home = R.o_home

    def far_out(i):
        here = pl.ds(pl.multiple_of(i * rows, rows), rows)
        return remote(R.out.at[here], o_home.at[mine, here], R.osend.at[i], R.orecv.at[i], to(partner))

    def attend(i, _):
        at = pl.ds(pl.multiple_of(i * rows, rows), rows)
        b = jnp.where(i < per, order[0], order[1])
        if keep:
            @pl.when(i >= per)
            def _():
                swap_cot(i - per).wait_recv()

        uq = R.u[b, pl.ds(pl.multiple_of(lax.rem(i, per) * rows, rows), rows), :]
        qb = (jnp.dot(uq, R.w[0:C, :], preferred_element_type=F32) + vec[8:9, :]).astype(B16)
        s = lax.dot_general(qb, R.k[...], nt, preferred_element_type=F32) * scale
        s = jnp.where(R.qid[at, :][:, :1] == key_ids, s, mask_fill)
        e = jnp.exp(s - jnp.max(s, axis=1, keepdims=True))
        p = e * (1.0 / jnp.sum(e, axis=1, keepdims=True))
        pb = p.astype(B16)
        R.out[at, :] = jnp.dot(pb, R.v[...], preferred_element_type=F32).astype(B16)
        if keep:
            R.pbuf[at, :] = pb
            R.q[at, :] = qb
            dout = lax.dot_general(
                R.dz[at, :], R.w[3 * C : 4 * C, :], nt, preferred_element_type=F32).astype(B16)
            R.dout[at, :] = dout
            dp = lax.dot_general(dout, R.v[...], nt, preferred_element_type=F32)
            delta = jnp.sum(p * dp, axis=1, keepdims=True)
            ds = (p * (dp - delta)).astype(B16)
            R.sbuf[at, :] = ds
            R.dq[at, :] = (jnp.dot(ds, R.k[...], preferred_element_type=F32) * scale).astype(B16)

        if not keep:
            @pl.when(i < per)
            def _():
                far_out(i).start()

        return 0

    lax.fori_loop(0, 2 * per, attend, 0)
    if not keep:
        own_out = pltpu.make_async_copy(R.out.at[own_rows], o_home.at[mine], R.lsem.at[2])
        own_out.start()
        own_out.wait()
        for i in range(per):
            far_out(i).wait()
        for cp in started:
            cp.wait_send()
        return
    all_out = pltpu.make_async_copy(R.out, o_home, R.lsem.at[2])
    all_out.start()
    zero = jnp.zeros((C, C), F32)
    pairs = 2 * mates

    def du_of(b, carry):
        dwk, dwv, dbv = carry
        at = block(b)
        dk = (lax.dot_general(R.sbuf[:, at], R.q[...], tn, preferred_element_type=F32) * scale).astype(B16)
        dvf = lax.dot_general(R.pbuf[:, at], R.dout[...], tn, preferred_element_type=F32)
        dv = dvf.astype(B16)
        du = lax.dot_general(dk, R.w[C : 2 * C, :], nt, preferred_element_type=F32)
        du = du + lax.dot_general(dv, R.w[2 * C : 3 * C, :], nt, preferred_element_type=F32)
        piece = R.u[b]
        dwk = dwk + lax.dot_general(piece, dk, tn, preferred_element_type=F32)
        dwv = dwv + lax.dot_general(piece, dv, tn, preferred_element_type=F32)
        return du, (dwk, dwv, dbv + jnp.sum(dvf, axis=0, keepdims=True))

    def place(t):
        far = 1 - t // mates
        return lax.rem(lax.rem(t, mates) + 1, mates), far

    def sib_copy(t):
        return remote(R.for_sib.at[t], R.from_sib.at[t], R.ssend.at[t], R.srecv.at[t], to(sibling))

    def mate_copy(t, part):
        j, _ = place(t)
        here = pl.ds(part * (seg // 2), seg // 2)
        return remote(R.sums.at[t, here], R.from_mate.at[t, here], R.msend.at[t, part], R.mrecv.at[t, part],
                      to(mate(j)))

    def home_copy(part):
        here = pl.ds(part * (seg // 2), seg // 2)
        return remote(R.for_home.at[here], R.from_partner.at[here], R.hsend.at[part], R.hrecv.at[part], to(partner))

    def gathered(far, part):
        count = seg // 2
        at = pl.ds((first_far if far else 1 - first_far) * seg + part * count, count)
        here = pl.ds(part * count, count)
        value = lax.dot_general(R.dq[at, :], R.w[0:C, :], nt, preferred_element_type=F32)
        first_t = 0 if far else mates
        value = value + R.sums[first_t + mates - 1, here, :].astype(F32)
        for t in range(first_t, first_t + mates - 1):
            mate_copy(t, part).wait_recv()
            value = value + R.from_mate[t, here, :].astype(F32)
        return value

    def send_home(part):
        R.for_home[pl.ds(part * (seg // 2), seg // 2), :] = gathered(1, part).astype(B16)
        home_copy(part).start()

    def back(t, carry):
        j, far = place(t)
        theirs, ours = mate(j, 1 - core), mate(j)
        du, carry = du_of(lax.rem(theirs + far * half, n), carry)
        R.for_sib[t] = du.astype(B16)
        sib_copy(t).start()
        du, carry = du_of(lax.rem(ours + far * half, n), carry)
        sib_copy(t).wait_recv()
        R.sums[t] = (du + R.from_sib[t].astype(F32)).astype(B16)

        @pl.when(j != 0)
        def _():
            for part in range(2):
                mate_copy(t, part).start()

        @pl.when(t == pairs - 2)
        def _():
            send_home(0)

        return carry

    dwk, dwv, dbv = lax.fori_loop(0, pairs, back, (zero, zero, jnp.zeros((1, C), F32)))
    send_home(1)
    for part in range(2):
        R.du[mine, pl.ds(part * (seg // 2), seg // 2), :] = gathered(0, part)
    R.dw[C : 2 * C, :] = dwk.astype(B16)
    R.dw[2 * C : 3 * C, :] = dwv.astype(B16)
    R.dw[3 * C : 4 * C, :] = lax.dot_general(
        R.out[...], R.dz[...], tn, preferred_element_type=F32).astype(B16)
    dwq = lax.dot_general(R.u[partner], R.dq[far_rows, :], tn, preferred_element_type=F32)
    dwq = dwq + lax.dot_general(R.u[me], R.dq[own_rows, :], tn, preferred_element_type=F32)
    R.dw[0:C, :] = dwq.astype(B16)
    R.dvec[...] = jnp.concatenate(
        [
            jnp.sum(R.dq[...].astype(F32), axis=0, keepdims=True),
            dbv,
            jnp.sum(R.dz[...].astype(F32), axis=0, keepdims=True),
            jnp.zeros((5, C), F32),
        ],
        axis=0,
    )
    for part in range(2):
        home_copy(part).wait()
    R.du[1 - mine] = R.from_partner[...].astype(F32)
    for move in moves:
        share(*move, False)
    all_out.wait()
    for i in range(per):
        swap_cot(i).wait_send()
    for cp in started:
        cp.wait_send()

    def drain(t, _):
        sib_copy(t).wait_send()

        @pl.when(place(t)[0] != 0)
        def _():
            for part in range(2):
                mate_copy(t, part).wait_send()

        return 0

    lax.fori_loop(0, pairs, drain, 0)


def attend_call(n, keep, cid, u, ids_all, vec, low, cot=None, state=None):
    seg = u.shape[1]
    half = n // 2
    mates = half // 2
    pairs = 2 * mates
    total = n * seg
    rows = min(256, seg)
    dma = pltpu.SemaphoreType.DMA
    inputs = dict(u_in=(u, anyw), ids_all=(ids_all, vmem), vec=(vec, vmem), low=(low, anyw))
    piece = (seg, C)
    home = (2,) + piece
    scratch = dict(
        u=pltpu.VMEM((n,) + piece, B16), w=pltpu.VMEM((4 * C, C), B16), k=pltpu.VMEM((total, C), B16),
        v=pltpu.VMEM((total, C), B16), qid=pltpu.VMEM((2 * seg, LANES), F32), out=pltpu.VMEM((2 * seg, C), B16),
        lsem=dma((4,)), gsend=dma((4 * mates,)), grecv=dma((n,)))
    if keep:
        inputs.update(cot=(cot, anyw), **{k: (a, anyw) for k, a in zip(("params", "first", "second"), state)})
        outputs = dict(o_home=((2 * seg, C), B16, anyw), dw=((4 * C, C), B16, vmem), dvec=((8, C), F32, vmem),
                       du=(home, F32, vmem), shares=((3, state[0].shape[0] // 2, C), F32, anyw))
        scratch.update(
            csend=dma((seg // rows,)), crecv=dma((seg // rows,)), dz=pltpu.VMEM((2 * seg, C), B16), dout=pltpu.VMEM((2 * seg, C), B16), q=pltpu.VMEM((2 * seg, C), B16),
            dq=pltpu.VMEM((2 * seg, C), B16), pbuf=pltpu.VMEM((2 * seg, total), B16),
            sbuf=pltpu.VMEM((2 * seg, total), B16), for_sib=pltpu.VMEM((pairs,) + piece, B16),
            from_sib=pltpu.VMEM((pairs,) + piece, B16), sums=pltpu.VMEM((pairs,) + piece, B16),
            from_mate=pltpu.VMEM((pairs - 1,) + piece, B16), for_home=pltpu.VMEM(piece, B16),
            from_partner=pltpu.VMEM(piece, B16), ssend=dma((pairs,)), srecv=dma((pairs,)), msend=dma((pairs, 2)),
            mrecv=dma((pairs, 2)), hsend=dma((2,)), hrecv=dma((2,)), wsend=dma((2, 3)), wrecv=dma((3,)))
    else:
        outputs = dict(o_home=(home, B16, anyw))
        scratch.update(osend=dma((seg // rows,)), orecv=dma((seg // rows,)))

    def kernel(R):
        R.rows = rows
        attend_kernel(n, keep, R)

    return named_call(kernel, "attend" if keep else "attend_again", cid, inputs, outputs, scratch)


def outputs_kernel(n, R):
    mine = lax.axis_index("height") // (n // 2)
    seg = R.o_back.shape[0]
    own, other = (pl.ds(pl.multiple_of(i * seg, seg), seg) for i in (mine, 1 - mine))
    loads = [
        pltpu.make_async_copy(R.low.at[pl.ds(R.low.shape[0] - C, C)], R.w.at[0], R.sem.at[0]),
        pltpu.make_async_copy(R.new_low.at[pl.ds(R.new_low.shape[0] - C, C)], R.w.at[1], R.sem.at[1]),
        pltpu.make_async_copy(R.hid, R.hid_in, R.sem.at[2]),
        pltpu.make_async_copy(R.hid2, R.hid2_in, R.sem.at[3]),
        pltpu.make_async_copy(R.o.at[pl.ds(0, seg)], R.o_in.at[0, own], R.sem.at[4]),
        pltpu.make_async_copy(R.o_back, R.o_in.at[0, other], R.sem.at[5]),
        pltpu.make_async_copy(R.o2, R.o_in.at[1], R.sem.at[6]),
        pltpu.make_async_copy(R.igrad, R.igrad_in, R.sem.at[7]),
    ]
    for cp in loads:
        cp.start()
    for cp in loads:
        cp.wait()
    backs = [
        pltpu.make_async_copy(R.hid_in, R.hid_out, R.sem.at[2]),
        pltpu.make_async_copy(R.igrad_in, R.igrad_out, R.sem.at[7]),
    ]
    for cp in backs:
        cp.start()
    count = R.part.shape[1]
    parts = R.hid.shape[0] // count
    last = {}
    for i in range(2 * parts):
        which, at = i // parts, pl.ds((i % parts) * count, count)
        base = (R.hid_in, R.hid2_in)[which]
        vec = (R.vec, R.new_vec)[which]
        slot = i % 2
        if slot in last:
            last[slot].wait()
        R.part[slot] = (
            base[at, :] + jnp.dot(R.o_in[which, at, :], R.w[which], preferred_element_type=F32) + vec[10:11, :])
        cp = pltpu.make_async_copy(R.part.at[slot], (R.first, R.second)[which].at[at], R.sem.at[8 + slot])
        cp.start()
        last[slot] = cp
    for cp in backs + list(last.values()):
        cp.wait()


def outputs_call(n, hid, hid2, o, o_back, o2, igrad, vec, new_vec, low, new_low):
    px = hid.shape[0]
    inputs = dict(hid=(hid, anyw), hid2=(hid2, anyw), o=(o, anyw), o_back=(o_back, anyw), o2=(o2, anyw),
                  igrad=(igrad, anyw),
                  vec=(vec, vmem), new_vec=(new_vec, vmem), low=(low, anyw), new_low=(new_low, anyw))
    whole = ((px, C), F32, anyw)
    outputs = dict(hid_out=whole, first=whole, second=whole, igrad_out=whole)
    scratch = dict(
        w=pltpu.VMEM((2, C, C), B16), hid_in=pltpu.VMEM((px, C), F32), hid2_in=pltpu.VMEM((px, C), F32),
        igrad_in=pltpu.VMEM((px, C), F32), o_in=pltpu.VMEM((2, px, C), B16), part=pltpu.VMEM((2, min(256, px), C), F32),
        sem=pltpu.SemaphoreType.DMA((10,)))
    return named_call(functools.partial(outputs_kernel, n), "outputs", None, inputs, outputs, scratch)


def rounded_vectors(vectors):
    return lax.reduce_precision(vectors, exponent_bits=8, mantissa_bits=7)


def body(columns, n, latents, crop_ids, params, vectors, first_moment, second_moment, vector_first, vector_second,
         cotangent):
    canvases, rows, width, channels = latents.shape
    dims = (canvases, rows, width)
    px = canvases * rows * width
    plane = rows * width
    half = n // 2
    me = lax.axis_index("height")
    mine = me // half
    partner = lax.rem(me + half, n)
    swap = [(i, (i + half) % n) for i in range(n)]
    count = vectors.shape[0]
    joined = columns == 4 and params.shape[0] % 32 == 0 and rows > 2

    ids = crop_ids.astype(F32)
    ids_lane = jnp.pad(ids.reshape(canvases, plane), ((0, 8 - canvases), (0, 0)))
    x = latents.reshape(px, channels)
    cot = cotangent.reshape(px, channels)
    cot3 = cotangent.reshape(canvases, plane, channels)
    shape = latents.shape
    if joined:
        first = first_call(columns, n, dims, x, ids_lane, vectors, params)
        ids_all, mean1, inv1, div, cnt, pick, spread, vec = (
            first[k] for k in ("ids_all", "mean1", "inv1", "div", "cnt", "pick", "spread", "vec"))
        masks = [first[k] for k in ("col_l", "col_r", "row_u", "row_d")]
        hid, u, y1, s1, s2 = (first[k] for k in ("hid", "u", "y1_out", "s1_out", "s2_out"))
        norms = [first[k] for k in ("mean2", "inv2", "mean3", "inv3")]
        top, low = first["top"], first["bottom"]
        att = attend_call(n, True, 4, u.reshape(canvases, plane, channels), ids_all, vec, low, cot3,
                          (params, first_moment, second_moment))
        du = att["du"].reshape(px, channels)
        back = back_call(columns, n, dims, cot, du, hid, y1, norms, s1, s2, pick, spread, div, masks, vec, top, low,
                         att["dw"], att["o_home"], params.shape[0])
        new = renew_call(columns, n, dims, back["grad"], back["dh"], x, mean1, inv1, pick, spread, div, cnt, masks, vec,
                         top, back["g_top"], back["sum_low"], back["dvec"], att["dvec"], params, first_moment,
                         second_moment, att["shares"], vectors, vector_first, vector_second)
        new_vec, new_att = new["new_vec"], new["new_att"]
        o2 = attend_call(n, False, 5, new["u"].reshape(canvases, plane, channels), ids_all, new_vec, new_att)["o_home"]
        last = outputs_call(n, hid, new["hid"], att["o_home"], back["o_back"], o2.reshape(px, channels), new["igrad"],
                            vec, new_vec, low, new_att)
        return (
            *(last[k].reshape(shape) for k in ("hid_out", "first", "second", "igrad_out")),
            *(new[k] for k in ("new_w", "new_m", "new_s", "new_vw", "new_vm", "new_vs")),
        )

    def padded(value):
        return jnp.pad(value, ((0, 16 - count), (0, 0)))

    wide_vectors = padded(vectors)
    vec = rounded_vectors(wide_vectors)
    cell_ids = crop_ids[:, :, ::UNIT] + CROPS * jnp.arange(canvases, dtype=jnp.int32)[:, None, None]
    cell_ids = cell_ids.reshape(1, -1)
    stat = jnp.arange(canvases * CROPS, dtype=jnp.int32)[:, None]
    pick = (cell_ids == stat).astype(B16)
    spread = (cell_ids.reshape(-1, 1) == stat.reshape(1, -1)).astype(B16)
    ids_px = jnp.broadcast_to(ids[..., None], (canvases, rows, width, LANES))
    whole = spread_call(columns, n, 8, params).reshape(-1, channels)
    top, low = whole[: 11 * C], whole[11 * C :]
    ids_all, mean1, inv1, div, cnt, *masks = layout_call(n, dims, x, pick, spread, ids_px, ids_lane)
    hid, u, y1, s1, s2, mean2, inv2, mean3, inv3 = resnet_forward_call(
        n, dims, True, x, pick, spread, cnt, mean1, inv1, masks, vec, top, low)
    own_cot = lax.dynamic_index_in_dim(cot3, mine, axis=0, keepdims=False)
    far_cot = lax.ppermute(
        lax.dynamic_index_in_dim(cot3, 1 - mine, axis=0, keepdims=False), "height", swap)
    dz = jnp.concatenate([own_cot, far_cot], axis=0)
    canvas_ids = lax.dynamic_index_in_dim(ids_all, mine, axis=1, keepdims=False)
    key_ids = canvas_ids.reshape(1, n * plane)
    query_ids = jnp.stack([canvas_ids[me], canvas_ids[partner]]).reshape(2 * plane, 1)
    query_ids = jnp.broadcast_to(query_ids, (2 * plane, LANES))
    offsets = jnp.stack([me, partner]) * plane

    def attention_output(o, hid, low, bias):
        back = lax.ppermute(o[plane:], "height", swap)
        ordered = jnp.where(mine == 0, jnp.stack([o[:plane], back]), jnp.stack([back, o[:plane]]))
        product = jnp.dot(ordered.reshape(px, channels), low[10 * C :], preferred_element_type=F32)
        return hid + product + bias

    ua = gather_call(n, 4, u.reshape(canvases, plane, channels))
    o, dup, dw_att, dvec_att = attention_call(True, ua, key_ids, query_ids, offsets, dz, vec, low)
    first_output = attention_output(o, hid, low, vec[10])
    du = scatter_call(n, 6, dup.reshape(n, plane, channels)).reshape(px, channels)
    norms = (mean1, inv1, mean2, inv2, mean3, inv3)
    input_grad, matrix_grad, dvec = resnet_backward_call(
        n, dims, 7, cot, du, hid, y1, x, norms, s1, s2, pick, spread, div, masks, vec, top, low, dw_att)
    vector_grad = jnp.concatenate([dvec, dvec_att], axis=0)
    new_params, new_first, new_second, *new_small, new_whole = step_call(
        columns, n, 9, matrix_grad.reshape((columns, half, 2) + params.shape), params, first_moment,
        second_moment, vector_grad, wide_vectors, padded(vector_first), padded(vector_second))
    new_whole = new_whole.reshape(-1, channels)
    new_top, new_low = new_whole[: 11 * C], new_whole[11 * C :]
    new_vec = rounded_vectors(new_small[0])
    hid2, u2 = resnet_forward_call(
        n, dims, False, x, pick, spread, cnt, mean1, inv1, masks, new_vec, new_top, new_low)
    ua2 = gather_call(n, 5, u2.reshape(canvases, plane, channels))
    (o2,) = attention_call(False, ua2, key_ids, query_ids, offsets, dz, new_vec, new_low)
    second_output = attention_output(o2, hid2, new_low, new_vec[10])
    return (
        *(a.reshape(shape) for a in (hid, first_output, second_output, input_grad)),
        new_params,
        new_first,
        new_second,
        *(a[:count] for a in new_small),
    )


def solution(mesh):
    spatial = P("canvas", "height", None, None)
    owned = P(("canvas", "height"), None)
    return jax.shard_map(
        functools.partial(body, mesh.shape["canvas"], mesh.shape["height"]),
        mesh=mesh,
        in_specs=(spatial, P("canvas", "height", None), owned, P(), owned, owned, P(), P(), spatial),
        out_specs=(spatial, spatial, spatial, spatial, owned, owned, owned, P(), P(), P()),
        check_vma=False,
    )
```

```python
import functools

import jax
import jax.numpy as jnp
from jax import lax
from jax.experimental import pallas as pl
from jax.experimental.pallas import tpu as pltpu
from jax.sharding import PartitionSpec as P

C = 512
GROUPS = 32
STEP = 5
CROPS = 16
SPAN = C // GROUPS
LANES = 128
TILES = C // LANES
UNIT = 8

norm_epsilon = 1e-06
adam_epsilon = 1e-08
matrix_rate = 0.015
vector_rate = 0.2
mask_fill = -1e30

HEIGHT = "height"
CANVAS = "canvas"
LOAD = "load"
STORE = "store"

F32 = jnp.float32
B16 = jnp.bfloat16
MESH = pl.DeviceIdType.MESH
VMEM_LIMIT = 60 * 2**20

vmem = pl.BlockSpec(memory_space=pltpu.VMEM)
smem = pl.BlockSpec(memory_space=pltpu.SMEM)
anyw = pl.BlockSpec(memory_space=pl.ANY)


def params_of(cid=None):
    if cid is None:
        return pltpu.CompilerParams(vmem_limit_bytes=VMEM_LIMIT)
    return pltpu.CompilerParams(
        vmem_limit_bytes=VMEM_LIMIT, collective_id=cid, has_side_effects=True
    )


def sds(shape, dtype):
    return jax.ShapeDtypeStruct(shape, dtype)


def split_dot(pick, value):
    total = None
    rest = value
    for _ in range(3):
        part = rest.astype(B16)
        term = jnp.dot(pick, part, preferred_element_type=F32)
        total = term if total is None else total + term
        rest = rest - part.astype(F32)
    return total


def lane_group_sum(piece):
    lane = lax.broadcasted_iota(jnp.int32, piece.shape, 1)
    step = 1
    while step < SPAN:
        ahead = pltpu.roll(piece, LANES - step, 1)
        behind = pltpu.roll(piece, step, 1)
        piece = piece + jnp.where((lane & step) == 0, ahead, behind)
        step *= 2
    return piece


def tiles_of(value):
    return [value[:, j * LANES : (j + 1) * LANES] for j in range(TILES)]


def wide(piece, times=TILES):
    return jnp.concatenate([piece] * times, axis=1)


def pack(quantities):
    shape = quantities[0][0].shape
    sub = lax.broadcasted_iota(jnp.int32, shape, 1) & (SPAN - 1)
    out = jnp.zeros(shape, F32)
    for q, pieces in enumerate(quantities):
        for j, piece in enumerate(pieces):
            out = jnp.where(sub == TILES * q + j, piece, out)
    return out


def unpack(packed):
    sub = lax.broadcasted_iota(jnp.int32, packed.shape, 1) & (SPAN - 1)
    return jnp.concatenate(
        [lane_group_sum(jnp.where(sub == j, packed, 0.0)) for j in range(TILES)], axis=1
    )


def shift_down(packed, q):
    return pltpu.roll(packed, LANES - TILES * q, packed.ndim - 1)


def no_pump():
    return None


def fold(packed):
    rows = packed.shape[0] // 2
    sub = lax.broadcasted_iota(jnp.int32, (rows, LANES), 1) & (SPAN - 1)
    return jnp.where(sub < 2 * TILES, packed[:rows], pltpu.roll(packed[rows:], 2 * TILES, 1))


def unfold(folded):
    return jnp.concatenate([folded, pltpu.roll(folded, LANES - 2 * TILES, folded.ndim - 1)], axis=folded.ndim - 2)


def greet(n):
    me = lax.axis_index(HEIGHT)
    barrier = pltpu.get_barrier_semaphore()
    for d in range(1, n):
        pl.semaphore_signal(
            barrier, inc=1, device_id={HEIGHT: lax.rem(me + d, n)}, device_id_type=MESH
        )
    pl.semaphore_wait(barrier, n - 1)


def spread_copies(n, buf, send, recv, rnd):
    me = lax.axis_index(HEIGHT)
    return [
        pltpu.make_async_remote_copy(
            src_ref=buf.at[rnd, 0],
            dst_ref=buf.at[rnd, d],
            send_sem=send.at[rnd, d],
            recv_sem=recv.at[rnd, d],
            device_id={HEIGHT: lax.rem(me + d, n)},
            device_id_type=MESH,
        )
        for d in sorted(range(1, n), key=lambda d: abs(d - n // 2))
    ]


def cell_totals(load, out_ref, cells):
    def body(i, _):
        out_ref[pl.ds(i * 16, 16), :] = jnp.sum(load(i).reshape(16, UNIT, C), axis=1)
        return 0

    lax.fori_loop(0, cells // 16, body, 0)


def over_cells(cell_ref, i):
    return jnp.broadcast_to(cell_ref[pl.ds(i * 16, 16), :][:, None, :], (16, UNIT, C)).reshape(
        16 * UNIT, C
    )


def group_totals(pick_ref, cell_value):
    return [lane_group_sum(t) for t in tiles_of(split_dot(pick_ref[...], cell_value))]


def stats_payload(load, pick_ref, spread_ref, count_ref, cells, tmp_a, tmp_b, counted=True):
    cell_totals(load, tmp_a, cells)
    sums = group_totals(pick_ref, tmp_a[...])
    count = count_ref[...]
    inv_count = 1.0 / jnp.maximum(count, 1.0)
    mean = jnp.concatenate([s * inv_count for s in sums], axis=1)
    tmp_b[...] = split_dot(spread_ref[...], mean)

    def centred(i):
        delta = load(i) - over_cells(tmp_b, i)
        return delta * delta

    cell_totals(centred, tmp_a, cells)
    squares = group_totals(pick_ref, tmp_a[...])
    return pack([sums, squares, [count] * TILES]) if counted else fold(pack([sums, squares]))


def combine_stats(gathered, counts=None):
    sums = gathered
    squares = shift_down(gathered, 1)
    counts = shift_down(gathered, 2) if counts is None else counts
    divisor = jnp.maximum(jnp.sum(counts, axis=0), 1.0)
    mean = jnp.sum(sums, axis=0) / divisor
    apart = sums / jnp.maximum(counts, 1.0) - mean[None]
    spread = jnp.sum(squares + counts * apart * apart, axis=0) / divisor
    return mean, lax.rsqrt(spread + norm_epsilon), divisor


def shift_columns(row, left_mask, right_mask):
    width = row.shape[0]
    left = pltpu.roll(row, 1, 0) * wide(left_mask)
    right = pltpu.roll(row, width - 1, 0) * wide(right_mask)
    return jnp.concatenate([left, row, right], axis=1).astype(B16)


def logistic(a):
    return 1.0 / (1.0 + jnp.exp(-a))


def silu(a):
    return a * logistic(a)


def silu_slope(a):
    s = logistic(a)
    return s * (1.0 + a * (1.0 - s))


def layout_kernel(n, dims, x, pick, spread, ids_px, ids_lane, ids_all, mean_c, inv_c, div, cnt,
                  col_l, col_r, row_u, row_d, *scratch):
    greet(n)
    layout_body(n, dims, x, pick, spread, ids_px, ids_lane, ids_all, mean_c, inv_c, div, cnt,
                col_l, col_r, row_u, row_d, *scratch)


def layout_body(n, dims, x, pick, spread, ids_px, ids_lane, ids_all, mean_c, inv_c, div, cnt,
                col_l, col_r, row_u, row_d, buf, idbuf, halo, tmp_a, tmp_b, send, recv, isend, irecv,
                hsend, hrecv, pump=no_pump, cnt_all=None):
    canvases, rows, width = dims
    cells = canvases * rows * width // UNIT
    me = lax.axis_index(HEIGHT)
    id_copies = []
    idbuf[0] = ids_lane[...]
    for d in range(1, n):
        cp = pltpu.make_async_remote_copy(
            src_ref=idbuf.at[0], dst_ref=idbuf.at[d], send_sem=isend.at[d], recv_sem=irecv.at[d],
            device_id={HEIGHT: lax.rem(me + d, n)}, device_id_type=MESH)
        cp.start()
        id_copies.append(cp)
    up, down = halo_copies(n, ids_px.at[:, 0], ids_px.at[:, rows - 1], halo, hsend, hrecv)
    start_halo(n, up, down)

    def load(i):
        return x[pl.ds(i * 16 * UNIT, 16 * UNIT), :].astype(F32)

    ones = jnp.sum(pick[...].astype(F32), axis=1, keepdims=True) * float(UNIT * SPAN)
    cnt[...] = jnp.broadcast_to(ones, cnt.shape)
    buf[0, 0] = stats_payload(load, pick, spread, cnt, cells, tmp_a, tmp_b)
    copies = spread_copies(n, buf, send, recv, 0)
    for cp in copies:
        cp.start()
    pump()
    wait_halo(n, up, down, halo, -1.0)
    column = lax.broadcasted_iota(jnp.int32, (width, LANES), 0)
    first, last = column == 0, column == width - 1
    for v in range(canvases):
        for r in range(rows + 2):
            here = halo[0, v] if r == 0 else halo[1, v] if r == rows + 1 else ids_px[v, r - 1]
            same_l = (pltpu.roll(here, 1, 0) == here) & jnp.logical_not(first)
            same_r = (pltpu.roll(here, width - 1, 0) == here) & jnp.logical_not(last)
            col_l[v, r] = same_l.astype(F32)
            col_r[v, r] = same_r.astype(F32)
            if 1 <= r <= rows:
                above = halo[0, v] if r == 1 else ids_px[v, r - 2]
                below = halo[1, v] if r == rows else ids_px[v, r]
                at = pl.ds((v * rows + r - 1) * width, width)
                row_u[at, :] = (above == here).astype(F32)
                row_d[at, :] = (below == here).astype(F32)
    pump()
    for cp in copies:
        cp.wait_recv()
    mean, inv, divisor = combine_stats(buf[0])
    if cnt_all is not None:
        cnt_all[...] = shift_down(buf[0], 2)
    mean_c[...] = split_dot(spread[...], unpack(mean))
    inv_c[...] = split_dot(spread[...], unpack(inv))
    div[...] = unpack(divisor)[:, :LANES]
    for cp in id_copies:
        cp.wait_recv()
    ids_all[me] = idbuf[0]
    for d in range(1, n):
        ids_all[lax.rem(me - d + n, n)] = idbuf[d]
    for cp in copies + id_copies:
        cp.wait_send()


def halo_copies(n, first_row, last_row, halo, hsend, hrecv):
    me = lax.axis_index(HEIGHT)
    up = pltpu.make_async_remote_copy(
        src_ref=first_row, dst_ref=halo.at[1], send_sem=hsend.at[0], recv_sem=hrecv.at[1],
        device_id={HEIGHT: lax.rem(me + n - 1, n)}, device_id_type=MESH)
    down = pltpu.make_async_remote_copy(
        src_ref=last_row, dst_ref=halo.at[0], send_sem=hsend.at[1], recv_sem=hrecv.at[0],
        device_id={HEIGHT: lax.rem(me + 1, n)}, device_id_type=MESH)
    return up, down


def start_halo(n, up, down):
    me = lax.axis_index(HEIGHT)

    @pl.when(me > 0)
    def _():
        up.start()

    @pl.when(me < n - 1)
    def _():
        down.start()


def wait_halo(n, up, down, halo, edge):
    me = lax.axis_index(HEIGHT)

    @pl.when(me > 0)
    def _():
        up.wait_send()
        down.wait_recv()

    @pl.when(me < n - 1)
    def _():
        down.wait_send()
        up.wait_recv()

    @pl.when(me == 0)
    def _():
        halo[0] = jnp.full(halo.shape[1:], edge, halo.dtype)

    @pl.when(me == n - 1)
    def _():
        halo[1] = jnp.full(halo.shape[1:], edge, halo.dtype)


def layout_scratch(n, dims, ids_lane):
    canvases, rows, width = dims
    cells = canvases * rows * width // UNIT
    return [
        pltpu.VMEM((1, n, canvases * CROPS, LANES), F32),
        pltpu.VMEM((n,) + ids_lane.shape, F32),
        pltpu.VMEM((2, canvases, width, LANES), F32),
        pltpu.VMEM((cells, C), F32),
        pltpu.VMEM((cells, C), F32),
        pltpu.SemaphoreType.DMA((1, n)),
        pltpu.SemaphoreType.DMA((1, n)),
        pltpu.SemaphoreType.DMA((n,)),
        pltpu.SemaphoreType.DMA((n,)),
        pltpu.SemaphoreType.DMA((2,)),
        pltpu.SemaphoreType.DMA((2,)),
    ]


def layout_call(n, dims, x, pick, spread, ids_px, ids_lane):
    canvases, rows, width = dims
    px = canvases * rows * width
    cells = px // UNIT
    stats = canvases * CROPS
    return pl.pallas_call(
        functools.partial(layout_kernel, n, dims),
        out_shape=[
            sds((n,) + ids_lane.shape, F32),
            sds((cells, C), F32),
            sds((cells, C), F32),
            sds((stats, LANES), F32),
            sds((stats, LANES), F32),
            sds((canvases, rows + 2, width, LANES), F32),
            sds((canvases, rows + 2, width, LANES), F32),
            sds((px, LANES), F32),
            sds((px, LANES), F32),
        ],
        in_specs=[vmem] * 5,
        out_specs=[vmem] * 9,
        scratch_shapes=layout_scratch(n, dims, ids_lane),
        compiler_params=params_of(1),
        name="layout",
    )(x, pick, spread, ids_px, ids_lane)


def second_matrix(top, low, dest, sem):
    return [
        pltpu.make_async_copy(top.at[pl.ds(9 * C, 2 * C)], dest.at[pl.ds(0, 2 * C)], sem.at[1]),
        pltpu.make_async_copy(low.at[pl.ds(0, 7 * C)], dest.at[pl.ds(2 * C, 7 * C)], sem.at[2]),
    ]


class Convolver:
    def __init__(self, n, dims, x, pick, spread, cnt, col_l, col_r, row_u, row_d, halo, buf, tmp_a, tmp_b, send,
                 recv, hsend, hrecv, cnt_all=None):
        self.n, self.dims, self.cnt_all = n, dims, cnt_all
        self.x, self.pick, self.spread, self.cnt = x, pick, spread, cnt
        self.col_l, self.col_r, self.row_u, self.row_d = col_l, col_r, row_u, row_d
        self.halo, self.buf, self.tmp_a, self.tmp_b = halo, buf, tmp_a, tmp_b
        self.send, self.recv, self.hsend, self.hrecv = send, recv, hsend, hrecv
        self.px = dims[0] * dims[1] * dims[2]
        self.cells = self.px // UNIT
        self.sent = []

    def activate(self, source, mean, inv, gain, bias, dest, rnd, pump=no_pump):
        canvases, rows, width = self.dims
        row_cells = width // UNIT
        col_l, col_r, halo = self.col_l, self.col_r, self.halo

        def one(v, r):
            at = pl.ds(pl.multiple_of((v * rows + r) * width, width), width)
            cell = pl.ds(pl.multiple_of((v * rows + r) * row_cells, row_cells), row_cells)
            value = source[at, :].astype(F32)
            m = jnp.broadcast_to(mean[cell, :][:, None, :], (row_cells, UNIT, C)).reshape(width, C)
            s = jnp.broadcast_to(inv[cell, :][:, None, :], (row_cells, UNIT, C)).reshape(width, C)
            a = (value - m) * s * gain + bias
            dest[v, r + 1] = shift_columns(silu(a), col_l[v, r + 1], col_r[v, r + 1])

        def edges(v, _):
            one(v, 0)
            if rows > 1:
                one(v, rows - 1)
            return 0

        lax.fori_loop(0, canvases, edges, 0)
        mid = pl.ds(C, C)
        up, down = halo_copies(self.n, dest.at[:, 1, :, mid], dest.at[:, rows, :, mid], halo.at[rnd],
                               self.hsend.at[rnd], self.hrecv.at[rnd])
        start_halo(self.n, up, down)
        pump()

        def inner(i, _):
            one(i // (rows - 2), 1 + lax.rem(i, rows - 2))
            return 0

        if rows > 2:
            lax.fori_loop(0, canvases * (rows - 2), inner, 0)
        pump()
        wait_halo(self.n, up, down, halo.at[rnd], 0.0)
        for v in range(canvases):
            for side, r in ((0, 0), (1, rows + 1)):
                dest[v, r] = shift_columns(halo[rnd, side, v].astype(F32), col_l[v, r], col_r[v, r])

    def convolve(self, source, weights, emit, pump=no_pump):
        canvases, rows, width = self.dims
        plane = rows * width
        for v in range(canvases):
            at = pl.ds(v * plane, plane)
            total = None
            for dr in (1, 0, 2):
                part = None
                for lo, hi, ref, row in weights(dr):
                    lhs = source[v, dr : dr + rows, :, lo:hi].reshape(plane, hi - lo)
                    term = jnp.dot(lhs, ref[row : row + hi - lo, :], preferred_element_type=F32)
                    part = term if part is None else part + term
                if dr == 0:
                    part = part * wide(self.row_u[at, :])
                if dr == 2:
                    part = part * wide(self.row_d[at, :])
                total = part if total is None else total + part
            emit(at, total)
            pump()

    def statistics(self, source, mean, inv, rnd, pump=no_pump):
        def load(i):
            return source[pl.ds(i * 16 * UNIT, 16 * UNIT), :]

        counted = self.cnt_all is None
        self.buf[rnd, 0] = stats_payload(
            load, self.pick, self.spread, self.cnt, self.cells, self.tmp_a, self.tmp_b, counted)
        copies = spread_copies(self.n, self.buf, self.send, self.recv, rnd)
        for cp in copies:
            cp.start()
        pump()
        for cp in copies:
            cp.wait_recv()
        m, s, _ = (
            combine_stats(self.buf[rnd]) if counted else combine_stats(unfold(self.buf[rnd]), self.cnt_all[...]))
        mean[...] = split_dot(self.spread[...], unpack(m))
        inv[...] = split_dot(self.spread[...], unpack(s))
        self.sent = self.sent + copies

    def normalise(self, source, mean, inv, gain, bias, dest):
        def last(i, _):
            at = pl.ds(i * 16 * UNIT, 16 * UNIT)
            value = (source[at, :] - over_cells(mean, i)) * over_cells(inv, i)
            dest[at, :] = (value * gain + bias).astype(B16)
            return 0

        lax.fori_loop(0, self.cells // 16, last, 0)


def resnet_forward_kernel(n, dims, keep, x, pick, spread, cnt, mean1, inv1, col_l, col_r, row_u, row_d,
                          vec, top, low, *refs):
    canvases, rows, width = dims
    px = canvases * rows * width
    cells = px // UNIT
    plane = rows * width
    if keep:
        hid, u, y1, s1, s2, mean2, inv2, mean3, inv3 = refs[:9]
        refs = refs[9:]
    else:
        hid, u = refs[:2]
        y1, s1, s2, mean2, inv2, mean3, inv3 = refs[2:9]
        refs = refs[9:]
    k1, k2, halo, buf, tmp_a, tmp_b, ksem, send, recv, hsend, hrecv = refs
    load1 = [pltpu.make_async_copy(top.at[pl.ds(0, 9 * C)], k1, ksem.at[0])]
    load2 = second_matrix(top, low, k2, ksem)
    for cp in load1 + load2:
        cp.start()
    greet(n)
    for_conv = Convolver(n, dims, x, pick, spread, cnt, col_l, col_r, row_u, row_d, halo, buf, tmp_a, tmp_b,
                         send, recv, hsend, hrecv)

    def wait_all(copies):
        for cp in copies:
            cp.wait()

    for_conv.activate(x, mean1, inv1, vec[0:1, :], vec[1:2, :], s1, 0)
    wait_all(load1)

    def emit_first(at, total):
        y1[at, :] = total + vec[2:3, :]

    for_conv.convolve(s1, lambda dr: [(0, 3 * C, k1, 3 * C * dr)], emit_first)
    for_conv.statistics(y1, mean2, inv2, 0)
    for_conv.activate(y1, mean2, inv2, vec[3:4, :], vec[4:5, :], s2, 1)
    wait_all(load2)

    def emit_second(at, total):
        hid[at, :] = total + vec[5:6, :] + x[at, :].astype(F32)

    for_conv.convolve(s2, lambda dr: [(0, 3 * C, k2, 3 * C * dr)], emit_second)
    for_conv.statistics(hid, mean3, inv3, 1)
    for_conv.normalise(hid, mean3, inv3, vec[6:7, :], vec[7:8, :], u)
    for cp in for_conv.sent:
        cp.wait_send()


def resnet_forward_call(n, dims, keep, x, pick, spread, cnt, mean1, inv1, masks, vec, top, low):
    canvases, rows, width = dims
    px = canvases * rows * width
    cells = px // UNIT
    stats = canvases * CROPS
    saved = [
        ((px, C), F32),
        ((canvases, rows + 2, width, 3 * C), B16),
        ((canvases, rows + 2, width, 3 * C), B16),
        ((cells, C), F32),
        ((cells, C), F32),
        ((cells, C), F32),
        ((cells, C), F32),
    ]
    main = [((px, C), F32), ((px, C), B16)]
    outs = main + (saved if keep else [])
    scratch = [] if keep else [pltpu.VMEM(*s) for s in saved]
    return pl.pallas_call(
        functools.partial(resnet_forward_kernel, n, dims, keep),
        out_shape=[sds(*s) for s in outs],
        in_specs=[vmem] * 11 + [anyw] * 2,
        out_specs=[vmem] * len(outs),
        scratch_shapes=scratch
        + [
            pltpu.VMEM((9 * C, C), B16),
            pltpu.VMEM((9 * C, C), B16),
            pltpu.VMEM((2, 2, canvases, width, C), B16),
            pltpu.VMEM((2, n, stats, LANES), F32),
            pltpu.VMEM((cells, C), F32),
            pltpu.VMEM((cells, C), F32),
            pltpu.SemaphoreType.DMA((3,)),
            pltpu.SemaphoreType.DMA((2, n)),
            pltpu.SemaphoreType.DMA((2, n)),
            pltpu.SemaphoreType.DMA((2, 2)),
            pltpu.SemaphoreType.DMA((2, 2)),
        ],
        compiler_params=params_of(2 if keep else 3),
        name="resnet_forward" if keep else "resnet_again",
    )(x, pick, spread, cnt, mean1, inv1, *masks, vec, top, low)


def attention_kernel(keep, chunk, block, ua, key_ids, query_ids, offsets, dz, vec, low, *refs):
    total = ua.shape[0] * ua.shape[1]
    queries = query_ids.shape[0]
    segment = ua.shape[1]
    scale = C ** (-0.5)
    if keep:
        out, dup, dw, dvec = refs[:4]
        u, w, k, v, pbuf, sbuf, q, dout, dq, usem, wsem = refs[4:]
    else:
        out = refs[0]
        u, w, k, v, usem, wsem = refs[1:]
    load_w = pltpu.make_async_copy(low.at[pl.ds(7 * C, 4 * C)], w, wsem.at[0])
    load_w.start()
    blocks = ua.shape[0]
    loads = [
        pltpu.make_async_copy(ua.at[i], u.at[pl.ds(i * segment, segment)], usem.at[i])
        for i in range(blocks)
    ]
    for cp in loads:
        cp.start()
    load_w.wait()
    for cp in loads:
        cp.wait()
    nt = (((1,), (1,)), ((), ()))
    tn = (((0,), (0,)), ((), ()))

    def project(i, _):
        at = pl.ds(pl.multiple_of(i * chunk, chunk), chunk)
        piece = u[at, :]
        k[at, :] = jnp.dot(piece, w[C : 2 * C, :], preferred_element_type=F32).astype(B16)
        v[at, :] = (
            jnp.dot(piece, w[2 * C : 3 * C, :], preferred_element_type=F32) + vec[9:10, :]
        ).astype(B16)
        return 0

    lax.fori_loop(0, total // chunk, project, 0)
    per = segment // block

    def place(i):
        return pl.multiple_of(offsets[i // per] + lax.rem(i, per) * block, block)

    def attend(i, _):
        at = pl.ds(pl.multiple_of(i * block, block), block)
        uq = u[pl.ds(place(i), block), :]
        qb = (
            jnp.dot(uq, w[0:C, :], preferred_element_type=F32) + vec[8:9, :]
        ).astype(B16)
        s = lax.dot_general(qb, k[...], nt, preferred_element_type=F32) * scale
        s = jnp.where(query_ids[at, :][:, :1] == key_ids[...], s, mask_fill)
        e = jnp.exp(s - jnp.max(s, axis=1, keepdims=True))
        p = e * (1.0 / jnp.sum(e, axis=1, keepdims=True))
        pb = p.astype(B16)
        ob = jnp.dot(pb, v[...], preferred_element_type=F32).astype(B16)
        out[at, :] = ob
        if keep:
            pbuf[at, :] = pb
            q[at, :] = qb
            do = lax.dot_general(
                dz[at, :], w[3 * C : 4 * C, :], nt, preferred_element_type=F32
            ).astype(B16)
            dout[at, :] = do
            dp = lax.dot_general(do, v[...], nt, preferred_element_type=F32)
            delta = jnp.sum(p * dp, axis=1, keepdims=True)
            ds = (p * (dp - delta)).astype(B16)
            sbuf[at, :] = ds
            dq[at, :] = (jnp.dot(ds, k[...], preferred_element_type=F32) * scale).astype(B16)
        return 0

    lax.fori_loop(0, queries // block, attend, 0)
    if not keep:
        return
    zero = jnp.zeros((C, C), F32)

    def back(i, carry):
        dwk, dwv, dbv = carry
        at = pl.ds(pl.multiple_of(i * chunk, chunk), chunk)
        dk = (
            lax.dot_general(sbuf[:, at], q[...], tn, preferred_element_type=F32) * scale
        ).astype(B16)
        dvf = lax.dot_general(pbuf[:, at], dout[...], tn, preferred_element_type=F32)
        dv = dvf.astype(B16)
        du = lax.dot_general(dk, w[C : 2 * C, :], nt, preferred_element_type=F32)
        du = du + lax.dot_general(dv, w[2 * C : 3 * C, :], nt, preferred_element_type=F32)
        dup[at, :] = du.astype(B16)
        piece = u[at, :]
        dwk = dwk + lax.dot_general(piece, dk, tn, preferred_element_type=F32)
        dwv = dwv + lax.dot_general(piece, dv, tn, preferred_element_type=F32)
        return dwk, dwv, dbv + jnp.sum(dvf, axis=0, keepdims=True)

    dwk, dwv, dbv = lax.fori_loop(0, total // chunk, back, (zero, zero, jnp.zeros((1, C), F32)))
    dw[C : 2 * C, :] = dwk.astype(B16)
    dw[2 * C : 3 * C, :] = dwv.astype(B16)
    dw[3 * C : 4 * C, :] = lax.dot_general(
        out[...], dz[...], tn, preferred_element_type=F32
    ).astype(B16)
    dwq = zero
    for s in range(2):
        where = pl.ds(pl.multiple_of(offsets[s], segment), segment)
        at = pl.ds(s * segment, segment)
        dwq = dwq + lax.dot_general(u[where, :], dq[at, :], tn, preferred_element_type=F32)
        du = lax.dot_general(dq[at, :], w[0:C, :], nt, preferred_element_type=F32)
        dup[where, :] = (dup[where, :].astype(F32) + du).astype(B16)
    dw[0:C, :] = dwq.astype(B16)
    dvec[...] = jnp.concatenate(
        [
            jnp.sum(dq[...].astype(F32), axis=0, keepdims=True),
            dbv,
            jnp.sum(dz[...].astype(F32), axis=0, keepdims=True),
            jnp.zeros((5, C), F32),
        ],
        axis=0,
    )


def attention_call(keep, ua, key_ids, query_ids, offsets, dz, vec, low):
    blocks, segment, _ = ua.shape
    total = blocks * segment
    queries = query_ids.shape[0]
    block = min(256, segment)
    chunk = 512
    outs = [sds((queries, C), B16)]
    scratch = [
        pltpu.VMEM((total, C), B16),
        pltpu.VMEM((4 * C, C), B16),
        pltpu.VMEM((total, C), B16),
        pltpu.VMEM((total, C), B16),
    ]
    if keep:
        outs += [sds((total, C), B16), sds((4 * C, C), B16), sds((8, C), F32)]
        scratch += [
            pltpu.VMEM((queries, total), B16),
            pltpu.VMEM((queries, total), B16),
            pltpu.VMEM((queries, C), B16),
            pltpu.VMEM((queries, C), B16),
            pltpu.VMEM((queries, C), B16),
        ]
    return pl.pallas_call(
        functools.partial(attention_kernel, keep, chunk, block),
        out_shape=outs,
        in_specs=[anyw, vmem, vmem, smem, vmem, vmem, anyw],
        out_specs=[vmem] * len(outs),
        scratch_shapes=scratch
        + [pltpu.SemaphoreType.DMA((blocks,)), pltpu.SemaphoreType.DMA((1,))],
        compiler_params=params_of(),
        name="attention" if keep else "attention_again",
    )(ua, key_ids, query_ids, offsets, dz, vec, low)


def other_core(h):
    return h + 1 - 2 * lax.rem(h, 2)


def gather_kernel(n, u, ua, lsem, send, recv):
    me = lax.axis_index(HEIGHT)
    half = n // 2
    mine = me // half
    base = mine * half
    core = lax.rem(me, 2)
    partner = lax.rem(me + half, n)
    sibling = other_core(me)
    mates = half // 2
    seat = (me - base) // 2

    def mate(j):
        return base + core + 2 * lax.rem(seat + j, mates)

    barrier = pltpu.get_barrier_semaphore()
    peers = [partner, sibling] + [mate(j) for j in range(1, mates)]
    for p in peers:
        pl.semaphore_signal(barrier, inc=1, device_id={HEIGHT: p}, device_id_type=MESH)
    pl.semaphore_wait(barrier, len(peers))
    count = [0]
    started = []

    def push(src, slot, to):
        cp = pltpu.make_async_remote_copy(
            src_ref=src, dst_ref=ua.at[slot], send_sem=send.at[count[0]], recv_sem=recv.at[slot],
            device_id={HEIGHT: to}, device_id_type=MESH)
        count[0] += 1
        cp.start()
        started.append(cp)

    def arrived(slot):
        pltpu.make_async_remote_copy(
            src_ref=u.at[0], dst_ref=ua.at[slot], send_sem=send.at[0], recv_sem=recv.at[slot],
            device_id={HEIGHT: partner}, device_id_type=MESH).wait_recv()

    own = pltpu.make_async_copy(u.at[mine], ua.at[me], lsem.at[0])
    own.start()
    push(u.at[1 - mine], me, partner)
    for j in range(1, mates):
        push(u.at[mine], me, mate(j))
    push(u.at[mine], me, sibling)
    arrived(partner)
    for j in range(1, mates):
        push(ua.at[partner], partner, mate(j))
    push(ua.at[partner], partner, sibling)
    for j in range(1, mates):
        friend = base + core + 2 * lax.rem(seat + mates - j, mates)
        far = lax.rem(friend + half, n)
        arrived(friend)
        push(ua.at[friend], friend, sibling)
        arrived(far)
        push(ua.at[far], far, sibling)
    arrived(sibling)
    arrived(lax.rem(sibling + half, n))
    for j in range(1, mates):
        friend = base + (1 - core) + 2 * lax.rem(seat + mates - j, mates)
        arrived(friend)
        arrived(lax.rem(friend + half, n))
    own.wait()
    for cp in started:
        cp.wait_send()


def gather_call(n, cid, u):
    half = n // 2
    sends = 2 * (half // 2) + 1 + 2 * (half // 2 - 1) + 1
    return pl.pallas_call(
        functools.partial(gather_kernel, n),
        out_shape=sds((n,) + u.shape[1:], B16),
        in_specs=[anyw],
        out_specs=anyw,
        scratch_shapes=[
            pltpu.SemaphoreType.DMA((1,)),
            pltpu.SemaphoreType.DMA((sends,)),
            pltpu.SemaphoreType.DMA((n,)),
        ],
        compiler_params=params_of(cid),
        name="gather_u",
    )(u)


def scatter_kernel(n, dup, out, from_sib, from_mate, mine_sum, from_partner, lsem, send, recv):
    me = lax.axis_index(HEIGHT)
    half = n // 2
    mine = me // half
    base = mine * half
    core = lax.rem(me, 2)
    partner = lax.rem(me + half, n)
    sibling = other_core(me)
    mates = half // 2
    seat = (me - base) // 2
    barrier = pltpu.get_barrier_semaphore()

    def mate(j, c=core):
        return base + c + 2 * lax.rem(seat + j, mates)

    peers = [partner, sibling] + [mate(j) for j in range(1, mates)]
    for p in peers:
        pl.semaphore_signal(barrier, inc=1, device_id={HEIGHT: p}, device_id_type=MESH)
    pl.semaphore_wait(barrier, len(peers))
    order = [(j, far) for j in range(1, mates) for far in (1, 0)] + [(0, 1), (0, 0)]

    def rows_of(j, far, c):
        owner = mate(j, c)
        return lax.rem(owner + half, n) if far else owner

    sib = []
    for t, (j, far) in enumerate(order):
        cp = pltpu.make_async_remote_copy(
            src_ref=dup.at[rows_of(j, far, 1 - core)], dst_ref=from_sib.at[t],
            send_sem=send.at[t], recv_sem=recv.at[t],
            device_id={HEIGHT: sibling}, device_id_type=MESH)
        cp.start()
        sib.append(cp)
    base_sem = len(order)
    out_copies = []
    for t, (j, far) in enumerate(order):
        sib[t].wait_recv()
        block = rows_of(j, far, core)
        if j > 0:
            mine_sum[t] = (dup[block].astype(F32) + from_sib[t].astype(F32)).astype(B16)
            at = (j - 1) * 2 + far
            cp = pltpu.make_async_remote_copy(
                src_ref=mine_sum.at[t], dst_ref=from_mate.at[at],
                send_sem=send.at[base_sem + at], recv_sem=recv.at[base_sem + at],
                device_id={HEIGHT: mate(j)}, device_id_type=MESH)
            cp.start()
            out_copies.append(cp)
    t_far, t_own = len(order) - 2, len(order) - 1
    total = dup[partner].astype(F32) + from_sib[t_far].astype(F32)
    for j in range(1, mates):
        at = (j - 1) * 2 + 1
        pltpu.make_async_remote_copy(
            src_ref=mine_sum.at[0], dst_ref=from_mate.at[at], send_sem=send.at[0],
            recv_sem=recv.at[base_sem + at], device_id={HEIGHT: sibling},
            device_id_type=MESH).wait_recv()
        total = total + from_mate[at].astype(F32)
    mine_sum[t_far] = total.astype(B16)
    last = base_sem + 2 * (mates - 1)
    home = pltpu.make_async_remote_copy(
        src_ref=mine_sum.at[t_far], dst_ref=from_partner, send_sem=send.at[last],
        recv_sem=recv.at[last], device_id={HEIGHT: partner}, device_id_type=MESH)
    home.start()
    total = dup[me].astype(F32) + from_sib[t_own].astype(F32)
    for j in range(1, mates):
        at = (j - 1) * 2
        pltpu.make_async_remote_copy(
            src_ref=mine_sum.at[0], dst_ref=from_mate.at[at], send_sem=send.at[0],
            recv_sem=recv.at[base_sem + at], device_id={HEIGHT: sibling},
            device_id_type=MESH).wait_recv()
        total = total + from_mate[at].astype(F32)
    out[mine] = total
    home.wait_recv()
    out[1 - mine] = from_partner[...].astype(F32)
    for cp in sib + out_copies + [home]:
        cp.wait_send()


def scatter_call(n, cid, dup):
    half = n // 2
    mates = half // 2
    copies = 2 * mates + 2 * (mates - 1) + 1
    seg = dup.shape[1:]
    return pl.pallas_call(
        functools.partial(scatter_kernel, n),
        out_shape=sds((2,) + seg, F32),
        in_specs=[vmem],
        out_specs=vmem,
        scratch_shapes=[
            pltpu.VMEM((2 * mates,) + seg, B16),
            pltpu.VMEM((max(2 * (mates - 1), 1),) + seg, B16),
            pltpu.VMEM((2 * mates,) + seg, B16),
            pltpu.VMEM(seg, B16),
            pltpu.SemaphoreType.DMA((1,)),
            pltpu.SemaphoreType.DMA((copies,)),
            pltpu.SemaphoreType.DMA((copies,)),
        ],
        compiler_params=params_of(cid),
        name="scatter_du",
    )(dup)


def resnet_backward_kernel(n, dims, cot, du, hid, y1, x, mean1, inv1, mean2, inv2, mean3, inv3, s1, s2, pick,
                           spread, div, col_l, col_r, row_u, row_d, vec, top, bottom, datt, igrad, grads, dvec,
                           dw1, dw2, k, dh, d3, low, low_u, low_d, part, norm, halo, buf, tmp_a, tmp_b, ksem, wsem, send,
                           recv, hsend, hrecv):
    canvases, rows, width = dims
    px = canvases * rows * width
    cells = px // UNIT
    plane = rows * width
    nt = (((1,), (1,)), ((), ()))
    tn = (((0,), (0,)), ((), ()))
    load2 = second_matrix(top, bottom, k, wsem)
    load1 = pltpu.make_async_copy(top.at[pl.ds(0, 9 * C)], k, wsem.at[0])
    for cp in load2:
        cp.start()
    out_att = pltpu.make_async_copy(datt, grads.at[pl.ds(18 * C, 4 * C)], ksem.at[2])
    out_two = pltpu.make_async_copy(dw2, grads.at[pl.ds(9 * C, 9 * C)], ksem.at[3])
    out_one = pltpu.make_async_copy(dw1, grads.at[pl.ds(0, 9 * C)], ksem.at[4])
    out_att.start()
    greet(n)
    zero_row = jnp.zeros((1, C), F32)

    def pixels(i):
        return pl.ds(i * 16 * UNIT, 16 * UNIT)

    def norm_sums(grad_of, source, mean, inv, gain):
        def body(i, carry):
            dg, db = carry
            at = pixels(i)
            unit = (source[at, :].astype(F32) - over_cells(mean, i)) * over_cells(inv, i)
            d = grad_of(i, unit)
            norm[at, :] = unit
            e = d * gain
            part[at, :] = e
            cross = d * unit
            here = pl.ds(i * 16, 16)
            tmp_a[here, :] = jnp.sum(e.reshape(16, UNIT, C), axis=1)
            tmp_b[here, :] = jnp.sum((cross * gain).reshape(16, UNIT, C), axis=1)
            return (dg + jnp.sum(cross, axis=0, keepdims=True), db + jnp.sum(d, axis=0, keepdims=True))

        dg, db = lax.fori_loop(0, cells // 16, body, (zero_row, zero_row))
        packed = pack([group_totals(pick, tmp_a[...]), group_totals(pick, tmp_b[...])])
        return packed, dg, db

    def send_sums(packed, rnd):
        buf[rnd, 0] = packed
        copies = spread_copies(n, buf, send, recv, rnd)
        for cp in copies:
            cp.start()
        return copies

    def norm_finish(copies, rnd, inv, emit):
        for cp in copies:
            cp.wait_recv()
        gathered = jnp.sum(buf[rnd], axis=0) / div[...]
        tmp_a[...] = split_dot(spread[...], unpack(gathered))
        tmp_b[...] = split_dot(spread[...], unpack(shift_down(gathered, 1)))

        def body(i, _):
            at = pixels(i)
            emit(i, over_cells(inv, i) * (part[at, :] - over_cells(tmp_a, i) - norm[at, :] * over_cells(tmp_b, i)))
            return 0

        lax.fori_loop(0, cells // 16, body, 0)

    def spread_rows(rnd):
        def row_at(v, r):
            return pl.ds(pl.multiple_of((v * rows + r) * width, width), width)

        def one(i, _):
            v, r = i // rows, lax.rem(i, rows)
            d3[v, r + 1] = shift_columns(low[row_at(v, r), :].astype(F32), col_l[v, r + 1], col_r[v, r + 1])
            return 0

        lax.fori_loop(0, canvases * rows, one, 0)
        mid = pl.ds(C, C)
        up, down = halo_copies(n, d3.at[:, 1, :, mid], d3.at[:, rows, :, mid], halo.at[rnd],
                               hsend.at[rnd], hrecv.at[rnd])
        start_halo(n, up, down)
        return up, down

    def finish_rows(up, down, rnd):
        wait_halo(n, up, down, halo.at[rnd], 0.0)
        for v in range(canvases):
            for side, r in ((0, 0), (1, rows + 1)):
                d3[v, r] = shift_columns(halo[rnd, side, v].astype(F32), col_l[v, r], col_r[v, r])

    def convolve_back(emit):
        def body(v, _):
            at = pl.ds(pl.multiple_of(v * plane, plane), plane)
            total = None
            for dr in (1, 0, 2):
                acc = None
                for dc in range(3):
                    tap = 3 * (2 - dr) + (2 - dc)
                    lhs = d3[v, dr : dr + rows, :, dc * C : (dc + 1) * C].reshape(plane, C)
                    term = lax.dot_general(lhs, k[tap * C : (tap + 1) * C, :], nt, preferred_element_type=F32)
                    acc = term if acc is None else acc + term
                if dr == 0:
                    acc = acc * wide(row_u[at, :])
                if dr == 2:
                    acc = acc * wide(row_d[at, :])
                total = acc if total is None else total + acc
            emit(at, total)
            return 0

        lax.fori_loop(0, canvases, body, 0)

    def mask_rows():
        def body(i, _):
            at = pixels(i)
            value = low[at, :].astype(F32)
            low_u[at, :] = (value * wide(row_u[at, :])).astype(B16)
            low_d[at, :] = (value * wide(row_d[at, :])).astype(B16)
            return 0

        lax.fori_loop(0, cells // 16, body, 0)

    def weight_grad(source, dest):
        for dr, grad in ((0, low_u), (1, low), (2, low_d)):
            def body(dc, _):
                acc = None
                for v in range(canvases):
                    lhs = source[v, dr : dr + rows, :, pl.ds(pl.multiple_of(dc * C, C), C)].reshape(plane, C)
                    term = lax.dot_general(
                        lhs, grad[v * plane : (v + 1) * plane, :], tn, preferred_element_type=F32)
                    acc = term if acc is None else acc + term
                dest[pl.ds(pl.multiple_of((3 * dr + dc) * C, C), C), :] = acc.astype(B16)
                return 0

            lax.fori_loop(0, 3, body, 0)

    packed, dg3, db3 = norm_sums(lambda i, unit: du[pixels(i), :], hid, mean3, inv3, vec[6:7, :])
    sent = send_sums(packed, 0)

    def emit_hidden(i, value):
        at = pixels(i)
        total = cot[at, :].astype(F32) + value
        dh[at, :] = total
        low[at, :] = total.astype(B16)

    norm_finish(sent, 0, inv3, emit_hidden)
    up, down = spread_rows(0)
    mask_rows()
    dc2 = jnp.sum(low[...].astype(F32), axis=0, keepdims=True)
    finish_rows(up, down, 0)
    for cp in load2:
        cp.wait()

    def emit_part(at, total):
        part[at, :] = total

    convolve_back(emit_part)
    load1.start()
    gain2, bias2 = vec[3:4, :], vec[4:5, :]

    def grad_two(i, unit):
        return part[pixels(i), :] * silu_slope(unit * gain2 + bias2)

    packed, dg2, db2 = norm_sums(grad_two, y1, mean2, inv2, gain2)
    more = send_sums(packed, 1)
    weight_grad(s2, dw2)
    out_two.start()

    def emit_low(i, value):
        low[pixels(i), :] = value.astype(B16)

    norm_finish(more, 1, inv2, emit_low)
    sent = sent + more
    up, down = spread_rows(1)
    mask_rows()
    dc1 = jnp.sum(low[...].astype(F32), axis=0, keepdims=True)
    weight_grad(s1, dw1)
    out_one.start()
    finish_rows(up, down, 1)
    load1.wait()
    convolve_back(emit_part)
    gain1, bias1 = vec[0:1, :], vec[1:2, :]

    def grad_one(i, unit):
        return part[pixels(i), :] * silu_slope(unit * gain1 + bias1)

    packed, dg1, db1 = norm_sums(grad_one, x, mean1, inv1, gain1)
    more = send_sums(packed, 2)
    dvec[...] = jnp.concatenate([dg1, db1, dc1, dg2, db2, dc2, dg3, db3], axis=0)

    def emit_input(i, value):
        igrad[pixels(i), :] = dh[pixels(i), :] + value

    norm_finish(more, 2, inv1, emit_input)
    sent = sent + more
    out_att.wait()
    out_two.wait()
    out_one.wait()
    for cp in sent:
        cp.wait_send()


def resnet_backward_call(n, dims, cid, cot, du, hid, y1, x, norms, s1, s2, pick, spread, div, masks, vec, top,
                         bottom, datt):
    canvases, rows, width = dims
    px = canvases * rows * width
    cells = px // UNIT
    stats = canvases * CROPS
    return pl.pallas_call(
        functools.partial(resnet_backward_kernel, n, dims),
        out_shape=[sds((px, C), F32), sds((22 * C, C), B16), sds((8, C), F32)],
        in_specs=[vmem] * 21 + [anyw] * 3,
        out_specs=[vmem, anyw, vmem],
        scratch_shapes=[
            pltpu.VMEM((9 * C, C), B16),
            pltpu.VMEM((9 * C, C), B16),
            pltpu.VMEM((9 * C, C), B16),
            pltpu.VMEM((px, C), F32),
            pltpu.VMEM((canvases, rows + 2, width, 3 * C), B16),
            pltpu.VMEM((px, C), B16),
            pltpu.VMEM((px, C), B16),
            pltpu.VMEM((px, C), B16),
            pltpu.VMEM((px, C), F32),
            pltpu.VMEM((px, C), F32),
            pltpu.VMEM((2, 2, canvases, width, C), B16),
            pltpu.VMEM((3, n, stats, LANES), F32),
            pltpu.VMEM((cells, C), F32),
            pltpu.VMEM((cells, C), F32),
            pltpu.SemaphoreType.DMA((5,)),
            pltpu.SemaphoreType.DMA((3,)),
            pltpu.SemaphoreType.DMA((3, n)),
            pltpu.SemaphoreType.DMA((3, n)),
            pltpu.SemaphoreType.DMA((2, 2)),
            pltpu.SemaphoreType.DMA((2, 2)),
        ],
        compiler_params=params_of(cid),
        name="resnet_backward",
    )(cot, du, hid, y1, x, *norms, s1, s2, pick, spread, div, *masks, vec, top, bottom, datt)


class Grid:
    def __init__(self, columns, n):
        self.columns, self.n, self.seats = columns, n, n // 2
        self.phases = columns.bit_length() - 1
        self.c = lax.axis_index(CANVAS)
        self.h = lax.axis_index(HEIGHT)
        self.seat, self.core = self.h // 2, lax.rem(self.h, 2)
        flips = [
            (1 - 2 * lax.rem(self.c // 2**t, 2)) * 2**t for t in range(self.phases)
        ]
        last = self.phases - 1
        self.flips = [
            (1 - self.core) * flips[last - k] + self.core * flips[k] for k in range(self.phases)
        ]
        self.other_flips = [
            self.core * flips[last - k] + (1 - self.core) * flips[k] for k in range(self.phases)
        ]

    def column(self, e, flips=None):
        flips = self.flips if flips is None else flips
        col = self.c
        for k in range(self.phases):
            if (e >> k) & 1:
                col = col + flips[k]
        return col

    def mate(self, k):
        return {CANVAS: self.c + self.flips[k], HEIGHT: self.h}

    def sibling(self):
        return {CANVAS: self.c, HEIGHT: 2 * self.seat + 1 - self.core}

    def beside(self, step):
        return {CANVAS: self.c, HEIGHT: self.h + 2 * step}

    def greet(self):
        barrier = pltpu.get_barrier_semaphore()
        for d in range(1, self.n):
            pl.semaphore_signal(
                barrier, inc=1, device_id={CANVAS: self.c, HEIGHT: lax.rem(self.h + d, self.n)},
                device_id_type=MESH)
        for k in range(self.phases):
            pl.semaphore_signal(barrier, inc=1, device_id=self.mate(k), device_id_type=MESH)
        pl.semaphore_wait(barrier, self.n - 1 + self.phases)


def remote(src, dst, send, recv, to):
    return pltpu.make_async_remote_copy(
        src_ref=src, dst_ref=dst, send_sem=send, recv_sem=recv, device_id=to, device_id_type=MESH)


def lowest_bit(e):
    return (e & -e).bit_length() - 1


def spread_blocks(grid, fresh, whole, own_sem, zsend, msend, ssend, recv, srecv):
    g = grid
    seats, phases = g.seats, g.phases
    own = pltpu.make_async_copy(fresh, whole.at[g.c, g.seat, g.core], own_sem)
    own.start()

    def slot(e, seat):
        return whole.at[g.column(e), seat, g.core]

    def forward(e, seat, src, start):
        k_top = phases if e == 0 else lowest_bit(e)
        for k in range(k_top - 1, -1, -1):
            cp = remote(src, slot(e, seat), msend.at[k, e, seat], recv.at[e | (1 << k), seat], g.mate(k))
            cp.start() if start else cp.wait_send()
        cp = remote(src, slot(e, seat), ssend.at[e, seat], srecv.at[e, seat], g.sibling())
        cp.start() if start else cp.wait_send()

    def along(seat, step, src, start):
        cp = remote(src, slot(0, seat), zsend.at[(step + 1) // 2, seat], recv.at[0, seat], g.beside(step))
        cp.start() if start else cp.wait_send()

    def line(seat, src, start):
        @pl.when((seat <= g.seat) & (g.seat < seats - 1))
        def _():
            along(seat, 1, src, start)

        @pl.when((seat >= g.seat) & (g.seat > 0))
        def _():
            along(seat, -1, src, start)

    def arrive(e, seat):
        remote(fresh, slot(e, seat), ssend.at[0, 0], recv.at[e, seat], g.sibling()).wait_recv()

    early = [e for e in range(1, 2**phases) if lowest_bit(e) > 0]
    early.sort(key=lambda e: -lowest_bit(e))
    late = [e for e in range(1, 2**phases) if lowest_bit(e) == 0]

    def handle(e, seat):
        arrive(e, seat)
        if e == 0:
            line(seat, slot(0, seat), True)
        forward(e, seat, slot(e, seat), True)

    def both_sides(d, todo):
        for side in (-1, 1):
            seat = g.seat + side * d

            @pl.when((seat >= 0) & (seat < seats))
            def _():
                for e in todo:
                    handle(e, seat)

    line(g.seat, fresh, True)
    forward(0, g.seat, fresh, True)
    for e in early:
        handle(e, g.seat)

    def further(d, _):
        both_sides(d, [0] + early)
        return 0

    lax.fori_loop(1, seats, further, 0)
    for e in late:
        handle(e, g.seat)

    def finish(d, _):
        both_sides(d, late)
        return 0

    lax.fori_loop(1, seats, finish, 0)

    def drain(seat, _):
        for e in range(2**phases):
            remote(fresh, whole.at[g.column(e, g.other_flips), seat, 1 - g.core], ssend.at[0, 0],
                   srecv.at[e, seat], g.sibling()).wait_recv()
            forward(e, seat, slot(e, seat), False)
        line(seat, slot(0, seat), False)
        return 0

    lax.fori_loop(0, seats, drain, 0)
    own.wait()


def spread_scratch(columns, n):
    seats, phases = n // 2, columns.bit_length() - 1
    dma = pltpu.SemaphoreType.DMA
    return [
        dma((1,)),
        dma((2, seats)),
        dma((phases, columns, seats)),
        dma((columns, seats)),
        dma((columns, seats)),
        dma((columns, seats)),
    ]


def spread_kernel(columns, n, block, whole, fresh, own, zsend, msend, ssend, recv, srecv):
    grid = Grid(columns, n)
    fresh[...] = block[...].astype(B16)
    grid.greet()
    spread_blocks(grid, fresh, whole, own.at[0], zsend, msend, ssend, recv, srecv)


def spread_call(columns, n, cid, block):
    return pl.pallas_call(
        functools.partial(spread_kernel, columns, n),
        out_shape=sds((columns, n // 2, 2) + block.shape, B16),
        in_specs=[vmem],
        out_specs=anyw,
        scratch_shapes=[pltpu.VMEM(block.shape, B16)] + spread_scratch(columns, n),
        compiler_params=params_of(cid),
        name="spread_weights",
    )(block)


def adam_update(current, gradient, moment_one, moment_two, learn_rate):
    first_new = 0.5 * moment_one + 0.5 * gradient
    second_new = 0.9 * moment_two + 0.1 * gradient * gradient
    first_hat = first_new / (1.0 - 0.5**STEP)
    second_hat = second_new / (1.0 - 0.9**STEP)
    return (
        current - learn_rate * first_hat / (jnp.sqrt(second_hat) + adam_epsilon),
        first_new,
        second_new,
    )


def step_kernel(columns, n, grads, w, m, s, dvec, vw, vm, vs, new_w, new_m, new_s, new_vw, new_vm, new_vs, whole,
                acc, sib, got, up, down, fresh, vbuf, vtrade, lsem, gsend, grecv, psend, precv, usend, urecv,
                vsend, vrecv, tsend, trecv, own, zsend, msend, ssend, recv, srecv):
    g = Grid(columns, n)
    seats, phases = g.seats, g.phases
    slots = 2**phases
    order = sorted(range(slots), key=lambda e: (lowest_bit(e) if e else phases, e == (e & -e)))
    loads = []
    for e in order:
        cp = pltpu.make_async_copy(grads.at[g.column(e), :, g.core], acc.at[e], lsem.at[e])
        cp.start()
        loads.append(cp)

    @pl.when(g.seat == 0)
    def _():
        up[...] = jnp.zeros(up.shape, B16)

    @pl.when(g.seat == seats - 1)
    def _():
        down[...] = jnp.zeros(down.shape, B16)

    vbuf[g.h] = dvec[...]
    g.greet()
    sib_copies = []
    for e in order:
        cp = remote(grads.at[g.column(e, g.other_flips), :, 1 - g.core], sib.at[e], gsend.at[e], grecv.at[e],
                    g.sibling())
        cp.start()
        sib_copies.append(cp)

    def vector_copy(d):
        src = lax.rem(g.h + d, n)
        return remote(vbuf.at[g.h], vbuf.at[g.h], vsend.at[d], vrecv.at[g.h],
                      {CANVAS: g.c, HEIGHT: src})

    def vector_arrival(d):
        src = lax.rem(g.h + d, n)
        return remote(vbuf.at[src], vbuf.at[src], vsend.at[d], vrecv.at[src],
                      {CANVAS: g.c, HEIGHT: src})

    for d in range(1, n):
        vector_copy(d).start()

    def local(e, seat, below):
        total = acc[e, seat].astype(F32) + sib[e, seat].astype(F32)
        for k in range(below):
            total = total + got[k, e >> (k + 1), seat].astype(F32)
        return total

    def in_turn(i):
        even = 1 - lax.rem(i, 2)
        return (i // 2) * even + (1 - even) * (seats - 1 - i // 2)

    def phase_copy(k, e, seat):
        return remote(acc.at[e, seat], got.at[k, e >> (k + 1), seat], psend.at[k, e >> (k + 1), seat],
                      precv.at[k, e >> (k + 1), seat], g.mate(k))

    ready = 0
    for e in order:
        loads[ready].wait()
        sib_copies[ready].wait_recv()
        ready += 1
        if e == 0:
            break
        k = lowest_bit(e)

        def one(i, _):
            seat = in_turn(i)
            for q in range(k):
                phase_copy(q, e | (1 << q), seat).wait_recv()
            acc[e, seat] = local(e, seat, k).astype(B16)
            phase_copy(k, e, seat).start()
            return 0

        lax.fori_loop(0, seats, one, 0)

    for d in range(1, n):
        vector_arrival(d).wait_recv()
    vtrade[0, 0] = jnp.sum(vbuf[...], axis=0)
    for k in range(phases):
        cp = remote(vtrade.at[k, 0], vtrade.at[k, 1], tsend.at[k], trecv.at[k], g.mate(k))
        cp.start()
        cp.wait_recv()
        vtrade[k + 1, 0] = vtrade[k, 0] + vtrade[k, 1]
    new_vw[...], new_vm[...], new_vs[...] = adam_update(vw[...], vtrade[phases, 0], vm[...], vs[...], vector_rate)

    def line_copy(step, seat):
        box = up if step > 0 else down
        at = (step + 1) // 2
        return remote(acc.at[0, seat], box.at[seat], usend.at[at, seat], urecv.at[at, seat], g.beside(step))

    def own_column(i, _):
        seat = in_turn(i)
        for q in range(phases):
            phase_copy(q, 1 << q, seat).wait_recv()

        @pl.when(seat > g.seat)
        def _():
            @pl.when(g.seat > 0)
            def _():
                line_copy(1, seat).wait_recv()

            acc[0, seat] = (local(0, seat, phases) + up[seat].astype(F32)).astype(B16)
            line_copy(1, seat).start()

        @pl.when(seat < g.seat)
        def _():
            @pl.when(g.seat < seats - 1)
            def _():
                line_copy(-1, seat).wait_recv()

            acc[0, seat] = (local(0, seat, phases) + down[seat].astype(F32)).astype(B16)
            line_copy(-1, seat).start()

        return 0

    lax.fori_loop(0, seats, own_column, 0)

    @pl.when(g.seat > 0)
    def _():
        line_copy(1, g.seat).wait_recv()

    @pl.when(g.seat < seats - 1)
    def _():
        line_copy(-1, g.seat).wait_recv()

    total = local(0, g.seat, phases) + up[g.seat].astype(F32) + down[g.seat].astype(F32)
    next_w, new_m[...], new_s[...] = adam_update(w[...], total, m[...], s[...], matrix_rate)
    new_w[...] = next_w
    fresh[...] = next_w.astype(B16)
    spread_blocks(g, fresh, whole, own.at[0], zsend, msend, ssend, recv, srecv)
    for cp in sib_copies:
        cp.wait_send()
    for d in range(1, n):
        vector_copy(d).wait_send()
    for k in range(phases):
        remote(vtrade.at[k, 0], vtrade.at[k, 1], tsend.at[k], trecv.at[k], g.mate(k)).wait_send()

    def drain(seat, _):
        for e in range(1, slots):
            phase_copy(lowest_bit(e), e, seat).wait_send()

        @pl.when(seat > g.seat)
        def _():
            line_copy(1, seat).wait_send()

        @pl.when(seat < g.seat)
        def _():
            line_copy(-1, seat).wait_send()

        return 0

    lax.fori_loop(0, seats, drain, 0)


def step_call(columns, n, cid, grads, w, m, s, dvec, vw, vm, vs):
    seats, phases = n // 2, columns.bit_length() - 1
    block = w.shape
    half = max(columns // 2, 1)
    dma = pltpu.SemaphoreType.DMA
    return pl.pallas_call(
        functools.partial(step_kernel, columns, n),
        out_shape=[sds(block, F32)] * 3 + [sds(vw.shape, F32)] * 3 + [sds((columns, seats, 2) + block, B16)],
        in_specs=[anyw] + [vmem] * 7,
        out_specs=[vmem] * 6 + [anyw],
        scratch_shapes=[
            pltpu.VMEM((columns, seats) + block, B16),
            pltpu.VMEM((columns, seats) + block, B16),
            pltpu.VMEM((phases, half, seats) + block, B16),
            pltpu.VMEM((seats,) + block, B16),
            pltpu.VMEM((seats,) + block, B16),
            pltpu.VMEM(block, B16),
            pltpu.VMEM((n,) + vw.shape, F32),
            pltpu.VMEM((phases + 1, 2) + vw.shape, F32),
            dma((columns,)),
            dma((columns,)),
            dma((columns,)),
            dma((phases, half, seats)),
            dma((phases, half, seats)),
            dma((2, seats)),
            dma((2, seats)),
            dma((n,)),
            dma((n,)),
            dma((phases,)),
            dma((phases,)),
        ]
        + spread_scratch(columns, n),
        compiler_params=params_of(cid),
        name="step_weights",
    )(grads, w, m, s, dvec, vw, vm, vs)


class Engine:
    def __init__(self, steps):
        self.steps = steps

    def pump(self, count=1):
        for _ in range(count):
            next(self.steps, None)

    def ready(self):
        for done in self.steps:
            if done:
                return

    def finish(self):
        for _ in self.steps:
            pass


class Group:
    def __init__(self, grid, number, half_rows, first=0, size=None):
        self.g, self.number, self.half = grid, number, half_rows
        self.first, self.size = first, half_rows if size is None else size
        self.owner = 2 * number + grid.c // 2
        self.is_owner = grid.c // 2 == number

    def row(self, q, seat, core):
        block = (q // 2) * self.g.n + 2 * seat + core
        return pl.multiple_of((2 * block + lax.rem(q, 2)) * self.half + self.first, 16)

    def rows(self, q, seat, core):
        return pl.ds(self.row(q, seat, core), self.size)

    def at_column(self, col):
        return {CANVAS: col, HEIGHT: self.g.h}

    def halves(self):
        first = 2 * lax.rem(self.g.c, 2)
        return [(0, first), (1, first + 1)]

    def part(self, ref, half):
        return ref.at[pl.ds(half * self.half, self.half)]

    def to_pieces(self, block, piece, send, recv, start):
        g = self.g

        @pl.when(self.is_owner)
        def _():
            for half, col in self.halves():
                @pl.when(col != g.c)
                def _():
                    cp = remote(self.part(block, half), piece, send.at[half], recv.at[0], self.at_column(col))
                    cp.start() if start else cp.wait_send()

                if start:
                    @pl.when(col == g.c)
                    def _():
                        piece[...] = block[half * self.half : (half + 1) * self.half, :]

    def piece_arrived(self, block, piece, send, recv):
        @pl.when(self.owner != self.g.c)
        def _():
            remote(self.part(block, 0), piece, send.at[0], recv.at[0], self.at_column(self.owner)).wait_recv()

    def to_owner(self, piece, block, send, recv, start):
        g = self.g
        half = lax.rem(g.c, 2)
        where = pl.ds(pl.multiple_of(half * self.half, 16), self.half)

        @pl.when(self.owner != g.c)
        def _():
            cp = remote(piece, block.at[where], send.at[0], recv.at[half], self.at_column(self.owner))
            cp.start() if start else cp.wait_send()

        if start:
            @pl.when(self.owner == g.c)
            def _():
                block[where, :] = piece[...]

    def block_arrived(self, piece, block, send, recv):
        g = self.g

        @pl.when(self.is_owner)
        def _():
            for half, col in self.halves():
                @pl.when(col != g.c)
                def _():
                    remote(piece, self.part(block, half), send.at[0], recv.at[half], self.at_column(col)).wait_recv()


def gather_pieces(group, piece, dest, own, zsend, msend, ssend, recv, srecv):
    g = group.g
    seats, phases = g.seats, g.phases
    local = pltpu.make_async_copy(piece, dest.at[group.rows(g.c, g.seat, g.core)], own.at[0])

    local.start()
    top = 1 << (phases - 1)
    lines = [0, top]

    def slot(e, seat):
        return dest.at[group.rows(g.column(e), seat, g.core)]

    def forward(e, seat, src, start):
        k_top = phases if e == 0 else lowest_bit(e)
        for k in range(k_top - 1, -1, -1):
            cp = remote(src, slot(e, seat), msend.at[k, e, seat], recv.at[e | (1 << k), seat], g.mate(k))
            do = cp.start if start else cp.wait_send
            if e == 0 and k == phases - 1:
                pl.when(seat == g.seat)(do)
            else:
                do()
        cp = remote(src, slot(e, seat), ssend.at[e, seat], srecv.at[e, seat], g.sibling())
        cp.start() if start else cp.wait_send()

    def along(e, seat, step, src, start):
        cp = remote(src, slot(e, seat), zsend.at[(step + 1) // 2, min(e, 1), seat], recv.at[e, seat], g.beside(step))
        cp.start() if start else cp.wait_send()

    def line(e, seat, src, start):
        @pl.when((seat <= g.seat) & (g.seat < seats - 1))
        def _():
            along(e, seat, 1, src, start)

        @pl.when((seat >= g.seat) & (g.seat > 0))
        def _():
            along(e, seat, -1, src, start)

    def handle(e, seat):
        remote(piece, slot(e, seat), ssend.at[0, 0], recv.at[e, seat], g.sibling()).wait_recv()
        if e in lines:
            line(e, seat, slot(e, seat), True)
        forward(e, seat, slot(e, seat), True)

    early = sorted((e for e in range(1, 2**phases) if lowest_bit(e) > 0), key=lambda e: -lowest_bit(e))
    late = [e for e in range(1, 2**phases) if lowest_bit(e) == 0]

    def both_sides(d, todo):
        for side in (-1, 1):
            seat = g.seat + side * d

            @pl.when((seat >= 0) & (seat < seats))
            def _():
                for e in todo:
                    handle(e, seat)

    forward(0, g.seat, piece, True)
    line(0, g.seat, piece, True)
    yield
    for e in early:
        handle(e, g.seat)
    yield
    for d in range(1, seats):
        both_sides(d, [0] + early)
        yield
    for e in late:
        handle(e, g.seat)
    yield
    for d in range(1, seats):
        both_sides(d, late)
        yield

    def siblings(seat, _):
        for e in range(2**phases):
            remote(piece, dest.at[group.rows(g.column(e, g.other_flips), seat, 1 - g.core)], ssend.at[0, 0],
                   srecv.at[e, seat], g.sibling()).wait_recv()
        return 0

    lax.fori_loop(0, seats, siblings, 0)
    local.wait()
    yield True

    def drain(seat, _):
        for e in range(2**phases):
            forward(e, seat, slot(e, seat), False)
            if e in lines:
                line(e, seat, slot(e, seat), False)
        return 0

    lax.fori_loop(0, seats, drain, 0)


def gather_pieces_scratch(columns, n):
    seats, phases = n // 2, columns.bit_length() - 1
    dma = pltpu.SemaphoreType.DMA
    return [
        dma((1,)),
        dma((2, 2, seats)),
        dma((phases, columns, seats)),
        dma((columns, seats)),
        dma((columns, seats)),
        dma((columns, seats)),
    ]


def reduce_pieces(group, src, piece, sib, got, box, gsend, grecv, psend, precv, usend, urecv):
    g = group.g
    seats, phases = g.seats, g.phases
    slots = 2**phases
    order = sorted(range(slots), key=lambda e: (lowest_bit(e) if e else phases, e == (e & -e)))
    turns = [i // 2 if i % 2 == 0 else seats - 1 - i // 2 for i in range(seats)]

    def mine(e, seat):
        return group.rows(g.column(e), seat, g.core)

    def sibling_copy(e, seat):
        return remote(src.at[group.rows(g.column(e, g.other_flips), seat, 1 - g.core)], sib.at[e, seat],
                      gsend.at[e, seat], grecv.at[e, seat], g.sibling())

    def phase_copy(k, e, seat):
        at = (k, e >> (k + 1), seat)
        return remote(src.at[mine(e, seat), :], got.at[at], psend.at[at], precv.at[at], g.mate(k))

    def line_copy(seat):
        return remote(src.at[mine(0, seat), :], box.at[g.seat], usend.at[seat], urecv.at[g.seat],
                      {CANVAS: g.c, HEIGHT: 2 * seat + g.core})

    def line_arrival(seat):
        return remote(src.at[mine(0, seat), :], box.at[seat], usend.at[seat], urecv.at[seat],
                      {CANVAS: g.c, HEIGHT: 2 * seat + g.core})

    def local(e, seat, below):
        total = src[mine(e, seat), :].astype(F32) + sib[e, seat].astype(F32)
        for k in range(below):
            total = total + got[k, e >> (k + 1), seat].astype(F32)
        return total

    for e in order:
        for seat in turns:
            sibling_copy(e, seat).start()
    yield

    def pass_on(e, k, seat):
        sibling_copy(e, seat).wait_recv()
        for q in range(k):
            phase_copy(q, e | (1 << q), seat).wait_recv()
        src[mine(e, seat), :] = local(e, seat, k).astype(B16)
        phase_copy(k, e, seat).start()

    for e in order:
        if e == 0:
            break
        for seat in turns:
            pass_on(e, lowest_bit(e), seat)
            yield

    def own_column(seat):
        sibling_copy(0, seat).wait_recv()
        for q in range(phases):
            phase_copy(q, 1 << q, seat).wait_recv()

        @pl.when(seat != g.seat)
        def _():
            src[mine(0, seat), :] = local(0, seat, phases).astype(B16)
            line_copy(seat).start()

    for seat in turns:
        own_column(seat)
        yield
    total = local(0, g.seat, phases)
    for seat in turns:
        @pl.when(seat != g.seat)
        def _():
            line_arrival(seat).wait_recv()

        total = total + jnp.where(seat == g.seat, 0.0, box[seat].astype(F32))
    piece[...] = total.astype(B16)
    yield True

    def drain(seat, _):
        for e in range(slots):
            sibling_copy(e, seat).wait_send()
            if e > 0:
                phase_copy(lowest_bit(e), e, seat).wait_send()

        @pl.when(seat != g.seat)
        def _():
            line_copy(seat).wait_send()

        return 0

    lax.fori_loop(0, seats, drain, 0)


def reduce_pieces_scratch(columns, n, half_rows):
    seats, phases = n // 2, columns.bit_length() - 1
    half = columns // 2
    dma = pltpu.SemaphoreType.DMA
    block = (half_rows, C)
    return [
        pltpu.VMEM((columns, seats) + block, B16),
        pltpu.VMEM((phases, half, seats) + block, B16),
        pltpu.VMEM((seats,) + block, B16),
        dma((columns, seats)),
        dma((columns, seats)),
        dma((phases, half, seats)),
        dma((phases, half, seats)),
        dma((seats,)),
        dma((seats,)),
    ]


class Named:
    def __init__(self, shapes, refs):
        refs = list(refs)
        for name, shape in shapes.items():
            if isinstance(shape, list):
                setattr(self, name, [refs.pop(0) for _ in shape])
            else:
                setattr(self, name, refs.pop(0))


def named_call(kernel, name, cid, inputs, outputs, scratch):
    loads = [k for k, (_, spec) in inputs.items() if spec == LOAD]
    stores = [k for k, (_, _, spec) in outputs.items() if spec == STORE]
    parts = 12
    shapes = {**inputs, **outputs, **scratch}
    flat = []
    for value in scratch.values():
        flat += value if isinstance(value, list) else [value]
    held = [pltpu.VMEM(inputs[k][0].shape, inputs[k][0].dtype) for k in loads]
    held += [pltpu.VMEM(*outputs[k][:2]) for k in stores]
    sems = [pltpu.SemaphoreType.DMA((max(len(loads), 1),)), pltpu.SemaphoreType.DMA((max(len(stores), 1), parts))]

    def wrapped(*refs):
        own = len(held) + len(sems)
        R = Named(shapes, refs[:-own])
        kept, (load_sem, store_sem) = refs[-own:-2], refs[-2:]
        waiting, begun, ends = {}, {k: 0 for k in stores}, []
        for i, k in enumerate(loads):
            waiting[k] = pltpu.make_async_copy(getattr(R, k), kept[i], load_sem.at[i])
            waiting[k].start()
            setattr(R, k, kept[i])
        targets = {}
        for i, k in enumerate(stores):
            targets[k] = getattr(R, k)
            setattr(R, k, kept[len(loads) + i])

        def need(*names):
            for k in names:
                if k in waiting:
                    waiting.pop(k).wait()

        def store(k, first=None, count=None):
            src, dst = getattr(R, k), targets[k]
            if first is not None:
                src, dst = src.at[pl.ds(first, count)], dst.at[pl.ds(first, count)]
            cp = pltpu.make_async_copy(src, dst, store_sem.at[stores.index(k), begun[k]])
            cp.start()
            begun[k] += 1
            ends.append(cp)

        R.need, R.store = need, store
        kernel(R)
        need(*list(waiting))
        for k in stores:
            if not begun[k]:
                store(k)
        for cp in ends:
            cp.wait()

    results = pl.pallas_call(
        wrapped,
        out_shape=[sds(shape, kind) for shape, kind, _ in outputs.values()],
        in_specs=[anyw if spec == LOAD else spec for _, spec in inputs.values()],
        out_specs=[anyw if spec == STORE else spec for _, _, spec in outputs.values()],
        scratch_shapes=flat + held + sems,
        compiler_params=params_of(cid),
        name=name,
    )(*[array for array, _ in inputs.values()])
    return dict(zip(outputs, results))


def greet_all(grid):
    barrier = pltpu.get_barrier_semaphore()
    for d in range(1, grid.n):
        pl.semaphore_signal(
            barrier, inc=1, device_id={CANVAS: grid.c, HEIGHT: lax.rem(grid.h + d, grid.n)}, device_id_type=MESH)
    for d in range(1, grid.columns):
        pl.semaphore_signal(
            barrier, inc=1, device_id={CANVAS: lax.rem(grid.c + d, grid.columns), HEIGHT: grid.h},
            device_id_type=MESH)
    pl.semaphore_wait(barrier, grid.n - 1 + grid.columns - 1)


def across(top, low):
    def taps(dr):
        if dr == 0:
            return [(0, 2 * C, top, 9 * C), (2 * C, 3 * C, low, 0)]
        return [(0, 3 * C, low, 3 * C * dr - 2 * C)]

    return taps


def first_kernel(columns, n, dims, R):
    g = Grid(columns, n)
    half = R.block.shape[0] // 2
    groups = [Group(g, i, half) for i in range(2)]
    R.low[...] = R.block[...].astype(B16)
    count = R.vectors.shape[0]
    R.vec[...] = jnp.zeros(R.vec.shape, F32)
    R.vec[0:count, :] = R.vectors[...].astype(B16).astype(F32)
    canvases, rows, width = dims
    turned = jnp.transpose(R.ids_lane[...])
    for v in range(canvases):
        R.ids_px[v] = jnp.broadcast_to(turned[:, v : v + 1], (rows * width, LANES)).reshape(rows, width, LANES)
    greet_all(g)
    for i, group in enumerate(groups):
        group.to_pieces(R.low, R.pieces.at[i], R.tsend.at[i], R.trecv.at[i], True)
    engines = [
        Engine(gather_pieces(groups[0], R.pieces.at[0], R.w_top, *R.gather0)),
        Engine(gather_pieces(groups[1], R.pieces.at[1], R.w_low, *R.gather1)),
    ]
    each = rows * width // UNIT
    for v in range(canvases):
        cell_ids = R.ids_px[v].reshape(each, UNIT, LANES)[:, 0, :] + float(CROPS * v)
        lane = lax.broadcasted_iota(jnp.int32, (each, LANES), 1).astype(F32)
        R.hot[v * each : (v + 1) * each, :] = (cell_ids == lane).astype(F32)
    stats = canvases * CROPS
    R.spread[...] = R.hot[:, :stats].astype(B16)
    R.pick[...] = jnp.transpose(R.hot[...])[:stats, :].astype(B16)
    turn = [0]
    lag = 2 * g.seats - 3

    def pump():
        if turn[0] == 0:
            groups[0].piece_arrived(R.low, R.pieces.at[0], R.tsend.at[0], R.trecv.at[0])
        if turn[0] < 2 * g.seats + 1:
            engines[0].pump()
        if turn[0] == lag:
            groups[1].piece_arrived(R.low, R.pieces.at[1], R.tsend.at[1], R.trecv.at[1])
        if turn[0] >= lag:
            engines[1].pump()
        turn[0] += 1

    R.need("x")
    layout_body(n, dims, R.x, R.pick, R.spread, R.ids_px, R.ids_lane, R.ids_all, R.mean1, R.inv1, R.div, R.cnt,
                R.col_l, R.col_r, R.row_u, R.row_d, *R.layout, pump=pump, cnt_all=R.cnt_all)
    for k in ("col_l", "col_r", "row_u", "row_d"):
        R.store(k)
    pump()
    conv = Convolver(n, dims, R.x, R.pick, R.spread, R.cnt, R.col_l, R.col_r, R.row_u, R.row_d, R.halo, R.buf,
                     R.tmp_a, R.tmp_b, R.send, R.recv, R.hsend, R.hrecv, R.cnt_all)
    vec = R.vec
    conv.activate(R.x, R.mean1, R.inv1, vec[0:1, :], vec[1:2, :], R.s1, 0, pump)
    out_s1 = pltpu.make_async_copy(R.s1, R.s1_out, R.osem.at[0])
    out_s1.start()
    while turn[0] < 2 * g.seats + 1:
        pump()
    engines[0].ready()
    out_top = pltpu.make_async_copy(R.w_top, R.top, R.osem.at[1])
    out_top.start()
    pump_low = engines[1].pump
    if turn[0] <= lag:
        groups[1].piece_arrived(R.low, R.pieces.at[1], R.tsend.at[1], R.trecv.at[1])
        pump_low()

    def emit_first(at, total):
        R.y1[at, :] = total + vec[2:3, :]

    conv.convolve(R.s1, lambda dr: [(0, 3 * C, R.w_top, 3 * C * dr)], emit_first, pump_low)
    out_y1 = pltpu.make_async_copy(R.y1, R.y1_out, R.osem.at[2])
    out_y1.start()
    conv.statistics(R.y1, R.mean2, R.inv2, 0, pump_low)
    conv.activate(R.y1, R.mean2, R.inv2, vec[3:4, :], vec[4:5, :], R.s2, 1, pump_low)
    out_s2 = pltpu.make_async_copy(R.s2, R.s2_out, R.osem.at[3])
    out_s2.start()
    engines[1].ready()
    out_low = pltpu.make_async_copy(R.w_low, R.bottom, R.osem.at[4])
    out_low.start()

    def emit_second(at, total):
        R.hid[at, :] = total + vec[5:6, :] + R.x[at, :].astype(F32)

    conv.convolve(R.s2, across(R.w_top, R.w_low), emit_second)
    R.store("hid")
    conv.statistics(R.hid, R.mean3, R.inv3, 1)
    conv.normalise(R.hid, R.mean3, R.inv3, vec[6:7, :], vec[7:8, :], R.u)
    for cp in conv.sent:
        cp.wait_send()
    for i, group in enumerate(groups):
        group.to_pieces(R.low, R.pieces.at[i], R.tsend.at[i], R.trecv.at[i], False)
    for cp in (out_s1, out_top, out_y1, out_s2, out_low):
        cp.wait()
    for engine in engines:
        engine.finish()


def first_call(columns, n, dims, x, ids_lane, vectors, block):
    canvases, rows, width = dims
    px = canvases * rows * width
    cells = px // UNIT
    stats = canvases * CROPS
    tall = (canvases, rows + 2, width)
    half = block.shape[0] // 2
    dma = pltpu.SemaphoreType.DMA
    inputs = dict(x=(x, LOAD), ids_lane=(ids_lane, vmem), vectors=(vectors, vmem), block=(block, vmem))
    cell = ((cells, C), F32, vmem)
    outputs = dict(
        vec=((16, C), F32, vmem), pick=((stats, cells), B16, vmem), spread=((cells, stats), B16, vmem),
        ids_all=((n,) + ids_lane.shape, F32, vmem), mean1=cell, inv1=cell, div=((stats, LANES), F32, vmem),
        cnt=((stats, LANES), F32, vmem), cnt_all=((n, stats, LANES), F32, vmem), col_l=(tall + (LANES,), F32, STORE), col_r=(tall + (LANES,), F32, STORE),
        row_u=((px, LANES), F32, STORE), row_d=((px, LANES), F32, STORE), hid=((px, C), F32, STORE),
        u=((px, C), B16, vmem), mean2=cell, inv2=cell, mean3=cell, inv3=cell, y1_out=((px, C), F32, anyw),
        s1_out=(tall + (3 * C,), B16, anyw), s2_out=(tall + (3 * C,), B16, anyw),
        top=((11 * C, C), B16, anyw), bottom=((11 * C, C), B16, anyw))
    scratch = dict(
        ids_px=pltpu.VMEM(dims + (LANES,), F32), hot=pltpu.VMEM((cells, LANES), F32),
        y1=pltpu.VMEM((px, C), F32), s1=pltpu.VMEM(tall + (3 * C,), B16), s2=pltpu.VMEM(tall + (3 * C,), B16),
        w_top=pltpu.VMEM((11 * C, C), B16), w_low=pltpu.VMEM((11 * C, C), B16), low=pltpu.VMEM(block.shape, B16),
        pieces=pltpu.VMEM((2, half, C), B16), tsend=dma((2, 2)), trecv=dma((2, 1)),
        gather0=gather_pieces_scratch(columns, n), gather1=gather_pieces_scratch(columns, n),
        layout=layout_scratch(n, dims, ids_lane), halo=pltpu.VMEM((2, 2, canvases, width, C), B16),
        buf=pltpu.VMEM((2, n, stats // 2, LANES), F32), tmp_a=pltpu.VMEM((cells, C), F32),
        tmp_b=pltpu.VMEM((cells, C), F32), send=dma((2, n)), recv=dma((2, n)), hsend=dma((2, 2)),
        hrecv=dma((2, 2)), osem=dma((5,)))
    return named_call(functools.partial(first_kernel, columns, n, dims), "first_forward", 1, inputs, outputs, scratch)


class Backer:
    def __init__(self, n, dims, R):
        self.n, self.dims, self.R = n, dims, R
        self.px = dims[0] * dims[1] * dims[2]
        self.cells = self.px // UNIT
        self.sent = []

    @staticmethod
    def pixels(i):
        return pl.ds(i * 16 * UNIT, 16 * UNIT)

    def norm_sums(self, grad_of, source, mean, inv, gain, rnd):
        R = self.R

        def body(i, carry):
            dg, db = carry
            at = self.pixels(i)
            unit = (source[at, :].astype(F32) - over_cells(mean, i)) * over_cells(inv, i)
            d = grad_of(i, unit)
            R.norm[at, :] = unit
            e = d * gain
            R.part[at, :] = e
            cross = d * unit
            here = pl.ds(i * 16, 16)
            R.tmp_a[here, :] = jnp.sum(e.reshape(16, UNIT, C), axis=1)
            R.tmp_b[here, :] = jnp.sum((cross * gain).reshape(16, UNIT, C), axis=1)
            return (dg + jnp.sum(cross, axis=0, keepdims=True), db + jnp.sum(d, axis=0, keepdims=True))

        zero = jnp.zeros((1, C), F32)
        dg, db = lax.fori_loop(0, self.cells // 16, body, (zero, zero))
        R.buf[rnd, 0] = fold(pack([group_totals(R.pick, R.tmp_a[...]), group_totals(R.pick, R.tmp_b[...])]))
        copies = spread_copies(self.n, R.buf, R.send, R.recv, rnd)
        for cp in copies:
            cp.start()
        self.sent = self.sent + copies
        return copies, dg, db

    def norm_finish(self, copies, rnd, inv, emit):
        R = self.R
        for cp in copies:
            cp.wait_recv()
        gathered = unfold(jnp.sum(R.buf[rnd], axis=0)) / R.div[...]
        R.tmp_a[...] = split_dot(R.spread[...], unpack(gathered))
        R.tmp_b[...] = split_dot(R.spread[...], unpack(shift_down(gathered, 1)))

        def body(i, _):
            at = self.pixels(i)
            emit(i, over_cells(inv, i) * (
                R.part[at, :] - over_cells(R.tmp_a, i) - R.norm[at, :] * over_cells(R.tmp_b, i)))
            return 0

        lax.fori_loop(0, self.cells // 16, body, 0)

    def send_rows(self, source, rnd):
        R = self.R
        canvases, rows, width = self.dims

        def one(v, r):
            at = pl.ds(pl.multiple_of((v * rows + r) * width, width), width)
            R.d3[v, r + 1] = shift_columns(source[at, :].astype(F32), R.col_l[v, r + 1], R.col_r[v, r + 1])

        def edges(v, _):
            one(v, 0)
            one(v, rows - 1)
            return 0

        lax.fori_loop(0, canvases, edges, 0)
        mid = pl.ds(C, C)
        up, down = halo_copies(self.n, R.d3.at[:, 1, :, mid], R.d3.at[:, rows, :, mid], R.halo.at[rnd],
                               R.hsend.at[rnd], R.hrecv.at[rnd])
        start_halo(self.n, up, down)

        def inner(i, _):
            one(i // (rows - 2), 1 + lax.rem(i, rows - 2))
            return 0

        if rows > 2:
            lax.fori_loop(0, canvases * (rows - 2), inner, 0)
        return up, down

    def finish_rows(self, up, down, rnd):
        R = self.R
        canvases, rows, _ = self.dims
        wait_halo(self.n, up, down, R.halo.at[rnd], 0.0)
        for v in range(canvases):
            for side, r in ((0, 0), (1, rows + 1)):
                R.d3[v, r] = shift_columns(R.halo[rnd, side, v].astype(F32), R.col_l[v, r], R.col_r[v, r])

    def convolve_back(self, weights, pump=no_pump):
        R = self.R
        canvases, rows, width = self.dims
        plane = rows * width
        nt = (((1,), (1,)), ((), ()))
        for v in range(canvases):
            at = pl.ds(v * plane, plane)
            total = None
            for dr in (1, 0, 2):
                acc = None
                for dc in range(3):
                    ref, row = weights(3 * (2 - dr) + (2 - dc))
                    lhs = R.d3[v, dr : dr + rows, :, dc * C : (dc + 1) * C].reshape(plane, C)
                    term = lax.dot_general(lhs, ref[row : row + C, :], nt, preferred_element_type=F32)
                    acc = term if acc is None else acc + term
                if dr == 0:
                    acc = acc * wide(R.row_u[at, :])
                if dr == 2:
                    acc = acc * wide(R.row_d[at, :])
                total = acc if total is None else total + acc
                pump()
            R.part[at, :] = total

    def mask_rows(self, source):
        R = self.R

        def body(i, _):
            at = self.pixels(i)
            value = source[at, :].astype(F32)
            R.low_u[at, :] = (value * wide(R.row_u[at, :])).astype(B16)
            R.low_d[at, :] = (value * wide(R.row_d[at, :])).astype(B16)
            return 0

        lax.fori_loop(0, self.cells // 16, body, 0)

    def weight_grad(self, s, grad, dest, pump=no_pump):
        R = self.R
        canvases, rows, width = self.dims
        plane = rows * width
        tn = (((0,), (0,)), ((), ()))
        for dr, source in ((0, R.low_u), (1, grad), (2, R.low_d)):
            for dc in range(3):
                acc = None
                for v in range(canvases):
                    lhs = s[v, dr : dr + rows, :, dc * C : (dc + 1) * C].reshape(plane, C)
                    term = lax.dot_general(
                        lhs, source[v * plane : (v + 1) * plane, :], tn, preferred_element_type=F32)
                    acc = term if acc is None else acc + term
                ref, row = dest(3 * dr + dc)
                ref[row : row + C, :] = acc.astype(B16)
                pump()


def back_kernel(columns, n, dims, R):
    g = Grid(columns, n)
    half = R.sum_low.shape[0]
    group = Group(g, 1, half)
    load_s = pltpu.make_async_copy(R.s2, R.s, R.lsem.at[0])
    load_s.start()
    load_k = second_matrix(R.top, R.bottom, R.k, R.ksem)
    load_att = pltpu.make_async_copy(R.datt, R.g_low.at[pl.ds(7 * C, 4 * C)], R.lsem.at[1])
    for cp in load_k + [load_att]:
        cp.start()
    greet_all(g)
    vec = R.vec
    back = Backer(n, dims, R)
    R.need("du", "hid")
    copies, dg3, db3 = back.norm_sums(lambda i, unit: R.du[back.pixels(i), :], R.hid, R.mean3, R.inv3, vec[6:7, :], 0)

    def emit_hidden(i, value):
        at = back.pixels(i)
        total = R.cot[at, :].astype(F32) + value
        R.dh[at, :] = total
        R.grad[at, :] = total.astype(B16)

    R.need("cot", "col_l", "col_r", "row_u", "row_d")
    back.norm_finish(copies, 0, R.inv3, emit_hidden)
    R.store("dh")
    up, down = back.send_rows(R.grad, 0)
    plane = dims[1] * dims[2]
    o_back = remote(R.o.at[pl.ds(plane, plane)], R.o_back, R.lsem.at[2], R.lsem.at[3],
                    {CANVAS: g.c, HEIGHT: lax.rem(g.h + n // 2, n)})
    o_back.start()
    back.mask_rows(R.grad)
    load_s.wait()

    def dest_two(tap):
        return (R.g_top, (9 + tap) * C) if tap < 2 else (R.g_low, (tap - 2) * C)

    back.weight_grad(R.s, R.grad, dest_two)
    load_att.wait()
    R.store("g_top", 9 * C, 2 * C)
    load_s = pltpu.make_async_copy(R.s1, R.s, R.lsem.at[0])
    load_s.start()
    engine = Engine(reduce_pieces(group, R.g_low, R.sum_low, *R.reduce))
    engine.pump()
    dc2 = jnp.sum(R.grad[...].astype(F32), axis=0, keepdims=True)
    back.finish_rows(up, down, 0)
    for cp in load_k:
        cp.wait()
    back.convolve_back(lambda tap: (R.k, tap * C), engine.pump)
    gain2, bias2 = vec[3:4, :], vec[4:5, :]

    def grad_two(i, unit):
        return R.part[back.pixels(i), :] * silu_slope(unit * gain2 + bias2)

    R.need("y1")
    copies, dg2, db2 = back.norm_sums(grad_two, R.y1, R.mean2, R.inv2, gain2, 1)
    engine.pump(2)

    def emit_grad(i, value):
        R.grad[back.pixels(i), :] = value.astype(B16)

    back.norm_finish(copies, 1, R.inv2, emit_grad)
    R.store("grad")
    engine.pump(2)
    back.mask_rows(R.grad)
    dc1 = jnp.sum(R.grad[...].astype(F32), axis=0, keepdims=True)
    load_s.wait()
    taps = []

    def after_tap():
        R.store("g_top", len(taps) * C, C)
        taps.append(None)
        engine.pump()

    back.weight_grad(R.s, R.grad, lambda tap: (R.g_top, tap * C), after_tap)
    R.dvec[...] = jnp.concatenate([dc1, dg2, db2, dc2, dg3, db3, jnp.zeros((2, C), F32)], axis=0)
    engine.ready()
    engine.finish()
    for cp in back.sent:
        cp.wait_send()
    o_back.wait()


def back_call(columns, n, dims, cot, du, hid, y1, norms, s1, s2, pick, spread, div, masks, vec, top, bottom, datt, o,
              block_rows):
    canvases, rows, width = dims
    px = canvases * rows * width
    cells = px // UNIT
    stats = canvases * CROPS
    dma = pltpu.SemaphoreType.DMA
    names = ("mean2", "inv2", "mean3", "inv3")
    inputs = dict(du=(du, LOAD), hid=(hid, LOAD), cot=(cot, LOAD),
                  **{k: (v, LOAD) for k, v in zip(("col_l", "col_r", "row_u", "row_d"), masks)}, y1=(y1, LOAD), s1=(s1, anyw), s2=(s2, anyw),
                  pick=(pick, vmem), spread=(spread, vmem), div=(div, vmem), vec=(vec, vmem), top=(top, anyw),
                  bottom=(bottom, anyw), datt=(datt, anyw), o=(o, anyw),
                  **{k: (v, vmem) for k, v in zip(names, norms)})
    outputs = dict(dh=((px, C), F32, STORE), grad=((px, C), B16, STORE), g_top=((11 * C, C), B16, STORE),
                   dvec=((8, C), F32, vmem), sum_low=((block_rows // 2, C), B16, vmem),
                   o_back=((px // canvases, C), B16, anyw))
    scratch = dict(
        g_low=pltpu.VMEM((11 * C, C), B16), s=pltpu.VMEM(s1.shape, B16), k=pltpu.VMEM((9 * C, C), B16),
        d3=pltpu.VMEM(s1.shape, B16), low_u=pltpu.VMEM((px, C), B16), low_d=pltpu.VMEM((px, C), B16),
        part=pltpu.VMEM((px, C), F32), norm=pltpu.VMEM((px, C), F32),
        halo=pltpu.VMEM((1, 2, canvases, width, C), B16), buf=pltpu.VMEM((2, n, stats // 2, LANES), F32),
        tmp_a=pltpu.VMEM((cells, C), F32), tmp_b=pltpu.VMEM((cells, C), F32),
        reduce=reduce_pieces_scratch(columns, n, block_rows // 2),
        lsem=dma((5,)), ksem=dma((3,)),
        send=dma((2, n)), recv=dma((2, n)), hsend=dma((1, 2)), hrecv=dma((1, 2)))
    return named_call(functools.partial(back_kernel, columns, n, dims), "back", 7, inputs, outputs, scratch)


def renew_kernel(columns, n, dims, R):
    g = Grid(columns, n)
    half = R.fresh.shape[0] // 2
    upper, lower = Group(g, 0, half), Group(g, 1, half)
    load_g = pltpu.make_async_copy(R.g_in, R.g_top, R.ksem.at[1])
    load_g.start()
    load_k = pltpu.make_async_copy(R.top.at[pl.ds(0, 9 * C)], R.k, R.ksem.at[0])
    load_k.start()
    loads = [
        pltpu.make_async_copy(src, dst, R.ksem.at[2 + i])
        for i, (src, dst) in enumerate(((R.w, R.new_w), (R.m, R.new_m), (R.v, R.new_s), (R.dh, R.igrad)))
    ]
    for cp in loads:
        cp.start()
    piece_loads = []
    for i, src in enumerate((R.w, R.m, R.v)):
        here = pltpu.make_async_copy(src.at[pl.ds(0, half)], R.piece_in.at[i], R.psem.at[i])
        there = pltpu.make_async_copy(R.shares.at[i], R.piece_in.at[i], R.psem.at[i])
        pl.when(g.c == 0)(here.start)
        pl.when(g.c != 0)(there.start)
        piece_loads.append(there)
    greet_all(g)
    vec = R.vec
    lower.to_owner(R.sum_low, R.totals.at[1], R.asend.at[1], R.arecv.at[1], True)
    load_g.wait()
    reducer = Engine(reduce_pieces(upper, R.g_top, R.sum_top, *R.reduce))
    reducer.pump()
    back = Backer(n, dims, R)
    R.need("grad", "col_l", "col_r", "row_u", "row_d")
    up, down = back.send_rows(R.grad, 0)
    reducer.pump(2)
    R.need("x")
    for cp in loads:
        cp.wait()

    def adam(group, totals):
        @pl.when(group.is_owner)
        def _():
            total = totals[...].astype(F32)
            next_w, R.new_m[...], R.new_s[...] = adam_update(
                R.new_w[...], total, R.new_m[...], R.new_s[...], matrix_rate)
            R.new_w[...] = next_w
            R.fresh[...] = next_w.astype(B16)

    lower.block_arrived(R.sum_low, R.totals.at[1], R.asend.at[1], R.arecv.at[1])
    adam(lower, R.totals.at[1])
    lower.to_pieces(R.fresh, R.pieces.at[1], R.tsend.at[1], R.trecv.at[1], True)
    reducer.pump(2)
    back.finish_rows(up, down, 0)
    load_k.wait()
    back.convolve_back(lambda tap: (R.k, tap * C), reducer.pump)
    gain1, bias1 = vec[0:1, :], vec[1:2, :]

    def grad_one(i, unit):
        return R.part[back.pixels(i), :] * silu_slope(unit * gain1 + bias1)

    copies, dg1, db1 = back.norm_sums(grad_one, R.x, R.mean1, R.inv1, gain1, 0)
    reducer.pump(2)
    R.vbuf[g.h] = jnp.concatenate([dg1, db1, R.dvec[0:6, :], R.dvec_att[...]], axis=0)
    vector_sends = [
        remote(R.vbuf.at[g.h], R.vbuf.at[g.h], R.vsend.at[d], R.vrecv.at[g.h],
               {CANVAS: g.c, HEIGHT: lax.rem(g.h + d, n)})
        for d in range(1, n)
    ]
    for cp in vector_sends:
        cp.start()
    lower.piece_arrived(R.fresh, R.pieces.at[1], R.tsend.at[1], R.trecv.at[1])
    gather_low = Engine(gather_pieces(lower, R.pieces.at[1], R.new_low, *R.gather1))
    gather_low.pump()
    reducer.ready()
    for cp in piece_loads:
        cp.wait()
    next_piece, _, _ = adam_update(
        R.piece_in[0], R.sum_top[...].astype(F32), R.piece_in[1], R.piece_in[2], matrix_rate)
    R.pieces[0] = next_piece.astype(B16)
    gather_top = Engine(gather_pieces(upper, R.pieces.at[0], R.new_top, *R.gather0))
    gather_top.pump()
    upper.to_owner(R.sum_top, R.totals.at[0], R.asend.at[0], R.arecv.at[0], True)

    def emit_input(i, value):
        at = back.pixels(i)
        R.igrad[at, :] = R.igrad[at, :] + value

    back.norm_finish(copies, 0, R.inv1, emit_input)
    R.store("igrad")
    gather_top.pump()
    for d in range(1, n):
        src = lax.rem(g.h + d, n)
        remote(R.vbuf.at[src], R.vbuf.at[src], R.vsend.at[d], R.vrecv.at[src],
               {CANVAS: g.c, HEIGHT: src}).wait_recv()
    R.vtrade[0, 0] = jnp.sum(R.vbuf[...], axis=0)

    def trade(k):
        return remote(R.vtrade.at[k, 0], R.vtrade.at[k, 1], R.qsend.at[k], R.qrecv.at[k], g.mate(k))

    trade(0).start()
    gather_top.pump()
    for k in range(g.phases):
        trade(k).wait_recv()
        R.vtrade[k + 1, 0] = R.vtrade[k, 0] + R.vtrade[k, 1]
        if k + 1 < g.phases:
            trade(k + 1).start()
        gather_top.pump()
    count = R.vw.shape[0]
    R.new_vw[...], R.new_vm[...], R.new_vs[...] = adam_update(
        R.vw[...], R.vtrade[g.phases, 0][0:count, :], R.vm[...], R.vs[...], vector_rate)
    R.new_vec[...] = jnp.zeros(R.new_vec.shape, F32)
    R.new_vec[0:count, :] = R.new_vw[...].astype(B16).astype(F32)
    new_vec, s1, y1 = R.new_vec, R.d3, R.part
    conv = Convolver(n, dims, R.x, R.pick, R.spread, R.cnt, R.col_l, R.col_r, R.row_u, R.row_d, R.chalo, R.cbuf,
                     R.tmp_a, R.tmp_b, R.csend, R.crecv, R.chsend, R.chrecv, R.cnt_all)
    conv.activate(R.x, R.mean1, R.inv1, new_vec[0:1, :], new_vec[1:2, :], s1, 0, gather_top.pump)
    gather_top.ready()
    pump = gather_low.pump
    pump()

    def emit_first(at, total):
        y1[at, :] = total + new_vec[2:3, :]

    conv.convolve(s1, lambda dr: [(0, 3 * C, R.new_top, 3 * C * dr)], emit_first, pump)
    conv.statistics(y1, R.mean2, R.inv2, 0, pump)
    conv.activate(y1, R.mean2, R.inv2, new_vec[3:4, :], new_vec[4:5, :], R.s2, 1, pump)
    gather_low.ready()
    out_att = pltpu.make_async_copy(R.new_low.at[pl.ds(7 * C, 4 * C)], R.new_att, R.ksem.at[0])
    out_att.start()

    def emit_second(at, total):
        R.hid[at, :] = total + new_vec[5:6, :] + R.x[at, :].astype(F32)

    conv.convolve(R.s2, across(R.new_top, R.new_low), emit_second)
    R.store("hid")
    upper.block_arrived(R.sum_top, R.totals.at[0], R.asend.at[0], R.arecv.at[0])
    adam(upper, R.totals.at[0])
    for k in ("new_w", "new_m", "new_s"):
        R.store(k)
    conv.statistics(R.hid, R.mean2, R.inv2, 1)
    conv.normalise(R.hid, R.mean2, R.inv2, new_vec[6:7, :], new_vec[7:8, :], R.u)
    for engine in (gather_low, gather_top, reducer):
        engine.finish()
    for cp in back.sent + conv.sent + vector_sends:
        cp.wait_send()
    for k in range(g.phases):
        trade(k).wait_send()
    for i, group in enumerate((upper, lower)):
        group.to_owner((R.sum_top, R.sum_low)[i], R.totals.at[i], R.asend.at[i], R.arecv.at[i], False)
    lower.to_pieces(R.fresh, R.pieces.at[1], R.tsend.at[1], R.trecv.at[1], False)
    out_att.wait()


def renew_call(columns, n, dims, grad, dh, x, mean1, inv1, pick, spread, div, cnt, cnt_all, masks, vec, top, g_top, sum_low,
               dvec, dvec_att, w, m, v, shares, vw, vm, vs):
    canvases, rows, width = dims
    px = canvases * rows * width
    cells = px // UNIT
    stats = canvases * CROPS
    block = w.shape
    half = block[0] // 2
    seats, phases = n // 2, columns.bit_length() - 1
    dma = pltpu.SemaphoreType.DMA
    tall = (canvases, rows + 2, width, 3 * C)
    arrays = dict(mean1=mean1, inv1=inv1, pick=pick, spread=spread, div=div, cnt=cnt, cnt_all=cnt_all, vec=vec,
                  sum_low=sum_low, dvec=dvec, dvec_att=dvec_att, vw=vw, vm=vm, vs=vs)
    inputs = dict(grad=(grad, LOAD),
                  **{k: (a, LOAD) for k, a in zip(("col_l", "col_r", "row_u", "row_d"), masks)}, x=(x, LOAD),
                  top=(top, anyw), g_in=(g_top, anyw), w=(w, anyw), m=(m, anyw), v=(v, anyw), shares=(shares, anyw), dh=(dh, anyw),
                  **{k: (a, vmem) for k, a in arrays.items()})
    outputs = dict(igrad=((px, C), F32, STORE), new_w=(block, F32, STORE), new_m=(block, F32, STORE),
                   new_s=(block, F32, STORE), new_vw=(vw.shape, F32, vmem), new_vm=(vw.shape, F32, vmem),
                   new_vs=(vw.shape, F32, vmem), new_vec=((16, C), F32, vmem), hid=((px, C), F32, STORE),
                   u=((px, C), B16, vmem), new_att=((4 * C, C), B16, anyw))
    scratch = dict(
        g_top=pltpu.VMEM((11 * C, C), B16), sum_top=pltpu.VMEM((half, C), B16), totals=pltpu.VMEM((2,) + block, B16),
        new_top=pltpu.VMEM((11 * C, C), B16), new_low=pltpu.VMEM((11 * C, C), B16),
        fresh=pltpu.VMEM(block, B16), pieces=pltpu.VMEM((2, half, C), B16), k=pltpu.VMEM((9 * C, C), B16),
        d3=pltpu.VMEM(tall, B16), s2=pltpu.VMEM(tall, B16), part=pltpu.VMEM((px, C), F32),
        norm=pltpu.VMEM((px, C), F32), mean2=pltpu.VMEM((cells, C), F32), inv2=pltpu.VMEM((cells, C), F32),
        halo=pltpu.VMEM((1, 2, canvases, width, C), B16), chalo=pltpu.VMEM((2, 2, canvases, width, C), B16),
        buf=pltpu.VMEM((1, n, stats // 2, LANES), F32), cbuf=pltpu.VMEM((2, n, stats // 2, LANES), F32),
        tmp_a=pltpu.VMEM((cells, C), F32), tmp_b=pltpu.VMEM((cells, C), F32),
        vbuf=pltpu.VMEM((n, 16, C), F32), vtrade=pltpu.VMEM((phases + 1, 2, 16, C), F32),
        reduce=reduce_pieces_scratch(columns, n, half), gather0=gather_pieces_scratch(columns, n),
        gather1=gather_pieces_scratch(columns, n),
        piece_in=pltpu.VMEM((3, half, C), F32), psem=dma((3,)), ksem=dma((6,)), asend=dma((2, 1)), arecv=dma((2, 2)),
        tsend=dma((2, 2)), trecv=dma((2, 1)), vsend=dma((n,)), vrecv=dma((n,)), qsend=dma((phases,)),
        qrecv=dma((phases,)), send=dma((1, n)), recv=dma((1, n)), hsend=dma((1, 2)), hrecv=dma((1, 2)),
        csend=dma((2, n)), crecv=dma((2, n)), chsend=dma((2, 2)), chrecv=dma((2, 2)))
    return named_call(functools.partial(renew_kernel, columns, n, dims), "renew", 9, inputs, outputs, scratch)


def attend_kernel(n, keep, R):
    me = lax.axis_index(HEIGHT)
    half = n // 2
    mine = me // half
    base = mine * half
    core = lax.rem(me, 2)
    partner = lax.rem(me + half, n)
    sibling = other_core(me)
    mates = half // 2
    seat = (me - base) // 2
    seg = R.u.shape[1]
    total = n * seg
    scale = C ** (-0.5)
    nt = (((1,), (1,)), ((), ()))
    tn = (((0,), (0,)), ((), ()))
    vec = R.vec

    def mate(j, c=core):
        return base + c + 2 * lax.rem(seat + j, mates)

    def far_of(b):
        return lax.rem(b + half, n)

    def to(h):
        return {CANVAS: lax.axis_index(CANVAS), HEIGHT: h}

    loads = [pltpu.make_async_copy(R.low.at[pl.ds(R.low.shape[0] - 4 * C, 4 * C)], R.w, R.lsem.at[0])]
    if keep:
        loads.append(pltpu.make_async_copy(R.cot.at[mine], R.dz.at[pl.ds(0, seg)], R.lsem.at[1]))
    for cp in loads:
        cp.start()
    own = pltpu.make_async_copy(R.u_in.at[mine], R.u.at[me], R.lsem.at[3])
    own.start()
    barrier = pltpu.get_barrier_semaphore()
    peers = [to(p) for p in [partner, sibling] + [mate(j) for j in range(1, mates)]]
    column = lax.axis_index(CANVAS)
    if keep:
        peers += [{CANVAS: lax.rem(column + d, 4), HEIGHT: me} for d in range(1, 4)]
    for p in peers:
        pl.semaphore_signal(barrier, inc=1, device_id=p, device_id_type=MESH)
    pl.semaphore_wait(barrier, len(peers))
    started = []

    def share(from_column, half_number, to_column, begin):
        rows = R.shares.shape[1]
        for i, src in enumerate((R.params, R.first, R.second)):
            cp = remote(src.at[pl.ds(half_number * rows, rows)], R.shares.at[i], R.wsend.at[half_number, i],
                        R.wrecv.at[i], {CANVAS: to_column, HEIGHT: me})
            if begin:
                pl.when(column == from_column)(cp.start)
            else:
                pl.when(column == from_column)(cp.wait_send)
                pl.when(column == to_column)(cp.wait_recv)

    moves = ((0, 1, 1), (1, 0, 2), (1, 1, 3))
    if keep:
        for move in moves:
            share(*move, True)

    def push(src, slot, dest):
        cp = remote(src, R.u.at[slot], R.gsend.at[len(started)], R.grecv.at[slot], to(dest))
        cp.start()
        started.append(cp)

    def block(b):
        return pl.ds(pl.multiple_of(b * seg, seg), seg)

    def project(b):
        piece = R.u[b]
        R.k[block(b), :] = jnp.dot(piece, R.w[C : 2 * C, :], preferred_element_type=F32).astype(B16)
        R.v[block(b), :] = (
            jnp.dot(piece, R.w[2 * C : 3 * C, :], preferred_element_type=F32) + vec[9:10, :]
        ).astype(B16)

    def arrived(slot):
        remote(R.u_in.at[0], R.u.at[slot], R.gsend.at[0], R.grecv.at[slot], to(partner)).wait_recv()

    push(R.u_in.at[1 - mine], me, partner)
    for j in range(1, mates):
        push(R.u_in.at[mine], me, mate(j))
    push(R.u_in.at[mine], me, sibling)
    for cp in loads:
        cp.wait()
    own.wait()
    project(me)
    arrived(sibling)
    project(sibling)
    key_ids = jnp.concatenate([R.ids_all[b, pl.ds(mine, 1), :] for b in range(n)], axis=1)
    order = (me, partner) if keep else (partner, me)
    first_far = 1 if keep else 0
    far_rows, own_rows = pl.ds(first_far * seg, seg), pl.ds((1 - first_far) * seg, seg)
    for i, b in enumerate(order):
        turned = jnp.transpose(R.ids_all[b])
        picked = jnp.where(mine == 0, turned[:, 0:1], turned[:, 1:2])
        R.qid[i * seg : (i + 1) * seg, :] = jnp.broadcast_to(picked, (seg, LANES))
    arrived(partner)
    for j in range(1, mates):
        push(R.u.at[partner], partner, mate(j))
    push(R.u.at[partner], partner, sibling)
    project(partner)
    for j in range(1, mates):
        friend = mate(mates - j)
        arrived(friend)
        push(R.u.at[friend], friend, sibling)
        project(friend)
    arrived(far_of(sibling))
    project(far_of(sibling))
    for j in range(1, mates):
        friend = far_of(mate(mates - j))
        arrived(friend)
        push(R.u.at[friend], friend, sibling)
        project(friend)
    for j in range(1, mates):
        friend = mate(mates - j, 1 - core)
        arrived(friend)
        project(friend)
        arrived(far_of(friend))
        project(far_of(friend))

    rows = R.rows
    per = seg // rows

    def swap_cot(i):
        here = pl.ds(pl.multiple_of(i * rows, rows), rows)
        there = pl.ds(pl.multiple_of(seg + i * rows, rows), rows)
        return remote(R.cot.at[1 - mine, here], R.dz.at[there], R.csend.at[i], R.crecv.at[i], to(partner))

    if keep:
        for i in range(per):
            swap_cot(i).start()
    o_home = R.o_home

    def far_out(i):
        here = pl.ds(pl.multiple_of(i * rows, rows), rows)
        return remote(R.out.at[here], o_home.at[mine, here], R.osend.at[i], R.orecv.at[i], to(partner))

    def attend(i, _):
        at = pl.ds(pl.multiple_of(i * rows, rows), rows)
        b = jnp.where(i < per, order[0], order[1])
        if keep:
            @pl.when(i >= per)
            def _():
                swap_cot(i - per).wait_recv()

        uq = R.u[b, pl.ds(pl.multiple_of(lax.rem(i, per) * rows, rows), rows), :]
        qb = (jnp.dot(uq, R.w[0:C, :], preferred_element_type=F32) + vec[8:9, :]).astype(B16)
        s = lax.dot_general(qb, R.k[...], nt, preferred_element_type=F32) * scale
        s = jnp.where(R.qid[at, :][:, :1] == key_ids, s, mask_fill)
        e = jnp.exp(s - jnp.max(s, axis=1, keepdims=True))
        p = e * (1.0 / jnp.sum(e, axis=1, keepdims=True))
        pb = p.astype(B16)
        R.out[at, :] = jnp.dot(pb, R.v[...], preferred_element_type=F32).astype(B16)
        if keep:
            R.pbuf[at, :] = pb
            R.q[at, :] = qb
            dout = lax.dot_general(
                R.dz[at, :], R.w[3 * C : 4 * C, :], nt, preferred_element_type=F32).astype(B16)
            R.dout[at, :] = dout
            dp = lax.dot_general(dout, R.v[...], nt, preferred_element_type=F32)
            delta = jnp.sum(p * dp, axis=1, keepdims=True)
            ds = (p * (dp - delta)).astype(B16)
            R.sbuf[at, :] = ds
            R.dq[at, :] = (jnp.dot(ds, R.k[...], preferred_element_type=F32) * scale).astype(B16)

        if not keep:
            @pl.when(i < per)
            def _():
                far_out(i).start()

        return 0

    lax.fori_loop(0, 2 * per, attend, 0)
    if not keep:
        own_out = pltpu.make_async_copy(R.out.at[own_rows], o_home.at[mine], R.lsem.at[2])
        own_out.start()
        own_out.wait()
        for i in range(per):
            far_out(i).wait()
        for cp in started:
            cp.wait_send()
        return
    all_out = pltpu.make_async_copy(R.out, o_home, R.lsem.at[2])
    all_out.start()
    zero = jnp.zeros((C, C), F32)
    pairs = 2 * mates

    def du_of(b, carry):
        dwk, dwv, dbv = carry
        at = block(b)
        dk = (lax.dot_general(R.sbuf[:, at], R.q[...], tn, preferred_element_type=F32) * scale).astype(B16)
        dvf = lax.dot_general(R.pbuf[:, at], R.dout[...], tn, preferred_element_type=F32)
        dv = dvf.astype(B16)
        du = lax.dot_general(dk, R.w[C : 2 * C, :], nt, preferred_element_type=F32)
        du = du + lax.dot_general(dv, R.w[2 * C : 3 * C, :], nt, preferred_element_type=F32)
        piece = R.u[b]
        dwk = dwk + lax.dot_general(piece, dk, tn, preferred_element_type=F32)
        dwv = dwv + lax.dot_general(piece, dv, tn, preferred_element_type=F32)
        return du, (dwk, dwv, dbv + jnp.sum(dvf, axis=0, keepdims=True))

    def place(t):
        far = 1 - t // mates
        return lax.rem(lax.rem(t, mates) + 1, mates), far

    def sib_copy(t):
        return remote(R.for_sib.at[t], R.from_sib.at[t], R.ssend.at[t], R.srecv.at[t], to(sibling))

    def mate_copy(t, part):
        j, _ = place(t)
        here = pl.ds(part * (seg // 2), seg // 2)
        return remote(R.sums.at[t, here], R.from_mate.at[t, here], R.msend.at[t, part], R.mrecv.at[t, part],
                      to(mate(j)))

    def home_copy(part):
        here = pl.ds(part * (seg // 2), seg // 2)
        return remote(R.for_home.at[here], R.from_partner.at[here], R.hsend.at[part], R.hrecv.at[part], to(partner))

    def gathered(far, part):
        count = seg // 2
        at = pl.ds((first_far if far else 1 - first_far) * seg + part * count, count)
        here = pl.ds(part * count, count)
        value = lax.dot_general(R.dq[at, :], R.w[0:C, :], nt, preferred_element_type=F32)
        first_t = 0 if far else mates
        value = value + R.sums[first_t + mates - 1, here, :].astype(F32)
        for t in range(first_t, first_t + mates - 1):
            mate_copy(t, part).wait_recv()
            value = value + R.from_mate[t, here, :].astype(F32)
        return value

    def send_home(part):
        R.for_home[pl.ds(part * (seg // 2), seg // 2), :] = gathered(1, part).astype(B16)
        home_copy(part).start()

    def back(t, carry):
        j, far = place(t)
        theirs, ours = mate(j, 1 - core), mate(j)
        du, carry = du_of(lax.rem(theirs + far * half, n), carry)
        R.for_sib[t] = du.astype(B16)
        sib_copy(t).start()
        du, carry = du_of(lax.rem(ours + far * half, n), carry)
        sib_copy(t).wait_recv()
        R.sums[t] = (du + R.from_sib[t].astype(F32)).astype(B16)

        @pl.when(j != 0)
        def _():
            for part in range(2):
                mate_copy(t, part).start()

        @pl.when(t == pairs - 2)
        def _():
            send_home(0)

        return carry

    dwk, dwv, dbv = lax.fori_loop(0, pairs, back, (zero, zero, jnp.zeros((1, C), F32)))
    send_home(1)
    for part in range(2):
        R.du[mine, pl.ds(part * (seg // 2), seg // 2), :] = gathered(0, part)
    R.dw[C : 2 * C, :] = dwk.astype(B16)
    R.dw[2 * C : 3 * C, :] = dwv.astype(B16)
    R.dw[3 * C : 4 * C, :] = lax.dot_general(
        R.out[...], R.dz[...], tn, preferred_element_type=F32).astype(B16)
    dwq = lax.dot_general(R.u[partner], R.dq[far_rows, :], tn, preferred_element_type=F32)
    dwq = dwq + lax.dot_general(R.u[me], R.dq[own_rows, :], tn, preferred_element_type=F32)
    R.dw[0:C, :] = dwq.astype(B16)
    R.store("dw")
    R.dvec[...] = jnp.concatenate(
        [
            jnp.sum(R.dq[...].astype(F32), axis=0, keepdims=True),
            dbv,
            jnp.sum(R.dz[...].astype(F32), axis=0, keepdims=True),
            jnp.zeros((5, C), F32),
        ],
        axis=0,
    )
    for part in range(2):
        home_copy(part).wait()
    R.du[1 - mine] = R.from_partner[...].astype(F32)
    for move in moves:
        share(*move, False)
    all_out.wait()
    for i in range(per):
        swap_cot(i).wait_send()
    for cp in started:
        cp.wait_send()

    def drain(t, _):
        sib_copy(t).wait_send()

        @pl.when(place(t)[0] != 0)
        def _():
            for part in range(2):
                mate_copy(t, part).wait_send()

        return 0

    lax.fori_loop(0, pairs, drain, 0)


def attend_call(n, keep, cid, u, ids_all, vec, low, cot=None, state=None):
    seg = u.shape[1]
    half = n // 2
    mates = half // 2
    pairs = 2 * mates
    total = n * seg
    rows = min(256, seg)
    dma = pltpu.SemaphoreType.DMA
    inputs = dict(u_in=(u, anyw), ids_all=(ids_all, vmem), vec=(vec, vmem), low=(low, anyw))
    piece = (seg, C)
    home = (2,) + piece
    scratch = dict(
        u=pltpu.VMEM((n,) + piece, B16), w=pltpu.VMEM((4 * C, C), B16), k=pltpu.VMEM((total, C), B16),
        v=pltpu.VMEM((total, C), B16), qid=pltpu.VMEM((2 * seg, LANES), F32), out=pltpu.VMEM((2 * seg, C), B16),
        lsem=dma((4,)), gsend=dma((4 * mates,)), grecv=dma((n,)))
    if keep:
        inputs.update(cot=(cot, anyw), **{k: (a, anyw) for k, a in zip(("params", "first", "second"), state)})
        outputs = dict(o_home=((2 * seg, C), B16, anyw), dw=((4 * C, C), B16, STORE), dvec=((8, C), F32, vmem),
                       du=(home, F32, vmem), shares=((3, state[0].shape[0] // 2, C), F32, anyw))
        scratch.update(
            csend=dma((seg // rows,)), crecv=dma((seg // rows,)), dz=pltpu.VMEM((2 * seg, C), B16), dout=pltpu.VMEM((2 * seg, C), B16), q=pltpu.VMEM((2 * seg, C), B16),
            dq=pltpu.VMEM((2 * seg, C), B16), pbuf=pltpu.VMEM((2 * seg, total), B16),
            sbuf=pltpu.VMEM((2 * seg, total), B16), for_sib=pltpu.VMEM((pairs,) + piece, B16),
            from_sib=pltpu.VMEM((pairs,) + piece, B16), sums=pltpu.VMEM((pairs,) + piece, B16),
            from_mate=pltpu.VMEM((pairs - 1,) + piece, B16), for_home=pltpu.VMEM(piece, B16),
            from_partner=pltpu.VMEM(piece, B16), ssend=dma((pairs,)), srecv=dma((pairs,)), msend=dma((pairs, 2)),
            mrecv=dma((pairs, 2)), hsend=dma((2,)), hrecv=dma((2,)), wsend=dma((2, 3)), wrecv=dma((3,)))
    else:
        outputs = dict(o_home=(home, B16, anyw))
        scratch.update(osend=dma((seg // rows,)), orecv=dma((seg // rows,)))

    def kernel(R):
        R.rows = rows
        attend_kernel(n, keep, R)

    return named_call(kernel, "attend" if keep else "attend_again", cid, inputs, outputs, scratch)


def outputs_kernel(n, R):
    mine = lax.axis_index(HEIGHT) // (n // 2)
    seg = R.o_back.shape[0]
    own, other = (pl.ds(pl.multiple_of(i * seg, seg), seg) for i in (mine, 1 - mine))
    loads = [
        pltpu.make_async_copy(R.low.at[pl.ds(R.low.shape[0] - C, C)], R.w.at[0], R.sem.at[0]),
        pltpu.make_async_copy(R.o.at[pl.ds(0, seg)], R.o_in.at[0, own], R.sem.at[1]),
        pltpu.make_async_copy(R.o_back, R.o_in.at[0, other], R.sem.at[2]),
        pltpu.make_async_copy(R.new_low.at[pl.ds(R.new_low.shape[0] - C, C)], R.w.at[1], R.sem.at[3]),
        pltpu.make_async_copy(R.o2, R.o_in.at[1], R.sem.at[4]),
    ]
    for cp in loads:
        cp.start()
    count = R.part.shape[2]
    parts = R.hid.shape[0] // count
    bases = {}
    for which, src in enumerate((R.hid, R.hid2, R.igrad)):
        for i in range(parts):
            at = pl.ds(i * count, count)
            bases[which, i] = pltpu.make_async_copy(src.at[at], R.held.at[which, at], R.hsem.at[which, i])
            bases[which, i].start()
    ends = []

    def out(src, dst, sem):
        cp = pltpu.make_async_copy(src, dst, sem)
        cp.start()
        ends.append(cp)

    for cp in loads[:3]:
        cp.wait()
    for which, (vec, dst) in enumerate(((R.vec, R.first), (R.new_vec, R.second))):
        if which == 1:
            for cp in loads[3:]:
                cp.wait()
        for i in range(parts):
            at = pl.ds(i * count, count)
            bases[which, i].wait()
            if which == 0:
                out(R.held.at[0, at], R.hid_out.at[at], R.osem.at[0, i])
            R.part[which, i] = (
                R.held[which, at, :]
                + jnp.dot(R.o_in[which, at, :], R.w[which], preferred_element_type=F32) + vec[10:11, :])
            out(R.part.at[which, i], dst.at[at], R.osem.at[1 + which, i])
    for i in range(parts):
        at = pl.ds(i * count, count)
        bases[2, i].wait()
        out(R.held.at[2, at], R.igrad_out.at[at], R.osem.at[3, i])
    for cp in ends:
        cp.wait()


def outputs_call(n, hid, hid2, o, o_back, o2, igrad, vec, new_vec, low, new_low):
    px = hid.shape[0]
    inputs = dict(hid=(hid, anyw), hid2=(hid2, anyw), o=(o, anyw), o_back=(o_back, anyw), o2=(o2, anyw),
                  igrad=(igrad, anyw),
                  vec=(vec, vmem), new_vec=(new_vec, vmem), low=(low, anyw), new_low=(new_low, anyw))
    whole = ((px, C), F32, anyw)
    outputs = dict(hid_out=whole, first=whole, second=whole, igrad_out=whole)
    count = min(256, px)
    parts = px // count
    dma = pltpu.SemaphoreType.DMA
    scratch = dict(
        w=pltpu.VMEM((2, C, C), B16), held=pltpu.VMEM((3, px, C), F32), o_in=pltpu.VMEM((2, px, C), B16),
        part=pltpu.VMEM((2, parts, count, C), F32), sem=dma((5,)), hsem=dma((3, parts)), osem=dma((4, parts)))
    return named_call(functools.partial(outputs_kernel, n), "outputs", None, inputs, outputs, scratch)


def rounded_vectors(vectors):
    return lax.reduce_precision(vectors, exponent_bits=8, mantissa_bits=7)


def body(columns, n, latents, crop_ids, params, vectors, first_moment, second_moment, vector_first, vector_second,
         cotangent):
    canvases, rows, width, channels = latents.shape
    dims = (canvases, rows, width)
    px = canvases * rows * width
    plane = rows * width
    half = n // 2
    me = lax.axis_index(HEIGHT)
    mine = me // half
    partner = lax.rem(me + half, n)
    swap = [(i, (i + half) % n) for i in range(n)]
    count = vectors.shape[0]
    joined = columns == 4 and params.shape[0] % 32 == 0 and rows > 2

    ids = crop_ids.astype(F32)
    ids_lane = jnp.pad(ids.reshape(canvases, plane), ((0, 8 - canvases), (0, 0)))
    x = latents.reshape(px, channels)
    cot = cotangent.reshape(px, channels)
    cot3 = cotangent.reshape(canvases, plane, channels)
    shape = latents.shape
    if joined:
        first = first_call(columns, n, dims, x, ids_lane, vectors, params)
        ids_all, mean1, inv1, div, cnt, pick, spread, vec = (
            first[k] for k in ("ids_all", "mean1", "inv1", "div", "cnt", "pick", "spread", "vec"))
        masks = [first[k] for k in ("col_l", "col_r", "row_u", "row_d")]
        hid, u, y1, s1, s2 = (first[k] for k in ("hid", "u", "y1_out", "s1_out", "s2_out"))
        norms = [first[k] for k in ("mean2", "inv2", "mean3", "inv3")]
        top, low = first["top"], first["bottom"]
        att = attend_call(n, True, 4, u.reshape(canvases, plane, channels), ids_all, vec, low, cot3,
                          (params, first_moment, second_moment))
        du = att["du"].reshape(px, channels)
        back = back_call(columns, n, dims, cot, du, hid, y1, norms, s1, s2, pick, spread, div, masks, vec, top, low,
                         att["dw"], att["o_home"], params.shape[0])
        new = renew_call(columns, n, dims, back["grad"], back["dh"], x, mean1, inv1, pick, spread, div, cnt, first["cnt_all"],
                         masks, vec, top, back["g_top"], back["sum_low"], back["dvec"], att["dvec"], params, first_moment,
                         second_moment, att["shares"], vectors, vector_first, vector_second)
        new_vec, new_att = new["new_vec"], new["new_att"]
        o2 = attend_call(n, False, 5, new["u"].reshape(canvases, plane, channels), ids_all, new_vec, new_att)["o_home"]
        last = outputs_call(n, hid, new["hid"], att["o_home"], back["o_back"], o2.reshape(px, channels), new["igrad"],
                            vec, new_vec, low, new_att)
        return (
            *(last[k].reshape(shape) for k in ("hid_out", "first", "second", "igrad_out")),
            *(new[k] for k in ("new_w", "new_m", "new_s", "new_vw", "new_vm", "new_vs")),
        )

    def padded(value):
        return jnp.pad(value, ((0, 16 - count), (0, 0)))

    wide_vectors = padded(vectors)
    vec = rounded_vectors(wide_vectors)
    cell_ids = crop_ids[:, :, ::UNIT] + CROPS * jnp.arange(canvases, dtype=jnp.int32)[:, None, None]
    cell_ids = cell_ids.reshape(1, -1)
    stat = jnp.arange(canvases * CROPS, dtype=jnp.int32)[:, None]
    pick = (cell_ids == stat).astype(B16)
    spread = (cell_ids.reshape(-1, 1) == stat.reshape(1, -1)).astype(B16)
    ids_px = jnp.broadcast_to(ids[..., None], (canvases, rows, width, LANES))
    whole = spread_call(columns, n, 8, params).reshape(-1, channels)
    top, low = whole[: 11 * C], whole[11 * C :]
    ids_all, mean1, inv1, div, cnt, *masks = layout_call(n, dims, x, pick, spread, ids_px, ids_lane)
    hid, u, y1, s1, s2, mean2, inv2, mean3, inv3 = resnet_forward_call(
        n, dims, True, x, pick, spread, cnt, mean1, inv1, masks, vec, top, low)
    own_cot = lax.dynamic_index_in_dim(cot3, mine, axis=0, keepdims=False)
    far_cot = lax.ppermute(
        lax.dynamic_index_in_dim(cot3, 1 - mine, axis=0, keepdims=False), HEIGHT, swap)
    dz = jnp.concatenate([own_cot, far_cot], axis=0)
    canvas_ids = lax.dynamic_index_in_dim(ids_all, mine, axis=1, keepdims=False)
    key_ids = canvas_ids.reshape(1, n * plane)
    query_ids = jnp.stack([canvas_ids[me], canvas_ids[partner]]).reshape(2 * plane, 1)
    query_ids = jnp.broadcast_to(query_ids, (2 * plane, LANES))
    offsets = jnp.stack([me, partner]) * plane

    def attention_output(o, hid, low, bias):
        back = lax.ppermute(o[plane:], HEIGHT, swap)
        ordered = jnp.where(mine == 0, jnp.stack([o[:plane], back]), jnp.stack([back, o[:plane]]))
        product = jnp.dot(ordered.reshape(px, channels), low[10 * C :], preferred_element_type=F32)
        return hid + product + bias

    ua = gather_call(n, 4, u.reshape(canvases, plane, channels))
    o, dup, dw_att, dvec_att = attention_call(True, ua, key_ids, query_ids, offsets, dz, vec, low)
    first_output = attention_output(o, hid, low, vec[10])
    du = scatter_call(n, 6, dup.reshape(n, plane, channels)).reshape(px, channels)
    norms = (mean1, inv1, mean2, inv2, mean3, inv3)
    input_grad, matrix_grad, dvec = resnet_backward_call(
        n, dims, 7, cot, du, hid, y1, x, norms, s1, s2, pick, spread, div, masks, vec, top, low, dw_att)
    vector_grad = jnp.concatenate([dvec, dvec_att], axis=0)
    new_params, new_first, new_second, *new_small, new_whole = step_call(
        columns, n, 9, matrix_grad.reshape((columns, half, 2) + params.shape), params, first_moment,
        second_moment, vector_grad, wide_vectors, padded(vector_first), padded(vector_second))
    new_whole = new_whole.reshape(-1, channels)
    new_top, new_low = new_whole[: 11 * C], new_whole[11 * C :]
    new_vec = rounded_vectors(new_small[0])
    hid2, u2 = resnet_forward_call(
        n, dims, False, x, pick, spread, cnt, mean1, inv1, masks, new_vec, new_top, new_low)
    ua2 = gather_call(n, 5, u2.reshape(canvases, plane, channels))
    (o2,) = attention_call(False, ua2, key_ids, query_ids, offsets, dz, new_vec, new_low)
    second_output = attention_output(o2, hid2, new_low, new_vec[10])
    return (
        *(a.reshape(shape) for a in (hid, first_output, second_output, input_grad)),
        new_params,
        new_first,
        new_second,
        *(a[:count] for a in new_small),
    )


def solution(mesh):
    spatial = P(CANVAS, HEIGHT, None, None)
    owned = P((CANVAS, HEIGHT), None)
    return jax.shard_map(
        functools.partial(body, mesh.shape[CANVAS], mesh.shape[HEIGHT]),
        mesh=mesh,
        in_specs=(spatial, P(CANVAS, HEIGHT, None), owned, P(), owned, owned, P(), P(), spatial),
        out_specs=(spatial, spatial, spatial, spatial, owned, owned, owned, P(), P(), P()),
        check_vma=False,
    )
```

```python
import functools

import jax
import jax.numpy as jnp
from jax import lax
from jax.experimental import pallas as pl
from jax.experimental.pallas import tpu as pltpu
from jax.sharding import PartitionSpec as P

C = 512
GROUPS = 32
STEP = 5
CROPS = 16
SPAN = C // GROUPS
LANES = 128
TILES = C // LANES
UNIT = 8

norm_epsilon = 1e-06
adam_epsilon = 1e-08
matrix_rate = 0.015
vector_rate = 0.2
mask_fill = -1e30

HEIGHT = "height"
CANVAS = "canvas"
LOAD = "load"
STORE = "store"

F32 = jnp.float32
B16 = jnp.bfloat16
MESH = pl.DeviceIdType.MESH
VMEM_LIMIT = 60 * 2**20

vmem = pl.BlockSpec(memory_space=pltpu.VMEM)
smem = pl.BlockSpec(memory_space=pltpu.SMEM)
anyw = pl.BlockSpec(memory_space=pl.ANY)


def params_of(cid=None):
    if cid is None:
        return pltpu.CompilerParams(vmem_limit_bytes=VMEM_LIMIT)
    return pltpu.CompilerParams(
        vmem_limit_bytes=VMEM_LIMIT, collective_id=cid, has_side_effects=True
    )


def sds(shape, dtype):
    return jax.ShapeDtypeStruct(shape, dtype)


def split_dot(pick, value):
    total = None
    rest = value
    for _ in range(3):
        part = rest.astype(B16)
        term = jnp.dot(pick, part, preferred_element_type=F32)
        total = term if total is None else total + term
        rest = rest - part.astype(F32)
    return total


def lane_group_sum(piece):
    lane = lax.broadcasted_iota(jnp.int32, piece.shape, 1)
    step = 1
    while step < SPAN:
        ahead = pltpu.roll(piece, LANES - step, 1)
        behind = pltpu.roll(piece, step, 1)
        piece = piece + jnp.where((lane & step) == 0, ahead, behind)
        step *= 2
    return piece


def tiles_of(value):
    return [value[:, j * LANES : (j + 1) * LANES] for j in range(TILES)]


def wide(piece, times=TILES):
    return jnp.concatenate([piece] * times, axis=1)


def pack(quantities):
    shape = quantities[0][0].shape
    sub = lax.broadcasted_iota(jnp.int32, shape, 1) & (SPAN - 1)
    out = jnp.zeros(shape, F32)
    for q, pieces in enumerate(quantities):
        for j, piece in enumerate(pieces):
            out = jnp.where(sub == TILES * q + j, piece, out)
    return out


def unpack(packed):
    sub = lax.broadcasted_iota(jnp.int32, packed.shape, 1) & (SPAN - 1)
    return jnp.concatenate(
        [lane_group_sum(jnp.where(sub == j, packed, 0.0)) for j in range(TILES)], axis=1
    )


def shift_down(packed, q):
    return pltpu.roll(packed, LANES - TILES * q, packed.ndim - 1)


def no_pump():
    return None


def fold(packed):
    rows = packed.shape[0] // 2
    sub = lax.broadcasted_iota(jnp.int32, (rows, LANES), 1) & (SPAN - 1)
    return jnp.where(sub < 2 * TILES, packed[:rows], pltpu.roll(packed[rows:], 2 * TILES, 1))


def unfold(folded):
    return jnp.concatenate([folded, pltpu.roll(folded, LANES - 2 * TILES, folded.ndim - 1)], axis=folded.ndim - 2)


def greet(n):
    me = lax.axis_index(HEIGHT)
    barrier = pltpu.get_barrier_semaphore()
    for d in range(1, n):
        pl.semaphore_signal(
            barrier, inc=1, device_id={HEIGHT: lax.rem(me + d, n)}, device_id_type=MESH
        )
    pl.semaphore_wait(barrier, n - 1)


def spread_copies(n, buf, send, recv, rnd):
    me = lax.axis_index(HEIGHT)
    return [
        pltpu.make_async_remote_copy(
            src_ref=buf.at[rnd, 0],
            dst_ref=buf.at[rnd, d],
            send_sem=send.at[rnd, d],
            recv_sem=recv.at[rnd, d],
            device_id={HEIGHT: lax.rem(me + d, n)},
            device_id_type=MESH,
        )
        for d in sorted(range(1, n), key=lambda d: abs(d - n // 2))
    ]


def cell_totals(load, out_ref, cells):
    def body(i, _):
        out_ref[pl.ds(i * 16, 16), :] = jnp.sum(load(i).reshape(16, UNIT, C), axis=1)
        return 0

    lax.fori_loop(0, cells // 16, body, 0)


def over_cells(cell_ref, i):
    return jnp.broadcast_to(cell_ref[pl.ds(i * 16, 16), :][:, None, :], (16, UNIT, C)).reshape(
        16 * UNIT, C
    )


def group_totals(pick_ref, cell_value):
    return [lane_group_sum(t) for t in tiles_of(split_dot(pick_ref[...], cell_value))]


def stats_payload(load, pick_ref, spread_ref, count_ref, cells, tmp_a, tmp_b, counted=True):
    cell_totals(load, tmp_a, cells)
    sums = group_totals(pick_ref, tmp_a[...])
    count = count_ref[...]
    inv_count = 1.0 / jnp.maximum(count, 1.0)
    mean = jnp.concatenate([s * inv_count for s in sums], axis=1)
    tmp_b[...] = split_dot(spread_ref[...], mean)

    def centred(i):
        delta = load(i) - over_cells(tmp_b, i)
        return delta * delta

    cell_totals(centred, tmp_a, cells)
    squares = group_totals(pick_ref, tmp_a[...])
    return pack([sums, squares, [count] * TILES]) if counted else fold(pack([sums, squares]))


def combine_stats(gathered, counts=None):
    sums = gathered
    squares = shift_down(gathered, 1)
    counts = shift_down(gathered, 2) if counts is None else counts
    divisor = jnp.maximum(jnp.sum(counts, axis=0), 1.0)
    mean = jnp.sum(sums, axis=0) / divisor
    apart = sums / jnp.maximum(counts, 1.0) - mean[None]
    spread = jnp.sum(squares + counts * apart * apart, axis=0) / divisor
    return mean, lax.rsqrt(spread + norm_epsilon), divisor


def shift_columns(row, left_mask, right_mask):
    width = row.shape[0]
    left = pltpu.roll(row, 1, 0) * wide(left_mask)
    right = pltpu.roll(row, width - 1, 0) * wide(right_mask)
    return jnp.concatenate([left, row, right], axis=1).astype(B16)


def logistic(a):
    return 1.0 / (1.0 + jnp.exp(-a))


def silu(a):
    return a * logistic(a)


def silu_slope(a):
    s = logistic(a)
    return s * (1.0 + a * (1.0 - s))


def layout_kernel(n, dims, x, pick, spread, ids_px, ids_lane, ids_all, mean_c, inv_c, div, cnt,
                  col_l, col_r, row_u, row_d, *scratch):
    greet(n)
    layout_body(n, dims, x, pick, spread, ids_px, ids_lane, ids_all, mean_c, inv_c, div, cnt,
                col_l, col_r, row_u, row_d, *scratch)


def layout_body(n, dims, x, pick, spread, ids_px, ids_lane, ids_all, mean_c, inv_c, div, cnt,
                col_l, col_r, row_u, row_d, buf, idbuf, halo, tmp_a, tmp_b, send, recv, isend, irecv,
                hsend, hrecv, pump=no_pump, cnt_all=None):
    canvases, rows, width = dims
    cells = canvases * rows * width // UNIT
    me = lax.axis_index(HEIGHT)
    id_copies = []
    idbuf[0] = ids_lane[...]
    for d in range(1, n):
        cp = pltpu.make_async_remote_copy(
            src_ref=idbuf.at[0], dst_ref=idbuf.at[d], send_sem=isend.at[d], recv_sem=irecv.at[d],
            device_id={HEIGHT: lax.rem(me + d, n)}, device_id_type=MESH)
        cp.start()
        id_copies.append(cp)
    up, down = halo_copies(n, ids_px.at[:, 0], ids_px.at[:, rows - 1], halo, hsend, hrecv)
    start_halo(n, up, down)

    def load(i):
        return x[pl.ds(i * 16 * UNIT, 16 * UNIT), :].astype(F32)

    ones = jnp.sum(pick[...].astype(F32), axis=1, keepdims=True) * float(UNIT * SPAN)
    cnt[...] = jnp.broadcast_to(ones, cnt.shape)
    buf[0, 0] = stats_payload(load, pick, spread, cnt, cells, tmp_a, tmp_b)
    copies = spread_copies(n, buf, send, recv, 0)
    for cp in copies:
        cp.start()
    pump()
    wait_halo(n, up, down, halo, -1.0)
    column = lax.broadcasted_iota(jnp.int32, (width, LANES), 0)
    first, last = column == 0, column == width - 1
    for v in range(canvases):
        for r in range(rows + 2):
            here = halo[0, v] if r == 0 else halo[1, v] if r == rows + 1 else ids_px[v, r - 1]
            same_l = (pltpu.roll(here, 1, 0) == here) & jnp.logical_not(first)
            same_r = (pltpu.roll(here, width - 1, 0) == here) & jnp.logical_not(last)
            col_l[v, r] = same_l.astype(F32)
            col_r[v, r] = same_r.astype(F32)
            if 1 <= r <= rows:
                above = halo[0, v] if r == 1 else ids_px[v, r - 2]
                below = halo[1, v] if r == rows else ids_px[v, r]
                at = pl.ds((v * rows + r - 1) * width, width)
                row_u[at, :] = (above == here).astype(F32)
                row_d[at, :] = (below == here).astype(F32)
    pump()
    for cp in copies:
        cp.wait_recv()
    mean, inv, divisor = combine_stats(buf[0])
    if cnt_all is not None:
        cnt_all[...] = shift_down(buf[0], 2)
    mean_c[...] = split_dot(spread[...], unpack(mean))
    inv_c[...] = split_dot(spread[...], unpack(inv))
    div[...] = unpack(divisor)[:, :LANES]
    for cp in id_copies:
        cp.wait_recv()
    ids_all[me] = idbuf[0]
    for d in range(1, n):
        ids_all[lax.rem(me - d + n, n)] = idbuf[d]
    for cp in copies + id_copies:
        cp.wait_send()


def halo_copies(n, first_row, last_row, halo, hsend, hrecv):
    me = lax.axis_index(HEIGHT)
    up = pltpu.make_async_remote_copy(
        src_ref=first_row, dst_ref=halo.at[1], send_sem=hsend.at[0], recv_sem=hrecv.at[1],
        device_id={HEIGHT: lax.rem(me + n - 1, n)}, device_id_type=MESH)
    down = pltpu.make_async_remote_copy(
        src_ref=last_row, dst_ref=halo.at[0], send_sem=hsend.at[1], recv_sem=hrecv.at[0],
        device_id={HEIGHT: lax.rem(me + 1, n)}, device_id_type=MESH)
    return up, down


def start_halo(n, up, down):
    me = lax.axis_index(HEIGHT)

    @pl.when(me > 0)
    def _():
        up.start()

    @pl.when(me < n - 1)
    def _():
        down.start()


def wait_halo(n, up, down, halo, edge):
    me = lax.axis_index(HEIGHT)

    @pl.when(me > 0)
    def _():
        up.wait_send()
        down.wait_recv()

    @pl.when(me < n - 1)
    def _():
        down.wait_send()
        up.wait_recv()

    @pl.when(me == 0)
    def _():
        halo[0] = jnp.full(halo.shape[1:], edge, halo.dtype)

    @pl.when(me == n - 1)
    def _():
        halo[1] = jnp.full(halo.shape[1:], edge, halo.dtype)


def layout_scratch(n, dims, ids_lane):
    canvases, rows, width = dims
    cells = canvases * rows * width // UNIT
    return [
        pltpu.VMEM((1, n, canvases * CROPS, LANES), F32),
        pltpu.VMEM((n,) + ids_lane.shape, F32),
        pltpu.VMEM((2, canvases, width, LANES), F32),
        pltpu.VMEM((cells, C), F32),
        pltpu.VMEM((cells, C), F32),
        pltpu.SemaphoreType.DMA((1, n)),
        pltpu.SemaphoreType.DMA((1, n)),
        pltpu.SemaphoreType.DMA((n,)),
        pltpu.SemaphoreType.DMA((n,)),
        pltpu.SemaphoreType.DMA((2,)),
        pltpu.SemaphoreType.DMA((2,)),
    ]


def layout_call(n, dims, x, pick, spread, ids_px, ids_lane):
    canvases, rows, width = dims
    px = canvases * rows * width
    cells = px // UNIT
    stats = canvases * CROPS
    return pl.pallas_call(
        functools.partial(layout_kernel, n, dims),
        out_shape=[
            sds((n,) + ids_lane.shape, F32),
            sds((cells, C), F32),
            sds((cells, C), F32),
            sds((stats, LANES), F32),
            sds((stats, LANES), F32),
            sds((canvases, rows + 2, width, LANES), F32),
            sds((canvases, rows + 2, width, LANES), F32),
            sds((px, LANES), F32),
            sds((px, LANES), F32),
        ],
        in_specs=[vmem] * 5,
        out_specs=[vmem] * 9,
        scratch_shapes=layout_scratch(n, dims, ids_lane),
        compiler_params=params_of(1),
        name="layout",
    )(x, pick, spread, ids_px, ids_lane)


def second_matrix(top, low, dest, sem):
    return [
        pltpu.make_async_copy(top.at[pl.ds(9 * C, 2 * C)], dest.at[pl.ds(0, 2 * C)], sem.at[1]),
        pltpu.make_async_copy(low.at[pl.ds(0, 7 * C)], dest.at[pl.ds(2 * C, 7 * C)], sem.at[2]),
    ]


class Convolver:
    def __init__(self, n, dims, x, pick, spread, cnt, col_l, col_r, row_u, row_d, halo, buf, tmp_a, tmp_b, send,
                 recv, hsend, hrecv, cnt_all=None):
        self.n, self.dims, self.cnt_all = n, dims, cnt_all
        self.x, self.pick, self.spread, self.cnt = x, pick, spread, cnt
        self.col_l, self.col_r, self.row_u, self.row_d = col_l, col_r, row_u, row_d
        self.halo, self.buf, self.tmp_a, self.tmp_b = halo, buf, tmp_a, tmp_b
        self.send, self.recv, self.hsend, self.hrecv = send, recv, hsend, hrecv
        self.px = dims[0] * dims[1] * dims[2]
        self.cells = self.px // UNIT
        self.sent = []

    def activate(self, source, mean, inv, gain, bias, dest, rnd, pump=no_pump):
        canvases, rows, width = self.dims
        row_cells = width // UNIT
        col_l, col_r, halo = self.col_l, self.col_r, self.halo

        def one(v, r):
            at = pl.ds(pl.multiple_of((v * rows + r) * width, width), width)
            cell = pl.ds(pl.multiple_of((v * rows + r) * row_cells, row_cells), row_cells)
            value = source[at, :].astype(F32)
            m = jnp.broadcast_to(mean[cell, :][:, None, :], (row_cells, UNIT, C)).reshape(width, C)
            s = jnp.broadcast_to(inv[cell, :][:, None, :], (row_cells, UNIT, C)).reshape(width, C)
            a = (value - m) * s * gain + bias
            dest[v, r + 1] = shift_columns(silu(a), col_l[v, r + 1], col_r[v, r + 1])

        def edges(v, _):
            one(v, 0)
            if rows > 1:
                one(v, rows - 1)
            return 0

        lax.fori_loop(0, canvases, edges, 0)
        mid = pl.ds(C, C)
        up, down = halo_copies(self.n, dest.at[:, 1, :, mid], dest.at[:, rows, :, mid], halo.at[rnd],
                               self.hsend.at[rnd], self.hrecv.at[rnd])
        start_halo(self.n, up, down)
        pump()

        def inner(i, _):
            one(i // (rows - 2), 1 + lax.rem(i, rows - 2))
            return 0

        if rows > 2:
            lax.fori_loop(0, canvases * (rows - 2), inner, 0)
        pump()
        wait_halo(self.n, up, down, halo.at[rnd], 0.0)
        for v in range(canvases):
            for side, r in ((0, 0), (1, rows + 1)):
                dest[v, r] = shift_columns(halo[rnd, side, v].astype(F32), col_l[v, r], col_r[v, r])

    def convolve(self, source, weights, emit, pump=no_pump):
        canvases, rows, width = self.dims
        plane = rows * width
        for v in range(canvases):
            at = pl.ds(v * plane, plane)
            total = None
            for dr in (1, 0, 2):
                part = None
                for lo, hi, ref, row in weights(dr):
                    lhs = source[v, dr : dr + rows, :, lo:hi].reshape(plane, hi - lo)
                    term = jnp.dot(lhs, ref[row : row + hi - lo, :], preferred_element_type=F32)
                    part = term if part is None else part + term
                if dr == 0:
                    part = part * wide(self.row_u[at, :])
                if dr == 2:
                    part = part * wide(self.row_d[at, :])
                total = part if total is None else total + part
            emit(at, total)
            pump()

    def statistics(self, source, mean, inv, rnd, pump=no_pump):
        def load(i):
            return source[pl.ds(i * 16 * UNIT, 16 * UNIT), :]

        counted = self.cnt_all is None
        self.buf[rnd, 0] = stats_payload(
            load, self.pick, self.spread, self.cnt, self.cells, self.tmp_a, self.tmp_b, counted)
        copies = spread_copies(self.n, self.buf, self.send, self.recv, rnd)
        for cp in copies:
            cp.start()
        pump()
        for cp in copies:
            cp.wait_recv()
        m, s, _ = (
            combine_stats(self.buf[rnd]) if counted else combine_stats(unfold(self.buf[rnd]), self.cnt_all[...]))
        mean[...] = split_dot(self.spread[...], unpack(m))
        inv[...] = split_dot(self.spread[...], unpack(s))
        self.sent = self.sent + copies

    def normalise(self, source, mean, inv, gain, bias, dest):
        def last(i, _):
            at = pl.ds(i * 16 * UNIT, 16 * UNIT)
            value = (source[at, :] - over_cells(mean, i)) * over_cells(inv, i)
            dest[at, :] = (value * gain + bias).astype(B16)
            return 0

        lax.fori_loop(0, self.cells // 16, last, 0)


def resnet_forward_kernel(n, dims, keep, x, pick, spread, cnt, mean1, inv1, col_l, col_r, row_u, row_d,
                          vec, top, low, *refs):
    canvases, rows, width = dims
    px = canvases * rows * width
    cells = px // UNIT
    plane = rows * width
    if keep:
        hid, u, y1, s1, s2, mean2, inv2, mean3, inv3 = refs[:9]
        refs = refs[9:]
    else:
        hid, u = refs[:2]
        y1, s1, s2, mean2, inv2, mean3, inv3 = refs[2:9]
        refs = refs[9:]
    k1, k2, halo, buf, tmp_a, tmp_b, ksem, send, recv, hsend, hrecv = refs
    load1 = [pltpu.make_async_copy(top.at[pl.ds(0, 9 * C)], k1, ksem.at[0])]
    load2 = second_matrix(top, low, k2, ksem)
    for cp in load1 + load2:
        cp.start()
    greet(n)
    for_conv = Convolver(n, dims, x, pick, spread, cnt, col_l, col_r, row_u, row_d, halo, buf, tmp_a, tmp_b,
                         send, recv, hsend, hrecv)

    def wait_all(copies):
        for cp in copies:
            cp.wait()

    for_conv.activate(x, mean1, inv1, vec[0:1, :], vec[1:2, :], s1, 0)
    wait_all(load1)

    def emit_first(at, total):
        y1[at, :] = total + vec[2:3, :]

    for_conv.convolve(s1, lambda dr: [(0, 3 * C, k1, 3 * C * dr)], emit_first)
    for_conv.statistics(y1, mean2, inv2, 0)
    for_conv.activate(y1, mean2, inv2, vec[3:4, :], vec[4:5, :], s2, 1)
    wait_all(load2)

    def emit_second(at, total):
        hid[at, :] = total + vec[5:6, :] + x[at, :].astype(F32)

    for_conv.convolve(s2, lambda dr: [(0, 3 * C, k2, 3 * C * dr)], emit_second)
    for_conv.statistics(hid, mean3, inv3, 1)
    for_conv.normalise(hid, mean3, inv3, vec[6:7, :], vec[7:8, :], u)
    for cp in for_conv.sent:
        cp.wait_send()


def resnet_forward_call(n, dims, keep, x, pick, spread, cnt, mean1, inv1, masks, vec, top, low):
    canvases, rows, width = dims
    px = canvases * rows * width
    cells = px // UNIT
    stats = canvases * CROPS
    saved = [
        ((px, C), F32),
        ((canvases, rows + 2, width, 3 * C), B16),
        ((canvases, rows + 2, width, 3 * C), B16),
        ((cells, C), F32),
        ((cells, C), F32),
        ((cells, C), F32),
        ((cells, C), F32),
    ]
    main = [((px, C), F32), ((px, C), B16)]
    outs = main + (saved if keep else [])
    scratch = [] if keep else [pltpu.VMEM(*s) for s in saved]
    return pl.pallas_call(
        functools.partial(resnet_forward_kernel, n, dims, keep),
        out_shape=[sds(*s) for s in outs],
        in_specs=[vmem] * 11 + [anyw] * 2,
        out_specs=[vmem] * len(outs),
        scratch_shapes=scratch
        + [
            pltpu.VMEM((9 * C, C), B16),
            pltpu.VMEM((9 * C, C), B16),
            pltpu.VMEM((2, 2, canvases, width, C), B16),
            pltpu.VMEM((2, n, stats, LANES), F32),
            pltpu.VMEM((cells, C), F32),
            pltpu.VMEM((cells, C), F32),
            pltpu.SemaphoreType.DMA((3,)),
            pltpu.SemaphoreType.DMA((2, n)),
            pltpu.SemaphoreType.DMA((2, n)),
            pltpu.SemaphoreType.DMA((2, 2)),
            pltpu.SemaphoreType.DMA((2, 2)),
        ],
        compiler_params=params_of(2 if keep else 3),
        name="resnet_forward" if keep else "resnet_again",
    )(x, pick, spread, cnt, mean1, inv1, *masks, vec, top, low)


def attention_kernel(keep, chunk, block, ua, key_ids, query_ids, offsets, dz, vec, low, *refs):
    total = ua.shape[0] * ua.shape[1]
    queries = query_ids.shape[0]
    segment = ua.shape[1]
    scale = C ** (-0.5)
    if keep:
        out, dup, dw, dvec = refs[:4]
        u, w, k, v, pbuf, sbuf, q, dout, dq, usem, wsem = refs[4:]
    else:
        out = refs[0]
        u, w, k, v, usem, wsem = refs[1:]
    load_w = pltpu.make_async_copy(low.at[pl.ds(7 * C, 4 * C)], w, wsem.at[0])
    load_w.start()
    blocks = ua.shape[0]
    loads = [
        pltpu.make_async_copy(ua.at[i], u.at[pl.ds(i * segment, segment)], usem.at[i])
        for i in range(blocks)
    ]
    for cp in loads:
        cp.start()
    load_w.wait()
    for cp in loads:
        cp.wait()
    nt = (((1,), (1,)), ((), ()))
    tn = (((0,), (0,)), ((), ()))

    def project(i, _):
        at = pl.ds(pl.multiple_of(i * chunk, chunk), chunk)
        piece = u[at, :]
        k[at, :] = jnp.dot(piece, w[C : 2 * C, :], preferred_element_type=F32).astype(B16)
        v[at, :] = (
            jnp.dot(piece, w[2 * C : 3 * C, :], preferred_element_type=F32) + vec[9:10, :]
        ).astype(B16)
        return 0

    lax.fori_loop(0, total // chunk, project, 0)
    per = segment // block

    def place(i):
        return pl.multiple_of(offsets[i // per] + lax.rem(i, per) * block, block)

    def attend(i, _):
        at = pl.ds(pl.multiple_of(i * block, block), block)
        uq = u[pl.ds(place(i), block), :]
        qb = (
            jnp.dot(uq, w[0:C, :], preferred_element_type=F32) + vec[8:9, :]
        ).astype(B16)
        s = lax.dot_general(qb, k[...], nt, preferred_element_type=F32) * scale
        s = jnp.where(query_ids[at, :][:, :1] == key_ids[...], s, mask_fill)
        e = jnp.exp(s - jnp.max(s, axis=1, keepdims=True))
        p = e * (1.0 / jnp.sum(e, axis=1, keepdims=True))
        pb = p.astype(B16)
        ob = jnp.dot(pb, v[...], preferred_element_type=F32).astype(B16)
        out[at, :] = ob
        if keep:
            pbuf[at, :] = pb
            q[at, :] = qb
            do = lax.dot_general(
                dz[at, :], w[3 * C : 4 * C, :], nt, preferred_element_type=F32
            ).astype(B16)
            dout[at, :] = do
            dp = lax.dot_general(do, v[...], nt, preferred_element_type=F32)
            delta = jnp.sum(p * dp, axis=1, keepdims=True)
            ds = (p * (dp - delta)).astype(B16)
            sbuf[at, :] = ds
            dq[at, :] = (jnp.dot(ds, k[...], preferred_element_type=F32) * scale).astype(B16)
        return 0

    lax.fori_loop(0, queries // block, attend, 0)
    if not keep:
        return
    zero = jnp.zeros((C, C), F32)

    def back(i, carry):
        dwk, dwv, dbv = carry
        at = pl.ds(pl.multiple_of(i * chunk, chunk), chunk)
        dk = (
            lax.dot_general(sbuf[:, at], q[...], tn, preferred_element_type=F32) * scale
        ).astype(B16)
        dvf = lax.dot_general(pbuf[:, at], dout[...], tn, preferred_element_type=F32)
        dv = dvf.astype(B16)
        du = lax.dot_general(dk, w[C : 2 * C, :], nt, preferred_element_type=F32)
        du = du + lax.dot_general(dv, w[2 * C : 3 * C, :], nt, preferred_element_type=F32)
        dup[at, :] = du.astype(B16)
        piece = u[at, :]
        dwk = dwk + lax.dot_general(piece, dk, tn, preferred_element_type=F32)
        dwv = dwv + lax.dot_general(piece, dv, tn, preferred_element_type=F32)
        return dwk, dwv, dbv + jnp.sum(dvf, axis=0, keepdims=True)

    dwk, dwv, dbv = lax.fori_loop(0, total // chunk, back, (zero, zero, jnp.zeros((1, C), F32)))
    dw[C : 2 * C, :] = dwk.astype(B16)
    dw[2 * C : 3 * C, :] = dwv.astype(B16)
    dw[3 * C : 4 * C, :] = lax.dot_general(
        out[...], dz[...], tn, preferred_element_type=F32
    ).astype(B16)
    dwq = zero
    for s in range(2):
        where = pl.ds(pl.multiple_of(offsets[s], segment), segment)
        at = pl.ds(s * segment, segment)
        dwq = dwq + lax.dot_general(u[where, :], dq[at, :], tn, preferred_element_type=F32)
        du = lax.dot_general(dq[at, :], w[0:C, :], nt, preferred_element_type=F32)
        dup[where, :] = (dup[where, :].astype(F32) + du).astype(B16)
    dw[0:C, :] = dwq.astype(B16)
    dvec[...] = jnp.concatenate(
        [
            jnp.sum(dq[...].astype(F32), axis=0, keepdims=True),
            dbv,
            jnp.sum(dz[...].astype(F32), axis=0, keepdims=True),
            jnp.zeros((5, C), F32),
        ],
        axis=0,
    )


def attention_call(keep, ua, key_ids, query_ids, offsets, dz, vec, low):
    blocks, segment, _ = ua.shape
    total = blocks * segment
    queries = query_ids.shape[0]
    block = min(256, segment)
    chunk = 512
    outs = [sds((queries, C), B16)]
    scratch = [
        pltpu.VMEM((total, C), B16),
        pltpu.VMEM((4 * C, C), B16),
        pltpu.VMEM((total, C), B16),
        pltpu.VMEM((total, C), B16),
    ]
    if keep:
        outs += [sds((total, C), B16), sds((4 * C, C), B16), sds((8, C), F32)]
        scratch += [
            pltpu.VMEM((queries, total), B16),
            pltpu.VMEM((queries, total), B16),
            pltpu.VMEM((queries, C), B16),
            pltpu.VMEM((queries, C), B16),
            pltpu.VMEM((queries, C), B16),
        ]
    return pl.pallas_call(
        functools.partial(attention_kernel, keep, chunk, block),
        out_shape=outs,
        in_specs=[anyw, vmem, vmem, smem, vmem, vmem, anyw],
        out_specs=[vmem] * len(outs),
        scratch_shapes=scratch
        + [pltpu.SemaphoreType.DMA((blocks,)), pltpu.SemaphoreType.DMA((1,))],
        compiler_params=params_of(),
        name="attention" if keep else "attention_again",
    )(ua, key_ids, query_ids, offsets, dz, vec, low)


def other_core(h):
    return h + 1 - 2 * lax.rem(h, 2)


def gather_kernel(n, u, ua, lsem, send, recv):
    me = lax.axis_index(HEIGHT)
    half = n // 2
    mine = me // half
    base = mine * half
    core = lax.rem(me, 2)
    partner = lax.rem(me + half, n)
    sibling = other_core(me)
    mates = half // 2
    seat = (me - base) // 2

    def mate(j):
        return base + core + 2 * lax.rem(seat + j, mates)

    barrier = pltpu.get_barrier_semaphore()
    peers = [partner, sibling] + [mate(j) for j in range(1, mates)]
    for p in peers:
        pl.semaphore_signal(barrier, inc=1, device_id={HEIGHT: p}, device_id_type=MESH)
    pl.semaphore_wait(barrier, len(peers))
    count = [0]
    started = []

    def push(src, slot, to):
        cp = pltpu.make_async_remote_copy(
            src_ref=src, dst_ref=ua.at[slot], send_sem=send.at[count[0]], recv_sem=recv.at[slot],
            device_id={HEIGHT: to}, device_id_type=MESH)
        count[0] += 1
        cp.start()
        started.append(cp)

    def arrived(slot):
        pltpu.make_async_remote_copy(
            src_ref=u.at[0], dst_ref=ua.at[slot], send_sem=send.at[0], recv_sem=recv.at[slot],
            device_id={HEIGHT: partner}, device_id_type=MESH).wait_recv()

    own = pltpu.make_async_copy(u.at[mine], ua.at[me], lsem.at[0])
    own.start()
    push(u.at[1 - mine], me, partner)
    for j in range(1, mates):
        push(u.at[mine], me, mate(j))
    push(u.at[mine], me, sibling)
    arrived(partner)
    for j in range(1, mates):
        push(ua.at[partner], partner, mate(j))
    push(ua.at[partner], partner, sibling)
    for j in range(1, mates):
        friend = base + core + 2 * lax.rem(seat + mates - j, mates)
        far = lax.rem(friend + half, n)
        arrived(friend)
        push(ua.at[friend], friend, sibling)
        arrived(far)
        push(ua.at[far], far, sibling)
    arrived(sibling)
    arrived(lax.rem(sibling + half, n))
    for j in range(1, mates):
        friend = base + (1 - core) + 2 * lax.rem(seat + mates - j, mates)
        arrived(friend)
        arrived(lax.rem(friend + half, n))
    own.wait()
    for cp in started:
        cp.wait_send()


def gather_call(n, cid, u):
    half = n // 2
    sends = 2 * (half // 2) + 1 + 2 * (half // 2 - 1) + 1
    return pl.pallas_call(
        functools.partial(gather_kernel, n),
        out_shape=sds((n,) + u.shape[1:], B16),
        in_specs=[anyw],
        out_specs=anyw,
        scratch_shapes=[
            pltpu.SemaphoreType.DMA((1,)),
            pltpu.SemaphoreType.DMA((sends,)),
            pltpu.SemaphoreType.DMA((n,)),
        ],
        compiler_params=params_of(cid),
        name="gather_u",
    )(u)


def scatter_kernel(n, dup, out, from_sib, from_mate, mine_sum, from_partner, lsem, send, recv):
    me = lax.axis_index(HEIGHT)
    half = n // 2
    mine = me // half
    base = mine * half
    core = lax.rem(me, 2)
    partner = lax.rem(me + half, n)
    sibling = other_core(me)
    mates = half // 2
    seat = (me - base) // 2
    barrier = pltpu.get_barrier_semaphore()

    def mate(j, c=core):
        return base + c + 2 * lax.rem(seat + j, mates)

    peers = [partner, sibling] + [mate(j) for j in range(1, mates)]
    for p in peers:
        pl.semaphore_signal(barrier, inc=1, device_id={HEIGHT: p}, device_id_type=MESH)
    pl.semaphore_wait(barrier, len(peers))
    order = [(j, far) for j in range(1, mates) for far in (1, 0)] + [(0, 1), (0, 0)]

    def rows_of(j, far, c):
        owner = mate(j, c)
        return lax.rem(owner + half, n) if far else owner

    sib = []
    for t, (j, far) in enumerate(order):
        cp = pltpu.make_async_remote_copy(
            src_ref=dup.at[rows_of(j, far, 1 - core)], dst_ref=from_sib.at[t],
            send_sem=send.at[t], recv_sem=recv.at[t],
            device_id={HEIGHT: sibling}, device_id_type=MESH)
        cp.start()
        sib.append(cp)
    base_sem = len(order)
    out_copies = []
    for t, (j, far) in enumerate(order):
        sib[t].wait_recv()
        block = rows_of(j, far, core)
        if j > 0:
            mine_sum[t] = (dup[block].astype(F32) + from_sib[t].astype(F32)).astype(B16)
            at = (j - 1) * 2 + far
            cp = pltpu.make_async_remote_copy(
                src_ref=mine_sum.at[t], dst_ref=from_mate.at[at],
                send_sem=send.at[base_sem + at], recv_sem=recv.at[base_sem + at],
                device_id={HEIGHT: mate(j)}, device_id_type=MESH)
            cp.start()
            out_copies.append(cp)
    t_far, t_own = len(order) - 2, len(order) - 1
    total = dup[partner].astype(F32) + from_sib[t_far].astype(F32)
    for j in range(1, mates):
        at = (j - 1) * 2 + 1
        pltpu.make_async_remote_copy(
            src_ref=mine_sum.at[0], dst_ref=from_mate.at[at], send_sem=send.at[0],
            recv_sem=recv.at[base_sem + at], device_id={HEIGHT: sibling},
            device_id_type=MESH).wait_recv()
        total = total + from_mate[at].astype(F32)
    mine_sum[t_far] = total.astype(B16)
    last = base_sem + 2 * (mates - 1)
    home = pltpu.make_async_remote_copy(
        src_ref=mine_sum.at[t_far], dst_ref=from_partner, send_sem=send.at[last],
        recv_sem=recv.at[last], device_id={HEIGHT: partner}, device_id_type=MESH)
    home.start()
    total = dup[me].astype(F32) + from_sib[t_own].astype(F32)
    for j in range(1, mates):
        at = (j - 1) * 2
        pltpu.make_async_remote_copy(
            src_ref=mine_sum.at[0], dst_ref=from_mate.at[at], send_sem=send.at[0],
            recv_sem=recv.at[base_sem + at], device_id={HEIGHT: sibling},
            device_id_type=MESH).wait_recv()
        total = total + from_mate[at].astype(F32)
    out[mine] = total
    home.wait_recv()
    out[1 - mine] = from_partner[...].astype(F32)
    for cp in sib + out_copies + [home]:
        cp.wait_send()


def scatter_call(n, cid, dup):
    half = n // 2
    mates = half // 2
    copies = 2 * mates + 2 * (mates - 1) + 1
    seg = dup.shape[1:]
    return pl.pallas_call(
        functools.partial(scatter_kernel, n),
        out_shape=sds((2,) + seg, F32),
        in_specs=[vmem],
        out_specs=vmem,
        scratch_shapes=[
            pltpu.VMEM((2 * mates,) + seg, B16),
            pltpu.VMEM((max(2 * (mates - 1), 1),) + seg, B16),
            pltpu.VMEM((2 * mates,) + seg, B16),
            pltpu.VMEM(seg, B16),
            pltpu.SemaphoreType.DMA((1,)),
            pltpu.SemaphoreType.DMA((copies,)),
            pltpu.SemaphoreType.DMA((copies,)),
        ],
        compiler_params=params_of(cid),
        name="scatter_du",
    )(dup)


def resnet_backward_kernel(n, dims, cot, du, hid, y1, x, mean1, inv1, mean2, inv2, mean3, inv3, s1, s2, pick,
                           spread, div, col_l, col_r, row_u, row_d, vec, top, bottom, datt, igrad, grads, dvec,
                           dw1, dw2, k, dh, d3, low, low_u, low_d, part, norm, halo, buf, tmp_a, tmp_b, ksem, wsem, send,
                           recv, hsend, hrecv):
    canvases, rows, width = dims
    px = canvases * rows * width
    cells = px // UNIT
    plane = rows * width
    nt = (((1,), (1,)), ((), ()))
    tn = (((0,), (0,)), ((), ()))
    load2 = second_matrix(top, bottom, k, wsem)
    load1 = pltpu.make_async_copy(top.at[pl.ds(0, 9 * C)], k, wsem.at[0])
    for cp in load2:
        cp.start()
    out_att = pltpu.make_async_copy(datt, grads.at[pl.ds(18 * C, 4 * C)], ksem.at[2])
    out_two = pltpu.make_async_copy(dw2, grads.at[pl.ds(9 * C, 9 * C)], ksem.at[3])
    out_one = pltpu.make_async_copy(dw1, grads.at[pl.ds(0, 9 * C)], ksem.at[4])
    out_att.start()
    greet(n)
    zero_row = jnp.zeros((1, C), F32)

    def pixels(i):
        return pl.ds(i * 16 * UNIT, 16 * UNIT)

    def norm_sums(grad_of, source, mean, inv, gain):
        def body(i, carry):
            dg, db = carry
            at = pixels(i)
            unit = (source[at, :].astype(F32) - over_cells(mean, i)) * over_cells(inv, i)
            d = grad_of(i, unit)
            norm[at, :] = unit
            e = d * gain
            part[at, :] = e
            cross = d * unit
            here = pl.ds(i * 16, 16)
            tmp_a[here, :] = jnp.sum(e.reshape(16, UNIT, C), axis=1)
            tmp_b[here, :] = jnp.sum((cross * gain).reshape(16, UNIT, C), axis=1)
            return (dg + jnp.sum(cross, axis=0, keepdims=True), db + jnp.sum(d, axis=0, keepdims=True))

        dg, db = lax.fori_loop(0, cells // 16, body, (zero_row, zero_row))
        packed = pack([group_totals(pick, tmp_a[...]), group_totals(pick, tmp_b[...])])
        return packed, dg, db

    def send_sums(packed, rnd):
        buf[rnd, 0] = packed
        copies = spread_copies(n, buf, send, recv, rnd)
        for cp in copies:
            cp.start()
        return copies

    def norm_finish(copies, rnd, inv, emit):
        for cp in copies:
            cp.wait_recv()
        gathered = jnp.sum(buf[rnd], axis=0) / div[...]
        tmp_a[...] = split_dot(spread[...], unpack(gathered))
        tmp_b[...] = split_dot(spread[...], unpack(shift_down(gathered, 1)))

        def body(i, _):
            at = pixels(i)
            emit(i, over_cells(inv, i) * (part[at, :] - over_cells(tmp_a, i) - norm[at, :] * over_cells(tmp_b, i)))
            return 0

        lax.fori_loop(0, cells // 16, body, 0)

    def spread_rows(rnd):
        def row_at(v, r):
            return pl.ds(pl.multiple_of((v * rows + r) * width, width), width)

        def one(i, _):
            v, r = i // rows, lax.rem(i, rows)
            d3[v, r + 1] = shift_columns(low[row_at(v, r), :].astype(F32), col_l[v, r + 1], col_r[v, r + 1])
            return 0

        lax.fori_loop(0, canvases * rows, one, 0)
        mid = pl.ds(C, C)
        up, down = halo_copies(n, d3.at[:, 1, :, mid], d3.at[:, rows, :, mid], halo.at[rnd],
                               hsend.at[rnd], hrecv.at[rnd])
        start_halo(n, up, down)
        return up, down

    def finish_rows(up, down, rnd):
        wait_halo(n, up, down, halo.at[rnd], 0.0)
        for v in range(canvases):
            for side, r in ((0, 0), (1, rows + 1)):
                d3[v, r] = shift_columns(halo[rnd, side, v].astype(F32), col_l[v, r], col_r[v, r])

    def convolve_back(emit):
        def body(v, _):
            at = pl.ds(pl.multiple_of(v * plane, plane), plane)
            total = None
            for dr in (1, 0, 2):
                acc = None
                for dc in range(3):
                    tap = 3 * (2 - dr) + (2 - dc)
                    lhs = d3[v, dr : dr + rows, :, dc * C : (dc + 1) * C].reshape(plane, C)
                    term = lax.dot_general(lhs, k[tap * C : (tap + 1) * C, :], nt, preferred_element_type=F32)
                    acc = term if acc is None else acc + term
                if dr == 0:
                    acc = acc * wide(row_u[at, :])
                if dr == 2:
                    acc = acc * wide(row_d[at, :])
                total = acc if total is None else total + acc
            emit(at, total)
            return 0

        lax.fori_loop(0, canvases, body, 0)

    def mask_rows():
        def body(i, _):
            at = pixels(i)
            value = low[at, :].astype(F32)
            low_u[at, :] = (value * wide(row_u[at, :])).astype(B16)
            low_d[at, :] = (value * wide(row_d[at, :])).astype(B16)
            return 0

        lax.fori_loop(0, cells // 16, body, 0)

    def weight_grad(source, dest):
        for dr, grad in ((0, low_u), (1, low), (2, low_d)):
            def body(dc, _):
                acc = None
                for v in range(canvases):
                    lhs = source[v, dr : dr + rows, :, pl.ds(pl.multiple_of(dc * C, C), C)].reshape(plane, C)
                    term = lax.dot_general(
                        lhs, grad[v * plane : (v + 1) * plane, :], tn, preferred_element_type=F32)
                    acc = term if acc is None else acc + term
                dest[pl.ds(pl.multiple_of((3 * dr + dc) * C, C), C), :] = acc.astype(B16)
                return 0

            lax.fori_loop(0, 3, body, 0)

    packed, dg3, db3 = norm_sums(lambda i, unit: du[pixels(i), :], hid, mean3, inv3, vec[6:7, :])
    sent = send_sums(packed, 0)

    def emit_hidden(i, value):
        at = pixels(i)
        total = cot[at, :].astype(F32) + value
        dh[at, :] = total
        low[at, :] = total.astype(B16)

    norm_finish(sent, 0, inv3, emit_hidden)
    up, down = spread_rows(0)
    mask_rows()
    dc2 = jnp.sum(low[...].astype(F32), axis=0, keepdims=True)
    finish_rows(up, down, 0)
    for cp in load2:
        cp.wait()

    def emit_part(at, total):
        part[at, :] = total

    convolve_back(emit_part)
    load1.start()
    gain2, bias2 = vec[3:4, :], vec[4:5, :]

    def grad_two(i, unit):
        return part[pixels(i), :] * silu_slope(unit * gain2 + bias2)

    packed, dg2, db2 = norm_sums(grad_two, y1, mean2, inv2, gain2)
    more = send_sums(packed, 1)
    weight_grad(s2, dw2)
    out_two.start()

    def emit_low(i, value):
        low[pixels(i), :] = value.astype(B16)

    norm_finish(more, 1, inv2, emit_low)
    sent = sent + more
    up, down = spread_rows(1)
    mask_rows()
    dc1 = jnp.sum(low[...].astype(F32), axis=0, keepdims=True)
    weight_grad(s1, dw1)
    out_one.start()
    finish_rows(up, down, 1)
    load1.wait()
    convolve_back(emit_part)
    gain1, bias1 = vec[0:1, :], vec[1:2, :]

    def grad_one(i, unit):
        return part[pixels(i), :] * silu_slope(unit * gain1 + bias1)

    packed, dg1, db1 = norm_sums(grad_one, x, mean1, inv1, gain1)
    more = send_sums(packed, 2)
    dvec[...] = jnp.concatenate([dg1, db1, dc1, dg2, db2, dc2, dg3, db3], axis=0)

    def emit_input(i, value):
        igrad[pixels(i), :] = dh[pixels(i), :] + value

    norm_finish(more, 2, inv1, emit_input)
    sent = sent + more
    out_att.wait()
    out_two.wait()
    out_one.wait()
    for cp in sent:
        cp.wait_send()


def resnet_backward_call(n, dims, cid, cot, du, hid, y1, x, norms, s1, s2, pick, spread, div, masks, vec, top,
                         bottom, datt):
    canvases, rows, width = dims
    px = canvases * rows * width
    cells = px // UNIT
    stats = canvases * CROPS
    return pl.pallas_call(
        functools.partial(resnet_backward_kernel, n, dims),
        out_shape=[sds((px, C), F32), sds((22 * C, C), B16), sds((8, C), F32)],
        in_specs=[vmem] * 21 + [anyw] * 3,
        out_specs=[vmem, anyw, vmem],
        scratch_shapes=[
            pltpu.VMEM((9 * C, C), B16),
            pltpu.VMEM((9 * C, C), B16),
            pltpu.VMEM((9 * C, C), B16),
            pltpu.VMEM((px, C), F32),
            pltpu.VMEM((canvases, rows + 2, width, 3 * C), B16),
            pltpu.VMEM((px, C), B16),
            pltpu.VMEM((px, C), B16),
            pltpu.VMEM((px, C), B16),
            pltpu.VMEM((px, C), F32),
            pltpu.VMEM((px, C), F32),
            pltpu.VMEM((2, 2, canvases, width, C), B16),
            pltpu.VMEM((3, n, stats, LANES), F32),
            pltpu.VMEM((cells, C), F32),
            pltpu.VMEM((cells, C), F32),
            pltpu.SemaphoreType.DMA((5,)),
            pltpu.SemaphoreType.DMA((3,)),
            pltpu.SemaphoreType.DMA((3, n)),
            pltpu.SemaphoreType.DMA((3, n)),
            pltpu.SemaphoreType.DMA((2, 2)),
            pltpu.SemaphoreType.DMA((2, 2)),
        ],
        compiler_params=params_of(cid),
        name="resnet_backward",
    )(cot, du, hid, y1, x, *norms, s1, s2, pick, spread, div, *masks, vec, top, bottom, datt)


class Grid:
    def __init__(self, columns, n):
        self.columns, self.n, self.seats = columns, n, n // 2
        self.phases = columns.bit_length() - 1
        self.c = lax.axis_index(CANVAS)
        self.h = lax.axis_index(HEIGHT)
        self.seat, self.core = self.h // 2, lax.rem(self.h, 2)
        flips = [
            (1 - 2 * lax.rem(self.c // 2**t, 2)) * 2**t for t in range(self.phases)
        ]
        last = self.phases - 1
        self.flips = [
            (1 - self.core) * flips[last - k] + self.core * flips[k] for k in range(self.phases)
        ]
        self.other_flips = [
            self.core * flips[last - k] + (1 - self.core) * flips[k] for k in range(self.phases)
        ]

    def column(self, e, flips=None):
        flips = self.flips if flips is None else flips
        col = self.c
        for k in range(self.phases):
            if (e >> k) & 1:
                col = col + flips[k]
        return col

    def mate(self, k):
        return {CANVAS: self.c + self.flips[k], HEIGHT: self.h}

    def sibling(self):
        return {CANVAS: self.c, HEIGHT: 2 * self.seat + 1 - self.core}

    def beside(self, step):
        return {CANVAS: self.c, HEIGHT: self.h + 2 * step}

    def greet(self):
        barrier = pltpu.get_barrier_semaphore()
        for d in range(1, self.n):
            pl.semaphore_signal(
                barrier, inc=1, device_id={CANVAS: self.c, HEIGHT: lax.rem(self.h + d, self.n)},
                device_id_type=MESH)
        for k in range(self.phases):
            pl.semaphore_signal(barrier, inc=1, device_id=self.mate(k), device_id_type=MESH)
        pl.semaphore_wait(barrier, self.n - 1 + self.phases)


def remote(src, dst, send, recv, to):
    return pltpu.make_async_remote_copy(
        src_ref=src, dst_ref=dst, send_sem=send, recv_sem=recv, device_id=to, device_id_type=MESH)


def lowest_bit(e):
    return (e & -e).bit_length() - 1


def spread_blocks(grid, fresh, whole, own_sem, zsend, msend, ssend, recv, srecv):
    g = grid
    seats, phases = g.seats, g.phases
    own = pltpu.make_async_copy(fresh, whole.at[g.c, g.seat, g.core], own_sem)
    own.start()

    def slot(e, seat):
        return whole.at[g.column(e), seat, g.core]

    def forward(e, seat, src, start):
        k_top = phases if e == 0 else lowest_bit(e)
        for k in range(k_top - 1, -1, -1):
            cp = remote(src, slot(e, seat), msend.at[k, e, seat], recv.at[e | (1 << k), seat], g.mate(k))
            cp.start() if start else cp.wait_send()
        cp = remote(src, slot(e, seat), ssend.at[e, seat], srecv.at[e, seat], g.sibling())
        cp.start() if start else cp.wait_send()

    def along(seat, step, src, start):
        cp = remote(src, slot(0, seat), zsend.at[(step + 1) // 2, seat], recv.at[0, seat], g.beside(step))
        cp.start() if start else cp.wait_send()

    def line(seat, src, start):
        @pl.when((seat <= g.seat) & (g.seat < seats - 1))
        def _():
            along(seat, 1, src, start)

        @pl.when((seat >= g.seat) & (g.seat > 0))
        def _():
            along(seat, -1, src, start)

    def arrive(e, seat):
        remote(fresh, slot(e, seat), ssend.at[0, 0], recv.at[e, seat], g.sibling()).wait_recv()

    early = [e for e in range(1, 2**phases) if lowest_bit(e) > 0]
    early.sort(key=lambda e: -lowest_bit(e))
    late = [e for e in range(1, 2**phases) if lowest_bit(e) == 0]

    def handle(e, seat):
        arrive(e, seat)
        if e == 0:
            line(seat, slot(0, seat), True)
        forward(e, seat, slot(e, seat), True)

    def both_sides(d, todo):
        for side in (-1, 1):
            seat = g.seat + side * d

            @pl.when((seat >= 0) & (seat < seats))
            def _():
                for e in todo:
                    handle(e, seat)

    line(g.seat, fresh, True)
    forward(0, g.seat, fresh, True)
    for e in early:
        handle(e, g.seat)

    def further(d, _):
        both_sides(d, [0] + early)
        return 0

    lax.fori_loop(1, seats, further, 0)
    for e in late:
        handle(e, g.seat)

    def finish(d, _):
        both_sides(d, late)
        return 0

    lax.fori_loop(1, seats, finish, 0)

    def drain(seat, _):
        for e in range(2**phases):
            remote(fresh, whole.at[g.column(e, g.other_flips), seat, 1 - g.core], ssend.at[0, 0],
                   srecv.at[e, seat], g.sibling()).wait_recv()
            forward(e, seat, slot(e, seat), False)
        line(seat, slot(0, seat), False)
        return 0

    lax.fori_loop(0, seats, drain, 0)
    own.wait()


def spread_scratch(columns, n):
    seats, phases = n // 2, columns.bit_length() - 1
    dma = pltpu.SemaphoreType.DMA
    return [
        dma((1,)),
        dma((2, seats)),
        dma((phases, columns, seats)),
        dma((columns, seats)),
        dma((columns, seats)),
        dma((columns, seats)),
    ]


def spread_kernel(columns, n, block, whole, fresh, own, zsend, msend, ssend, recv, srecv):
    grid = Grid(columns, n)
    fresh[...] = block[...].astype(B16)
    grid.greet()
    spread_blocks(grid, fresh, whole, own.at[0], zsend, msend, ssend, recv, srecv)


def spread_call(columns, n, cid, block):
    return pl.pallas_call(
        functools.partial(spread_kernel, columns, n),
        out_shape=sds((columns, n // 2, 2) + block.shape, B16),
        in_specs=[vmem],
        out_specs=anyw,
        scratch_shapes=[pltpu.VMEM(block.shape, B16)] + spread_scratch(columns, n),
        compiler_params=params_of(cid),
        name="spread_weights",
    )(block)


def adam_update(current, gradient, moment_one, moment_two, learn_rate):
    first_new = 0.5 * moment_one + 0.5 * gradient
    second_new = 0.9 * moment_two + 0.1 * gradient * gradient
    first_hat = first_new / (1.0 - 0.5**STEP)
    second_hat = second_new / (1.0 - 0.9**STEP)
    return (
        current - learn_rate * first_hat / (jnp.sqrt(second_hat) + adam_epsilon),
        first_new,
        second_new,
    )


def step_kernel(columns, n, grads, w, m, s, dvec, vw, vm, vs, new_w, new_m, new_s, new_vw, new_vm, new_vs, whole,
                acc, sib, got, up, down, fresh, vbuf, vtrade, lsem, gsend, grecv, psend, precv, usend, urecv,
                vsend, vrecv, tsend, trecv, own, zsend, msend, ssend, recv, srecv):
    g = Grid(columns, n)
    seats, phases = g.seats, g.phases
    slots = 2**phases
    order = sorted(range(slots), key=lambda e: (lowest_bit(e) if e else phases, e == (e & -e)))
    loads = []
    for e in order:
        cp = pltpu.make_async_copy(grads.at[g.column(e), :, g.core], acc.at[e], lsem.at[e])
        cp.start()
        loads.append(cp)

    @pl.when(g.seat == 0)
    def _():
        up[...] = jnp.zeros(up.shape, B16)

    @pl.when(g.seat == seats - 1)
    def _():
        down[...] = jnp.zeros(down.shape, B16)

    vbuf[g.h] = dvec[...]
    g.greet()
    sib_copies = []
    for e in order:
        cp = remote(grads.at[g.column(e, g.other_flips), :, 1 - g.core], sib.at[e], gsend.at[e], grecv.at[e],
                    g.sibling())
        cp.start()
        sib_copies.append(cp)

    def vector_copy(d):
        src = lax.rem(g.h + d, n)
        return remote(vbuf.at[g.h], vbuf.at[g.h], vsend.at[d], vrecv.at[g.h],
                      {CANVAS: g.c, HEIGHT: src})

    def vector_arrival(d):
        src = lax.rem(g.h + d, n)
        return remote(vbuf.at[src], vbuf.at[src], vsend.at[d], vrecv.at[src],
                      {CANVAS: g.c, HEIGHT: src})

    for d in range(1, n):
        vector_copy(d).start()

    def local(e, seat, below):
        total = acc[e, seat].astype(F32) + sib[e, seat].astype(F32)
        for k in range(below):
            total = total + got[k, e >> (k + 1), seat].astype(F32)
        return total

    def in_turn(i):
        even = 1 - lax.rem(i, 2)
        return (i // 2) * even + (1 - even) * (seats - 1 - i // 2)

    def phase_copy(k, e, seat):
        return remote(acc.at[e, seat], got.at[k, e >> (k + 1), seat], psend.at[k, e >> (k + 1), seat],
                      precv.at[k, e >> (k + 1), seat], g.mate(k))

    ready = 0
    for e in order:
        loads[ready].wait()
        sib_copies[ready].wait_recv()
        ready += 1
        if e == 0:
            break
        k = lowest_bit(e)

        def one(i, _):
            seat = in_turn(i)
            for q in range(k):
                phase_copy(q, e | (1 << q), seat).wait_recv()
            acc[e, seat] = local(e, seat, k).astype(B16)
            phase_copy(k, e, seat).start()
            return 0

        lax.fori_loop(0, seats, one, 0)

    for d in range(1, n):
        vector_arrival(d).wait_recv()
    vtrade[0, 0] = jnp.sum(vbuf[...], axis=0)
    for k in range(phases):
        cp = remote(vtrade.at[k, 0], vtrade.at[k, 1], tsend.at[k], trecv.at[k], g.mate(k))
        cp.start()
        cp.wait_recv()
        vtrade[k + 1, 0] = vtrade[k, 0] + vtrade[k, 1]
    new_vw[...], new_vm[...], new_vs[...] = adam_update(vw[...], vtrade[phases, 0], vm[...], vs[...], vector_rate)

    def line_copy(step, seat):
        box = up if step > 0 else down
        at = (step + 1) // 2
        return remote(acc.at[0, seat], box.at[seat], usend.at[at, seat], urecv.at[at, seat], g.beside(step))

    def own_column(i, _):
        seat = in_turn(i)
        for q in range(phases):
            phase_copy(q, 1 << q, seat).wait_recv()

        @pl.when(seat > g.seat)
        def _():
            @pl.when(g.seat > 0)
            def _():
                line_copy(1, seat).wait_recv()

            acc[0, seat] = (local(0, seat, phases) + up[seat].astype(F32)).astype(B16)
            line_copy(1, seat).start()

        @pl.when(seat < g.seat)
        def _():
            @pl.when(g.seat < seats - 1)
            def _():
                line_copy(-1, seat).wait_recv()

            acc[0, seat] = (local(0, seat, phases) + down[seat].astype(F32)).astype(B16)
            line_copy(-1, seat).start()

        return 0

    lax.fori_loop(0, seats, own_column, 0)

    @pl.when(g.seat > 0)
    def _():
        line_copy(1, g.seat).wait_recv()

    @pl.when(g.seat < seats - 1)
    def _():
        line_copy(-1, g.seat).wait_recv()

    total = local(0, g.seat, phases) + up[g.seat].astype(F32) + down[g.seat].astype(F32)
    next_w, new_m[...], new_s[...] = adam_update(w[...], total, m[...], s[...], matrix_rate)
    new_w[...] = next_w
    fresh[...] = next_w.astype(B16)
    spread_blocks(g, fresh, whole, own.at[0], zsend, msend, ssend, recv, srecv)
    for cp in sib_copies:
        cp.wait_send()
    for d in range(1, n):
        vector_copy(d).wait_send()
    for k in range(phases):
        remote(vtrade.at[k, 0], vtrade.at[k, 1], tsend.at[k], trecv.at[k], g.mate(k)).wait_send()

    def drain(seat, _):
        for e in range(1, slots):
            phase_copy(lowest_bit(e), e, seat).wait_send()

        @pl.when(seat > g.seat)
        def _():
            line_copy(1, seat).wait_send()

        @pl.when(seat < g.seat)
        def _():
            line_copy(-1, seat).wait_send()

        return 0

    lax.fori_loop(0, seats, drain, 0)


def step_call(columns, n, cid, grads, w, m, s, dvec, vw, vm, vs):
    seats, phases = n // 2, columns.bit_length() - 1
    block = w.shape
    half = max(columns // 2, 1)
    dma = pltpu.SemaphoreType.DMA
    return pl.pallas_call(
        functools.partial(step_kernel, columns, n),
        out_shape=[sds(block, F32)] * 3 + [sds(vw.shape, F32)] * 3 + [sds((columns, seats, 2) + block, B16)],
        in_specs=[anyw] + [vmem] * 7,
        out_specs=[vmem] * 6 + [anyw],
        scratch_shapes=[
            pltpu.VMEM((columns, seats) + block, B16),
            pltpu.VMEM((columns, seats) + block, B16),
            pltpu.VMEM((phases, half, seats) + block, B16),
            pltpu.VMEM((seats,) + block, B16),
            pltpu.VMEM((seats,) + block, B16),
            pltpu.VMEM(block, B16),
            pltpu.VMEM((n,) + vw.shape, F32),
            pltpu.VMEM((phases + 1, 2) + vw.shape, F32),
            dma((columns,)),
            dma((columns,)),
            dma((columns,)),
            dma((phases, half, seats)),
            dma((phases, half, seats)),
            dma((2, seats)),
            dma((2, seats)),
            dma((n,)),
            dma((n,)),
            dma((phases,)),
            dma((phases,)),
        ]
        + spread_scratch(columns, n),
        compiler_params=params_of(cid),
        name="step_weights",
    )(grads, w, m, s, dvec, vw, vm, vs)


class Engine:
    def __init__(self, steps):
        self.steps = steps

    def pump(self, count=1):
        for _ in range(count):
            next(self.steps, None)

    def ready(self):
        for done in self.steps:
            if done:
                return

    def finish(self):
        for _ in self.steps:
            pass


class Group:
    def __init__(self, grid, number, half_rows, first=0, size=None):
        self.g, self.number, self.half = grid, number, half_rows
        self.first, self.size = first, half_rows if size is None else size
        self.owner = 2 * number + grid.c // 2
        self.is_owner = grid.c // 2 == number

    def row(self, q, seat, core):
        block = (q // 2) * self.g.n + 2 * seat + core
        return pl.multiple_of((2 * block + lax.rem(q, 2)) * self.half + self.first, 16)

    def rows(self, q, seat, core):
        return pl.ds(self.row(q, seat, core), self.size)

    def at_column(self, col):
        return {CANVAS: col, HEIGHT: self.g.h}

    def halves(self):
        first = 2 * lax.rem(self.g.c, 2)
        return [(0, first), (1, first + 1)]

    def part(self, ref, half):
        return ref.at[pl.ds(half * self.half, self.half)]

    def to_pieces(self, block, piece, send, recv, start):
        g = self.g

        @pl.when(self.is_owner)
        def _():
            for half, col in self.halves():
                @pl.when(col != g.c)
                def _():
                    cp = remote(self.part(block, half), piece, send.at[half], recv.at[0], self.at_column(col))
                    cp.start() if start else cp.wait_send()

                if start:
                    @pl.when(col == g.c)
                    def _():
                        piece[...] = block[half * self.half : (half + 1) * self.half, :]

    def piece_arrived(self, block, piece, send, recv):
        @pl.when(self.owner != self.g.c)
        def _():
            remote(self.part(block, 0), piece, send.at[0], recv.at[0], self.at_column(self.owner)).wait_recv()

    def to_owner(self, piece, block, send, recv, start):
        g = self.g
        half = lax.rem(g.c, 2)
        where = pl.ds(pl.multiple_of(half * self.half, 16), self.half)

        @pl.when(self.owner != g.c)
        def _():
            cp = remote(piece, block.at[where], send.at[0], recv.at[half], self.at_column(self.owner))
            cp.start() if start else cp.wait_send()

        if start:
            @pl.when(self.owner == g.c)
            def _():
                block[where, :] = piece[...]

    def block_arrived(self, piece, block, send, recv):
        g = self.g

        @pl.when(self.is_owner)
        def _():
            for half, col in self.halves():
                @pl.when(col != g.c)
                def _():
                    remote(piece, self.part(block, half), send.at[0], recv.at[half], self.at_column(col)).wait_recv()


def gather_pieces(group, piece, dest, own, zsend, msend, ssend, recv, srecv):
    g = group.g
    seats, phases = g.seats, g.phases
    local = pltpu.make_async_copy(piece, dest.at[group.rows(g.c, g.seat, g.core)], own.at[0])

    local.start()
    top = 1 << (phases - 1)
    lines = [0, top]

    def slot(e, seat):
        return dest.at[group.rows(g.column(e), seat, g.core)]

    def forward(e, seat, src, start):
        k_top = phases if e == 0 else lowest_bit(e)
        for k in range(k_top - 1, -1, -1):
            cp = remote(src, slot(e, seat), msend.at[k, e, seat], recv.at[e | (1 << k), seat], g.mate(k))
            do = cp.start if start else cp.wait_send
            if e == 0 and k == phases - 1:
                pl.when(seat == g.seat)(do)
            else:
                do()
        cp = remote(src, slot(e, seat), ssend.at[e, seat], srecv.at[e, seat], g.sibling())
        cp.start() if start else cp.wait_send()

    def along(e, seat, step, src, start):
        cp = remote(src, slot(e, seat), zsend.at[(step + 1) // 2, min(e, 1), seat], recv.at[e, seat], g.beside(step))
        cp.start() if start else cp.wait_send()

    def line(e, seat, src, start):
        @pl.when((seat <= g.seat) & (g.seat < seats - 1))
        def _():
            along(e, seat, 1, src, start)

        @pl.when((seat >= g.seat) & (g.seat > 0))
        def _():
            along(e, seat, -1, src, start)

    def handle(e, seat):
        remote(piece, slot(e, seat), ssend.at[0, 0], recv.at[e, seat], g.sibling()).wait_recv()
        if e in lines:
            line(e, seat, slot(e, seat), True)
        forward(e, seat, slot(e, seat), True)

    early = sorted((e for e in range(1, 2**phases) if lowest_bit(e) > 0), key=lambda e: -lowest_bit(e))
    late = [e for e in range(1, 2**phases) if lowest_bit(e) == 0]

    def both_sides(d, todo):
        for side in (-1, 1):
            seat = g.seat + side * d

            @pl.when((seat >= 0) & (seat < seats))
            def _():
                for e in todo:
                    handle(e, seat)

    forward(0, g.seat, piece, True)
    line(0, g.seat, piece, True)
    yield
    for e in early:
        handle(e, g.seat)
    yield
    for d in range(1, seats):
        both_sides(d, [0] + early)
        yield
    for e in late:
        handle(e, g.seat)
    yield
    for d in range(1, seats):
        both_sides(d, late)
        yield

    def siblings(seat, _):
        for e in range(2**phases):
            remote(piece, dest.at[group.rows(g.column(e, g.other_flips), seat, 1 - g.core)], ssend.at[0, 0],
                   srecv.at[e, seat], g.sibling()).wait_recv()
        return 0

    lax.fori_loop(0, seats, siblings, 0)
    local.wait()
    yield True

    def drain(seat, _):
        for e in range(2**phases):
            forward(e, seat, slot(e, seat), False)
            if e in lines:
                line(e, seat, slot(e, seat), False)
        return 0

    lax.fori_loop(0, seats, drain, 0)


def gather_pieces_scratch(columns, n):
    seats, phases = n // 2, columns.bit_length() - 1
    dma = pltpu.SemaphoreType.DMA
    return [
        dma((1,)),
        dma((2, 2, seats)),
        dma((phases, columns, seats)),
        dma((columns, seats)),
        dma((columns, seats)),
        dma((columns, seats)),
    ]


def fold_columns(group, src, column, sib, got, gsend, grecv, psend, precv):
    g = group.g
    seats, phases = g.seats, g.phases
    slots = 2**phases
    turns = [i // 2 if i % 2 == 0 else seats - 1 - i // 2 for i in range(seats)]
    order = sorted(range(slots), key=lambda e: (lowest_bit(e) if e else phases, e == (e & -e)))

    def mine(e, seat):
        return group.rows(g.column(e), seat, g.core)

    def sibling_copy(e, seat):
        return remote(src.at[group.rows(g.column(e, g.other_flips), seat, 1 - g.core)], sib.at[e, seat],
                      gsend.at[e, seat], grecv.at[e, seat], g.sibling())

    def phase_copy(k, e, seat):
        at = (k, e >> (k + 1), seat)
        return remote(src.at[mine(e, seat), :], got.at[at], psend.at[at], precv.at[at], g.mate(k))

    for e in order:
        for seat in turns:
            sibling_copy(e, seat).start()
    yield
    for e in order:
        k = lowest_bit(e) if e else phases
        for seat in turns:
            sibling_copy(e, seat).wait_recv()
            total = src[mine(e, seat), :].astype(F32) + sib[e, seat].astype(F32)
            for q in range(k):
                phase_copy(q, e | (1 << q), seat).wait_recv()
                total = total + got[q, e >> (q + 1), seat].astype(F32)
            if e:
                src[mine(e, seat), :] = total.astype(B16)
                phase_copy(k, e, seat).start()
            else:
                column[seat] = total.astype(B16)
            yield
    yield True

    def drain(seat, _):
        for e in range(slots):
            sibling_copy(e, seat).wait_send()
            if e:
                phase_copy(lowest_bit(e), e, seat).wait_send()
        return 0

    lax.fori_loop(0, seats, drain, 0)


def fold_columns_scratch(columns, n, half_rows):
    seats, phases = n // 2, columns.bit_length() - 1
    dma = pltpu.SemaphoreType.DMA
    block = (half_rows, C)
    return [
        pltpu.VMEM((columns, seats) + block, B16),
        pltpu.VMEM((phases, columns // 2, seats) + block, B16),
        dma((columns, seats)),
        dma((columns, seats)),
        dma((phases, columns // 2, seats)),
        dma((phases, columns // 2, seats)),
    ]


def fold_seats(group, column, piece, box, usend, urecv):
    g = group.g
    seats = g.seats

    def line_copy(seat):
        return remote(column.at[seat], box.at[g.seat], usend.at[seat], urecv.at[g.seat],
                      {CANVAS: g.c, HEIGHT: 2 * seat + g.core})

    def line_arrival(seat):
        return remote(column.at[seat], box.at[seat], usend.at[seat], urecv.at[seat],
                      {CANVAS: g.c, HEIGHT: 2 * seat + g.core})

    for seat in range(seats):
        pl.when(seat != g.seat)(line_copy(seat).start)
    yield
    total = column[g.seat].astype(F32)
    for seat in range(seats):
        pl.when(seat != g.seat)(line_arrival(seat).wait_recv)
        total = total + jnp.where(seat == g.seat, 0.0, box[seat].astype(F32))
    piece[...] = total.astype(B16)
    yield True
    for seat in range(seats):
        pl.when(seat != g.seat)(line_copy(seat).wait_send)


def fold_seats_scratch(n, half_rows):
    seats = n // 2
    dma = pltpu.SemaphoreType.DMA
    return [pltpu.VMEM((seats, half_rows, C), B16), dma((seats,)), dma((seats,))]


def reduce_pieces(group, src, piece, sib, got, box, gsend, grecv, psend, precv, usend, urecv):
    g = group.g
    seats, phases = g.seats, g.phases
    slots = 2**phases
    order = sorted(range(slots), key=lambda e: (lowest_bit(e) if e else phases, e == (e & -e)))
    turns = [i // 2 if i % 2 == 0 else seats - 1 - i // 2 for i in range(seats)]

    def mine(e, seat):
        return group.rows(g.column(e), seat, g.core)

    def sibling_copy(e, seat):
        return remote(src.at[group.rows(g.column(e, g.other_flips), seat, 1 - g.core)], sib.at[e, seat],
                      gsend.at[e, seat], grecv.at[e, seat], g.sibling())

    def phase_copy(k, e, seat):
        at = (k, e >> (k + 1), seat)
        return remote(src.at[mine(e, seat), :], got.at[at], psend.at[at], precv.at[at], g.mate(k))

    def line_copy(seat):
        return remote(src.at[mine(0, seat), :], box.at[g.seat], usend.at[seat], urecv.at[g.seat],
                      {CANVAS: g.c, HEIGHT: 2 * seat + g.core})

    def line_arrival(seat):
        return remote(src.at[mine(0, seat), :], box.at[seat], usend.at[seat], urecv.at[seat],
                      {CANVAS: g.c, HEIGHT: 2 * seat + g.core})

    def local(e, seat, below):
        total = src[mine(e, seat), :].astype(F32) + sib[e, seat].astype(F32)
        for k in range(below):
            total = total + got[k, e >> (k + 1), seat].astype(F32)
        return total

    for e in order:
        for seat in turns:
            sibling_copy(e, seat).start()
    yield

    def pass_on(e, k, seat):
        sibling_copy(e, seat).wait_recv()
        for q in range(k):
            phase_copy(q, e | (1 << q), seat).wait_recv()
        src[mine(e, seat), :] = local(e, seat, k).astype(B16)
        phase_copy(k, e, seat).start()

    for e in order:
        if e == 0:
            break
        for seat in turns:
            pass_on(e, lowest_bit(e), seat)
            yield

    def own_column(seat):
        sibling_copy(0, seat).wait_recv()
        for q in range(phases):
            phase_copy(q, 1 << q, seat).wait_recv()

        @pl.when(seat != g.seat)
        def _():
            src[mine(0, seat), :] = local(0, seat, phases).astype(B16)
            line_copy(seat).start()

    for seat in turns:
        own_column(seat)
        yield
    total = local(0, g.seat, phases)
    for seat in turns:
        @pl.when(seat != g.seat)
        def _():
            line_arrival(seat).wait_recv()

        total = total + jnp.where(seat == g.seat, 0.0, box[seat].astype(F32))
    piece[...] = total.astype(B16)
    yield True

    def drain(seat, _):
        for e in range(slots):
            sibling_copy(e, seat).wait_send()
            if e > 0:
                phase_copy(lowest_bit(e), e, seat).wait_send()

        @pl.when(seat != g.seat)
        def _():
            line_copy(seat).wait_send()

        return 0

    lax.fori_loop(0, seats, drain, 0)


def reduce_pieces_scratch(columns, n, half_rows):
    seats, phases = n // 2, columns.bit_length() - 1
    half = columns // 2
    dma = pltpu.SemaphoreType.DMA
    block = (half_rows, C)
    return [
        pltpu.VMEM((columns, seats) + block, B16),
        pltpu.VMEM((phases, half, seats) + block, B16),
        pltpu.VMEM((seats,) + block, B16),
        dma((columns, seats)),
        dma((columns, seats)),
        dma((phases, half, seats)),
        dma((phases, half, seats)),
        dma((seats,)),
        dma((seats,)),
    ]


class Named:
    def __init__(self, shapes, refs):
        refs = list(refs)
        for name, shape in shapes.items():
            if isinstance(shape, list):
                setattr(self, name, [refs.pop(0) for _ in shape])
            else:
                setattr(self, name, refs.pop(0))


def named_call(kernel, name, cid, inputs, outputs, scratch):
    loads = [k for k, (_, spec) in inputs.items() if spec == LOAD]
    stores = [k for k, (_, _, spec) in outputs.items() if spec == STORE]
    parts = 12
    shapes = {**inputs, **outputs, **scratch}
    flat = []
    for value in scratch.values():
        flat += value if isinstance(value, list) else [value]
    held = [pltpu.VMEM(inputs[k][0].shape, inputs[k][0].dtype) for k in loads]
    held += [pltpu.VMEM(*outputs[k][:2]) for k in stores]
    sems = [pltpu.SemaphoreType.DMA((max(len(loads), 1),)), pltpu.SemaphoreType.DMA((max(len(stores), 1), parts))]

    def wrapped(*refs):
        own = len(held) + len(sems)
        R = Named(shapes, refs[:-own])
        kept, (load_sem, store_sem) = refs[-own:-2], refs[-2:]
        waiting, begun, ends = {}, {k: 0 for k in stores}, []
        for i, k in enumerate(loads):
            waiting[k] = pltpu.make_async_copy(getattr(R, k), kept[i], load_sem.at[i])
            waiting[k].start()
            setattr(R, k, kept[i])
        targets = {}
        for i, k in enumerate(stores):
            targets[k] = getattr(R, k)
            setattr(R, k, kept[len(loads) + i])

        def need(*names):
            for k in names:
                if k in waiting:
                    waiting.pop(k).wait()

        def store(k, first=None, count=None):
            src, dst = getattr(R, k), targets[k]
            if first is not None:
                src, dst = src.at[pl.ds(first, count)], dst.at[pl.ds(first, count)]
            cp = pltpu.make_async_copy(src, dst, store_sem.at[stores.index(k), begun[k]])
            cp.start()
            begun[k] += 1
            ends.append(cp)

        R.need, R.store = need, store
        kernel(R)
        need(*list(waiting))
        for k in stores:
            if not begun[k]:
                store(k)
        for cp in ends:
            cp.wait()

    results = pl.pallas_call(
        wrapped,
        out_shape=[sds(shape, kind) for shape, kind, _ in outputs.values()],
        in_specs=[anyw if spec == LOAD else spec for _, spec in inputs.values()],
        out_specs=[anyw if spec == STORE else spec for _, _, spec in outputs.values()],
        scratch_shapes=flat + held + sems,
        compiler_params=params_of(cid),
        name=name,
    )(*[array for array, _ in inputs.values()])
    return dict(zip(outputs, results))


def greet_all(grid):
    barrier = pltpu.get_barrier_semaphore()
    for d in range(1, grid.n):
        pl.semaphore_signal(
            barrier, inc=1, device_id={CANVAS: grid.c, HEIGHT: lax.rem(grid.h + d, grid.n)}, device_id_type=MESH)
    for d in range(1, grid.columns):
        pl.semaphore_signal(
            barrier, inc=1, device_id={CANVAS: lax.rem(grid.c + d, grid.columns), HEIGHT: grid.h},
            device_id_type=MESH)
    pl.semaphore_wait(barrier, grid.n - 1 + grid.columns - 1)


def across(top, low):
    def taps(dr):
        if dr == 0:
            return [(0, 2 * C, top, 9 * C), (2 * C, 3 * C, low, 0)]
        return [(0, 3 * C, low, 3 * C * dr - 2 * C)]

    return taps


def first_kernel(columns, n, dims, R):
    g = Grid(columns, n)
    half = R.block.shape[0] // 2
    groups = [Group(g, i, half) for i in range(2)]
    R.low[...] = R.block[...].astype(B16)
    count = R.vectors.shape[0]
    R.vec[...] = jnp.zeros(R.vec.shape, F32)
    R.vec[0:count, :] = R.vectors[...].astype(B16).astype(F32)
    canvases, rows, width = dims
    turned = jnp.transpose(R.ids_lane[...])
    for v in range(canvases):
        R.ids_px[v] = jnp.broadcast_to(turned[:, v : v + 1], (rows * width, LANES)).reshape(rows, width, LANES)
    greet_all(g)
    for i, group in enumerate(groups):
        group.to_pieces(R.low, R.pieces.at[i], R.tsend.at[i], R.trecv.at[i], True)
    engines = [
        Engine(gather_pieces(groups[0], R.pieces.at[0], R.w_top, *R.gather0)),
        Engine(gather_pieces(groups[1], R.pieces.at[1], R.w_low, *R.gather1)),
    ]
    each = rows * width // UNIT
    for v in range(canvases):
        cell_ids = R.ids_px[v].reshape(each, UNIT, LANES)[:, 0, :] + float(CROPS * v)
        lane = lax.broadcasted_iota(jnp.int32, (each, LANES), 1).astype(F32)
        R.hot[v * each : (v + 1) * each, :] = (cell_ids == lane).astype(F32)
    stats = canvases * CROPS
    R.spread[...] = R.hot[:, :stats].astype(B16)
    R.pick[...] = jnp.transpose(R.hot[...])[:stats, :].astype(B16)
    turn = [0]
    lag = 2 * g.seats - 3

    def pump():
        if turn[0] == 0:
            groups[0].piece_arrived(R.low, R.pieces.at[0], R.tsend.at[0], R.trecv.at[0])
        if turn[0] < 2 * g.seats + 1:
            engines[0].pump()
        if turn[0] == lag:
            groups[1].piece_arrived(R.low, R.pieces.at[1], R.tsend.at[1], R.trecv.at[1])
        if turn[0] >= lag:
            engines[1].pump()
        turn[0] += 1

    R.need("x")
    layout_body(n, dims, R.x, R.pick, R.spread, R.ids_px, R.ids_lane, R.ids_all, R.mean1, R.inv1, R.div, R.cnt,
                R.col_l, R.col_r, R.row_u, R.row_d, *R.layout, pump=pump, cnt_all=R.cnt_all)
    for k in ("col_l", "col_r", "row_u", "row_d"):
        R.store(k)
    pump()
    conv = Convolver(n, dims, R.x, R.pick, R.spread, R.cnt, R.col_l, R.col_r, R.row_u, R.row_d, R.halo, R.buf,
                     R.tmp_a, R.tmp_b, R.send, R.recv, R.hsend, R.hrecv, R.cnt_all)
    vec = R.vec
    conv.activate(R.x, R.mean1, R.inv1, vec[0:1, :], vec[1:2, :], R.s1, 0, pump)
    out_s1 = pltpu.make_async_copy(R.s1, R.s1_out, R.osem.at[0])
    out_s1.start()
    while turn[0] < 2 * g.seats + 1:
        pump()
    engines[0].ready()
    out_top = pltpu.make_async_copy(R.w_top, R.top, R.osem.at[1])
    out_top.start()
    pump_low = engines[1].pump
    if turn[0] <= lag:
        groups[1].piece_arrived(R.low, R.pieces.at[1], R.tsend.at[1], R.trecv.at[1])
        pump_low()

    def emit_first(at, total):
        R.y1[at, :] = total + vec[2:3, :]

    conv.convolve(R.s1, lambda dr: [(0, 3 * C, R.w_top, 3 * C * dr)], emit_first, pump_low)
    out_y1 = pltpu.make_async_copy(R.y1, R.y1_out, R.osem.at[2])
    out_y1.start()
    conv.statistics(R.y1, R.mean2, R.inv2, 0, pump_low)
    conv.activate(R.y1, R.mean2, R.inv2, vec[3:4, :], vec[4:5, :], R.s2, 1, pump_low)
    out_s2 = pltpu.make_async_copy(R.s2, R.s2_out, R.osem.at[3])
    out_s2.start()
    engines[1].ready()
    out_low = pltpu.make_async_copy(R.w_low, R.bottom, R.osem.at[4])
    out_low.start()

    def emit_second(at, total):
        R.hid[at, :] = total + vec[5:6, :] + R.x[at, :].astype(F32)

    conv.convolve(R.s2, across(R.w_top, R.w_low), emit_second)
    R.store("hid")
    conv.statistics(R.hid, R.mean3, R.inv3, 1)
    conv.normalise(R.hid, R.mean3, R.inv3, vec[6:7, :], vec[7:8, :], R.u)
    for cp in conv.sent:
        cp.wait_send()
    for i, group in enumerate(groups):
        group.to_pieces(R.low, R.pieces.at[i], R.tsend.at[i], R.trecv.at[i], False)
    for cp in (out_s1, out_top, out_y1, out_s2, out_low):
        cp.wait()
    for engine in engines:
        engine.finish()


def first_call(columns, n, dims, x, ids_lane, vectors, block):
    canvases, rows, width = dims
    px = canvases * rows * width
    cells = px // UNIT
    stats = canvases * CROPS
    tall = (canvases, rows + 2, width)
    half = block.shape[0] // 2
    dma = pltpu.SemaphoreType.DMA
    inputs = dict(x=(x, LOAD), ids_lane=(ids_lane, vmem), vectors=(vectors, vmem), block=(block, vmem))
    cell = ((cells, C), F32, vmem)
    outputs = dict(
        vec=((16, C), F32, vmem), pick=((stats, cells), B16, vmem), spread=((cells, stats), B16, vmem),
        ids_all=((n,) + ids_lane.shape, F32, vmem), mean1=cell, inv1=cell, div=((stats, LANES), F32, vmem),
        cnt=((stats, LANES), F32, vmem), cnt_all=((n, stats, LANES), F32, vmem), col_l=(tall + (LANES,), F32, STORE), col_r=(tall + (LANES,), F32, STORE),
        row_u=((px, LANES), F32, STORE), row_d=((px, LANES), F32, STORE), hid=((px, C), F32, STORE),
        u=((px, C), B16, vmem), mean2=cell, inv2=cell, mean3=cell, inv3=cell, y1_out=((px, C), F32, anyw),
        s1_out=(tall + (3 * C,), B16, anyw), s2_out=(tall + (3 * C,), B16, anyw),
        top=((11 * C, C), B16, anyw), bottom=((11 * C, C), B16, anyw))
    scratch = dict(
        ids_px=pltpu.VMEM(dims + (LANES,), F32), hot=pltpu.VMEM((cells, LANES), F32),
        y1=pltpu.VMEM((px, C), F32), s1=pltpu.VMEM(tall + (3 * C,), B16), s2=pltpu.VMEM(tall + (3 * C,), B16),
        w_top=pltpu.VMEM((11 * C, C), B16), w_low=pltpu.VMEM((11 * C, C), B16), low=pltpu.VMEM(block.shape, B16),
        pieces=pltpu.VMEM((2, half, C), B16), tsend=dma((2, 2)), trecv=dma((2, 1)),
        gather0=gather_pieces_scratch(columns, n), gather1=gather_pieces_scratch(columns, n),
        layout=layout_scratch(n, dims, ids_lane), halo=pltpu.VMEM((2, 2, canvases, width, C), B16),
        buf=pltpu.VMEM((2, n, stats // 2, LANES), F32), tmp_a=pltpu.VMEM((cells, C), F32),
        tmp_b=pltpu.VMEM((cells, C), F32), send=dma((2, n)), recv=dma((2, n)), hsend=dma((2, 2)),
        hrecv=dma((2, 2)), osem=dma((5,)))
    return named_call(functools.partial(first_kernel, columns, n, dims), "first_forward", 1, inputs, outputs, scratch)


class Backer:
    def __init__(self, n, dims, R):
        self.n, self.dims, self.R = n, dims, R
        self.px = dims[0] * dims[1] * dims[2]
        self.cells = self.px // UNIT
        self.sent = []

    @staticmethod
    def pixels(i):
        return pl.ds(i * 16 * UNIT, 16 * UNIT)

    def norm_sums(self, grad_of, source, mean, inv, gain, rnd):
        R = self.R

        def body(i, carry):
            dg, db = carry
            at = self.pixels(i)
            unit = (source[at, :].astype(F32) - over_cells(mean, i)) * over_cells(inv, i)
            d = grad_of(i, unit)
            R.norm[at, :] = unit
            e = d * gain
            R.part[at, :] = e
            cross = d * unit
            here = pl.ds(i * 16, 16)
            R.tmp_a[here, :] = jnp.sum(e.reshape(16, UNIT, C), axis=1)
            R.tmp_b[here, :] = jnp.sum((cross * gain).reshape(16, UNIT, C), axis=1)
            return (dg + jnp.sum(cross, axis=0, keepdims=True), db + jnp.sum(d, axis=0, keepdims=True))

        zero = jnp.zeros((1, C), F32)
        dg, db = lax.fori_loop(0, self.cells // 16, body, (zero, zero))
        R.buf[rnd, 0] = fold(pack([group_totals(R.pick, R.tmp_a[...]), group_totals(R.pick, R.tmp_b[...])]))
        copies = spread_copies(self.n, R.buf, R.send, R.recv, rnd)
        for cp in copies:
            cp.start()
        self.sent = self.sent + copies
        return copies, dg, db

    def norm_finish(self, copies, rnd, inv, emit):
        R = self.R
        for cp in copies:
            cp.wait_recv()
        gathered = unfold(jnp.sum(R.buf[rnd], axis=0)) / R.div[...]
        R.tmp_a[...] = split_dot(R.spread[...], unpack(gathered))
        R.tmp_b[...] = split_dot(R.spread[...], unpack(shift_down(gathered, 1)))

        def body(i, _):
            at = self.pixels(i)
            emit(i, over_cells(inv, i) * (
                R.part[at, :] - over_cells(R.tmp_a, i) - R.norm[at, :] * over_cells(R.tmp_b, i)))
            return 0

        lax.fori_loop(0, self.cells // 16, body, 0)

    def send_rows(self, source, rnd):
        R = self.R
        canvases, rows, width = self.dims

        def one(v, r):
            at = pl.ds(pl.multiple_of((v * rows + r) * width, width), width)
            R.d3[v, r + 1] = shift_columns(source[at, :].astype(F32), R.col_l[v, r + 1], R.col_r[v, r + 1])

        def edges(v, _):
            one(v, 0)
            one(v, rows - 1)
            return 0

        lax.fori_loop(0, canvases, edges, 0)
        mid = pl.ds(C, C)
        up, down = halo_copies(self.n, R.d3.at[:, 1, :, mid], R.d3.at[:, rows, :, mid], R.halo.at[rnd],
                               R.hsend.at[rnd], R.hrecv.at[rnd])
        start_halo(self.n, up, down)

        def inner(i, _):
            one(i // (rows - 2), 1 + lax.rem(i, rows - 2))
            return 0

        if rows > 2:
            lax.fori_loop(0, canvases * (rows - 2), inner, 0)
        return up, down

    def finish_rows(self, up, down, rnd):
        R = self.R
        canvases, rows, _ = self.dims
        wait_halo(self.n, up, down, R.halo.at[rnd], 0.0)
        for v in range(canvases):
            for side, r in ((0, 0), (1, rows + 1)):
                R.d3[v, r] = shift_columns(R.halo[rnd, side, v].astype(F32), R.col_l[v, r], R.col_r[v, r])

    def convolve_back(self, weights, pump=no_pump):
        R = self.R
        canvases, rows, width = self.dims
        plane = rows * width
        nt = (((1,), (1,)), ((), ()))
        for v in range(canvases):
            at = pl.ds(v * plane, plane)
            total = None
            for dr in (1, 0, 2):
                acc = None
                for dc in range(3):
                    ref, row = weights(3 * (2 - dr) + (2 - dc))
                    lhs = R.d3[v, dr : dr + rows, :, dc * C : (dc + 1) * C].reshape(plane, C)
                    term = lax.dot_general(lhs, ref[row : row + C, :], nt, preferred_element_type=F32)
                    acc = term if acc is None else acc + term
                if dr == 0:
                    acc = acc * wide(R.row_u[at, :])
                if dr == 2:
                    acc = acc * wide(R.row_d[at, :])
                total = acc if total is None else total + acc
                pump()
            R.part[at, :] = total

    def mask_rows(self, source):
        R = self.R

        def body(i, _):
            at = self.pixels(i)
            value = source[at, :].astype(F32)
            R.low_u[at, :] = (value * wide(R.row_u[at, :])).astype(B16)
            R.low_d[at, :] = (value * wide(R.row_d[at, :])).astype(B16)
            return 0

        lax.fori_loop(0, self.cells // 16, body, 0)

    def weight_grad(self, s, grad, dest, pump=no_pump):
        R = self.R
        canvases, rows, width = self.dims
        plane = rows * width
        tn = (((0,), (0,)), ((), ()))
        for dr, source in ((0, R.low_u), (1, grad), (2, R.low_d)):
            for dc in range(3):
                acc = None
                for v in range(canvases):
                    lhs = s[v, dr : dr + rows, :, dc * C : (dc + 1) * C].reshape(plane, C)
                    term = lax.dot_general(
                        lhs, source[v * plane : (v + 1) * plane, :], tn, preferred_element_type=F32)
                    acc = term if acc is None else acc + term
                ref, row = dest(3 * dr + dc)
                ref[row : row + C, :] = acc.astype(B16)
                pump()


def back_kernel(columns, n, dims, R):
    g = Grid(columns, n)
    group = Group(g, 1, R.halves.shape[1])
    load_s = pltpu.make_async_copy(R.s2, R.s, R.lsem.at[0])
    load_s.start()
    load_k = second_matrix(R.top, R.bottom, R.k, R.ksem)
    load_att = pltpu.make_async_copy(R.datt, R.g_low.at[pl.ds(7 * C, 4 * C)], R.lsem.at[1])
    for cp in load_k + [load_att]:
        cp.start()
    greet_all(g)
    vec = R.vec
    back = Backer(n, dims, R)
    R.need("du", "hid")
    copies, dg3, db3 = back.norm_sums(lambda i, unit: R.du[back.pixels(i), :], R.hid, R.mean3, R.inv3, vec[6:7, :], 0)

    def emit_hidden(i, value):
        at = back.pixels(i)
        total = R.cot[at, :].astype(F32) + value
        R.dh[at, :] = total
        R.grad[at, :] = total.astype(B16)

    R.need("cot", "col_l", "col_r", "row_u", "row_d")
    back.norm_finish(copies, 0, R.inv3, emit_hidden)
    R.store("dh")
    up, down = back.send_rows(R.grad, 0)
    plane = dims[1] * dims[2]
    o_back = remote(R.o.at[pl.ds(plane, plane)], R.o_back, R.lsem.at[2], R.lsem.at[3],
                    {CANVAS: g.c, HEIGHT: lax.rem(g.h + n // 2, n)})
    o_back.start()
    back.mask_rows(R.grad)
    load_s.wait()

    def dest_two(tap):
        return (R.g_top, (9 + tap) * C) if tap < 2 else (R.g_low, (tap - 2) * C)

    back.weight_grad(R.s, R.grad, dest_two)
    load_att.wait()
    R.store("g_top", 9 * C, 2 * C)
    load_s = pltpu.make_async_copy(R.s1, R.s, R.lsem.at[0])
    load_s.start()
    engine = Engine(fold_columns(group, R.g_low, R.halves, *R.reduce))
    engine.pump()
    dc2 = jnp.sum(R.grad[...].astype(F32), axis=0, keepdims=True)
    back.finish_rows(up, down, 0)
    for cp in load_k:
        cp.wait()
    back.convolve_back(lambda tap: (R.k, tap * C), engine.pump)
    gain2, bias2 = vec[3:4, :], vec[4:5, :]

    def grad_two(i, unit):
        return R.part[back.pixels(i), :] * silu_slope(unit * gain2 + bias2)

    R.need("y1")
    copies, dg2, db2 = back.norm_sums(grad_two, R.y1, R.mean2, R.inv2, gain2, 1)
    engine.pump(2)

    def emit_grad(i, value):
        R.grad[back.pixels(i), :] = value.astype(B16)

    back.norm_finish(copies, 1, R.inv2, emit_grad)
    R.store("grad")
    engine.pump(2)
    back.mask_rows(R.grad)
    dc1 = jnp.sum(R.grad[...].astype(F32), axis=0, keepdims=True)
    load_s.wait()
    taps = []

    def after_tap():
        R.store("g_top", len(taps) * C, C)
        taps.append(None)
        engine.pump()

    back.weight_grad(R.s, R.grad, lambda tap: (R.g_top, tap * C), after_tap)
    R.dvec[...] = jnp.concatenate([dc1, dg2, db2, dc2, dg3, db3, jnp.zeros((2, C), F32)], axis=0)
    engine.ready()
    engine.finish()
    for cp in back.sent:
        cp.wait_send()
    o_back.wait()


def back_call(columns, n, dims, cot, du, hid, y1, norms, s1, s2, pick, spread, div, masks, vec, top, bottom, datt, o,
              block_rows):
    canvases, rows, width = dims
    px = canvases * rows * width
    cells = px // UNIT
    stats = canvases * CROPS
    dma = pltpu.SemaphoreType.DMA
    names = ("mean2", "inv2", "mean3", "inv3")
    inputs = dict(du=(du, LOAD), hid=(hid, LOAD), cot=(cot, LOAD),
                  **{k: (v, LOAD) for k, v in zip(("col_l", "col_r", "row_u", "row_d"), masks)}, y1=(y1, LOAD), s1=(s1, anyw), s2=(s2, anyw),
                  pick=(pick, vmem), spread=(spread, vmem), div=(div, vmem), vec=(vec, vmem), top=(top, anyw),
                  bottom=(bottom, anyw), datt=(datt, anyw), o=(o, anyw),
                  **{k: (v, vmem) for k, v in zip(names, norms)})
    outputs = dict(dh=((px, C), F32, STORE), grad=((px, C), B16, STORE), g_top=((11 * C, C), B16, STORE),
                   dvec=((8, C), F32, vmem), halves=((n // 2, block_rows // 2, C), B16, STORE),
                   o_back=((px // canvases, C), B16, anyw))
    scratch = dict(
        g_low=pltpu.VMEM((11 * C, C), B16), s=pltpu.VMEM(s1.shape, B16), k=pltpu.VMEM((9 * C, C), B16),
        d3=pltpu.VMEM(s1.shape, B16), low_u=pltpu.VMEM((px, C), B16), low_d=pltpu.VMEM((px, C), B16),
        part=pltpu.VMEM((px, C), F32), norm=pltpu.VMEM((px, C), F32),
        halo=pltpu.VMEM((1, 2, canvases, width, C), B16), buf=pltpu.VMEM((2, n, stats // 2, LANES), F32),
        tmp_a=pltpu.VMEM((cells, C), F32), tmp_b=pltpu.VMEM((cells, C), F32),
        reduce=fold_columns_scratch(columns, n, block_rows // 2),
        lsem=dma((5,)), ksem=dma((3,)),
        send=dma((2, n)), recv=dma((2, n)), hsend=dma((1, 2)), hrecv=dma((1, 2)))
    return named_call(functools.partial(back_kernel, columns, n, dims), "back", 7, inputs, outputs, scratch)


def renew_kernel(columns, n, dims, R):
    g = Grid(columns, n)
    half = R.fresh.shape[0] // 2
    upper, lower = Group(g, 0, half), Group(g, 1, half)
    load_g = pltpu.make_async_copy(R.g_in, R.g_top, R.ksem.at[1])
    load_g.start()
    load_k = pltpu.make_async_copy(R.top.at[pl.ds(0, 9 * C)], R.k, R.ksem.at[0])
    load_k.start()
    loads = [
        pltpu.make_async_copy(src, dst, R.ksem.at[2 + i])
        for i, (src, dst) in enumerate(((R.w, R.new_w), (R.m, R.new_m), (R.v, R.new_s), (R.dh, R.igrad)))
    ]
    for cp in loads:
        cp.start()
    piece_loads = []
    for i, src in enumerate((R.w, R.m, R.v)):
        here = pltpu.make_async_copy(src.at[pl.ds(0, half)], R.piece_in.at[i], R.psem.at[i])
        there = pltpu.make_async_copy(R.shares.at[i], R.piece_in.at[i], R.psem.at[i])
        pl.when(g.c == 0)(here.start)
        pl.when(g.c != 0)(there.start)
        piece_loads.append(there)
    greet_all(g)
    vec = R.vec
    R.need("halves")
    folder = Engine(fold_seats(lower, R.halves, R.sum_low, *R.fold))
    load_g.wait()
    reducer = Engine(reduce_pieces(upper, R.g_top, R.sum_top, *R.reduce))
    reducer.pump()
    back = Backer(n, dims, R)
    R.need("grad", "col_l", "col_r", "row_u", "row_d")
    up, down = back.send_rows(R.grad, 0)
    folder.pump()
    reducer.pump(2)
    R.need("x")
    for cp in loads:
        cp.wait()

    def adam(group, totals):
        @pl.when(group.is_owner)
        def _():
            total = totals[...].astype(F32)
            next_w, R.new_m[...], R.new_s[...] = adam_update(
                R.new_w[...], total, R.new_m[...], R.new_s[...], matrix_rate)
            R.new_w[...] = next_w
            R.fresh[...] = next_w.astype(B16)

    reducer.pump(2)
    back.finish_rows(up, down, 0)
    load_k.wait()
    turn = []

    def pump_both():
        reducer.pump()
        turn.append(None)
        if len(turn) == 4:
            folder.ready()
            lower.to_owner(R.sum_low, R.totals, R.asend.at[1], R.arecv.at[1], True)

    back.convolve_back(lambda tap: (R.k, tap * C), pump_both)
    gain1, bias1 = vec[0:1, :], vec[1:2, :]

    def grad_one(i, unit):
        return R.part[back.pixels(i), :] * silu_slope(unit * gain1 + bias1)

    copies, dg1, db1 = back.norm_sums(grad_one, R.x, R.mean1, R.inv1, gain1, 0)
    reducer.pump(2)
    lower.block_arrived(R.sum_low, R.totals, R.asend.at[1], R.arecv.at[1])
    adam(lower, R.totals)
    lower.to_pieces(R.fresh, R.pieces.at[1], R.tsend.at[1], R.trecv.at[1], True)
    R.vbuf[g.h] = jnp.concatenate([dg1, db1, R.dvec[0:6, :], R.dvec_att[...]], axis=0)
    vector_sends = [
        remote(R.vbuf.at[g.h], R.vbuf.at[g.h], R.vsend.at[d], R.vrecv.at[g.h],
               {CANVAS: g.c, HEIGHT: lax.rem(g.h + d, n)})
        for d in range(1, n)
    ]
    for cp in vector_sends:
        cp.start()
    reducer.ready()
    for cp in piece_loads:
        cp.wait()
    next_piece, _, _ = adam_update(
        R.piece_in[0], R.sum_top[...].astype(F32), R.piece_in[1], R.piece_in[2], matrix_rate)
    R.pieces[0] = next_piece.astype(B16)
    gather_top = Engine(gather_pieces(upper, R.pieces.at[0], R.new_top, *R.gather0))
    gather_top.pump()
    lower.piece_arrived(R.fresh, R.pieces.at[1], R.tsend.at[1], R.trecv.at[1])
    gather_low = Engine(gather_pieces(lower, R.pieces.at[1], R.new_low, *R.gather1))
    gather_low.pump()
    upper.to_owner(R.sum_top, R.totals, R.asend.at[0], R.arecv.at[0], True)

    def emit_input(i, value):
        at = back.pixels(i)
        R.igrad[at, :] = R.igrad[at, :] + value

    back.norm_finish(copies, 0, R.inv1, emit_input)
    R.store("igrad")
    gather_top.pump()
    for d in range(1, n):
        src = lax.rem(g.h + d, n)
        remote(R.vbuf.at[src], R.vbuf.at[src], R.vsend.at[d], R.vrecv.at[src],
               {CANVAS: g.c, HEIGHT: src}).wait_recv()
    R.vtrade[0, 0] = jnp.sum(R.vbuf[...], axis=0)

    def trade(k):
        return remote(R.vtrade.at[k, 0], R.vtrade.at[k, 1], R.qsend.at[k], R.qrecv.at[k], g.mate(k))

    trade(0).start()
    gather_top.pump()
    for k in range(g.phases):
        trade(k).wait_recv()
        R.vtrade[k + 1, 0] = R.vtrade[k, 0] + R.vtrade[k, 1]
        if k + 1 < g.phases:
            trade(k + 1).start()
        gather_top.pump()
    count = R.vw.shape[0]
    R.new_vw[...], R.new_vm[...], R.new_vs[...] = adam_update(
        R.vw[...], R.vtrade[g.phases, 0][0:count, :], R.vm[...], R.vs[...], vector_rate)
    R.new_vec[...] = jnp.zeros(R.new_vec.shape, F32)
    R.new_vec[0:count, :] = R.new_vw[...].astype(B16).astype(F32)
    new_vec, s1, y1, hid = R.new_vec, R.d3, R.part, R.norm
    conv = Convolver(n, dims, R.x, R.pick, R.spread, R.cnt, R.col_l, R.col_r, R.row_u, R.row_d, R.chalo, R.cbuf,
                     R.tmp_a, R.tmp_b, R.csend, R.crecv, R.chsend, R.chrecv, R.cnt_all)
    conv.activate(R.x, R.mean1, R.inv1, new_vec[0:1, :], new_vec[1:2, :], s1, 0, gather_top.pump)
    gather_top.ready()
    pump = gather_low.pump
    pump()

    def emit_first(at, total):
        y1[at, :] = total + new_vec[2:3, :]

    conv.convolve(s1, lambda dr: [(0, 3 * C, R.new_top, 3 * C * dr)], emit_first, pump)
    conv.statistics(y1, R.mean2, R.inv2, 0, pump)
    conv.activate(y1, R.mean2, R.inv2, new_vec[3:4, :], new_vec[4:5, :], R.s2, 1, pump)
    gather_low.ready()
    out_att = pltpu.make_async_copy(R.new_low.at[pl.ds(7 * C, 4 * C)], R.new_att, R.ksem.at[0])
    out_att.start()

    def emit_second(at, total):
        hid[at, :] = total + new_vec[5:6, :] + R.x[at, :].astype(F32)

    conv.convolve(R.s2, across(R.new_top, R.new_low), emit_second)
    out_hid = pltpu.make_async_copy(hid, R.hid, R.ksem.at[1])
    out_hid.start()

    def update_owned():
        upper.block_arrived(R.sum_top, R.totals, R.asend.at[0], R.arecv.at[0])
        adam(upper, R.totals)
        for k in ("new_w", "new_m", "new_s"):
            R.store(k)

    conv.statistics(hid, R.mean2, R.inv2, 1, update_owned)
    conv.normalise(hid, R.mean2, R.inv2, new_vec[6:7, :], new_vec[7:8, :], R.u)
    for engine in (gather_low, gather_top, reducer, folder):
        engine.finish()
    for cp in back.sent + conv.sent + vector_sends:
        cp.wait_send()
    for k in range(g.phases):
        trade(k).wait_send()
    for i, group in enumerate((upper, lower)):
        group.to_owner((R.sum_top, R.sum_low)[i], R.totals, R.asend.at[i], R.arecv.at[i], False)
    lower.to_pieces(R.fresh, R.pieces.at[1], R.tsend.at[1], R.trecv.at[1], False)
    out_att.wait()
    out_hid.wait()


def renew_call(columns, n, dims, grad, dh, x, mean1, inv1, pick, spread, div, cnt, cnt_all, masks, vec, top, g_top, halves,
               dvec, dvec_att, w, m, v, shares, vw, vm, vs):
    canvases, rows, width = dims
    px = canvases * rows * width
    cells = px // UNIT
    stats = canvases * CROPS
    block = w.shape
    half = block[0] // 2
    seats, phases = n // 2, columns.bit_length() - 1
    dma = pltpu.SemaphoreType.DMA
    tall = (canvases, rows + 2, width, 3 * C)
    arrays = dict(mean1=mean1, inv1=inv1, pick=pick, spread=spread, div=div, cnt=cnt, cnt_all=cnt_all, vec=vec,
                  dvec=dvec, dvec_att=dvec_att, vw=vw, vm=vm, vs=vs)
    inputs = dict(halves=(halves, LOAD), grad=(grad, LOAD),
                  **{k: (a, LOAD) for k, a in zip(("col_l", "col_r", "row_u", "row_d"), masks)}, x=(x, LOAD),
                  top=(top, anyw), g_in=(g_top, anyw), w=(w, anyw), m=(m, anyw), v=(v, anyw), shares=(shares, anyw), dh=(dh, anyw),
                  **{k: (a, vmem) for k, a in arrays.items()})
    outputs = dict(igrad=((px, C), F32, STORE), new_w=(block, F32, STORE), new_m=(block, F32, STORE),
                   new_s=(block, F32, STORE), new_vw=(vw.shape, F32, vmem), new_vm=(vw.shape, F32, vmem),
                   new_vs=(vw.shape, F32, vmem), new_vec=((16, C), F32, vmem), hid=((px, C), F32, anyw),
                   u=((px, C), B16, vmem), new_att=((4 * C, C), B16, anyw))
    scratch = dict(
        g_top=pltpu.VMEM((11 * C, C), B16), sum_top=pltpu.VMEM((half, C), B16),
        sum_low=pltpu.VMEM((half, C), B16), fold=fold_seats_scratch(n, half), totals=pltpu.VMEM(block, B16),
        new_top=pltpu.VMEM((11 * C, C), B16), new_low=pltpu.VMEM((11 * C, C), B16),
        fresh=pltpu.VMEM(block, B16), pieces=pltpu.VMEM((2, half, C), B16), k=pltpu.VMEM((9 * C, C), B16),
        d3=pltpu.VMEM(tall, B16), s2=pltpu.VMEM(tall, B16), part=pltpu.VMEM((px, C), F32),
        norm=pltpu.VMEM((px, C), F32), mean2=pltpu.VMEM((cells, C), F32), inv2=pltpu.VMEM((cells, C), F32),
        halo=pltpu.VMEM((1, 2, canvases, width, C), B16), chalo=pltpu.VMEM((2, 2, canvases, width, C), B16),
        buf=pltpu.VMEM((1, n, stats // 2, LANES), F32), cbuf=pltpu.VMEM((2, n, stats // 2, LANES), F32),
        tmp_a=pltpu.VMEM((cells, C), F32), tmp_b=pltpu.VMEM((cells, C), F32),
        vbuf=pltpu.VMEM((n, 16, C), F32), vtrade=pltpu.VMEM((phases + 1, 2, 16, C), F32),
        reduce=reduce_pieces_scratch(columns, n, half), gather0=gather_pieces_scratch(columns, n),
        gather1=gather_pieces_scratch(columns, n),
        piece_in=pltpu.VMEM((3, half, C), F32), psem=dma((3,)), ksem=dma((6,)), asend=dma((2, 1)), arecv=dma((2, 2)),
        tsend=dma((2, 2)), trecv=dma((2, 1)), vsend=dma((n,)), vrecv=dma((n,)), qsend=dma((phases,)),
        qrecv=dma((phases,)), send=dma((1, n)), recv=dma((1, n)), hsend=dma((1, 2)), hrecv=dma((1, 2)),
        csend=dma((2, n)), crecv=dma((2, n)), chsend=dma((2, 2)), chrecv=dma((2, 2)))
    return named_call(functools.partial(renew_kernel, columns, n, dims), "renew", 9, inputs, outputs, scratch)


def attend_kernel(n, keep, R):
    me = lax.axis_index(HEIGHT)
    half = n // 2
    mine = me // half
    base = mine * half
    core = lax.rem(me, 2)
    partner = lax.rem(me + half, n)
    sibling = other_core(me)
    mates = half // 2
    seat = (me - base) // 2
    seg = R.u.shape[1]
    total = n * seg
    scale = C ** (-0.5)
    nt = (((1,), (1,)), ((), ()))
    tn = (((0,), (0,)), ((), ()))
    vec = R.vec

    def mate(j, c=core):
        return base + c + 2 * lax.rem(seat + j, mates)

    def far_of(b):
        return lax.rem(b + half, n)

    def to(h):
        return {CANVAS: lax.axis_index(CANVAS), HEIGHT: h}

    loads = [pltpu.make_async_copy(R.low.at[pl.ds(R.low.shape[0] - 4 * C, 4 * C)], R.w, R.lsem.at[0])]
    if keep:
        loads.append(pltpu.make_async_copy(R.cot.at[mine], R.dz.at[pl.ds(0, seg)], R.lsem.at[1]))
    for cp in loads:
        cp.start()
    own = pltpu.make_async_copy(R.u_in.at[mine], R.u.at[me], R.lsem.at[3])
    own.start()
    barrier = pltpu.get_barrier_semaphore()
    peers = [to(p) for p in [partner, sibling] + [mate(j) for j in range(1, mates)]]
    column = lax.axis_index(CANVAS)
    if keep:
        peers += [{CANVAS: lax.rem(column + d, 4), HEIGHT: me} for d in range(1, 4)]
    for p in peers:
        pl.semaphore_signal(barrier, inc=1, device_id=p, device_id_type=MESH)
    pl.semaphore_wait(barrier, len(peers))
    started = []

    def share(from_column, half_number, to_column, begin):
        rows = R.shares.shape[1]
        for i, src in enumerate((R.params, R.first, R.second)):
            cp = remote(src.at[pl.ds(half_number * rows, rows)], R.shares.at[i], R.wsend.at[half_number, i],
                        R.wrecv.at[i], {CANVAS: to_column, HEIGHT: me})
            if begin:
                pl.when(column == from_column)(cp.start)
            else:
                pl.when(column == from_column)(cp.wait_send)
                pl.when(column == to_column)(cp.wait_recv)

    moves = ((0, 1, 1), (1, 0, 2), (1, 1, 3))
    if keep:
        for move in moves:
            share(*move, True)

    def push(src, slot, dest):
        cp = remote(src, R.u.at[slot], R.gsend.at[len(started)], R.grecv.at[slot], to(dest))
        cp.start()
        started.append(cp)

    def block(b):
        return pl.ds(pl.multiple_of(b * seg, seg), seg)

    def project(b):
        piece = R.u[b]
        R.k[block(b), :] = jnp.dot(piece, R.w[C : 2 * C, :], preferred_element_type=F32).astype(B16)
        R.v[block(b), :] = (
            jnp.dot(piece, R.w[2 * C : 3 * C, :], preferred_element_type=F32) + vec[9:10, :]
        ).astype(B16)

    def arrived(slot):
        remote(R.u_in.at[0], R.u.at[slot], R.gsend.at[0], R.grecv.at[slot], to(partner)).wait_recv()

    push(R.u_in.at[1 - mine], me, partner)
    for j in range(1, mates):
        push(R.u_in.at[mine], me, mate(j))
    push(R.u_in.at[mine], me, sibling)
    for cp in loads:
        cp.wait()
    own.wait()
    project(me)
    arrived(sibling)
    project(sibling)
    key_ids = jnp.concatenate([R.ids_all[b, pl.ds(mine, 1), :] for b in range(n)], axis=1)
    order = (me, partner) if keep else (partner, me)
    first_far = 1 if keep else 0
    far_rows, own_rows = pl.ds(first_far * seg, seg), pl.ds((1 - first_far) * seg, seg)
    for i, b in enumerate(order):
        turned = jnp.transpose(R.ids_all[b])
        picked = jnp.where(mine == 0, turned[:, 0:1], turned[:, 1:2])
        R.qid[i * seg : (i + 1) * seg, :] = jnp.broadcast_to(picked, (seg, LANES))
    arrived(partner)
    for j in range(1, mates):
        push(R.u.at[partner], partner, mate(j))
    push(R.u.at[partner], partner, sibling)
    project(partner)
    for j in range(1, mates):
        friend = mate(mates - j)
        arrived(friend)
        push(R.u.at[friend], friend, sibling)
        project(friend)
    arrived(far_of(sibling))
    project(far_of(sibling))
    for j in range(1, mates):
        friend = far_of(mate(mates - j))
        arrived(friend)
        push(R.u.at[friend], friend, sibling)
        project(friend)
    for j in range(1, mates):
        friend = mate(mates - j, 1 - core)
        arrived(friend)
        project(friend)
        arrived(far_of(friend))
        project(far_of(friend))

    rows = R.rows
    per = seg // rows

    def swap_cot(i):
        here = pl.ds(pl.multiple_of(i * rows, rows), rows)
        there = pl.ds(pl.multiple_of(seg + i * rows, rows), rows)
        return remote(R.cot.at[1 - mine, here], R.dz.at[there], R.csend.at[i], R.crecv.at[i], to(partner))

    if keep:
        for i in range(per):
            swap_cot(i).start()
    o_home = R.o_home

    def far_out(i):
        here = pl.ds(pl.multiple_of(i * rows, rows), rows)
        return remote(R.out.at[here], o_home.at[mine, here], R.osend.at[i], R.orecv.at[i], to(partner))

    def attend(i, _):
        at = pl.ds(pl.multiple_of(i * rows, rows), rows)
        b = jnp.where(i < per, order[0], order[1])
        if keep:
            @pl.when(i >= per)
            def _():
                swap_cot(i - per).wait_recv()

        uq = R.u[b, pl.ds(pl.multiple_of(lax.rem(i, per) * rows, rows), rows), :]
        qb = (jnp.dot(uq, R.w[0:C, :], preferred_element_type=F32) + vec[8:9, :]).astype(B16)
        s = lax.dot_general(qb, R.k[...], nt, preferred_element_type=F32) * scale
        s = jnp.where(R.qid[at, :][:, :1] == key_ids, s, mask_fill)
        e = jnp.exp(s - jnp.max(s, axis=1, keepdims=True))
        p = e * (1.0 / jnp.sum(e, axis=1, keepdims=True))
        pb = p.astype(B16)
        R.out[at, :] = jnp.dot(pb, R.v[...], preferred_element_type=F32).astype(B16)
        if keep:
            R.pbuf[at, :] = pb
            R.q[at, :] = qb
            dout = lax.dot_general(
                R.dz[at, :], R.w[3 * C : 4 * C, :], nt, preferred_element_type=F32).astype(B16)
            R.dout[at, :] = dout
            dp = lax.dot_general(dout, R.v[...], nt, preferred_element_type=F32)
            delta = jnp.sum(p * dp, axis=1, keepdims=True)
            ds = (p * (dp - delta)).astype(B16)
            R.sbuf[at, :] = ds
            R.dq[at, :] = (jnp.dot(ds, R.k[...], preferred_element_type=F32) * scale).astype(B16)

        if not keep:
            @pl.when(i < per)
            def _():
                far_out(i).start()

        return 0

    lax.fori_loop(0, 2 * per, attend, 0)
    if not keep:
        own_out = pltpu.make_async_copy(R.out.at[own_rows], o_home.at[mine], R.lsem.at[2])
        own_out.start()
        own_out.wait()
        for i in range(per):
            far_out(i).wait()
        for cp in started:
            cp.wait_send()
        return
    all_out = pltpu.make_async_copy(R.out, o_home, R.lsem.at[2])
    all_out.start()
    zero = jnp.zeros((C, C), F32)
    pairs = 2 * mates

    def du_of(b, carry):
        dwk, dwv, dbv = carry
        at = block(b)
        dk = (lax.dot_general(R.sbuf[:, at], R.q[...], tn, preferred_element_type=F32) * scale).astype(B16)
        dvf = lax.dot_general(R.pbuf[:, at], R.dout[...], tn, preferred_element_type=F32)
        dv = dvf.astype(B16)
        du = lax.dot_general(dk, R.w[C : 2 * C, :], nt, preferred_element_type=F32)
        du = du + lax.dot_general(dv, R.w[2 * C : 3 * C, :], nt, preferred_element_type=F32)
        piece = R.u[b]
        dwk = dwk + lax.dot_general(piece, dk, tn, preferred_element_type=F32)
        dwv = dwv + lax.dot_general(piece, dv, tn, preferred_element_type=F32)
        return du, (dwk, dwv, dbv + jnp.sum(dvf, axis=0, keepdims=True))

    def place(t):
        far = 1 - t // mates
        return lax.rem(lax.rem(t, mates) + 1, mates), far

    def sib_copy(t):
        return remote(R.for_sib.at[t], R.from_sib.at[t], R.ssend.at[t], R.srecv.at[t], to(sibling))

    def mate_copy(t, part):
        j, _ = place(t)
        here = pl.ds(part * (seg // 2), seg // 2)
        return remote(R.sums.at[t, here], R.from_mate.at[t, here], R.msend.at[t, part], R.mrecv.at[t, part],
                      to(mate(j)))

    def home_copy(part):
        here = pl.ds(part * (seg // 2), seg // 2)
        return remote(R.for_home.at[here], R.from_partner.at[here], R.hsend.at[part], R.hrecv.at[part], to(partner))

    def gathered(far, part):
        count = seg // 2
        at = pl.ds((first_far if far else 1 - first_far) * seg + part * count, count)
        here = pl.ds(part * count, count)
        value = lax.dot_general(R.dq[at, :], R.w[0:C, :], nt, preferred_element_type=F32)
        first_t = 0 if far else mates
        value = value + R.sums[first_t + mates - 1, here, :].astype(F32)
        for t in range(first_t, first_t + mates - 1):
            mate_copy(t, part).wait_recv()
            value = value + R.from_mate[t, here, :].astype(F32)
        return value

    def send_home(part):
        R.for_home[pl.ds(part * (seg // 2), seg // 2), :] = gathered(1, part).astype(B16)
        home_copy(part).start()

    def back(t, carry):
        j, far = place(t)
        theirs, ours = mate(j, 1 - core), mate(j)
        du, carry = du_of(lax.rem(theirs + far * half, n), carry)
        R.for_sib[t] = du.astype(B16)
        sib_copy(t).start()
        du, carry = du_of(lax.rem(ours + far * half, n), carry)
        sib_copy(t).wait_recv()
        R.sums[t] = (du + R.from_sib[t].astype(F32)).astype(B16)

        @pl.when(j != 0)
        def _():
            for part in range(2):
                mate_copy(t, part).start()

        @pl.when(t == pairs - 2)
        def _():
            send_home(0)

        return carry

    dwk, dwv, dbv = lax.fori_loop(0, pairs, back, (zero, zero, jnp.zeros((1, C), F32)))
    send_home(1)
    for part in range(2):
        R.du[mine, pl.ds(part * (seg // 2), seg // 2), :] = gathered(0, part)
    R.dw[C : 2 * C, :] = dwk.astype(B16)
    R.dw[2 * C : 3 * C, :] = dwv.astype(B16)
    R.dw[3 * C : 4 * C, :] = lax.dot_general(
        R.out[...], R.dz[...], tn, preferred_element_type=F32).astype(B16)
    dwq = lax.dot_general(R.u[partner], R.dq[far_rows, :], tn, preferred_element_type=F32)
    dwq = dwq + lax.dot_general(R.u[me], R.dq[own_rows, :], tn, preferred_element_type=F32)
    R.dw[0:C, :] = dwq.astype(B16)
    R.store("dw")
    R.dvec[...] = jnp.concatenate(
        [
            jnp.sum(R.dq[...].astype(F32), axis=0, keepdims=True),
            dbv,
            jnp.sum(R.dz[...].astype(F32), axis=0, keepdims=True),
            jnp.zeros((5, C), F32),
        ],
        axis=0,
    )
    for part in range(2):
        home_copy(part).wait()
    R.du[1 - mine] = R.from_partner[...].astype(F32)
    for move in moves:
        share(*move, False)
    all_out.wait()
    for i in range(per):
        swap_cot(i).wait_send()
    for cp in started:
        cp.wait_send()

    def drain(t, _):
        sib_copy(t).wait_send()

        @pl.when(place(t)[0] != 0)
        def _():
            for part in range(2):
                mate_copy(t, part).wait_send()

        return 0

    lax.fori_loop(0, pairs, drain, 0)


def attend_call(n, keep, cid, u, ids_all, vec, low, cot=None, state=None):
    seg = u.shape[1]
    half = n // 2
    mates = half // 2
    pairs = 2 * mates
    total = n * seg
    rows = min(256 if keep else 128, seg)
    dma = pltpu.SemaphoreType.DMA
    inputs = dict(u_in=(u, anyw), ids_all=(ids_all, vmem), vec=(vec, vmem), low=(low, anyw))
    piece = (seg, C)
    home = (2,) + piece
    scratch = dict(
        u=pltpu.VMEM((n,) + piece, B16), w=pltpu.VMEM((4 * C, C), B16), k=pltpu.VMEM((total, C), B16),
        v=pltpu.VMEM((total, C), B16), qid=pltpu.VMEM((2 * seg, LANES), F32), out=pltpu.VMEM((2 * seg, C), B16),
        lsem=dma((4,)), gsend=dma((4 * mates,)), grecv=dma((n,)))
    if keep:
        inputs.update(cot=(cot, anyw), **{k: (a, anyw) for k, a in zip(("params", "first", "second"), state)})
        outputs = dict(o_home=((2 * seg, C), B16, anyw), dw=((4 * C, C), B16, STORE), dvec=((8, C), F32, vmem),
                       du=(home, F32, vmem), shares=((3, state[0].shape[0] // 2, C), F32, anyw))
        scratch.update(
            csend=dma((seg // rows,)), crecv=dma((seg // rows,)), dz=pltpu.VMEM((2 * seg, C), B16), dout=pltpu.VMEM((2 * seg, C), B16), q=pltpu.VMEM((2 * seg, C), B16),
            dq=pltpu.VMEM((2 * seg, C), B16), pbuf=pltpu.VMEM((2 * seg, total), B16),
            sbuf=pltpu.VMEM((2 * seg, total), B16), for_sib=pltpu.VMEM((pairs,) + piece, B16),
            from_sib=pltpu.VMEM((pairs,) + piece, B16), sums=pltpu.VMEM((pairs,) + piece, B16),
            from_mate=pltpu.VMEM((pairs - 1,) + piece, B16), for_home=pltpu.VMEM(piece, B16),
            from_partner=pltpu.VMEM(piece, B16), ssend=dma((pairs,)), srecv=dma((pairs,)), msend=dma((pairs, 2)),
            mrecv=dma((pairs, 2)), hsend=dma((2,)), hrecv=dma((2,)), wsend=dma((2, 3)), wrecv=dma((3,)))
    else:
        outputs = dict(o_home=(home, B16, anyw))
        scratch.update(osend=dma((seg // rows,)), orecv=dma((seg // rows,)))

    def kernel(R):
        R.rows = rows
        attend_kernel(n, keep, R)

    return named_call(kernel, "attend" if keep else "attend_again", cid, inputs, outputs, scratch)


def outputs_kernel(n, R):
    mine = lax.axis_index(HEIGHT) // (n // 2)
    seg = R.o_back.shape[0]
    own, other = (pl.ds(pl.multiple_of(i * seg, seg), seg) for i in (mine, 1 - mine))
    loads = [
        pltpu.make_async_copy(R.low.at[pl.ds(R.low.shape[0] - C, C)], R.w.at[0], R.sem.at[0]),
        pltpu.make_async_copy(R.o.at[pl.ds(0, seg)], R.o_in.at[0, own], R.sem.at[1]),
        pltpu.make_async_copy(R.o_back, R.o_in.at[0, other], R.sem.at[2]),
        pltpu.make_async_copy(R.new_low.at[pl.ds(R.new_low.shape[0] - C, C)], R.w.at[1], R.sem.at[3]),
        pltpu.make_async_copy(R.o2, R.o_in.at[1], R.sem.at[4]),
    ]
    for cp in loads:
        cp.start()
    count = R.part.shape[2]
    parts = R.hid.shape[0] // count
    bases = {}
    for which, src in enumerate((R.hid, R.hid2, R.igrad)):
        for i in range(parts):
            at = pl.ds(i * count, count)
            bases[which, i] = pltpu.make_async_copy(src.at[at], R.held.at[which, at], R.hsem.at[which, i])
            bases[which, i].start()
    ends = []

    def out(src, dst, sem):
        cp = pltpu.make_async_copy(src, dst, sem)
        cp.start()
        ends.append(cp)

    for cp in loads[:3]:
        cp.wait()
    for which, (vec, dst) in enumerate(((R.vec, R.first), (R.new_vec, R.second))):
        if which == 1:
            for cp in loads[3:]:
                cp.wait()
        for i in range(parts):
            at = pl.ds(i * count, count)
            bases[which, i].wait()
            if which == 0:
                out(R.held.at[0, at], R.hid_out.at[at], R.osem.at[0, i])
            R.part[which, i] = (
                R.held[which, at, :]
                + jnp.dot(R.o_in[which, at, :], R.w[which], preferred_element_type=F32) + vec[10:11, :])
            out(R.part.at[which, i], dst.at[at], R.osem.at[1 + which, i])
    for i in range(parts):
        at = pl.ds(i * count, count)
        bases[2, i].wait()
        out(R.held.at[2, at], R.igrad_out.at[at], R.osem.at[3, i])
    for cp in ends:
        cp.wait()


def outputs_call(n, hid, hid2, o, o_back, o2, igrad, vec, new_vec, low, new_low):
    px = hid.shape[0]
    inputs = dict(hid=(hid, anyw), hid2=(hid2, anyw), o=(o, anyw), o_back=(o_back, anyw), o2=(o2, anyw),
                  igrad=(igrad, anyw),
                  vec=(vec, vmem), new_vec=(new_vec, vmem), low=(low, anyw), new_low=(new_low, anyw))
    whole = ((px, C), F32, anyw)
    outputs = dict(hid_out=whole, first=whole, second=whole, igrad_out=whole)
    count = min(256, px)
    parts = px // count
    dma = pltpu.SemaphoreType.DMA
    scratch = dict(
        w=pltpu.VMEM((2, C, C), B16), held=pltpu.VMEM((3, px, C), F32), o_in=pltpu.VMEM((2, px, C), B16),
        part=pltpu.VMEM((2, parts, count, C), F32), sem=dma((5,)), hsem=dma((3, parts)), osem=dma((4, parts)))
    return named_call(functools.partial(outputs_kernel, n), "outputs", None, inputs, outputs, scratch)


def rounded_vectors(vectors):
    return lax.reduce_precision(vectors, exponent_bits=8, mantissa_bits=7)


def body(columns, n, latents, crop_ids, params, vectors, first_moment, second_moment, vector_first, vector_second,
         cotangent):
    canvases, rows, width, channels = latents.shape
    dims = (canvases, rows, width)
    px = canvases * rows * width
    plane = rows * width
    half = n // 2
    me = lax.axis_index(HEIGHT)
    mine = me // half
    partner = lax.rem(me + half, n)
    swap = [(i, (i + half) % n) for i in range(n)]
    count = vectors.shape[0]
    joined = columns == 4 and params.shape[0] % 32 == 0 and rows > 2

    ids = crop_ids.astype(F32)
    ids_lane = jnp.pad(ids.reshape(canvases, plane), ((0, 8 - canvases), (0, 0)))
    x = latents.reshape(px, channels)
    cot = cotangent.reshape(px, channels)
    cot3 = cotangent.reshape(canvases, plane, channels)
    shape = latents.shape
    if joined:
        first = first_call(columns, n, dims, x, ids_lane, vectors, params)
        ids_all, mean1, inv1, div, cnt, pick, spread, vec = (
            first[k] for k in ("ids_all", "mean1", "inv1", "div", "cnt", "pick", "spread", "vec"))
        masks = [first[k] for k in ("col_l", "col_r", "row_u", "row_d")]
        hid, u, y1, s1, s2 = (first[k] for k in ("hid", "u", "y1_out", "s1_out", "s2_out"))
        norms = [first[k] for k in ("mean2", "inv2", "mean3", "inv3")]
        top, low = first["top"], first["bottom"]
        att = attend_call(n, True, 4, u.reshape(canvases, plane, channels), ids_all, vec, low, cot3,
                          (params, first_moment, second_moment))
        du = att["du"].reshape(px, channels)
        back = back_call(columns, n, dims, cot, du, hid, y1, norms, s1, s2, pick, spread, div, masks, vec, top, low,
                         att["dw"], att["o_home"], params.shape[0])
        new = renew_call(columns, n, dims, back["grad"], back["dh"], x, mean1, inv1, pick, spread, div, cnt, first["cnt_all"],
                         masks, vec, top, back["g_top"], back["halves"], back["dvec"], att["dvec"], params, first_moment,
                         second_moment, att["shares"], vectors, vector_first, vector_second)
        new_vec, new_att = new["new_vec"], new["new_att"]
        o2 = attend_call(n, False, 5, new["u"].reshape(canvases, plane, channels), ids_all, new_vec, new_att)["o_home"]
        last = outputs_call(n, hid, new["hid"], att["o_home"], back["o_back"], o2.reshape(px, channels), new["igrad"],
                            vec, new_vec, low, new_att)
        return (
            *(last[k].reshape(shape) for k in ("hid_out", "first", "second", "igrad_out")),
            *(new[k] for k in ("new_w", "new_m", "new_s", "new_vw", "new_vm", "new_vs")),
        )

    def padded(value):
        return jnp.pad(value, ((0, 16 - count), (0, 0)))

    wide_vectors = padded(vectors)
    vec = rounded_vectors(wide_vectors)
    cell_ids = crop_ids[:, :, ::UNIT] + CROPS * jnp.arange(canvases, dtype=jnp.int32)[:, None, None]
    cell_ids = cell_ids.reshape(1, -1)
    stat = jnp.arange(canvases * CROPS, dtype=jnp.int32)[:, None]
    pick = (cell_ids == stat).astype(B16)
    spread = (cell_ids.reshape(-1, 1) == stat.reshape(1, -1)).astype(B16)
    ids_px = jnp.broadcast_to(ids[..., None], (canvases, rows, width, LANES))
    whole = spread_call(columns, n, 8, params).reshape(-1, channels)
    top, low = whole[: 11 * C], whole[11 * C :]
    ids_all, mean1, inv1, div, cnt, *masks = layout_call(n, dims, x, pick, spread, ids_px, ids_lane)
    hid, u, y1, s1, s2, mean2, inv2, mean3, inv3 = resnet_forward_call(
        n, dims, True, x, pick, spread, cnt, mean1, inv1, masks, vec, top, low)
    own_cot = lax.dynamic_index_in_dim(cot3, mine, axis=0, keepdims=False)
    far_cot = lax.ppermute(
        lax.dynamic_index_in_dim(cot3, 1 - mine, axis=0, keepdims=False), HEIGHT, swap)
    dz = jnp.concatenate([own_cot, far_cot], axis=0)
    canvas_ids = lax.dynamic_index_in_dim(ids_all, mine, axis=1, keepdims=False)
    key_ids = canvas_ids.reshape(1, n * plane)
    query_ids = jnp.stack([canvas_ids[me], canvas_ids[partner]]).reshape(2 * plane, 1)
    query_ids = jnp.broadcast_to(query_ids, (2 * plane, LANES))
    offsets = jnp.stack([me, partner]) * plane

    def attention_output(o, hid, low, bias):
        back = lax.ppermute(o[plane:], HEIGHT, swap)
        ordered = jnp.where(mine == 0, jnp.stack([o[:plane], back]), jnp.stack([back, o[:plane]]))
        product = jnp.dot(ordered.reshape(px, channels), low[10 * C :], preferred_element_type=F32)
        return hid + product + bias

    ua = gather_call(n, 4, u.reshape(canvases, plane, channels))
    o, dup, dw_att, dvec_att = attention_call(True, ua, key_ids, query_ids, offsets, dz, vec, low)
    first_output = attention_output(o, hid, low, vec[10])
    du = scatter_call(n, 6, dup.reshape(n, plane, channels)).reshape(px, channels)
    norms = (mean1, inv1, mean2, inv2, mean3, inv3)
    input_grad, matrix_grad, dvec = resnet_backward_call(
        n, dims, 7, cot, du, hid, y1, x, norms, s1, s2, pick, spread, div, masks, vec, top, low, dw_att)
    vector_grad = jnp.concatenate([dvec, dvec_att], axis=0)
    new_params, new_first, new_second, *new_small, new_whole = step_call(
        columns, n, 9, matrix_grad.reshape((columns, half, 2) + params.shape), params, first_moment,
        second_moment, vector_grad, wide_vectors, padded(vector_first), padded(vector_second))
    new_whole = new_whole.reshape(-1, channels)
    new_top, new_low = new_whole[: 11 * C], new_whole[11 * C :]
    new_vec = rounded_vectors(new_small[0])
    hid2, u2 = resnet_forward_call(
        n, dims, False, x, pick, spread, cnt, mean1, inv1, masks, new_vec, new_top, new_low)
    ua2 = gather_call(n, 5, u2.reshape(canvases, plane, channels))
    (o2,) = attention_call(False, ua2, key_ids, query_ids, offsets, dz, new_vec, new_low)
    second_output = attention_output(o2, hid2, new_low, new_vec[10])
    return (
        *(a.reshape(shape) for a in (hid, first_output, second_output, input_grad)),
        new_params,
        new_first,
        new_second,
        *(a[:count] for a in new_small),
    )


def solution(mesh):
    spatial = P(CANVAS, HEIGHT, None, None)
    owned = P((CANVAS, HEIGHT), None)
    return jax.shard_map(
        functools.partial(body, mesh.shape[CANVAS], mesh.shape[HEIGHT]),
        mesh=mesh,
        in_specs=(spatial, P(CANVAS, HEIGHT, None), owned, P(), owned, owned, P(), P(), spatial),
        out_specs=(spatial, spatial, spatial, spatial, owned, owned, owned, P(), P(), P()),
        check_vma=False,
    )
```

```python
import functools

import jax
import jax.numpy as jnp
from jax import lax
from jax.experimental import pallas as pl
from jax.experimental.pallas import tpu as pltpu
from jax.sharding import PartitionSpec as P

C = 512
GROUPS = 32
STEP = 5
CROPS = 16
SPAN = C // GROUPS
LANES = 128
TILES = C // LANES
UNIT = 8

norm_epsilon = 1e-06
adam_epsilon = 1e-08
matrix_rate = 0.015
vector_rate = 0.2
mask_fill = -1e30

HEIGHT = "height"
CANVAS = "canvas"
LOAD = "load"
STORE = "store"

F32 = jnp.float32
B16 = jnp.bfloat16
MESH = pl.DeviceIdType.MESH
VMEM_LIMIT = 60 * 2**20

vmem = pl.BlockSpec(memory_space=pltpu.VMEM)
smem = pl.BlockSpec(memory_space=pltpu.SMEM)
anyw = pl.BlockSpec(memory_space=pl.ANY)


def params_of(cid=None):
    if cid is None:
        return pltpu.CompilerParams(vmem_limit_bytes=VMEM_LIMIT)
    return pltpu.CompilerParams(
        vmem_limit_bytes=VMEM_LIMIT, collective_id=cid, has_side_effects=True
    )


def sds(shape, dtype):
    return jax.ShapeDtypeStruct(shape, dtype)


def split_dot(pick, value):
    total = None
    rest = value
    for _ in range(3):
        part = rest.astype(B16)
        term = jnp.dot(pick, part, preferred_element_type=F32)
        total = term if total is None else total + term
        rest = rest - part.astype(F32)
    return total


def lane_group_sum(piece):
    lane = lax.broadcasted_iota(jnp.int32, piece.shape, 1)
    step = 1
    while step < SPAN:
        ahead = pltpu.roll(piece, LANES - step, 1)
        behind = pltpu.roll(piece, step, 1)
        piece = piece + jnp.where((lane & step) == 0, ahead, behind)
        step *= 2
    return piece


def tiles_of(value):
    return [value[:, j * LANES : (j + 1) * LANES] for j in range(TILES)]


def wide(piece, times=TILES):
    return jnp.concatenate([piece] * times, axis=1)


def pack(quantities):
    shape = quantities[0][0].shape
    sub = lax.broadcasted_iota(jnp.int32, shape, 1) & (SPAN - 1)
    out = jnp.zeros(shape, F32)
    for q, pieces in enumerate(quantities):
        for j, piece in enumerate(pieces):
            out = jnp.where(sub == TILES * q + j, piece, out)
    return out


def unpack(packed):
    sub = lax.broadcasted_iota(jnp.int32, packed.shape, 1) & (SPAN - 1)
    return jnp.concatenate(
        [lane_group_sum(jnp.where(sub == j, packed, 0.0)) for j in range(TILES)], axis=1
    )


def shift_down(packed, q):
    return pltpu.roll(packed, LANES - TILES * q, packed.ndim - 1)


def no_pump():
    return None


def fold(packed):
    rows = packed.shape[0] // 2
    sub = lax.broadcasted_iota(jnp.int32, (rows, LANES), 1) & (SPAN - 1)
    return jnp.where(sub < 2 * TILES, packed[:rows], pltpu.roll(packed[rows:], 2 * TILES, 1))


def unfold(folded):
    return jnp.concatenate([folded, pltpu.roll(folded, LANES - 2 * TILES, folded.ndim - 1)], axis=folded.ndim - 2)


def greet(n):
    me = lax.axis_index(HEIGHT)
    barrier = pltpu.get_barrier_semaphore()
    for d in range(1, n):
        pl.semaphore_signal(
            barrier, inc=1, device_id={HEIGHT: lax.rem(me + d, n)}, device_id_type=MESH
        )
    pl.semaphore_wait(barrier, n - 1)


def spread_copies(n, buf, send, recv, rnd):
    me = lax.axis_index(HEIGHT)
    return [
        pltpu.make_async_remote_copy(
            src_ref=buf.at[rnd, 0],
            dst_ref=buf.at[rnd, d],
            send_sem=send.at[rnd, d],
            recv_sem=recv.at[rnd, d],
            device_id={HEIGHT: lax.rem(me + d, n)},
            device_id_type=MESH,
        )
        for d in sorted(range(1, n), key=lambda d: abs(d - n // 2))
    ]


def cell_totals(load, out_ref, cells):
    def body(i, _):
        out_ref[pl.ds(i * 16, 16), :] = jnp.sum(load(i).reshape(16, UNIT, C), axis=1)
        return 0

    lax.fori_loop(0, cells // 16, body, 0)


def over_cells(cell_ref, i):
    return jnp.broadcast_to(cell_ref[pl.ds(i * 16, 16), :][:, None, :], (16, UNIT, C)).reshape(
        16 * UNIT, C
    )


def group_totals(pick_ref, cell_value):
    return [lane_group_sum(t) for t in tiles_of(split_dot(pick_ref[...], cell_value))]


def stats_payload(load, pick_ref, spread_ref, count_ref, cells, tmp_a, tmp_b, counted=True):
    cell_totals(load, tmp_a, cells)
    sums = group_totals(pick_ref, tmp_a[...])
    count = count_ref[...]
    inv_count = 1.0 / jnp.maximum(count, 1.0)
    mean = jnp.concatenate([s * inv_count for s in sums], axis=1)
    tmp_b[...] = split_dot(spread_ref[...], mean)

    def centred(i):
        delta = load(i) - over_cells(tmp_b, i)
        return delta * delta

    cell_totals(centred, tmp_a, cells)
    squares = group_totals(pick_ref, tmp_a[...])
    return pack([sums, squares, [count] * TILES]) if counted else fold(pack([sums, squares]))


def combine_stats(gathered, counts=None):
    sums = gathered
    squares = shift_down(gathered, 1)
    counts = shift_down(gathered, 2) if counts is None else counts
    divisor = jnp.maximum(jnp.sum(counts, axis=0), 1.0)
    mean = jnp.sum(sums, axis=0) / divisor
    apart = sums / jnp.maximum(counts, 1.0) - mean[None]
    spread = jnp.sum(squares + counts * apart * apart, axis=0) / divisor
    return mean, lax.rsqrt(spread + norm_epsilon), divisor


def shift_columns(row, left_mask, right_mask):
    width = row.shape[0]
    left = pltpu.roll(row, 1, 0) * wide(left_mask)
    right = pltpu.roll(row, width - 1, 0) * wide(right_mask)
    return jnp.concatenate([left, row, right], axis=1).astype(B16)


def logistic(a):
    return 1.0 / (1.0 + jnp.exp(-a))


def silu(a):
    return a * logistic(a)


def silu_slope(a):
    s = logistic(a)
    return s * (1.0 + a * (1.0 - s))


def layout_kernel(n, dims, x, pick, spread, ids_px, ids_lane, ids_all, mean_c, inv_c, div, cnt,
                  col_l, col_r, row_u, row_d, *scratch):
    greet(n)
    layout_body(n, dims, x, pick, spread, ids_px, ids_lane, ids_all, mean_c, inv_c, div, cnt,
                col_l, col_r, row_u, row_d, *scratch)


def layout_body(n, dims, x, pick, spread, ids_px, ids_lane, ids_all, mean_c, inv_c, div, cnt,
                col_l, col_r, row_u, row_d, buf, idbuf, halo, tmp_a, tmp_b, send, recv, isend, irecv,
                hsend, hrecv, pump=no_pump, cnt_all=None):
    canvases, rows, width = dims
    cells = canvases * rows * width // UNIT
    me = lax.axis_index(HEIGHT)
    id_copies = []
    idbuf[0] = ids_lane[...]
    for d in range(1, n):
        cp = pltpu.make_async_remote_copy(
            src_ref=idbuf.at[0], dst_ref=idbuf.at[d], send_sem=isend.at[d], recv_sem=irecv.at[d],
            device_id={HEIGHT: lax.rem(me + d, n)}, device_id_type=MESH)
        cp.start()
        id_copies.append(cp)
    up, down = halo_copies(n, ids_px.at[:, 0], ids_px.at[:, rows - 1], halo, hsend, hrecv)
    start_halo(n, up, down)

    def load(i):
        return x[pl.ds(i * 16 * UNIT, 16 * UNIT), :].astype(F32)

    ones = jnp.sum(pick[...].astype(F32), axis=1, keepdims=True) * float(UNIT * SPAN)
    cnt[...] = jnp.broadcast_to(ones, cnt.shape)
    buf[0, 0] = stats_payload(load, pick, spread, cnt, cells, tmp_a, tmp_b)
    copies = spread_copies(n, buf, send, recv, 0)
    for cp in copies:
        cp.start()
    pump()
    wait_halo(n, up, down, halo, -1.0)
    column = lax.broadcasted_iota(jnp.int32, (width, LANES), 0)
    first, last = column == 0, column == width - 1
    for v in range(canvases):
        for r in range(rows + 2):
            here = halo[0, v] if r == 0 else halo[1, v] if r == rows + 1 else ids_px[v, r - 1]
            same_l = (pltpu.roll(here, 1, 0) == here) & jnp.logical_not(first)
            same_r = (pltpu.roll(here, width - 1, 0) == here) & jnp.logical_not(last)
            col_l[v, r] = same_l.astype(F32)
            col_r[v, r] = same_r.astype(F32)
            if 1 <= r <= rows:
                above = halo[0, v] if r == 1 else ids_px[v, r - 2]
                below = halo[1, v] if r == rows else ids_px[v, r]
                at = pl.ds((v * rows + r - 1) * width, width)
                row_u[at, :] = (above == here).astype(F32)
                row_d[at, :] = (below == here).astype(F32)
    pump()
    for cp in copies:
        cp.wait_recv()
    mean, inv, divisor = combine_stats(buf[0])
    if cnt_all is not None:
        cnt_all[...] = shift_down(buf[0], 2)
    mean_c[...] = split_dot(spread[...], unpack(mean))
    inv_c[...] = split_dot(spread[...], unpack(inv))
    div[...] = unpack(divisor)[:, :LANES]
    for cp in id_copies:
        cp.wait_recv()
    ids_all[me] = idbuf[0]
    for d in range(1, n):
        ids_all[lax.rem(me - d + n, n)] = idbuf[d]
    for cp in copies + id_copies:
        cp.wait_send()


def halo_copies(n, first_row, last_row, halo, hsend, hrecv):
    me = lax.axis_index(HEIGHT)
    up = pltpu.make_async_remote_copy(
        src_ref=first_row, dst_ref=halo.at[1], send_sem=hsend.at[0], recv_sem=hrecv.at[1],
        device_id={HEIGHT: lax.rem(me + n - 1, n)}, device_id_type=MESH)
    down = pltpu.make_async_remote_copy(
        src_ref=last_row, dst_ref=halo.at[0], send_sem=hsend.at[1], recv_sem=hrecv.at[0],
        device_id={HEIGHT: lax.rem(me + 1, n)}, device_id_type=MESH)
    return up, down


def start_halo(n, up, down):
    me = lax.axis_index(HEIGHT)

    @pl.when(me > 0)
    def _():
        up.start()

    @pl.when(me < n - 1)
    def _():
        down.start()


def wait_halo(n, up, down, halo, edge):
    me = lax.axis_index(HEIGHT)

    @pl.when(me > 0)
    def _():
        up.wait_send()
        down.wait_recv()

    @pl.when(me < n - 1)
    def _():
        down.wait_send()
        up.wait_recv()

    @pl.when(me == 0)
    def _():
        halo[0] = jnp.full(halo.shape[1:], edge, halo.dtype)

    @pl.when(me == n - 1)
    def _():
        halo[1] = jnp.full(halo.shape[1:], edge, halo.dtype)


def layout_scratch(n, dims, ids_lane):
    canvases, rows, width = dims
    cells = canvases * rows * width // UNIT
    return [
        pltpu.VMEM((1, n, canvases * CROPS, LANES), F32),
        pltpu.VMEM((n,) + ids_lane.shape, F32),
        pltpu.VMEM((2, canvases, width, LANES), F32),
        pltpu.VMEM((cells, C), F32),
        pltpu.VMEM((cells, C), F32),
        pltpu.SemaphoreType.DMA((1, n)),
        pltpu.SemaphoreType.DMA((1, n)),
        pltpu.SemaphoreType.DMA((n,)),
        pltpu.SemaphoreType.DMA((n,)),
        pltpu.SemaphoreType.DMA((2,)),
        pltpu.SemaphoreType.DMA((2,)),
    ]


def layout_call(n, dims, x, pick, spread, ids_px, ids_lane):
    canvases, rows, width = dims
    px = canvases * rows * width
    cells = px // UNIT
    stats = canvases * CROPS
    return pl.pallas_call(
        functools.partial(layout_kernel, n, dims),
        out_shape=[
            sds((n,) + ids_lane.shape, F32),
            sds((cells, C), F32),
            sds((cells, C), F32),
            sds((stats, LANES), F32),
            sds((stats, LANES), F32),
            sds((canvases, rows + 2, width, LANES), F32),
            sds((canvases, rows + 2, width, LANES), F32),
            sds((px, LANES), F32),
            sds((px, LANES), F32),
        ],
        in_specs=[vmem] * 5,
        out_specs=[vmem] * 9,
        scratch_shapes=layout_scratch(n, dims, ids_lane),
        compiler_params=params_of(1),
        name="layout",
    )(x, pick, spread, ids_px, ids_lane)


def second_matrix(top, low, dest, sem):
    return [
        pltpu.make_async_copy(top.at[pl.ds(9 * C, 2 * C)], dest.at[pl.ds(0, 2 * C)], sem.at[1]),
        pltpu.make_async_copy(low.at[pl.ds(0, 7 * C)], dest.at[pl.ds(2 * C, 7 * C)], sem.at[2]),
    ]


class Convolver:
    def __init__(self, n, dims, x, pick, spread, cnt, col_l, col_r, row_u, row_d, halo, buf, tmp_a, tmp_b, send,
                 recv, hsend, hrecv, cnt_all=None):
        self.n, self.dims, self.cnt_all = n, dims, cnt_all
        self.x, self.pick, self.spread, self.cnt = x, pick, spread, cnt
        self.col_l, self.col_r, self.row_u, self.row_d = col_l, col_r, row_u, row_d
        self.halo, self.buf, self.tmp_a, self.tmp_b = halo, buf, tmp_a, tmp_b
        self.send, self.recv, self.hsend, self.hrecv = send, recv, hsend, hrecv
        self.px = dims[0] * dims[1] * dims[2]
        self.cells = self.px // UNIT
        self.sent = []

    def activate(self, source, mean, inv, gain, bias, dest, rnd, pump=no_pump):
        canvases, rows, width = self.dims
        row_cells = width // UNIT
        col_l, col_r, halo = self.col_l, self.col_r, self.halo

        def one(v, r):
            at = pl.ds(pl.multiple_of((v * rows + r) * width, width), width)
            cell = pl.ds(pl.multiple_of((v * rows + r) * row_cells, row_cells), row_cells)
            value = source[at, :].astype(F32)
            m = jnp.broadcast_to(mean[cell, :][:, None, :], (row_cells, UNIT, C)).reshape(width, C)
            s = jnp.broadcast_to(inv[cell, :][:, None, :], (row_cells, UNIT, C)).reshape(width, C)
            a = (value - m) * s * gain + bias
            dest[v, r + 1] = shift_columns(silu(a), col_l[v, r + 1], col_r[v, r + 1])

        def edges(v, _):
            one(v, 0)
            if rows > 1:
                one(v, rows - 1)
            return 0

        lax.fori_loop(0, canvases, edges, 0)
        mid = pl.ds(C, C)
        up, down = halo_copies(self.n, dest.at[:, 1, :, mid], dest.at[:, rows, :, mid], halo.at[rnd],
                               self.hsend.at[rnd], self.hrecv.at[rnd])
        start_halo(self.n, up, down)
        pump()

        def inner(i, _):
            one(i // (rows - 2), 1 + lax.rem(i, rows - 2))
            return 0

        if rows > 2:
            lax.fori_loop(0, canvases * (rows - 2), inner, 0)
        pump()
        wait_halo(self.n, up, down, halo.at[rnd], 0.0)
        for v in range(canvases):
            for side, r in ((0, 0), (1, rows + 1)):
                dest[v, r] = shift_columns(halo[rnd, side, v].astype(F32), col_l[v, r], col_r[v, r])

    def convolve(self, source, weights, emit, pump=no_pump):
        canvases, rows, width = self.dims
        plane = rows * width
        for v in range(canvases):
            at = pl.ds(v * plane, plane)
            total = None
            for dr in (1, 0, 2):
                part = None
                for lo, hi, ref, row in weights(dr):
                    lhs = source[v, dr : dr + rows, :, lo:hi].reshape(plane, hi - lo)
                    term = jnp.dot(lhs, ref[row : row + hi - lo, :], preferred_element_type=F32)
                    part = term if part is None else part + term
                if dr == 0:
                    part = part * wide(self.row_u[at, :])
                if dr == 2:
                    part = part * wide(self.row_d[at, :])
                total = part if total is None else total + part
            emit(at, total)
            pump()

    def statistics(self, source, mean, inv, rnd, pump=no_pump):
        def load(i):
            return source[pl.ds(i * 16 * UNIT, 16 * UNIT), :]

        counted = self.cnt_all is None
        self.buf[rnd, 0] = stats_payload(
            load, self.pick, self.spread, self.cnt, self.cells, self.tmp_a, self.tmp_b, counted)
        copies = spread_copies(self.n, self.buf, self.send, self.recv, rnd)
        for cp in copies:
            cp.start()
        pump()
        for cp in copies:
            cp.wait_recv()
        m, s, _ = (
            combine_stats(self.buf[rnd]) if counted else combine_stats(unfold(self.buf[rnd]), self.cnt_all[...]))
        mean[...] = split_dot(self.spread[...], unpack(m))
        inv[...] = split_dot(self.spread[...], unpack(s))
        self.sent = self.sent + copies

    def normalise(self, source, mean, inv, gain, bias, dest):
        def last(i, _):
            at = pl.ds(i * 16 * UNIT, 16 * UNIT)
            value = (source[at, :] - over_cells(mean, i)) * over_cells(inv, i)
            dest[at, :] = (value * gain + bias).astype(B16)
            return 0

        lax.fori_loop(0, self.cells // 16, last, 0)


def resnet_forward_kernel(n, dims, keep, x, pick, spread, cnt, mean1, inv1, col_l, col_r, row_u, row_d,
                          vec, top, low, *refs):
    canvases, rows, width = dims
    px = canvases * rows * width
    cells = px // UNIT
    plane = rows * width
    if keep:
        hid, u, y1, s1, s2, mean2, inv2, mean3, inv3 = refs[:9]
        refs = refs[9:]
    else:
        hid, u = refs[:2]
        y1, s1, s2, mean2, inv2, mean3, inv3 = refs[2:9]
        refs = refs[9:]
    k1, k2, halo, buf, tmp_a, tmp_b, ksem, send, recv, hsend, hrecv = refs
    load1 = [pltpu.make_async_copy(top.at[pl.ds(0, 9 * C)], k1, ksem.at[0])]
    load2 = second_matrix(top, low, k2, ksem)
    for cp in load1 + load2:
        cp.start()
    greet(n)
    for_conv = Convolver(n, dims, x, pick, spread, cnt, col_l, col_r, row_u, row_d, halo, buf, tmp_a, tmp_b,
                         send, recv, hsend, hrecv)

    def wait_all(copies):
        for cp in copies:
            cp.wait()

    for_conv.activate(x, mean1, inv1, vec[0:1, :], vec[1:2, :], s1, 0)
    wait_all(load1)

    def emit_first(at, total):
        y1[at, :] = total + vec[2:3, :]

    for_conv.convolve(s1, lambda dr: [(0, 3 * C, k1, 3 * C * dr)], emit_first)
    for_conv.statistics(y1, mean2, inv2, 0)
    for_conv.activate(y1, mean2, inv2, vec[3:4, :], vec[4:5, :], s2, 1)
    wait_all(load2)

    def emit_second(at, total):
        hid[at, :] = total + vec[5:6, :] + x[at, :].astype(F32)

    for_conv.convolve(s2, lambda dr: [(0, 3 * C, k2, 3 * C * dr)], emit_second)
    for_conv.statistics(hid, mean3, inv3, 1)
    for_conv.normalise(hid, mean3, inv3, vec[6:7, :], vec[7:8, :], u)
    for cp in for_conv.sent:
        cp.wait_send()


def resnet_forward_call(n, dims, keep, x, pick, spread, cnt, mean1, inv1, masks, vec, top, low):
    canvases, rows, width = dims
    px = canvases * rows * width
    cells = px // UNIT
    stats = canvases * CROPS
    saved = [
        ((px, C), F32),
        ((canvases, rows + 2, width, 3 * C), B16),
        ((canvases, rows + 2, width, 3 * C), B16),
        ((cells, C), F32),
        ((cells, C), F32),
        ((cells, C), F32),
        ((cells, C), F32),
    ]
    main = [((px, C), F32), ((px, C), B16)]
    outs = main + (saved if keep else [])
    scratch = [] if keep else [pltpu.VMEM(*s) for s in saved]
    return pl.pallas_call(
        functools.partial(resnet_forward_kernel, n, dims, keep),
        out_shape=[sds(*s) for s in outs],
        in_specs=[vmem] * 11 + [anyw] * 2,
        out_specs=[vmem] * len(outs),
        scratch_shapes=scratch
        + [
            pltpu.VMEM((9 * C, C), B16),
            pltpu.VMEM((9 * C, C), B16),
            pltpu.VMEM((2, 2, canvases, width, C), B16),
            pltpu.VMEM((2, n, stats, LANES), F32),
            pltpu.VMEM((cells, C), F32),
            pltpu.VMEM((cells, C), F32),
            pltpu.SemaphoreType.DMA((3,)),
            pltpu.SemaphoreType.DMA((2, n)),
            pltpu.SemaphoreType.DMA((2, n)),
            pltpu.SemaphoreType.DMA((2, 2)),
            pltpu.SemaphoreType.DMA((2, 2)),
        ],
        compiler_params=params_of(2 if keep else 3),
        name="resnet_forward" if keep else "resnet_again",
    )(x, pick, spread, cnt, mean1, inv1, *masks, vec, top, low)


def attention_kernel(keep, chunk, block, ua, key_ids, query_ids, offsets, dz, vec, low, *refs):
    total = ua.shape[0] * ua.shape[1]
    queries = query_ids.shape[0]
    segment = ua.shape[1]
    scale = C ** (-0.5)
    if keep:
        out, dup, dw, dvec = refs[:4]
        u, w, k, v, pbuf, sbuf, q, dout, dq, usem, wsem = refs[4:]
    else:
        out = refs[0]
        u, w, k, v, usem, wsem = refs[1:]
    load_w = pltpu.make_async_copy(low.at[pl.ds(7 * C, 4 * C)], w, wsem.at[0])
    load_w.start()
    blocks = ua.shape[0]
    loads = [
        pltpu.make_async_copy(ua.at[i], u.at[pl.ds(i * segment, segment)], usem.at[i])
        for i in range(blocks)
    ]
    for cp in loads:
        cp.start()
    load_w.wait()
    for cp in loads:
        cp.wait()
    nt = (((1,), (1,)), ((), ()))
    tn = (((0,), (0,)), ((), ()))

    def project(i, _):
        at = pl.ds(pl.multiple_of(i * chunk, chunk), chunk)
        piece = u[at, :]
        k[at, :] = jnp.dot(piece, w[C : 2 * C, :], preferred_element_type=F32).astype(B16)
        v[at, :] = (
            jnp.dot(piece, w[2 * C : 3 * C, :], preferred_element_type=F32) + vec[9:10, :]
        ).astype(B16)
        return 0

    lax.fori_loop(0, total // chunk, project, 0)
    per = segment // block

    def place(i):
        return pl.multiple_of(offsets[i // per] + lax.rem(i, per) * block, block)

    def attend(i, _):
        at = pl.ds(pl.multiple_of(i * block, block), block)
        uq = u[pl.ds(place(i), block), :]
        qb = (
            jnp.dot(uq, w[0:C, :], preferred_element_type=F32) + vec[8:9, :]
        ).astype(B16)
        s = lax.dot_general(qb, k[...], nt, preferred_element_type=F32) * scale
        s = jnp.where(query_ids[at, :][:, :1] == key_ids[...], s, mask_fill)
        e = jnp.exp(s - jnp.max(s, axis=1, keepdims=True))
        p = e * (1.0 / jnp.sum(e, axis=1, keepdims=True))
        pb = p.astype(B16)
        ob = jnp.dot(pb, v[...], preferred_element_type=F32).astype(B16)
        out[at, :] = ob
        if keep:
            pbuf[at, :] = pb
            q[at, :] = qb
            do = lax.dot_general(
                dz[at, :], w[3 * C : 4 * C, :], nt, preferred_element_type=F32
            ).astype(B16)
            dout[at, :] = do
            dp = lax.dot_general(do, v[...], nt, preferred_element_type=F32)
            delta = jnp.sum(p * dp, axis=1, keepdims=True)
            ds = (p * (dp - delta)).astype(B16)
            sbuf[at, :] = ds
            dq[at, :] = (jnp.dot(ds, k[...], preferred_element_type=F32) * scale).astype(B16)
        return 0

    lax.fori_loop(0, queries // block, attend, 0)
    if not keep:
        return
    zero = jnp.zeros((C, C), F32)

    def back(i, carry):
        dwk, dwv, dbv = carry
        at = pl.ds(pl.multiple_of(i * chunk, chunk), chunk)
        dk = (
            lax.dot_general(sbuf[:, at], q[...], tn, preferred_element_type=F32) * scale
        ).astype(B16)
        dvf = lax.dot_general(pbuf[:, at], dout[...], tn, preferred_element_type=F32)
        dv = dvf.astype(B16)
        du = lax.dot_general(dk, w[C : 2 * C, :], nt, preferred_element_type=F32)
        du = du + lax.dot_general(dv, w[2 * C : 3 * C, :], nt, preferred_element_type=F32)
        dup[at, :] = du.astype(B16)
        piece = u[at, :]
        dwk = dwk + lax.dot_general(piece, dk, tn, preferred_element_type=F32)
        dwv = dwv + lax.dot_general(piece, dv, tn, preferred_element_type=F32)
        return dwk, dwv, dbv + jnp.sum(dvf, axis=0, keepdims=True)

    dwk, dwv, dbv = lax.fori_loop(0, total // chunk, back, (zero, zero, jnp.zeros((1, C), F32)))
    dw[C : 2 * C, :] = dwk.astype(B16)
    dw[2 * C : 3 * C, :] = dwv.astype(B16)
    dw[3 * C : 4 * C, :] = lax.dot_general(
        out[...], dz[...], tn, preferred_element_type=F32
    ).astype(B16)
    dwq = zero
    for s in range(2):
        where = pl.ds(pl.multiple_of(offsets[s], segment), segment)
        at = pl.ds(s * segment, segment)
        dwq = dwq + lax.dot_general(u[where, :], dq[at, :], tn, preferred_element_type=F32)
        du = lax.dot_general(dq[at, :], w[0:C, :], nt, preferred_element_type=F32)
        dup[where, :] = (dup[where, :].astype(F32) + du).astype(B16)
    dw[0:C, :] = dwq.astype(B16)
    dvec[...] = jnp.concatenate(
        [
            jnp.sum(dq[...].astype(F32), axis=0, keepdims=True),
            dbv,
            jnp.sum(dz[...].astype(F32), axis=0, keepdims=True),
            jnp.zeros((5, C), F32),
        ],
        axis=0,
    )


def attention_call(keep, ua, key_ids, query_ids, offsets, dz, vec, low):
    blocks, segment, _ = ua.shape
    total = blocks * segment
    queries = query_ids.shape[0]
    block = min(256, segment)
    chunk = 512
    outs = [sds((queries, C), B16)]
    scratch = [
        pltpu.VMEM((total, C), B16),
        pltpu.VMEM((4 * C, C), B16),
        pltpu.VMEM((total, C), B16),
        pltpu.VMEM((total, C), B16),
    ]
    if keep:
        outs += [sds((total, C), B16), sds((4 * C, C), B16), sds((8, C), F32)]
        scratch += [
            pltpu.VMEM((queries, total), B16),
            pltpu.VMEM((queries, total), B16),
            pltpu.VMEM((queries, C), B16),
            pltpu.VMEM((queries, C), B16),
            pltpu.VMEM((queries, C), B16),
        ]
    return pl.pallas_call(
        functools.partial(attention_kernel, keep, chunk, block),
        out_shape=outs,
        in_specs=[anyw, vmem, vmem, smem, vmem, vmem, anyw],
        out_specs=[vmem] * len(outs),
        scratch_shapes=scratch
        + [pltpu.SemaphoreType.DMA((blocks,)), pltpu.SemaphoreType.DMA((1,))],
        compiler_params=params_of(),
        name="attention" if keep else "attention_again",
    )(ua, key_ids, query_ids, offsets, dz, vec, low)


def other_core(h):
    return h + 1 - 2 * lax.rem(h, 2)


def gather_kernel(n, u, ua, lsem, send, recv):
    me = lax.axis_index(HEIGHT)
    half = n // 2
    mine = me // half
    base = mine * half
    core = lax.rem(me, 2)
    partner = lax.rem(me + half, n)
    sibling = other_core(me)
    mates = half // 2
    seat = (me - base) // 2

    def mate(j):
        return base + core + 2 * lax.rem(seat + j, mates)

    barrier = pltpu.get_barrier_semaphore()
    peers = [partner, sibling] + [mate(j) for j in range(1, mates)]
    for p in peers:
        pl.semaphore_signal(barrier, inc=1, device_id={HEIGHT: p}, device_id_type=MESH)
    pl.semaphore_wait(barrier, len(peers))
    count = [0]
    started = []

    def push(src, slot, to):
        cp = pltpu.make_async_remote_copy(
            src_ref=src, dst_ref=ua.at[slot], send_sem=send.at[count[0]], recv_sem=recv.at[slot],
            device_id={HEIGHT: to}, device_id_type=MESH)
        count[0] += 1
        cp.start()
        started.append(cp)

    def arrived(slot):
        pltpu.make_async_remote_copy(
            src_ref=u.at[0], dst_ref=ua.at[slot], send_sem=send.at[0], recv_sem=recv.at[slot],
            device_id={HEIGHT: partner}, device_id_type=MESH).wait_recv()

    own = pltpu.make_async_copy(u.at[mine], ua.at[me], lsem.at[0])
    own.start()
    push(u.at[1 - mine], me, partner)
    for j in range(1, mates):
        push(u.at[mine], me, mate(j))
    push(u.at[mine], me, sibling)
    arrived(partner)
    for j in range(1, mates):
        push(ua.at[partner], partner, mate(j))
    push(ua.at[partner], partner, sibling)
    for j in range(1, mates):
        friend = base + core + 2 * lax.rem(seat + mates - j, mates)
        far = lax.rem(friend + half, n)
        arrived(friend)
        push(ua.at[friend], friend, sibling)
        arrived(far)
        push(ua.at[far], far, sibling)
    arrived(sibling)
    arrived(lax.rem(sibling + half, n))
    for j in range(1, mates):
        friend = base + (1 - core) + 2 * lax.rem(seat + mates - j, mates)
        arrived(friend)
        arrived(lax.rem(friend + half, n))
    own.wait()
    for cp in started:
        cp.wait_send()


def gather_call(n, cid, u):
    half = n // 2
    sends = 2 * (half // 2) + 1 + 2 * (half // 2 - 1) + 1
    return pl.pallas_call(
        functools.partial(gather_kernel, n),
        out_shape=sds((n,) + u.shape[1:], B16),
        in_specs=[anyw],
        out_specs=anyw,
        scratch_shapes=[
            pltpu.SemaphoreType.DMA((1,)),
            pltpu.SemaphoreType.DMA((sends,)),
            pltpu.SemaphoreType.DMA((n,)),
        ],
        compiler_params=params_of(cid),
        name="gather_u",
    )(u)


def scatter_kernel(n, dup, out, from_sib, from_mate, mine_sum, from_partner, lsem, send, recv):
    me = lax.axis_index(HEIGHT)
    half = n // 2
    mine = me // half
    base = mine * half
    core = lax.rem(me, 2)
    partner = lax.rem(me + half, n)
    sibling = other_core(me)
    mates = half // 2
    seat = (me - base) // 2
    barrier = pltpu.get_barrier_semaphore()

    def mate(j, c=core):
        return base + c + 2 * lax.rem(seat + j, mates)

    peers = [partner, sibling] + [mate(j) for j in range(1, mates)]
    for p in peers:
        pl.semaphore_signal(barrier, inc=1, device_id={HEIGHT: p}, device_id_type=MESH)
    pl.semaphore_wait(barrier, len(peers))
    order = [(j, far) for j in range(1, mates) for far in (1, 0)] + [(0, 1), (0, 0)]

    def rows_of(j, far, c):
        owner = mate(j, c)
        return lax.rem(owner + half, n) if far else owner

    sib = []
    for t, (j, far) in enumerate(order):
        cp = pltpu.make_async_remote_copy(
            src_ref=dup.at[rows_of(j, far, 1 - core)], dst_ref=from_sib.at[t],
            send_sem=send.at[t], recv_sem=recv.at[t],
            device_id={HEIGHT: sibling}, device_id_type=MESH)
        cp.start()
        sib.append(cp)
    base_sem = len(order)
    out_copies = []
    for t, (j, far) in enumerate(order):
        sib[t].wait_recv()
        block = rows_of(j, far, core)
        if j > 0:
            mine_sum[t] = (dup[block].astype(F32) + from_sib[t].astype(F32)).astype(B16)
            at = (j - 1) * 2 + far
            cp = pltpu.make_async_remote_copy(
                src_ref=mine_sum.at[t], dst_ref=from_mate.at[at],
                send_sem=send.at[base_sem + at], recv_sem=recv.at[base_sem + at],
                device_id={HEIGHT: mate(j)}, device_id_type=MESH)
            cp.start()
            out_copies.append(cp)
    t_far, t_own = len(order) - 2, len(order) - 1
    total = dup[partner].astype(F32) + from_sib[t_far].astype(F32)
    for j in range(1, mates):
        at = (j - 1) * 2 + 1
        pltpu.make_async_remote_copy(
            src_ref=mine_sum.at[0], dst_ref=from_mate.at[at], send_sem=send.at[0],
            recv_sem=recv.at[base_sem + at], device_id={HEIGHT: sibling},
            device_id_type=MESH).wait_recv()
        total = total + from_mate[at].astype(F32)
    mine_sum[t_far] = total.astype(B16)
    last = base_sem + 2 * (mates - 1)
    home = pltpu.make_async_remote_copy(
        src_ref=mine_sum.at[t_far], dst_ref=from_partner, send_sem=send.at[last],
        recv_sem=recv.at[last], device_id={HEIGHT: partner}, device_id_type=MESH)
    home.start()
    total = dup[me].astype(F32) + from_sib[t_own].astype(F32)
    for j in range(1, mates):
        at = (j - 1) * 2
        pltpu.make_async_remote_copy(
            src_ref=mine_sum.at[0], dst_ref=from_mate.at[at], send_sem=send.at[0],
            recv_sem=recv.at[base_sem + at], device_id={HEIGHT: sibling},
            device_id_type=MESH).wait_recv()
        total = total + from_mate[at].astype(F32)
    out[mine] = total
    home.wait_recv()
    out[1 - mine] = from_partner[...].astype(F32)
    for cp in sib + out_copies + [home]:
        cp.wait_send()


def scatter_call(n, cid, dup):
    half = n // 2
    mates = half // 2
    copies = 2 * mates + 2 * (mates - 1) + 1
    seg = dup.shape[1:]
    return pl.pallas_call(
        functools.partial(scatter_kernel, n),
        out_shape=sds((2,) + seg, F32),
        in_specs=[vmem],
        out_specs=vmem,
        scratch_shapes=[
            pltpu.VMEM((2 * mates,) + seg, B16),
            pltpu.VMEM((max(2 * (mates - 1), 1),) + seg, B16),
            pltpu.VMEM((2 * mates,) + seg, B16),
            pltpu.VMEM(seg, B16),
            pltpu.SemaphoreType.DMA((1,)),
            pltpu.SemaphoreType.DMA((copies,)),
            pltpu.SemaphoreType.DMA((copies,)),
        ],
        compiler_params=params_of(cid),
        name="scatter_du",
    )(dup)


def resnet_backward_kernel(n, dims, cot, du, hid, y1, x, mean1, inv1, mean2, inv2, mean3, inv3, s1, s2, pick,
                           spread, div, col_l, col_r, row_u, row_d, vec, top, bottom, datt, igrad, grads, dvec,
                           dw1, dw2, k, dh, d3, low, low_u, low_d, part, norm, halo, buf, tmp_a, tmp_b, ksem, wsem, send,
                           recv, hsend, hrecv):
    canvases, rows, width = dims
    px = canvases * rows * width
    cells = px // UNIT
    plane = rows * width
    nt = (((1,), (1,)), ((), ()))
    tn = (((0,), (0,)), ((), ()))
    load2 = second_matrix(top, bottom, k, wsem)
    load1 = pltpu.make_async_copy(top.at[pl.ds(0, 9 * C)], k, wsem.at[0])
    for cp in load2:
        cp.start()
    out_att = pltpu.make_async_copy(datt, grads.at[pl.ds(18 * C, 4 * C)], ksem.at[2])
    out_two = pltpu.make_async_copy(dw2, grads.at[pl.ds(9 * C, 9 * C)], ksem.at[3])
    out_one = pltpu.make_async_copy(dw1, grads.at[pl.ds(0, 9 * C)], ksem.at[4])
    out_att.start()
    greet(n)
    zero_row = jnp.zeros((1, C), F32)

    def pixels(i):
        return pl.ds(i * 16 * UNIT, 16 * UNIT)

    def norm_sums(grad_of, source, mean, inv, gain):
        def body(i, carry):
            dg, db = carry
            at = pixels(i)
            unit = (source[at, :].astype(F32) - over_cells(mean, i)) * over_cells(inv, i)
            d = grad_of(i, unit)
            norm[at, :] = unit
            e = d * gain
            part[at, :] = e
            cross = d * unit
            here = pl.ds(i * 16, 16)
            tmp_a[here, :] = jnp.sum(e.reshape(16, UNIT, C), axis=1)
            tmp_b[here, :] = jnp.sum((cross * gain).reshape(16, UNIT, C), axis=1)
            return (dg + jnp.sum(cross, axis=0, keepdims=True), db + jnp.sum(d, axis=0, keepdims=True))

        dg, db = lax.fori_loop(0, cells // 16, body, (zero_row, zero_row))
        packed = pack([group_totals(pick, tmp_a[...]), group_totals(pick, tmp_b[...])])
        return packed, dg, db

    def send_sums(packed, rnd):
        buf[rnd, 0] = packed
        copies = spread_copies(n, buf, send, recv, rnd)
        for cp in copies:
            cp.start()
        return copies

    def norm_finish(copies, rnd, inv, emit):
        for cp in copies:
            cp.wait_recv()
        gathered = jnp.sum(buf[rnd], axis=0) / div[...]
        tmp_a[...] = split_dot(spread[...], unpack(gathered))
        tmp_b[...] = split_dot(spread[...], unpack(shift_down(gathered, 1)))

        def body(i, _):
            at = pixels(i)
            emit(i, over_cells(inv, i) * (part[at, :] - over_cells(tmp_a, i) - norm[at, :] * over_cells(tmp_b, i)))
            return 0

        lax.fori_loop(0, cells // 16, body, 0)

    def spread_rows(rnd):
        def row_at(v, r):
            return pl.ds(pl.multiple_of((v * rows + r) * width, width), width)

        def one(i, _):
            v, r = i // rows, lax.rem(i, rows)
            d3[v, r + 1] = shift_columns(low[row_at(v, r), :].astype(F32), col_l[v, r + 1], col_r[v, r + 1])
            return 0

        lax.fori_loop(0, canvases * rows, one, 0)
        mid = pl.ds(C, C)
        up, down = halo_copies(n, d3.at[:, 1, :, mid], d3.at[:, rows, :, mid], halo.at[rnd],
                               hsend.at[rnd], hrecv.at[rnd])
        start_halo(n, up, down)
        return up, down

    def finish_rows(up, down, rnd):
        wait_halo(n, up, down, halo.at[rnd], 0.0)
        for v in range(canvases):
            for side, r in ((0, 0), (1, rows + 1)):
                d3[v, r] = shift_columns(halo[rnd, side, v].astype(F32), col_l[v, r], col_r[v, r])

    def convolve_back(emit):
        def body(v, _):
            at = pl.ds(pl.multiple_of(v * plane, plane), plane)
            total = None
            for dr in (1, 0, 2):
                acc = None
                for dc in range(3):
                    tap = 3 * (2 - dr) + (2 - dc)
                    lhs = d3[v, dr : dr + rows, :, dc * C : (dc + 1) * C].reshape(plane, C)
                    term = lax.dot_general(lhs, k[tap * C : (tap + 1) * C, :], nt, preferred_element_type=F32)
                    acc = term if acc is None else acc + term
                if dr == 0:
                    acc = acc * wide(row_u[at, :])
                if dr == 2:
                    acc = acc * wide(row_d[at, :])
                total = acc if total is None else total + acc
            emit(at, total)
            return 0

        lax.fori_loop(0, canvases, body, 0)

    def mask_rows():
        def body(i, _):
            at = pixels(i)
            value = low[at, :].astype(F32)
            low_u[at, :] = (value * wide(row_u[at, :])).astype(B16)
            low_d[at, :] = (value * wide(row_d[at, :])).astype(B16)
            return 0

        lax.fori_loop(0, cells // 16, body, 0)

    def weight_grad(source, dest):
        for dr, grad in ((0, low_u), (1, low), (2, low_d)):
            def body(dc, _):
                acc = None
                for v in range(canvases):
                    lhs = source[v, dr : dr + rows, :, pl.ds(pl.multiple_of(dc * C, C), C)].reshape(plane, C)
                    term = lax.dot_general(
                        lhs, grad[v * plane : (v + 1) * plane, :], tn, preferred_element_type=F32)
                    acc = term if acc is None else acc + term
                dest[pl.ds(pl.multiple_of((3 * dr + dc) * C, C), C), :] = acc.astype(B16)
                return 0

            lax.fori_loop(0, 3, body, 0)

    packed, dg3, db3 = norm_sums(lambda i, unit: du[pixels(i), :], hid, mean3, inv3, vec[6:7, :])
    sent = send_sums(packed, 0)

    def emit_hidden(i, value):
        at = pixels(i)
        total = cot[at, :].astype(F32) + value
        dh[at, :] = total
        low[at, :] = total.astype(B16)

    norm_finish(sent, 0, inv3, emit_hidden)
    up, down = spread_rows(0)
    mask_rows()
    dc2 = jnp.sum(low[...].astype(F32), axis=0, keepdims=True)
    finish_rows(up, down, 0)
    for cp in load2:
        cp.wait()

    def emit_part(at, total):
        part[at, :] = total

    convolve_back(emit_part)
    load1.start()
    gain2, bias2 = vec[3:4, :], vec[4:5, :]

    def grad_two(i, unit):
        return part[pixels(i), :] * silu_slope(unit * gain2 + bias2)

    packed, dg2, db2 = norm_sums(grad_two, y1, mean2, inv2, gain2)
    more = send_sums(packed, 1)
    weight_grad(s2, dw2)
    out_two.start()

    def emit_low(i, value):
        low[pixels(i), :] = value.astype(B16)

    norm_finish(more, 1, inv2, emit_low)
    sent = sent + more
    up, down = spread_rows(1)
    mask_rows()
    dc1 = jnp.sum(low[...].astype(F32), axis=0, keepdims=True)
    weight_grad(s1, dw1)
    out_one.start()
    finish_rows(up, down, 1)
    load1.wait()
    convolve_back(emit_part)
    gain1, bias1 = vec[0:1, :], vec[1:2, :]

    def grad_one(i, unit):
        return part[pixels(i), :] * silu_slope(unit * gain1 + bias1)

    packed, dg1, db1 = norm_sums(grad_one, x, mean1, inv1, gain1)
    more = send_sums(packed, 2)
    dvec[...] = jnp.concatenate([dg1, db1, dc1, dg2, db2, dc2, dg3, db3], axis=0)

    def emit_input(i, value):
        igrad[pixels(i), :] = dh[pixels(i), :] + value

    norm_finish(more, 2, inv1, emit_input)
    sent = sent + more
    out_att.wait()
    out_two.wait()
    out_one.wait()
    for cp in sent:
        cp.wait_send()


def resnet_backward_call(n, dims, cid, cot, du, hid, y1, x, norms, s1, s2, pick, spread, div, masks, vec, top,
                         bottom, datt):
    canvases, rows, width = dims
    px = canvases * rows * width
    cells = px // UNIT
    stats = canvases * CROPS
    return pl.pallas_call(
        functools.partial(resnet_backward_kernel, n, dims),
        out_shape=[sds((px, C), F32), sds((22 * C, C), B16), sds((8, C), F32)],
        in_specs=[vmem] * 21 + [anyw] * 3,
        out_specs=[vmem, anyw, vmem],
        scratch_shapes=[
            pltpu.VMEM((9 * C, C), B16),
            pltpu.VMEM((9 * C, C), B16),
            pltpu.VMEM((9 * C, C), B16),
            pltpu.VMEM((px, C), F32),
            pltpu.VMEM((canvases, rows + 2, width, 3 * C), B16),
            pltpu.VMEM((px, C), B16),
            pltpu.VMEM((px, C), B16),
            pltpu.VMEM((px, C), B16),
            pltpu.VMEM((px, C), F32),
            pltpu.VMEM((px, C), F32),
            pltpu.VMEM((2, 2, canvases, width, C), B16),
            pltpu.VMEM((3, n, stats, LANES), F32),
            pltpu.VMEM((cells, C), F32),
            pltpu.VMEM((cells, C), F32),
            pltpu.SemaphoreType.DMA((5,)),
            pltpu.SemaphoreType.DMA((3,)),
            pltpu.SemaphoreType.DMA((3, n)),
            pltpu.SemaphoreType.DMA((3, n)),
            pltpu.SemaphoreType.DMA((2, 2)),
            pltpu.SemaphoreType.DMA((2, 2)),
        ],
        compiler_params=params_of(cid),
        name="resnet_backward",
    )(cot, du, hid, y1, x, *norms, s1, s2, pick, spread, div, *masks, vec, top, bottom, datt)


class Grid:
    def __init__(self, columns, n):
        self.columns, self.n, self.seats = columns, n, n // 2
        self.phases = columns.bit_length() - 1
        self.c = lax.axis_index(CANVAS)
        self.h = lax.axis_index(HEIGHT)
        self.seat, self.core = self.h // 2, lax.rem(self.h, 2)
        flips = [
            (1 - 2 * lax.rem(self.c // 2**t, 2)) * 2**t for t in range(self.phases)
        ]
        last = self.phases - 1
        self.flips = [
            (1 - self.core) * flips[last - k] + self.core * flips[k] for k in range(self.phases)
        ]
        self.other_flips = [
            self.core * flips[last - k] + (1 - self.core) * flips[k] for k in range(self.phases)
        ]

    def column(self, e, flips=None):
        flips = self.flips if flips is None else flips
        col = self.c
        for k in range(self.phases):
            if (e >> k) & 1:
                col = col + flips[k]
        return col

    def mate(self, k):
        return {CANVAS: self.c + self.flips[k], HEIGHT: self.h}

    def sibling(self):
        return {CANVAS: self.c, HEIGHT: 2 * self.seat + 1 - self.core}

    def beside(self, step):
        return {CANVAS: self.c, HEIGHT: self.h + 2 * step}

    def greet(self):
        barrier = pltpu.get_barrier_semaphore()
        for d in range(1, self.n):
            pl.semaphore_signal(
                barrier, inc=1, device_id={CANVAS: self.c, HEIGHT: lax.rem(self.h + d, self.n)},
                device_id_type=MESH)
        for k in range(self.phases):
            pl.semaphore_signal(barrier, inc=1, device_id=self.mate(k), device_id_type=MESH)
        pl.semaphore_wait(barrier, self.n - 1 + self.phases)


def remote(src, dst, send, recv, to):
    return pltpu.make_async_remote_copy(
        src_ref=src, dst_ref=dst, send_sem=send, recv_sem=recv, device_id=to, device_id_type=MESH)


def lowest_bit(e):
    return (e & -e).bit_length() - 1


def spread_blocks(grid, fresh, whole, own_sem, zsend, msend, ssend, recv, srecv):
    g = grid
    seats, phases = g.seats, g.phases
    own = pltpu.make_async_copy(fresh, whole.at[g.c, g.seat, g.core], own_sem)
    own.start()

    def slot(e, seat):
        return whole.at[g.column(e), seat, g.core]

    def forward(e, seat, src, start):
        k_top = phases if e == 0 else lowest_bit(e)
        for k in range(k_top - 1, -1, -1):
            cp = remote(src, slot(e, seat), msend.at[k, e, seat], recv.at[e | (1 << k), seat], g.mate(k))
            cp.start() if start else cp.wait_send()
        cp = remote(src, slot(e, seat), ssend.at[e, seat], srecv.at[e, seat], g.sibling())
        cp.start() if start else cp.wait_send()

    def along(seat, step, src, start):
        cp = remote(src, slot(0, seat), zsend.at[(step + 1) // 2, seat], recv.at[0, seat], g.beside(step))
        cp.start() if start else cp.wait_send()

    def line(seat, src, start):
        @pl.when((seat <= g.seat) & (g.seat < seats - 1))
        def _():
            along(seat, 1, src, start)

        @pl.when((seat >= g.seat) & (g.seat > 0))
        def _():
            along(seat, -1, src, start)

    def arrive(e, seat):
        remote(fresh, slot(e, seat), ssend.at[0, 0], recv.at[e, seat], g.sibling()).wait_recv()

    early = [e for e in range(1, 2**phases) if lowest_bit(e) > 0]
    early.sort(key=lambda e: -lowest_bit(e))
    late = [e for e in range(1, 2**phases) if lowest_bit(e) == 0]

    def handle(e, seat):
        arrive(e, seat)
        if e == 0:
            line(seat, slot(0, seat), True)
        forward(e, seat, slot(e, seat), True)

    def both_sides(d, todo):
        for side in (-1, 1):
            seat = g.seat + side * d

            @pl.when((seat >= 0) & (seat < seats))
            def _():
                for e in todo:
                    handle(e, seat)

    line(g.seat, fresh, True)
    forward(0, g.seat, fresh, True)
    for e in early:
        handle(e, g.seat)

    def further(d, _):
        both_sides(d, [0] + early)
        return 0

    lax.fori_loop(1, seats, further, 0)
    for e in late:
        handle(e, g.seat)

    def finish(d, _):
        both_sides(d, late)
        return 0

    lax.fori_loop(1, seats, finish, 0)

    def drain(seat, _):
        for e in range(2**phases):
            remote(fresh, whole.at[g.column(e, g.other_flips), seat, 1 - g.core], ssend.at[0, 0],
                   srecv.at[e, seat], g.sibling()).wait_recv()
            forward(e, seat, slot(e, seat), False)
        line(seat, slot(0, seat), False)
        return 0

    lax.fori_loop(0, seats, drain, 0)
    own.wait()


def spread_scratch(columns, n):
    seats, phases = n // 2, columns.bit_length() - 1
    dma = pltpu.SemaphoreType.DMA
    return [
        dma((1,)),
        dma((2, seats)),
        dma((phases, columns, seats)),
        dma((columns, seats)),
        dma((columns, seats)),
        dma((columns, seats)),
    ]


def spread_kernel(columns, n, block, whole, fresh, own, zsend, msend, ssend, recv, srecv):
    grid = Grid(columns, n)
    fresh[...] = block[...].astype(B16)
    grid.greet()
    spread_blocks(grid, fresh, whole, own.at[0], zsend, msend, ssend, recv, srecv)


def spread_call(columns, n, cid, block):
    return pl.pallas_call(
        functools.partial(spread_kernel, columns, n),
        out_shape=sds((columns, n // 2, 2) + block.shape, B16),
        in_specs=[vmem],
        out_specs=anyw,
        scratch_shapes=[pltpu.VMEM(block.shape, B16)] + spread_scratch(columns, n),
        compiler_params=params_of(cid),
        name="spread_weights",
    )(block)


def adam_update(current, gradient, moment_one, moment_two, learn_rate):
    first_new = 0.5 * moment_one + 0.5 * gradient
    second_new = 0.9 * moment_two + 0.1 * gradient * gradient
    first_hat = first_new / (1.0 - 0.5**STEP)
    second_hat = second_new / (1.0 - 0.9**STEP)
    return (
        current - learn_rate * first_hat / (jnp.sqrt(second_hat) + adam_epsilon),
        first_new,
        second_new,
    )


def step_kernel(columns, n, grads, w, m, s, dvec, vw, vm, vs, new_w, new_m, new_s, new_vw, new_vm, new_vs, whole,
                acc, sib, got, up, down, fresh, vbuf, vtrade, lsem, gsend, grecv, psend, precv, usend, urecv,
                vsend, vrecv, tsend, trecv, own, zsend, msend, ssend, recv, srecv):
    g = Grid(columns, n)
    seats, phases = g.seats, g.phases
    slots = 2**phases
    order = sorted(range(slots), key=lambda e: (lowest_bit(e) if e else phases, e == (e & -e)))
    loads = []
    for e in order:
        cp = pltpu.make_async_copy(grads.at[g.column(e), :, g.core], acc.at[e], lsem.at[e])
        cp.start()
        loads.append(cp)

    @pl.when(g.seat == 0)
    def _():
        up[...] = jnp.zeros(up.shape, B16)

    @pl.when(g.seat == seats - 1)
    def _():
        down[...] = jnp.zeros(down.shape, B16)

    vbuf[g.h] = dvec[...]
    g.greet()
    sib_copies = []
    for e in order:
        cp = remote(grads.at[g.column(e, g.other_flips), :, 1 - g.core], sib.at[e], gsend.at[e], grecv.at[e],
                    g.sibling())
        cp.start()
        sib_copies.append(cp)

    def vector_copy(d):
        src = lax.rem(g.h + d, n)
        return remote(vbuf.at[g.h], vbuf.at[g.h], vsend.at[d], vrecv.at[g.h],
                      {CANVAS: g.c, HEIGHT: src})

    def vector_arrival(d):
        src = lax.rem(g.h + d, n)
        return remote(vbuf.at[src], vbuf.at[src], vsend.at[d], vrecv.at[src],
                      {CANVAS: g.c, HEIGHT: src})

    for d in range(1, n):
        vector_copy(d).start()

    def local(e, seat, below):
        total = acc[e, seat].astype(F32) + sib[e, seat].astype(F32)
        for k in range(below):
            total = total + got[k, e >> (k + 1), seat].astype(F32)
        return total

    def in_turn(i):
        even = 1 - lax.rem(i, 2)
        return (i // 2) * even + (1 - even) * (seats - 1 - i // 2)

    def phase_copy(k, e, seat):
        return remote(acc.at[e, seat], got.at[k, e >> (k + 1), seat], psend.at[k, e >> (k + 1), seat],
                      precv.at[k, e >> (k + 1), seat], g.mate(k))

    ready = 0
    for e in order:
        loads[ready].wait()
        sib_copies[ready].wait_recv()
        ready += 1
        if e == 0:
            break
        k = lowest_bit(e)

        def one(i, _):
            seat = in_turn(i)
            for q in range(k):
                phase_copy(q, e | (1 << q), seat).wait_recv()
            acc[e, seat] = local(e, seat, k).astype(B16)
            phase_copy(k, e, seat).start()
            return 0

        lax.fori_loop(0, seats, one, 0)

    for d in range(1, n):
        vector_arrival(d).wait_recv()
    vtrade[0, 0] = jnp.sum(vbuf[...], axis=0)
    for k in range(phases):
        cp = remote(vtrade.at[k, 0], vtrade.at[k, 1], tsend.at[k], trecv.at[k], g.mate(k))
        cp.start()
        cp.wait_recv()
        vtrade[k + 1, 0] = vtrade[k, 0] + vtrade[k, 1]
    new_vw[...], new_vm[...], new_vs[...] = adam_update(vw[...], vtrade[phases, 0], vm[...], vs[...], vector_rate)

    def line_copy(step, seat):
        box = up if step > 0 else down
        at = (step + 1) // 2
        return remote(acc.at[0, seat], box.at[seat], usend.at[at, seat], urecv.at[at, seat], g.beside(step))

    def own_column(i, _):
        seat = in_turn(i)
        for q in range(phases):
            phase_copy(q, 1 << q, seat).wait_recv()

        @pl.when(seat > g.seat)
        def _():
            @pl.when(g.seat > 0)
            def _():
                line_copy(1, seat).wait_recv()

            acc[0, seat] = (local(0, seat, phases) + up[seat].astype(F32)).astype(B16)
            line_copy(1, seat).start()

        @pl.when(seat < g.seat)
        def _():
            @pl.when(g.seat < seats - 1)
            def _():
                line_copy(-1, seat).wait_recv()

            acc[0, seat] = (local(0, seat, phases) + down[seat].astype(F32)).astype(B16)
            line_copy(-1, seat).start()

        return 0

    lax.fori_loop(0, seats, own_column, 0)

    @pl.when(g.seat > 0)
    def _():
        line_copy(1, g.seat).wait_recv()

    @pl.when(g.seat < seats - 1)
    def _():
        line_copy(-1, g.seat).wait_recv()

    total = local(0, g.seat, phases) + up[g.seat].astype(F32) + down[g.seat].astype(F32)
    next_w, new_m[...], new_s[...] = adam_update(w[...], total, m[...], s[...], matrix_rate)
    new_w[...] = next_w
    fresh[...] = next_w.astype(B16)
    spread_blocks(g, fresh, whole, own.at[0], zsend, msend, ssend, recv, srecv)
    for cp in sib_copies:
        cp.wait_send()
    for d in range(1, n):
        vector_copy(d).wait_send()
    for k in range(phases):
        remote(vtrade.at[k, 0], vtrade.at[k, 1], tsend.at[k], trecv.at[k], g.mate(k)).wait_send()

    def drain(seat, _):
        for e in range(1, slots):
            phase_copy(lowest_bit(e), e, seat).wait_send()

        @pl.when(seat > g.seat)
        def _():
            line_copy(1, seat).wait_send()

        @pl.when(seat < g.seat)
        def _():
            line_copy(-1, seat).wait_send()

        return 0

    lax.fori_loop(0, seats, drain, 0)


def step_call(columns, n, cid, grads, w, m, s, dvec, vw, vm, vs):
    seats, phases = n // 2, columns.bit_length() - 1
    block = w.shape
    half = max(columns // 2, 1)
    dma = pltpu.SemaphoreType.DMA
    return pl.pallas_call(
        functools.partial(step_kernel, columns, n),
        out_shape=[sds(block, F32)] * 3 + [sds(vw.shape, F32)] * 3 + [sds((columns, seats, 2) + block, B16)],
        in_specs=[anyw] + [vmem] * 7,
        out_specs=[vmem] * 6 + [anyw],
        scratch_shapes=[
            pltpu.VMEM((columns, seats) + block, B16),
            pltpu.VMEM((columns, seats) + block, B16),
            pltpu.VMEM((phases, half, seats) + block, B16),
            pltpu.VMEM((seats,) + block, B16),
            pltpu.VMEM((seats,) + block, B16),
            pltpu.VMEM(block, B16),
            pltpu.VMEM((n,) + vw.shape, F32),
            pltpu.VMEM((phases + 1, 2) + vw.shape, F32),
            dma((columns,)),
            dma((columns,)),
            dma((columns,)),
            dma((phases, half, seats)),
            dma((phases, half, seats)),
            dma((2, seats)),
            dma((2, seats)),
            dma((n,)),
            dma((n,)),
            dma((phases,)),
            dma((phases,)),
        ]
        + spread_scratch(columns, n),
        compiler_params=params_of(cid),
        name="step_weights",
    )(grads, w, m, s, dvec, vw, vm, vs)


class Engine:
    def __init__(self, steps):
        self.steps = steps

    def pump(self, count=1):
        for _ in range(count):
            next(self.steps, None)

    def ready(self):
        for done in self.steps:
            if done:
                return

    def finish(self):
        for _ in self.steps:
            pass


class Group:
    def __init__(self, grid, number, half_rows, first=0, size=None):
        self.g, self.number, self.half = grid, number, half_rows
        self.first, self.size = first, half_rows if size is None else size
        self.owner = 2 * number + grid.c // 2
        self.is_owner = grid.c // 2 == number

    def row(self, q, seat, core):
        block = (q // 2) * self.g.n + 2 * seat + core
        return pl.multiple_of((2 * block + lax.rem(q, 2)) * self.half + self.first, 16)

    def rows(self, q, seat, core):
        return pl.ds(self.row(q, seat, core), self.size)

    def at_column(self, col):
        return {CANVAS: col, HEIGHT: self.g.h}

    def halves(self):
        first = 2 * lax.rem(self.g.c, 2)
        return [(0, first), (1, first + 1)]

    def part(self, ref, half):
        return ref.at[pl.ds(half * self.half, self.half)]

    def to_pieces(self, block, piece, send, recv, start):
        g = self.g

        @pl.when(self.is_owner)
        def _():
            for half, col in self.halves():
                @pl.when(col != g.c)
                def _():
                    cp = remote(self.part(block, half), piece, send.at[half], recv.at[0], self.at_column(col))
                    cp.start() if start else cp.wait_send()

                if start:
                    @pl.when(col == g.c)
                    def _():
                        piece[...] = block[half * self.half : (half + 1) * self.half, :]

    def piece_arrived(self, block, piece, send, recv):
        @pl.when(self.owner != self.g.c)
        def _():
            remote(self.part(block, 0), piece, send.at[0], recv.at[0], self.at_column(self.owner)).wait_recv()

    def to_owner(self, piece, block, send, recv, start):
        g = self.g
        half = lax.rem(g.c, 2)
        where = pl.ds(pl.multiple_of(half * self.half, 16), self.half)

        @pl.when(self.owner != g.c)
        def _():
            cp = remote(piece, block.at[where], send.at[0], recv.at[half], self.at_column(self.owner))
            cp.start() if start else cp.wait_send()

        if start:
            @pl.when(self.owner == g.c)
            def _():
                block[where, :] = piece[...]

    def block_arrived(self, piece, block, send, recv):
        g = self.g

        @pl.when(self.is_owner)
        def _():
            for half, col in self.halves():
                @pl.when(col != g.c)
                def _():
                    remote(piece, self.part(block, half), send.at[0], recv.at[half], self.at_column(col)).wait_recv()


def gather_pieces(group, piece, dest, own, zsend, msend, ssend, recv, srecv):
    g = group.g
    seats, phases = g.seats, g.phases
    local = pltpu.make_async_copy(piece, dest.at[group.rows(g.c, g.seat, g.core)], own.at[0])

    local.start()
    top = 1 << (phases - 1)
    lines = [0, top]

    def slot(e, seat):
        return dest.at[group.rows(g.column(e), seat, g.core)]

    def forward(e, seat, src, start):
        k_top = phases if e == 0 else lowest_bit(e)
        for k in range(k_top - 1, -1, -1):
            cp = remote(src, slot(e, seat), msend.at[k, e, seat], recv.at[e | (1 << k), seat], g.mate(k))
            do = cp.start if start else cp.wait_send
            if e == 0 and k == phases - 1:
                pl.when(seat == g.seat)(do)
            else:
                do()
        cp = remote(src, slot(e, seat), ssend.at[e, seat], srecv.at[e, seat], g.sibling())
        cp.start() if start else cp.wait_send()

    def along(e, seat, step, src, start):
        cp = remote(src, slot(e, seat), zsend.at[(step + 1) // 2, min(e, 1), seat], recv.at[e, seat], g.beside(step))
        cp.start() if start else cp.wait_send()

    def line(e, seat, src, start):
        @pl.when((seat <= g.seat) & (g.seat < seats - 1))
        def _():
            along(e, seat, 1, src, start)

        @pl.when((seat >= g.seat) & (g.seat > 0))
        def _():
            along(e, seat, -1, src, start)

    def handle(e, seat):
        remote(piece, slot(e, seat), ssend.at[0, 0], recv.at[e, seat], g.sibling()).wait_recv()
        if e in lines:
            line(e, seat, slot(e, seat), True)
        forward(e, seat, slot(e, seat), True)

    early = sorted((e for e in range(1, 2**phases) if lowest_bit(e) > 0), key=lambda e: -lowest_bit(e))
    late = [e for e in range(1, 2**phases) if lowest_bit(e) == 0]

    def both_sides(d, todo):
        for side in (-1, 1):
            seat = g.seat + side * d

            @pl.when((seat >= 0) & (seat < seats))
            def _():
                for e in todo:
                    handle(e, seat)

    forward(0, g.seat, piece, True)
    line(0, g.seat, piece, True)
    yield
    for e in early:
        handle(e, g.seat)
    yield
    for d in range(1, seats):
        both_sides(d, [0] + early)
        yield
    for e in late:
        handle(e, g.seat)
    yield
    for d in range(1, seats):
        both_sides(d, late)
        yield

    def siblings(seat, _):
        for e in range(2**phases):
            remote(piece, dest.at[group.rows(g.column(e, g.other_flips), seat, 1 - g.core)], ssend.at[0, 0],
                   srecv.at[e, seat], g.sibling()).wait_recv()
        return 0

    lax.fori_loop(0, seats, siblings, 0)
    local.wait()
    yield True

    def drain(seat, _):
        for e in range(2**phases):
            forward(e, seat, slot(e, seat), False)
            if e in lines:
                line(e, seat, slot(e, seat), False)
        return 0

    lax.fori_loop(0, seats, drain, 0)


def gather_pieces_scratch(columns, n):
    seats, phases = n // 2, columns.bit_length() - 1
    dma = pltpu.SemaphoreType.DMA
    return [
        dma((1,)),
        dma((2, 2, seats)),
        dma((phases, columns, seats)),
        dma((columns, seats)),
        dma((columns, seats)),
        dma((columns, seats)),
    ]


def fold_columns(group, src, column, sib, got, gsend, grecv, psend, precv):
    g = group.g
    seats, phases = g.seats, g.phases
    slots = 2**phases
    turns = [i // 2 if i % 2 == 0 else seats - 1 - i // 2 for i in range(seats)]
    order = sorted(range(slots), key=lambda e: (lowest_bit(e) if e else phases, e == (e & -e)))

    def mine(e, seat):
        return group.rows(g.column(e), seat, g.core)

    def sibling_copy(e, seat):
        return remote(src.at[group.rows(g.column(e, g.other_flips), seat, 1 - g.core)], sib.at[e, seat],
                      gsend.at[e, seat], grecv.at[e, seat], g.sibling())

    def phase_copy(k, e, seat):
        at = (k, e >> (k + 1), seat)
        return remote(src.at[mine(e, seat), :], got.at[at], psend.at[at], precv.at[at], g.mate(k))

    for e in order:
        for seat in turns:
            sibling_copy(e, seat).start()
    yield
    for e in order:
        k = lowest_bit(e) if e else phases
        for seat in turns:
            sibling_copy(e, seat).wait_recv()
            total = src[mine(e, seat), :].astype(F32) + sib[e, seat].astype(F32)
            for q in range(k):
                phase_copy(q, e | (1 << q), seat).wait_recv()
                total = total + got[q, e >> (q + 1), seat].astype(F32)
            if e:
                src[mine(e, seat), :] = total.astype(B16)
                phase_copy(k, e, seat).start()
            else:
                column[seat] = total.astype(B16)
            yield
    yield True

    def drain(seat, _):
        for e in range(slots):
            sibling_copy(e, seat).wait_send()
            if e:
                phase_copy(lowest_bit(e), e, seat).wait_send()
        return 0

    lax.fori_loop(0, seats, drain, 0)


def fold_columns_scratch(columns, n, half_rows):
    seats, phases = n // 2, columns.bit_length() - 1
    dma = pltpu.SemaphoreType.DMA
    block = (half_rows, C)
    return [
        pltpu.VMEM((columns, seats) + block, B16),
        pltpu.VMEM((phases, columns // 2, seats) + block, B16),
        dma((columns, seats)),
        dma((columns, seats)),
        dma((phases, columns // 2, seats)),
        dma((phases, columns // 2, seats)),
    ]


def fold_seats(group, column, piece, box, usend, urecv):
    g = group.g
    seats = g.seats

    def line_copy(seat):
        return remote(column.at[seat], box.at[g.seat], usend.at[seat], urecv.at[g.seat],
                      {CANVAS: g.c, HEIGHT: 2 * seat + g.core})

    def line_arrival(seat):
        return remote(column.at[seat], box.at[seat], usend.at[seat], urecv.at[seat],
                      {CANVAS: g.c, HEIGHT: 2 * seat + g.core})

    for seat in range(seats):
        pl.when(seat != g.seat)(line_copy(seat).start)
    yield
    total = column[g.seat].astype(F32)
    for seat in range(seats):
        pl.when(seat != g.seat)(line_arrival(seat).wait_recv)
        total = total + jnp.where(seat == g.seat, 0.0, box[seat].astype(F32))
    piece[...] = total.astype(B16)
    yield True
    for seat in range(seats):
        pl.when(seat != g.seat)(line_copy(seat).wait_send)


def fold_seats_scratch(n, half_rows):
    seats = n // 2
    dma = pltpu.SemaphoreType.DMA
    return [pltpu.VMEM((seats, half_rows, C), B16), dma((seats,)), dma((seats,))]


def reduce_pieces(group, src, piece, sib, got, box, gsend, grecv, psend, precv, usend, urecv):
    g = group.g
    seats, phases = g.seats, g.phases
    slots = 2**phases
    order = sorted(range(slots), key=lambda e: (lowest_bit(e) if e else phases, e == (e & -e)))
    turns = [i // 2 if i % 2 == 0 else seats - 1 - i // 2 for i in range(seats)]

    def mine(e, seat):
        return group.rows(g.column(e), seat, g.core)

    def sibling_copy(e, seat):
        return remote(src.at[group.rows(g.column(e, g.other_flips), seat, 1 - g.core)], sib.at[e, seat],
                      gsend.at[e, seat], grecv.at[e, seat], g.sibling())

    def phase_copy(k, e, seat):
        at = (k, e >> (k + 1), seat)
        return remote(src.at[mine(e, seat), :], got.at[at], psend.at[at], precv.at[at], g.mate(k))

    def line_copy(seat):
        return remote(src.at[mine(0, seat), :], box.at[g.seat], usend.at[seat], urecv.at[g.seat],
                      {CANVAS: g.c, HEIGHT: 2 * seat + g.core})

    def line_arrival(seat):
        return remote(src.at[mine(0, seat), :], box.at[seat], usend.at[seat], urecv.at[seat],
                      {CANVAS: g.c, HEIGHT: 2 * seat + g.core})

    def local(e, seat, below):
        total = src[mine(e, seat), :].astype(F32) + sib[e, seat].astype(F32)
        for k in range(below):
            total = total + got[k, e >> (k + 1), seat].astype(F32)
        return total

    for e in order:
        for seat in turns:
            sibling_copy(e, seat).start()
    yield

    def pass_on(e, k, seat):
        sibling_copy(e, seat).wait_recv()
        for q in range(k):
            phase_copy(q, e | (1 << q), seat).wait_recv()
        src[mine(e, seat), :] = local(e, seat, k).astype(B16)
        phase_copy(k, e, seat).start()

    for e in order:
        if e == 0:
            break
        for seat in turns:
            pass_on(e, lowest_bit(e), seat)
            yield

    def own_column(seat):
        sibling_copy(0, seat).wait_recv()
        for q in range(phases):
            phase_copy(q, 1 << q, seat).wait_recv()

        @pl.when(seat != g.seat)
        def _():
            src[mine(0, seat), :] = local(0, seat, phases).astype(B16)
            line_copy(seat).start()

    for seat in turns:
        own_column(seat)
        yield
    total = local(0, g.seat, phases)
    for seat in turns:
        @pl.when(seat != g.seat)
        def _():
            line_arrival(seat).wait_recv()

        total = total + jnp.where(seat == g.seat, 0.0, box[seat].astype(F32))
    piece[...] = total.astype(B16)
    yield True

    def drain(seat, _):
        for e in range(slots):
            sibling_copy(e, seat).wait_send()
            if e > 0:
                phase_copy(lowest_bit(e), e, seat).wait_send()

        @pl.when(seat != g.seat)
        def _():
            line_copy(seat).wait_send()

        return 0

    lax.fori_loop(0, seats, drain, 0)


def reduce_pieces_scratch(columns, n, half_rows):
    seats, phases = n // 2, columns.bit_length() - 1
    half = columns // 2
    dma = pltpu.SemaphoreType.DMA
    block = (half_rows, C)
    return [
        pltpu.VMEM((columns, seats) + block, B16),
        pltpu.VMEM((phases, half, seats) + block, B16),
        pltpu.VMEM((seats,) + block, B16),
        dma((columns, seats)),
        dma((columns, seats)),
        dma((phases, half, seats)),
        dma((phases, half, seats)),
        dma((seats,)),
        dma((seats,)),
    ]


class Named:
    def __init__(self, shapes, refs):
        refs = list(refs)
        for name, shape in shapes.items():
            if isinstance(shape, list):
                setattr(self, name, [refs.pop(0) for _ in shape])
            else:
                setattr(self, name, refs.pop(0))


def named_call(kernel, name, cid, inputs, outputs, scratch):
    loads = [k for k, (_, spec) in inputs.items() if spec == LOAD]
    stores = [k for k, (_, _, spec) in outputs.items() if spec == STORE]
    parts = 12
    shapes = {**inputs, **outputs, **scratch}
    flat = []
    for value in scratch.values():
        flat += value if isinstance(value, list) else [value]
    held = [pltpu.VMEM(inputs[k][0].shape, inputs[k][0].dtype) for k in loads]
    held += [pltpu.VMEM(*outputs[k][:2]) for k in stores]
    sems = [pltpu.SemaphoreType.DMA((max(len(loads), 1),)), pltpu.SemaphoreType.DMA((max(len(stores), 1), parts))]

    def wrapped(*refs):
        own = len(held) + len(sems)
        R = Named(shapes, refs[:-own])
        kept, (load_sem, store_sem) = refs[-own:-2], refs[-2:]
        waiting, begun, ends = {}, {k: 0 for k in stores}, []
        for i, k in enumerate(loads):
            waiting[k] = pltpu.make_async_copy(getattr(R, k), kept[i], load_sem.at[i])
            waiting[k].start()
            setattr(R, k, kept[i])
        targets = {}
        for i, k in enumerate(stores):
            targets[k] = getattr(R, k)
            setattr(R, k, kept[len(loads) + i])

        def need(*names):
            for k in names:
                if k in waiting:
                    waiting.pop(k).wait()

        def store(k, first=None, count=None):
            src, dst = getattr(R, k), targets[k]
            if first is not None:
                src, dst = src.at[pl.ds(first, count)], dst.at[pl.ds(first, count)]
            cp = pltpu.make_async_copy(src, dst, store_sem.at[stores.index(k), begun[k]])
            cp.start()
            begun[k] += 1
            ends.append(cp)

        R.need, R.store = need, store
        kernel(R)
        need(*list(waiting))
        for k in stores:
            if not begun[k]:
                store(k)
        for cp in ends:
            cp.wait()

    results = pl.pallas_call(
        wrapped,
        out_shape=[sds(shape, kind) for shape, kind, _ in outputs.values()],
        in_specs=[anyw if spec == LOAD else spec for _, spec in inputs.values()],
        out_specs=[anyw if spec == STORE else spec for _, _, spec in outputs.values()],
        scratch_shapes=flat + held + sems,
        compiler_params=params_of(cid),
        name=name,
    )(*[array for array, _ in inputs.values()])
    return dict(zip(outputs, results))


def greet_all(grid):
    barrier = pltpu.get_barrier_semaphore()
    for d in range(1, grid.n):
        pl.semaphore_signal(
            barrier, inc=1, device_id={CANVAS: grid.c, HEIGHT: lax.rem(grid.h + d, grid.n)}, device_id_type=MESH)
    for d in range(1, grid.columns):
        pl.semaphore_signal(
            barrier, inc=1, device_id={CANVAS: lax.rem(grid.c + d, grid.columns), HEIGHT: grid.h},
            device_id_type=MESH)
    pl.semaphore_wait(barrier, grid.n - 1 + grid.columns - 1)


def across(top, low):
    def taps(dr):
        if dr == 0:
            return [(0, 2 * C, top, 9 * C), (2 * C, 3 * C, low, 0)]
        return [(0, 3 * C, low, 3 * C * dr - 2 * C)]

    return taps


def first_kernel(columns, n, dims, R):
    g = Grid(columns, n)
    half = R.block.shape[0] // 2
    groups = [Group(g, i, half) for i in range(2)]
    R.low[...] = R.block[...].astype(B16)
    count = R.vectors.shape[0]
    R.vec[...] = jnp.zeros(R.vec.shape, F32)
    R.vec[0:count, :] = R.vectors[...].astype(B16).astype(F32)
    canvases, rows, width = dims
    turned = jnp.transpose(R.ids_lane[...])
    for v in range(canvases):
        R.ids_px[v] = jnp.broadcast_to(turned[:, v : v + 1], (rows * width, LANES)).reshape(rows, width, LANES)
    greet_all(g)
    for i, group in enumerate(groups):
        group.to_pieces(R.low, R.pieces.at[i], R.tsend.at[i], R.trecv.at[i], True)
    engines = [
        Engine(gather_pieces(groups[0], R.pieces.at[0], R.w_top, *R.gather0)),
        Engine(gather_pieces(groups[1], R.pieces.at[1], R.w_low, *R.gather1)),
    ]
    each = rows * width // UNIT
    for v in range(canvases):
        cell_ids = R.ids_px[v].reshape(each, UNIT, LANES)[:, 0, :] + float(CROPS * v)
        lane = lax.broadcasted_iota(jnp.int32, (each, LANES), 1).astype(F32)
        R.hot[v * each : (v + 1) * each, :] = (cell_ids == lane).astype(F32)
    stats = canvases * CROPS
    R.spread[...] = R.hot[:, :stats].astype(B16)
    R.pick[...] = jnp.transpose(R.hot[...])[:stats, :].astype(B16)
    turn = [0]
    lag = 2 * g.seats - 3

    def pump():
        if turn[0] == 0:
            groups[0].piece_arrived(R.low, R.pieces.at[0], R.tsend.at[0], R.trecv.at[0])
        if turn[0] < 2 * g.seats + 1:
            engines[0].pump()
        if turn[0] == lag:
            groups[1].piece_arrived(R.low, R.pieces.at[1], R.tsend.at[1], R.trecv.at[1])
        if turn[0] >= lag:
            engines[1].pump()
        turn[0] += 1

    R.need("x")
    layout_body(n, dims, R.x, R.pick, R.spread, R.ids_px, R.ids_lane, R.ids_all, R.mean1, R.inv1, R.div, R.cnt,
                R.col_l, R.col_r, R.row_u, R.row_d, *R.layout, pump=pump, cnt_all=R.cnt_all)
    for k in ("col_l", "col_r", "row_u", "row_d", "mean1", "inv1"):
        R.store(k)
    pump()
    conv = Convolver(n, dims, R.x, R.pick, R.spread, R.cnt, R.col_l, R.col_r, R.row_u, R.row_d, R.halo, R.buf,
                     R.tmp_a, R.tmp_b, R.send, R.recv, R.hsend, R.hrecv, R.cnt_all)
    vec = R.vec
    conv.activate(R.x, R.mean1, R.inv1, vec[0:1, :], vec[1:2, :], R.s1, 0, pump)
    out_s1 = pltpu.make_async_copy(R.s1, R.s1_out, R.osem.at[0])
    out_s1.start()
    while turn[0] < 2 * g.seats + 1:
        pump()
    engines[0].ready()
    out_top = pltpu.make_async_copy(R.w_top, R.top, R.osem.at[1])
    out_top.start()
    pump_low = engines[1].pump
    if turn[0] <= lag:
        groups[1].piece_arrived(R.low, R.pieces.at[1], R.tsend.at[1], R.trecv.at[1])
        pump_low()

    def emit_first(at, total):
        R.y1[at, :] = total + vec[2:3, :]

    conv.convolve(R.s1, lambda dr: [(0, 3 * C, R.w_top, 3 * C * dr)], emit_first, pump_low)
    out_y1 = pltpu.make_async_copy(R.y1, R.y1_out, R.osem.at[2])
    out_y1.start()
    conv.statistics(R.y1, R.mean2, R.inv2, 0, pump_low)
    R.store("mean2")
    R.store("inv2")
    conv.activate(R.y1, R.mean2, R.inv2, vec[3:4, :], vec[4:5, :], R.s2, 1, pump_low)
    out_s2 = pltpu.make_async_copy(R.s2, R.s2_out, R.osem.at[3])
    out_s2.start()
    engines[1].ready()
    out_low = pltpu.make_async_copy(R.w_low, R.bottom, R.osem.at[4])
    out_low.start()

    def emit_second(at, total):
        R.hid[at, :] = total + vec[5:6, :] + R.x[at, :].astype(F32)

    conv.convolve(R.s2, across(R.w_top, R.w_low), emit_second)
    R.store("hid")
    conv.statistics(R.hid, R.mean3, R.inv3, 1)
    R.store("mean3")
    R.store("inv3")
    conv.normalise(R.hid, R.mean3, R.inv3, vec[6:7, :], vec[7:8, :], R.u)
    for cp in conv.sent:
        cp.wait_send()
    for i, group in enumerate(groups):
        group.to_pieces(R.low, R.pieces.at[i], R.tsend.at[i], R.trecv.at[i], False)
    for cp in (out_s1, out_top, out_y1, out_s2, out_low):
        cp.wait()
    for engine in engines:
        engine.finish()


def first_call(columns, n, dims, x, ids_lane, vectors, block):
    canvases, rows, width = dims
    px = canvases * rows * width
    cells = px // UNIT
    stats = canvases * CROPS
    tall = (canvases, rows + 2, width)
    half = block.shape[0] // 2
    dma = pltpu.SemaphoreType.DMA
    inputs = dict(x=(x, LOAD), ids_lane=(ids_lane, vmem), vectors=(vectors, vmem), block=(block, vmem))
    cell = ((cells, C), F32, STORE)
    outputs = dict(
        vec=((16, C), F32, vmem), pick=((stats, cells), B16, vmem), spread=((cells, stats), B16, vmem),
        ids_all=((n,) + ids_lane.shape, F32, vmem), mean1=cell, inv1=cell, div=((stats, LANES), F32, vmem),
        cnt=((stats, LANES), F32, vmem), cnt_all=((n, stats, LANES), F32, vmem), col_l=(tall + (LANES,), F32, STORE), col_r=(tall + (LANES,), F32, STORE),
        row_u=((px, LANES), F32, STORE), row_d=((px, LANES), F32, STORE), hid=((px, C), F32, STORE),
        u=((px, C), B16, vmem), mean2=cell, inv2=cell, mean3=cell, inv3=cell, y1_out=((px, C), F32, anyw),
        s1_out=(tall + (3 * C,), B16, anyw), s2_out=(tall + (3 * C,), B16, anyw),
        top=((11 * C, C), B16, anyw), bottom=((11 * C, C), B16, anyw))
    scratch = dict(
        ids_px=pltpu.VMEM(dims + (LANES,), F32), hot=pltpu.VMEM((cells, LANES), F32),
        y1=pltpu.VMEM((px, C), F32), s1=pltpu.VMEM(tall + (3 * C,), B16), s2=pltpu.VMEM(tall + (3 * C,), B16),
        w_top=pltpu.VMEM((11 * C, C), B16), w_low=pltpu.VMEM((11 * C, C), B16), low=pltpu.VMEM(block.shape, B16),
        pieces=pltpu.VMEM((2, half, C), B16), tsend=dma((2, 2)), trecv=dma((2, 1)),
        gather0=gather_pieces_scratch(columns, n), gather1=gather_pieces_scratch(columns, n),
        layout=layout_scratch(n, dims, ids_lane), halo=pltpu.VMEM((2, 2, canvases, width, C), B16),
        buf=pltpu.VMEM((2, n, stats // 2, LANES), F32), tmp_a=pltpu.VMEM((cells, C), F32),
        tmp_b=pltpu.VMEM((cells, C), F32), send=dma((2, n)), recv=dma((2, n)), hsend=dma((2, 2)),
        hrecv=dma((2, 2)), osem=dma((5,)))
    return named_call(functools.partial(first_kernel, columns, n, dims), "first_forward", 1, inputs, outputs, scratch)


class Backer:
    def __init__(self, n, dims, R):
        self.n, self.dims, self.R = n, dims, R
        self.px = dims[0] * dims[1] * dims[2]
        self.cells = self.px // UNIT
        self.sent = []

    @staticmethod
    def pixels(i):
        return pl.ds(i * 16 * UNIT, 16 * UNIT)

    def norm_sums(self, grad_of, source, mean, inv, gain, rnd):
        R = self.R

        def body(i, carry):
            dg, db = carry
            at = self.pixels(i)
            unit = (source[at, :].astype(F32) - over_cells(mean, i)) * over_cells(inv, i)
            d = grad_of(i, unit)
            R.norm[at, :] = unit
            e = d * gain
            R.part[at, :] = e
            cross = d * unit
            here = pl.ds(i * 16, 16)
            R.tmp_a[here, :] = jnp.sum(e.reshape(16, UNIT, C), axis=1)
            R.tmp_b[here, :] = jnp.sum((cross * gain).reshape(16, UNIT, C), axis=1)
            return (dg + jnp.sum(cross, axis=0, keepdims=True), db + jnp.sum(d, axis=0, keepdims=True))

        zero = jnp.zeros((1, C), F32)
        dg, db = lax.fori_loop(0, self.cells // 16, body, (zero, zero))
        R.buf[rnd, 0] = fold(pack([group_totals(R.pick, R.tmp_a[...]), group_totals(R.pick, R.tmp_b[...])]))
        copies = spread_copies(self.n, R.buf, R.send, R.recv, rnd)
        for cp in copies:
            cp.start()
        self.sent = self.sent + copies
        return copies, dg, db

    def norm_finish(self, copies, rnd, inv, emit):
        R = self.R
        for cp in copies:
            cp.wait_recv()
        gathered = unfold(jnp.sum(R.buf[rnd], axis=0)) / R.div[...]
        R.tmp_a[...] = split_dot(R.spread[...], unpack(gathered))
        R.tmp_b[...] = split_dot(R.spread[...], unpack(shift_down(gathered, 1)))

        def body(i, _):
            at = self.pixels(i)
            emit(i, over_cells(inv, i) * (
                R.part[at, :] - over_cells(R.tmp_a, i) - R.norm[at, :] * over_cells(R.tmp_b, i)))
            return 0

        lax.fori_loop(0, self.cells // 16, body, 0)

    def send_rows(self, source, rnd):
        R = self.R
        canvases, rows, width = self.dims

        def one(v, r):
            at = pl.ds(pl.multiple_of((v * rows + r) * width, width), width)
            R.d3[v, r + 1] = shift_columns(source[at, :].astype(F32), R.col_l[v, r + 1], R.col_r[v, r + 1])

        def edges(v, _):
            one(v, 0)
            one(v, rows - 1)
            return 0

        lax.fori_loop(0, canvases, edges, 0)
        mid = pl.ds(C, C)
        up, down = halo_copies(self.n, R.d3.at[:, 1, :, mid], R.d3.at[:, rows, :, mid], R.halo.at[rnd],
                               R.hsend.at[rnd], R.hrecv.at[rnd])
        start_halo(self.n, up, down)

        def inner(i, _):
            one(i // (rows - 2), 1 + lax.rem(i, rows - 2))
            return 0

        if rows > 2:
            lax.fori_loop(0, canvases * (rows - 2), inner, 0)
        return up, down

    def finish_rows(self, up, down, rnd):
        R = self.R
        canvases, rows, _ = self.dims
        wait_halo(self.n, up, down, R.halo.at[rnd], 0.0)
        for v in range(canvases):
            for side, r in ((0, 0), (1, rows + 1)):
                R.d3[v, r] = shift_columns(R.halo[rnd, side, v].astype(F32), R.col_l[v, r], R.col_r[v, r])

    def convolve_back(self, weights, pump=no_pump):
        R = self.R
        canvases, rows, width = self.dims
        plane = rows * width
        nt = (((1,), (1,)), ((), ()))
        for v in range(canvases):
            at = pl.ds(v * plane, plane)
            total = None
            for dr in (1, 0, 2):
                acc = None
                for dc in range(3):
                    ref, row = weights(3 * (2 - dr) + (2 - dc))
                    lhs = R.d3[v, dr : dr + rows, :, dc * C : (dc + 1) * C].reshape(plane, C)
                    term = lax.dot_general(lhs, ref[row : row + C, :], nt, preferred_element_type=F32)
                    acc = term if acc is None else acc + term
                if dr == 0:
                    acc = acc * wide(R.row_u[at, :])
                if dr == 2:
                    acc = acc * wide(R.row_d[at, :])
                total = acc if total is None else total + acc
                pump()
            R.part[at, :] = total

    def mask_rows(self, source):
        R = self.R

        def body(i, _):
            at = self.pixels(i)
            value = source[at, :].astype(F32)
            R.low_u[at, :] = (value * wide(R.row_u[at, :])).astype(B16)
            R.low_d[at, :] = (value * wide(R.row_d[at, :])).astype(B16)
            return 0

        lax.fori_loop(0, self.cells // 16, body, 0)

    def weight_grad(self, s, grad, dest, pump=no_pump):
        R = self.R
        canvases, rows, width = self.dims
        plane = rows * width
        tn = (((0,), (0,)), ((), ()))
        for dr, source in ((0, R.low_u), (1, grad), (2, R.low_d)):
            for dc in range(3):
                acc = None
                for v in range(canvases):
                    lhs = s[v, dr : dr + rows, :, dc * C : (dc + 1) * C].reshape(plane, C)
                    term = lax.dot_general(
                        lhs, source[v * plane : (v + 1) * plane, :], tn, preferred_element_type=F32)
                    acc = term if acc is None else acc + term
                ref, row = dest(3 * dr + dc)
                ref[row : row + C, :] = acc.astype(B16)
                pump()


def back_kernel(columns, n, dims, R):
    g = Grid(columns, n)
    group = Group(g, 1, R.halves.shape[1])
    load_s = pltpu.make_async_copy(R.s2, R.s, R.lsem.at[0])
    load_s.start()
    load_k = second_matrix(R.top, R.bottom, R.k, R.ksem)
    load_att = pltpu.make_async_copy(R.datt, R.g_low.at[pl.ds(7 * C, 4 * C)], R.lsem.at[1])
    for cp in load_k + [load_att]:
        cp.start()
    greet_all(g)
    vec = R.vec
    back = Backer(n, dims, R)
    R.need("mean3", "inv3", "du", "hid")
    copies, dg3, db3 = back.norm_sums(lambda i, unit: R.du[back.pixels(i), :], R.hid, R.mean3, R.inv3, vec[6:7, :], 0)

    def emit_hidden(i, value):
        at = back.pixels(i)
        total = R.cot[at, :].astype(F32) + value
        R.dh[at, :] = total
        R.grad[at, :] = total.astype(B16)

    R.need("cot", "col_l", "col_r", "row_u", "row_d")
    back.norm_finish(copies, 0, R.inv3, emit_hidden)
    R.store("dh")
    up, down = back.send_rows(R.grad, 0)
    plane = dims[1] * dims[2]
    o_back = remote(R.o.at[pl.ds(plane, plane)], R.o_back, R.lsem.at[2], R.lsem.at[3],
                    {CANVAS: g.c, HEIGHT: lax.rem(g.h + n // 2, n)})
    o_back.start()
    back.mask_rows(R.grad)
    load_s.wait()

    def dest_two(tap):
        return (R.g_top, (9 + tap) * C) if tap < 2 else (R.g_low, (tap - 2) * C)

    back.weight_grad(R.s, R.grad, dest_two)
    load_att.wait()
    R.store("g_top", 9 * C, 2 * C)
    load_s = pltpu.make_async_copy(R.s1, R.s, R.lsem.at[0])
    load_s.start()
    engine = Engine(fold_columns(group, R.g_low, R.halves, *R.reduce))
    engine.pump()
    dc2 = jnp.sum(R.grad[...].astype(F32), axis=0, keepdims=True)
    back.finish_rows(up, down, 0)
    for cp in load_k:
        cp.wait()
    back.convolve_back(lambda tap: (R.k, tap * C), engine.pump)
    gain2, bias2 = vec[3:4, :], vec[4:5, :]

    def grad_two(i, unit):
        return R.part[back.pixels(i), :] * silu_slope(unit * gain2 + bias2)

    R.need("y1", "mean2", "inv2")
    copies, dg2, db2 = back.norm_sums(grad_two, R.y1, R.mean2, R.inv2, gain2, 1)
    engine.pump(2)

    def emit_grad(i, value):
        R.grad[back.pixels(i), :] = value.astype(B16)

    back.norm_finish(copies, 1, R.inv2, emit_grad)
    R.store("grad")
    engine.pump(2)
    back.mask_rows(R.grad)
    dc1 = jnp.sum(R.grad[...].astype(F32), axis=0, keepdims=True)
    load_s.wait()
    taps = []

    def after_tap():
        R.store("g_top", len(taps) * C, C)
        taps.append(None)
        engine.pump()

    back.weight_grad(R.s, R.grad, lambda tap: (R.g_top, tap * C), after_tap)
    R.dvec[...] = jnp.concatenate([dc1, dg2, db2, dc2, dg3, db3, jnp.zeros((2, C), F32)], axis=0)
    engine.ready()
    engine.finish()
    for cp in back.sent:
        cp.wait_send()
    o_back.wait()


def back_call(columns, n, dims, cot, du, hid, y1, norms, s1, s2, pick, spread, div, masks, vec, top, bottom, datt, o,
              block_rows):
    canvases, rows, width = dims
    px = canvases * rows * width
    cells = px // UNIT
    stats = canvases * CROPS
    dma = pltpu.SemaphoreType.DMA
    names = ("mean2", "inv2", "mean3", "inv3")
    inputs = dict(du=(du, LOAD), hid=(hid, LOAD), cot=(cot, LOAD),
                  **{k: (v, LOAD) for k, v in zip(("col_l", "col_r", "row_u", "row_d"), masks)}, y1=(y1, LOAD), s1=(s1, anyw), s2=(s2, anyw),
                  pick=(pick, vmem), spread=(spread, vmem), div=(div, vmem), vec=(vec, vmem), top=(top, anyw),
                  bottom=(bottom, anyw), datt=(datt, anyw), o=(o, anyw),
                  **{k: (v, LOAD) for k, v in zip(names, norms)})
    outputs = dict(dh=((px, C), F32, STORE), grad=((px, C), B16, STORE), g_top=((11 * C, C), B16, STORE),
                   dvec=((8, C), F32, vmem), halves=((n // 2, block_rows // 2, C), B16, STORE),
                   o_back=((px // canvases, C), B16, anyw))
    scratch = dict(
        g_low=pltpu.VMEM((11 * C, C), B16), s=pltpu.VMEM(s1.shape, B16), k=pltpu.VMEM((9 * C, C), B16),
        d3=pltpu.VMEM(s1.shape, B16), low_u=pltpu.VMEM((px, C), B16), low_d=pltpu.VMEM((px, C), B16),
        part=pltpu.VMEM((px, C), F32), norm=pltpu.VMEM((px, C), F32),
        halo=pltpu.VMEM((1, 2, canvases, width, C), B16), buf=pltpu.VMEM((2, n, stats // 2, LANES), F32),
        tmp_a=pltpu.VMEM((cells, C), F32), tmp_b=pltpu.VMEM((cells, C), F32),
        reduce=fold_columns_scratch(columns, n, block_rows // 2),
        lsem=dma((5,)), ksem=dma((3,)),
        send=dma((2, n)), recv=dma((2, n)), hsend=dma((1, 2)), hrecv=dma((1, 2)))
    return named_call(functools.partial(back_kernel, columns, n, dims), "back", 7, inputs, outputs, scratch)


def renew_kernel(columns, n, dims, R):
    g = Grid(columns, n)
    half = R.fresh.shape[0] // 2
    upper, lower = Group(g, 0, half), Group(g, 1, half)
    load_g = pltpu.make_async_copy(R.g_in, R.g_top, R.ksem.at[1])
    load_g.start()
    load_k = pltpu.make_async_copy(R.top.at[pl.ds(0, 9 * C)], R.k, R.ksem.at[0])
    load_k.start()
    loads = [
        pltpu.make_async_copy(src, dst, R.ksem.at[2 + i])
        for i, (src, dst) in enumerate(((R.w, R.new_w), (R.m, R.new_m), (R.v, R.new_s), (R.dh, R.igrad)))
    ]
    for cp in loads:
        cp.start()
    piece_loads = []
    for i, src in enumerate((R.w, R.m, R.v)):
        here = pltpu.make_async_copy(src.at[pl.ds(0, half)], R.piece_in.at[i], R.psem.at[i])
        there = pltpu.make_async_copy(R.shares.at[i], R.piece_in.at[i], R.psem.at[i])
        pl.when(g.c == 0)(here.start)
        pl.when(g.c != 0)(there.start)
        piece_loads.append(there)
    greet_all(g)
    vec = R.vec
    R.need("halves")
    folder = Engine(fold_seats(lower, R.halves, R.sum_low, *R.fold))
    load_g.wait()
    reducer = Engine(reduce_pieces(upper, R.g_top, R.sum_top, *R.reduce))
    reducer.pump()
    back = Backer(n, dims, R)
    R.need("grad", "col_l", "col_r", "row_u", "row_d")
    up, down = back.send_rows(R.grad, 0)
    folder.pump()
    reducer.pump(2)
    R.need("x", "mean1", "inv1")
    for cp in loads:
        cp.wait()

    def adam(group, totals):
        @pl.when(group.is_owner)
        def _():
            total = totals[...].astype(F32)
            next_w, R.new_m[...], R.new_s[...] = adam_update(
                R.new_w[...], total, R.new_m[...], R.new_s[...], matrix_rate)
            R.new_w[...] = next_w
            R.fresh[...] = next_w.astype(B16)

    reducer.pump(2)
    back.finish_rows(up, down, 0)
    load_k.wait()
    turn = []

    def pump_both():
        reducer.pump()
        turn.append(None)
        if len(turn) == 4:
            folder.ready()
            lower.to_owner(R.sum_low, R.totals, R.asend.at[1], R.arecv.at[1], True)

    back.convolve_back(lambda tap: (R.k, tap * C), pump_both)
    gain1, bias1 = vec[0:1, :], vec[1:2, :]

    def grad_one(i, unit):
        return R.part[back.pixels(i), :] * silu_slope(unit * gain1 + bias1)

    copies, dg1, db1 = back.norm_sums(grad_one, R.x, R.mean1, R.inv1, gain1, 0)
    reducer.pump(2)
    lower.block_arrived(R.sum_low, R.totals, R.asend.at[1], R.arecv.at[1])
    adam(lower, R.totals)
    lower.to_pieces(R.fresh, R.pieces.at[1], R.tsend.at[1], R.trecv.at[1], True)
    R.vbuf[g.h] = jnp.concatenate([dg1, db1, R.dvec[0:6, :], R.dvec_att[...]], axis=0)
    vector_sends = [
        remote(R.vbuf.at[g.h], R.vbuf.at[g.h], R.vsend.at[d], R.vrecv.at[g.h],
               {CANVAS: g.c, HEIGHT: lax.rem(g.h + d, n)})
        for d in range(1, n)
    ]
    for cp in vector_sends:
        cp.start()
    reducer.ready()
    for cp in piece_loads:
        cp.wait()
    next_piece, _, _ = adam_update(
        R.piece_in[0], R.sum_top[...].astype(F32), R.piece_in[1], R.piece_in[2], matrix_rate)
    R.pieces[0] = next_piece.astype(B16)
    gather_top = Engine(gather_pieces(upper, R.pieces.at[0], R.new_top, *R.gather0))
    gather_top.pump()
    lower.piece_arrived(R.fresh, R.pieces.at[1], R.tsend.at[1], R.trecv.at[1])
    gather_low = Engine(gather_pieces(lower, R.pieces.at[1], R.new_low, *R.gather1))
    gather_low.pump()
    upper.to_owner(R.sum_top, R.totals, R.asend.at[0], R.arecv.at[0], True)

    def emit_input(i, value):
        at = back.pixels(i)
        R.igrad[at, :] = R.igrad[at, :] + value

    back.norm_finish(copies, 0, R.inv1, emit_input)
    R.store("igrad")
    gather_top.pump()
    for d in range(1, n):
        src = lax.rem(g.h + d, n)
        remote(R.vbuf.at[src], R.vbuf.at[src], R.vsend.at[d], R.vrecv.at[src],
               {CANVAS: g.c, HEIGHT: src}).wait_recv()
    R.vtrade[0, 0] = jnp.sum(R.vbuf[...], axis=0)

    def trade(k):
        return remote(R.vtrade.at[k, 0], R.vtrade.at[k, 1], R.qsend.at[k], R.qrecv.at[k], g.mate(k))

    trade(0).start()
    gather_top.pump()
    for k in range(g.phases):
        trade(k).wait_recv()
        R.vtrade[k + 1, 0] = R.vtrade[k, 0] + R.vtrade[k, 1]
        if k + 1 < g.phases:
            trade(k + 1).start()
        gather_top.pump()
    count = R.vw.shape[0]
    R.new_vw[...], R.new_vm[...], R.new_vs[...] = adam_update(
        R.vw[...], R.vtrade[g.phases, 0][0:count, :], R.vm[...], R.vs[...], vector_rate)
    R.new_vec[...] = jnp.zeros(R.new_vec.shape, F32)
    R.new_vec[0:count, :] = R.new_vw[...].astype(B16).astype(F32)
    new_vec, s1, y1, hid = R.new_vec, R.d3, R.part, R.norm
    conv = Convolver(n, dims, R.x, R.pick, R.spread, R.cnt, R.col_l, R.col_r, R.row_u, R.row_d, R.chalo, R.cbuf,
                     R.tmp_a, R.tmp_b, R.csend, R.crecv, R.chsend, R.chrecv, R.cnt_all)
    conv.activate(R.x, R.mean1, R.inv1, new_vec[0:1, :], new_vec[1:2, :], s1, 0, gather_top.pump)
    gather_top.ready()
    pump = gather_low.pump
    pump()

    def emit_first(at, total):
        y1[at, :] = total + new_vec[2:3, :]

    conv.convolve(s1, lambda dr: [(0, 3 * C, R.new_top, 3 * C * dr)], emit_first, pump)
    conv.statistics(y1, R.mean2, R.inv2, 0, pump)
    conv.activate(y1, R.mean2, R.inv2, new_vec[3:4, :], new_vec[4:5, :], R.s2, 1, pump)
    gather_low.ready()
    out_att = pltpu.make_async_copy(R.new_low.at[pl.ds(7 * C, 4 * C)], R.new_att, R.ksem.at[0])
    out_att.start()

    def emit_second(at, total):
        hid[at, :] = total + new_vec[5:6, :] + R.x[at, :].astype(F32)

    conv.convolve(R.s2, across(R.new_top, R.new_low), emit_second)
    out_hid = pltpu.make_async_copy(hid, R.hid, R.ksem.at[1])
    out_hid.start()

    def update_owned():
        upper.block_arrived(R.sum_top, R.totals, R.asend.at[0], R.arecv.at[0])
        adam(upper, R.totals)
        for k in ("new_w", "new_m", "new_s"):
            R.store(k)

    conv.statistics(hid, R.mean2, R.inv2, 1, update_owned)
    conv.normalise(hid, R.mean2, R.inv2, new_vec[6:7, :], new_vec[7:8, :], R.u)
    for engine in (gather_low, gather_top, reducer, folder):
        engine.finish()
    for cp in back.sent + conv.sent + vector_sends:
        cp.wait_send()
    for k in range(g.phases):
        trade(k).wait_send()
    for i, group in enumerate((upper, lower)):
        group.to_owner((R.sum_top, R.sum_low)[i], R.totals, R.asend.at[i], R.arecv.at[i], False)
    lower.to_pieces(R.fresh, R.pieces.at[1], R.tsend.at[1], R.trecv.at[1], False)
    out_att.wait()
    out_hid.wait()


def renew_call(columns, n, dims, grad, dh, x, mean1, inv1, pick, spread, div, cnt, cnt_all, masks, vec, top, g_top, halves,
               dvec, dvec_att, w, m, v, shares, vw, vm, vs):
    canvases, rows, width = dims
    px = canvases * rows * width
    cells = px // UNIT
    stats = canvases * CROPS
    block = w.shape
    half = block[0] // 2
    seats, phases = n // 2, columns.bit_length() - 1
    dma = pltpu.SemaphoreType.DMA
    tall = (canvases, rows + 2, width, 3 * C)
    arrays = dict(pick=pick, spread=spread, div=div, cnt=cnt, cnt_all=cnt_all, vec=vec,
                  dvec=dvec, dvec_att=dvec_att, vw=vw, vm=vm, vs=vs)
    inputs = dict(halves=(halves, LOAD), grad=(grad, LOAD),
                  **{k: (a, LOAD) for k, a in zip(("col_l", "col_r", "row_u", "row_d"), masks)}, x=(x, LOAD), mean1=(mean1, LOAD), inv1=(inv1, LOAD),
                  top=(top, anyw), g_in=(g_top, anyw), w=(w, anyw), m=(m, anyw), v=(v, anyw), shares=(shares, anyw), dh=(dh, anyw),
                  **{k: (a, vmem) for k, a in arrays.items()})
    outputs = dict(igrad=((px, C), F32, STORE), new_w=(block, F32, STORE), new_m=(block, F32, STORE),
                   new_s=(block, F32, STORE), new_vw=(vw.shape, F32, vmem), new_vm=(vw.shape, F32, vmem),
                   new_vs=(vw.shape, F32, vmem), new_vec=((16, C), F32, vmem), hid=((px, C), F32, anyw),
                   u=((px, C), B16, vmem), new_att=((4 * C, C), B16, anyw))
    scratch = dict(
        g_top=pltpu.VMEM((11 * C, C), B16), sum_top=pltpu.VMEM((half, C), B16),
        sum_low=pltpu.VMEM((half, C), B16), fold=fold_seats_scratch(n, half), totals=pltpu.VMEM(block, B16),
        new_top=pltpu.VMEM((11 * C, C), B16), new_low=pltpu.VMEM((11 * C, C), B16),
        fresh=pltpu.VMEM(block, B16), pieces=pltpu.VMEM((2, half, C), B16), k=pltpu.VMEM((9 * C, C), B16),
        d3=pltpu.VMEM(tall, B16), s2=pltpu.VMEM(tall, B16), part=pltpu.VMEM((px, C), F32),
        norm=pltpu.VMEM((px, C), F32), mean2=pltpu.VMEM((cells, C), F32), inv2=pltpu.VMEM((cells, C), F32),
        halo=pltpu.VMEM((1, 2, canvases, width, C), B16), chalo=pltpu.VMEM((2, 2, canvases, width, C), B16),
        buf=pltpu.VMEM((1, n, stats // 2, LANES), F32), cbuf=pltpu.VMEM((2, n, stats // 2, LANES), F32),
        tmp_a=pltpu.VMEM((cells, C), F32), tmp_b=pltpu.VMEM((cells, C), F32),
        vbuf=pltpu.VMEM((n, 16, C), F32), vtrade=pltpu.VMEM((phases + 1, 2, 16, C), F32),
        reduce=reduce_pieces_scratch(columns, n, half), gather0=gather_pieces_scratch(columns, n),
        gather1=gather_pieces_scratch(columns, n),
        piece_in=pltpu.VMEM((3, half, C), F32), psem=dma((3,)), ksem=dma((6,)), asend=dma((2, 1)), arecv=dma((2, 2)),
        tsend=dma((2, 2)), trecv=dma((2, 1)), vsend=dma((n,)), vrecv=dma((n,)), qsend=dma((phases,)),
        qrecv=dma((phases,)), send=dma((1, n)), recv=dma((1, n)), hsend=dma((1, 2)), hrecv=dma((1, 2)),
        csend=dma((2, n)), crecv=dma((2, n)), chsend=dma((2, 2)), chrecv=dma((2, 2)))
    return named_call(functools.partial(renew_kernel, columns, n, dims), "renew", 9, inputs, outputs, scratch)


def attend_kernel(n, keep, R):
    me = lax.axis_index(HEIGHT)
    half = n // 2
    mine = me // half
    base = mine * half
    core = lax.rem(me, 2)
    partner = lax.rem(me + half, n)
    sibling = other_core(me)
    mates = half // 2
    seat = (me - base) // 2
    seg = R.u.shape[1]
    total = n * seg
    scale = C ** (-0.5)
    nt = (((1,), (1,)), ((), ()))
    tn = (((0,), (0,)), ((), ()))
    vec = R.vec

    def mate(j, c=core):
        return base + c + 2 * lax.rem(seat + j, mates)

    def far_of(b):
        return lax.rem(b + half, n)

    def to(h):
        return {CANVAS: lax.axis_index(CANVAS), HEIGHT: h}

    loads = [pltpu.make_async_copy(R.low.at[pl.ds(R.low.shape[0] - 4 * C, 4 * C)], R.w, R.lsem.at[0])]
    if keep:
        loads.append(pltpu.make_async_copy(R.cot.at[mine], R.dz.at[pl.ds(0, seg)], R.lsem.at[1]))
    for cp in loads:
        cp.start()
    own = pltpu.make_async_copy(R.u_in.at[mine], R.u.at[me], R.lsem.at[3])
    own.start()
    barrier = pltpu.get_barrier_semaphore()
    peers = [to(p) for p in [partner, sibling] + [mate(j) for j in range(1, mates)]]
    column = lax.axis_index(CANVAS)
    if keep:
        peers += [{CANVAS: lax.rem(column + d, 4), HEIGHT: me} for d in range(1, 4)]
    for p in peers:
        pl.semaphore_signal(barrier, inc=1, device_id=p, device_id_type=MESH)
    pl.semaphore_wait(barrier, len(peers))
    started = []

    def share(from_column, half_number, to_column, begin):
        rows = R.shares.shape[1]
        for i, src in enumerate((R.params, R.first, R.second)):
            cp = remote(src.at[pl.ds(half_number * rows, rows)], R.shares.at[i], R.wsend.at[half_number, i],
                        R.wrecv.at[i], {CANVAS: to_column, HEIGHT: me})
            if begin:
                pl.when(column == from_column)(cp.start)
            else:
                pl.when(column == from_column)(cp.wait_send)
                pl.when(column == to_column)(cp.wait_recv)

    moves = ((0, 1, 1), (1, 0, 2), (1, 1, 3))
    if keep:
        for move in moves:
            share(*move, True)

    def push(src, slot, dest):
        cp = remote(src, R.u.at[slot], R.gsend.at[len(started)], R.grecv.at[slot], to(dest))
        cp.start()
        started.append(cp)

    def block(b):
        return pl.ds(pl.multiple_of(b * seg, seg), seg)

    def project(b):
        piece = R.u[b]
        R.k[block(b), :] = jnp.dot(piece, R.w[C : 2 * C, :], preferred_element_type=F32).astype(B16)
        R.v[block(b), :] = (
            jnp.dot(piece, R.w[2 * C : 3 * C, :], preferred_element_type=F32) + vec[9:10, :]
        ).astype(B16)

    def arrived(slot):
        remote(R.u_in.at[0], R.u.at[slot], R.gsend.at[0], R.grecv.at[slot], to(partner)).wait_recv()

    push(R.u_in.at[1 - mine], me, partner)
    for j in range(1, mates):
        push(R.u_in.at[mine], me, mate(j))
    push(R.u_in.at[mine], me, sibling)
    for cp in loads:
        cp.wait()
    own.wait()
    project(me)
    arrived(sibling)
    project(sibling)
    key_ids = jnp.concatenate([R.ids_all[b, pl.ds(mine, 1), :] for b in range(n)], axis=1)
    order = (me, partner) if keep else (partner, me)
    first_far = 1 if keep else 0
    far_rows, own_rows = pl.ds(first_far * seg, seg), pl.ds((1 - first_far) * seg, seg)
    for i, b in enumerate(order):
        turned = jnp.transpose(R.ids_all[b])
        picked = jnp.where(mine == 0, turned[:, 0:1], turned[:, 1:2])
        R.qid[i * seg : (i + 1) * seg, :] = jnp.broadcast_to(picked, (seg, LANES))
    arrived(partner)
    for j in range(1, mates):
        push(R.u.at[partner], partner, mate(j))
    push(R.u.at[partner], partner, sibling)
    project(partner)
    for j in range(1, mates):
        friend = mate(mates - j)
        arrived(friend)
        push(R.u.at[friend], friend, sibling)
        project(friend)
    arrived(far_of(sibling))
    project(far_of(sibling))
    for j in range(1, mates):
        friend = far_of(mate(mates - j))
        arrived(friend)
        push(R.u.at[friend], friend, sibling)
        project(friend)
    for j in range(1, mates):
        friend = mate(mates - j, 1 - core)
        arrived(friend)
        project(friend)
        arrived(far_of(friend))
        project(far_of(friend))

    rows = R.rows
    per = seg // rows

    def swap_cot(i):
        here = pl.ds(pl.multiple_of(i * rows, rows), rows)
        there = pl.ds(pl.multiple_of(seg + i * rows, rows), rows)
        return remote(R.cot.at[1 - mine, here], R.dz.at[there], R.csend.at[i], R.crecv.at[i], to(partner))

    if keep:
        for i in range(per):
            swap_cot(i).start()
    o_home = R.o_home

    def far_out(i):
        here = pl.ds(pl.multiple_of(i * rows, rows), rows)
        return remote(R.out.at[here], o_home.at[mine, here], R.osend.at[i], R.orecv.at[i], to(partner))

    def attend(i, _):
        at = pl.ds(pl.multiple_of(i * rows, rows), rows)
        b = jnp.where(i < per, order[0], order[1])
        if keep:
            @pl.when(i >= per)
            def _():
                swap_cot(i - per).wait_recv()

        uq = R.u[b, pl.ds(pl.multiple_of(lax.rem(i, per) * rows, rows), rows), :]
        qb = (jnp.dot(uq, R.w[0:C, :], preferred_element_type=F32) + vec[8:9, :]).astype(B16)
        s = lax.dot_general(qb, R.k[...], nt, preferred_element_type=F32) * scale
        s = jnp.where(R.qid[at, :][:, :1] == key_ids, s, mask_fill)
        e = jnp.exp(s - jnp.max(s, axis=1, keepdims=True))
        p = e * (1.0 / jnp.sum(e, axis=1, keepdims=True))
        pb = p.astype(B16)
        R.out[at, :] = jnp.dot(pb, R.v[...], preferred_element_type=F32).astype(B16)
        if keep:
            R.pbuf[at, :] = pb
            R.q[at, :] = qb
            dout = lax.dot_general(
                R.dz[at, :], R.w[3 * C : 4 * C, :], nt, preferred_element_type=F32).astype(B16)
            R.dout[at, :] = dout
            dp = lax.dot_general(dout, R.v[...], nt, preferred_element_type=F32)
            delta = jnp.sum(p * dp, axis=1, keepdims=True)
            ds = (p * (dp - delta)).astype(B16)
            R.sbuf[at, :] = ds
            R.dq[at, :] = (jnp.dot(ds, R.k[...], preferred_element_type=F32) * scale).astype(B16)

        if not keep:
            @pl.when(i < per)
            def _():
                far_out(i).start()

        return 0

    lax.fori_loop(0, 2 * per, attend, 0)
    if not keep:
        own_out = pltpu.make_async_copy(R.out.at[own_rows], o_home.at[mine], R.lsem.at[2])
        own_out.start()
        own_out.wait()
        for i in range(per):
            far_out(i).wait()
        for cp in started:
            cp.wait_send()
        return
    all_out = pltpu.make_async_copy(R.out, o_home, R.lsem.at[2])
    all_out.start()
    zero = jnp.zeros((C, C), F32)
    pairs = 2 * mates

    def du_of(b):
        at = block(b)
        dk = (lax.dot_general(R.sbuf[:, at], R.q[...], tn, preferred_element_type=F32) * scale).astype(B16)
        dvf = lax.dot_general(R.pbuf[:, at], R.dout[...], tn, preferred_element_type=F32)
        dv = dvf.astype(B16)
        du = lax.dot_general(dk, R.w[C : 2 * C, :], nt, preferred_element_type=F32)
        du = du + lax.dot_general(dv, R.w[2 * C : 3 * C, :], nt, preferred_element_type=F32)
        return du, (b, dk, dv, jnp.sum(dvf, axis=0, keepdims=True))

    def weigh(found, carry):
        b, dk, dv, total = found
        dwk, dwv, dbv = carry
        piece = R.u[b]
        dwk = dwk + lax.dot_general(piece, dk, tn, preferred_element_type=F32)
        dwv = dwv + lax.dot_general(piece, dv, tn, preferred_element_type=F32)
        return dwk, dwv, dbv + total

    def place(t):
        far = 1 - t // mates
        return lax.rem(lax.rem(t, mates) + 1, mates), far

    def sib_copy(t):
        return remote(R.for_sib.at[t], R.from_sib.at[t], R.ssend.at[t], R.srecv.at[t], to(sibling))

    def mate_copy(t, part):
        j, _ = place(t)
        here = pl.ds(part * (seg // 2), seg // 2)
        return remote(R.sums.at[t, here], R.from_mate.at[t, here], R.msend.at[t, part], R.mrecv.at[t, part],
                      to(mate(j)))

    def home_copy(part):
        here = pl.ds(part * (seg // 2), seg // 2)
        return remote(R.for_home.at[here], R.from_partner.at[here], R.hsend.at[part], R.hrecv.at[part], to(partner))

    def gathered(far, part):
        count = seg // 2
        at = pl.ds((first_far if far else 1 - first_far) * seg + part * count, count)
        here = pl.ds(part * count, count)
        value = lax.dot_general(R.dq[at, :], R.w[0:C, :], nt, preferred_element_type=F32)
        first_t = 0 if far else mates
        value = value + R.sums[first_t + mates - 1, here, :].astype(F32)
        for t in range(first_t, first_t + mates - 1):
            mate_copy(t, part).wait_recv()
            value = value + R.from_mate[t, here, :].astype(F32)
        return value

    def send_home(part):
        R.for_home[pl.ds(part * (seg // 2), seg // 2), :] = gathered(1, part).astype(B16)
        home_copy(part).start()

    def back(t, carry):
        j, far = place(t)
        theirs, ours = mate(j, 1 - core), mate(j)
        du, found = du_of(lax.rem(theirs + far * half, n))
        R.for_sib[t] = du.astype(B16)
        sib_copy(t).start()
        carry = weigh(found, carry)
        du, found = du_of(lax.rem(ours + far * half, n))
        sib_copy(t).wait_recv()
        R.sums[t] = (du + R.from_sib[t].astype(F32)).astype(B16)

        @pl.when(j != 0)
        def _():
            for part in range(2):
                mate_copy(t, part).start()

        @pl.when(t == pairs - 2)
        def _():
            send_home(0)

        return weigh(found, carry)

    dwk, dwv, dbv = lax.fori_loop(0, pairs, back, (zero, zero, jnp.zeros((1, C), F32)))
    send_home(1)
    for part in range(2):
        R.du[mine, pl.ds(part * (seg // 2), seg // 2), :] = gathered(0, part)
    R.store("du", mine, 1)
    R.dw[C : 2 * C, :] = dwk.astype(B16)
    R.dw[2 * C : 3 * C, :] = dwv.astype(B16)
    R.dw[3 * C : 4 * C, :] = lax.dot_general(
        R.out[...], R.dz[...], tn, preferred_element_type=F32).astype(B16)
    dwq = lax.dot_general(R.u[partner], R.dq[far_rows, :], tn, preferred_element_type=F32)
    dwq = dwq + lax.dot_general(R.u[me], R.dq[own_rows, :], tn, preferred_element_type=F32)
    R.dw[0:C, :] = dwq.astype(B16)
    R.store("dw")
    R.dvec[...] = jnp.concatenate(
        [
            jnp.sum(R.dq[...].astype(F32), axis=0, keepdims=True),
            dbv,
            jnp.sum(R.dz[...].astype(F32), axis=0, keepdims=True),
            jnp.zeros((5, C), F32),
        ],
        axis=0,
    )
    for part in range(2):
        home_copy(part).wait()
    R.du[1 - mine] = R.from_partner[...].astype(F32)
    R.store("du", 1 - mine, 1)
    for move in moves:
        share(*move, False)
    all_out.wait()
    for i in range(per):
        swap_cot(i).wait_send()
    for cp in started:
        cp.wait_send()

    def drain(t, _):
        sib_copy(t).wait_send()

        @pl.when(place(t)[0] != 0)
        def _():
            for part in range(2):
                mate_copy(t, part).wait_send()

        return 0

    lax.fori_loop(0, pairs, drain, 0)


def attend_call(n, keep, cid, u, ids_all, vec, low, cot=None, state=None):
    seg = u.shape[1]
    half = n // 2
    mates = half // 2
    pairs = 2 * mates
    total = n * seg
    rows = min(256 if keep else 128, seg)
    dma = pltpu.SemaphoreType.DMA
    inputs = dict(u_in=(u, anyw), ids_all=(ids_all, vmem), vec=(vec, vmem), low=(low, anyw))
    piece = (seg, C)
    home = (2,) + piece
    scratch = dict(
        u=pltpu.VMEM((n,) + piece, B16), w=pltpu.VMEM((4 * C, C), B16), k=pltpu.VMEM((total, C), B16),
        v=pltpu.VMEM((total, C), B16), qid=pltpu.VMEM((2 * seg, LANES), F32), out=pltpu.VMEM((2 * seg, C), B16),
        lsem=dma((4,)), gsend=dma((4 * mates,)), grecv=dma((n,)))
    if keep:
        inputs.update(cot=(cot, anyw), **{k: (a, anyw) for k, a in zip(("params", "first", "second"), state)})
        outputs = dict(o_home=((2 * seg, C), B16, anyw), dw=((4 * C, C), B16, STORE), dvec=((8, C), F32, vmem),
                       du=(home, F32, STORE), shares=((3, state[0].shape[0] // 2, C), F32, anyw))
        scratch.update(
            csend=dma((seg // rows,)), crecv=dma((seg // rows,)), dz=pltpu.VMEM((2 * seg, C), B16), dout=pltpu.VMEM((2 * seg, C), B16), q=pltpu.VMEM((2 * seg, C), B16),
            dq=pltpu.VMEM((2 * seg, C), B16), pbuf=pltpu.VMEM((2 * seg, total), B16),
            sbuf=pltpu.VMEM((2 * seg, total), B16), for_sib=pltpu.VMEM((pairs,) + piece, B16),
            from_sib=pltpu.VMEM((pairs,) + piece, B16), sums=pltpu.VMEM((pairs,) + piece, B16),
            from_mate=pltpu.VMEM((pairs - 1,) + piece, B16), for_home=pltpu.VMEM(piece, B16),
            from_partner=pltpu.VMEM(piece, B16), ssend=dma((pairs,)), srecv=dma((pairs,)), msend=dma((pairs, 2)),
            mrecv=dma((pairs, 2)), hsend=dma((2,)), hrecv=dma((2,)), wsend=dma((2, 3)), wrecv=dma((3,)))
    else:
        outputs = dict(o_home=(home, B16, anyw))
        scratch.update(osend=dma((seg // rows,)), orecv=dma((seg // rows,)))

    def kernel(R):
        R.rows = rows
        attend_kernel(n, keep, R)

    return named_call(kernel, "attend" if keep else "attend_again", cid, inputs, outputs, scratch)


def outputs_kernel(n, R):
    mine = lax.axis_index(HEIGHT) // (n // 2)
    seg = R.o_back.shape[0]
    own, other = (pl.ds(pl.multiple_of(i * seg, seg), seg) for i in (mine, 1 - mine))
    loads = [
        pltpu.make_async_copy(R.low.at[pl.ds(R.low.shape[0] - C, C)], R.w.at[0], R.sem.at[0]),
        pltpu.make_async_copy(R.o.at[pl.ds(0, seg)], R.o_in.at[0, own], R.sem.at[1]),
        pltpu.make_async_copy(R.o_back, R.o_in.at[0, other], R.sem.at[2]),
        pltpu.make_async_copy(R.new_low.at[pl.ds(R.new_low.shape[0] - C, C)], R.w.at[1], R.sem.at[3]),
        pltpu.make_async_copy(R.o2, R.o_in.at[1], R.sem.at[4]),
    ]
    for cp in loads:
        cp.start()
    count = R.part.shape[2]
    parts = R.hid.shape[0] // count
    bases = {}
    for which, src in enumerate((R.hid, R.hid2, R.igrad)):
        for i in range(parts):
            at = pl.ds(i * count, count)
            bases[which, i] = pltpu.make_async_copy(src.at[at], R.held.at[which, at], R.hsem.at[which, i])
            bases[which, i].start()
    ends = []

    def out(src, dst, sem):
        cp = pltpu.make_async_copy(src, dst, sem)
        cp.start()
        ends.append(cp)

    for cp in loads[:3]:
        cp.wait()
    for which, (vec, dst) in enumerate(((R.vec, R.first), (R.new_vec, R.second))):
        if which == 1:
            for cp in loads[3:]:
                cp.wait()
        for i in range(parts):
            at = pl.ds(i * count, count)
            bases[which, i].wait()
            if which == 0:
                out(R.held.at[0, at], R.hid_out.at[at], R.osem.at[0, i])
            R.part[which, i] = (
                R.held[which, at, :]
                + jnp.dot(R.o_in[which, at, :], R.w[which], preferred_element_type=F32) + vec[10:11, :])
            out(R.part.at[which, i], dst.at[at], R.osem.at[1 + which, i])
    for i in range(parts):
        at = pl.ds(i * count, count)
        bases[2, i].wait()
        out(R.held.at[2, at], R.igrad_out.at[at], R.osem.at[3, i])
    for cp in ends:
        cp.wait()


def outputs_call(n, hid, hid2, o, o_back, o2, igrad, vec, new_vec, low, new_low):
    px = hid.shape[0]
    inputs = dict(hid=(hid, anyw), hid2=(hid2, anyw), o=(o, anyw), o_back=(o_back, anyw), o2=(o2, anyw),
                  igrad=(igrad, anyw),
                  vec=(vec, vmem), new_vec=(new_vec, vmem), low=(low, anyw), new_low=(new_low, anyw))
    whole = ((px, C), F32, anyw)
    outputs = dict(hid_out=whole, first=whole, second=whole, igrad_out=whole)
    count = min(256, px)
    parts = px // count
    dma = pltpu.SemaphoreType.DMA
    scratch = dict(
        w=pltpu.VMEM((2, C, C), B16), held=pltpu.VMEM((3, px, C), F32), o_in=pltpu.VMEM((2, px, C), B16),
        part=pltpu.VMEM((2, parts, count, C), F32), sem=dma((5,)), hsem=dma((3, parts)), osem=dma((4, parts)))
    return named_call(functools.partial(outputs_kernel, n), "outputs", None, inputs, outputs, scratch)


def rounded_vectors(vectors):
    return lax.reduce_precision(vectors, exponent_bits=8, mantissa_bits=7)


def body(columns, n, latents, crop_ids, params, vectors, first_moment, second_moment, vector_first, vector_second,
         cotangent):
    canvases, rows, width, channels = latents.shape
    dims = (canvases, rows, width)
    px = canvases * rows * width
    plane = rows * width
    half = n // 2
    me = lax.axis_index(HEIGHT)
    mine = me // half
    partner = lax.rem(me + half, n)
    swap = [(i, (i + half) % n) for i in range(n)]
    count = vectors.shape[0]
    joined = columns == 4 and params.shape[0] % 32 == 0 and rows > 2

    ids = crop_ids.astype(F32)
    ids_lane = jnp.pad(ids.reshape(canvases, plane), ((0, 8 - canvases), (0, 0)))
    x = latents.reshape(px, channels)
    cot = cotangent.reshape(px, channels)
    cot3 = cotangent.reshape(canvases, plane, channels)
    shape = latents.shape
    if joined:
        first = first_call(columns, n, dims, x, ids_lane, vectors, params)
        ids_all, mean1, inv1, div, cnt, pick, spread, vec = (
            first[k] for k in ("ids_all", "mean1", "inv1", "div", "cnt", "pick", "spread", "vec"))
        masks = [first[k] for k in ("col_l", "col_r", "row_u", "row_d")]
        hid, u, y1, s1, s2 = (first[k] for k in ("hid", "u", "y1_out", "s1_out", "s2_out"))
        norms = [first[k] for k in ("mean2", "inv2", "mean3", "inv3")]
        top, low = first["top"], first["bottom"]
        att = attend_call(n, True, 4, u.reshape(canvases, plane, channels), ids_all, vec, low, cot3,
                          (params, first_moment, second_moment))
        du = att["du"].reshape(px, channels)
        back = back_call(columns, n, dims, cot, du, hid, y1, norms, s1, s2, pick, spread, div, masks, vec, top, low,
                         att["dw"], att["o_home"], params.shape[0])
        new = renew_call(columns, n, dims, back["grad"], back["dh"], x, mean1, inv1, pick, spread, div, cnt, first["cnt_all"],
                         masks, vec, top, back["g_top"], back["halves"], back["dvec"], att["dvec"], params, first_moment,
                         second_moment, att["shares"], vectors, vector_first, vector_second)
        new_vec, new_att = new["new_vec"], new["new_att"]
        o2 = attend_call(n, False, 5, new["u"].reshape(canvases, plane, channels), ids_all, new_vec, new_att)["o_home"]
        last = outputs_call(n, hid, new["hid"], att["o_home"], back["o_back"], o2.reshape(px, channels), new["igrad"],
                            vec, new_vec, low, new_att)
        return (
            *(last[k].reshape(shape) for k in ("hid_out", "first", "second", "igrad_out")),
            *(new[k] for k in ("new_w", "new_m", "new_s", "new_vw", "new_vm", "new_vs")),
        )

    def padded(value):
        return jnp.pad(value, ((0, 16 - count), (0, 0)))

    wide_vectors = padded(vectors)
    vec = rounded_vectors(wide_vectors)
    cell_ids = crop_ids[:, :, ::UNIT] + CROPS * jnp.arange(canvases, dtype=jnp.int32)[:, None, None]
    cell_ids = cell_ids.reshape(1, -1)
    stat = jnp.arange(canvases * CROPS, dtype=jnp.int32)[:, None]
    pick = (cell_ids == stat).astype(B16)
    spread = (cell_ids.reshape(-1, 1) == stat.reshape(1, -1)).astype(B16)
    ids_px = jnp.broadcast_to(ids[..., None], (canvases, rows, width, LANES))
    whole = spread_call(columns, n, 8, params).reshape(-1, channels)
    top, low = whole[: 11 * C], whole[11 * C :]
    ids_all, mean1, inv1, div, cnt, *masks = layout_call(n, dims, x, pick, spread, ids_px, ids_lane)
    hid, u, y1, s1, s2, mean2, inv2, mean3, inv3 = resnet_forward_call(
        n, dims, True, x, pick, spread, cnt, mean1, inv1, masks, vec, top, low)
    own_cot = lax.dynamic_index_in_dim(cot3, mine, axis=0, keepdims=False)
    far_cot = lax.ppermute(
        lax.dynamic_index_in_dim(cot3, 1 - mine, axis=0, keepdims=False), HEIGHT, swap)
    dz = jnp.concatenate([own_cot, far_cot], axis=0)
    canvas_ids = lax.dynamic_index_in_dim(ids_all, mine, axis=1, keepdims=False)
    key_ids = canvas_ids.reshape(1, n * plane)
    query_ids = jnp.stack([canvas_ids[me], canvas_ids[partner]]).reshape(2 * plane, 1)
    query_ids = jnp.broadcast_to(query_ids, (2 * plane, LANES))
    offsets = jnp.stack([me, partner]) * plane

    def attention_output(o, hid, low, bias):
        back = lax.ppermute(o[plane:], HEIGHT, swap)
        ordered = jnp.where(mine == 0, jnp.stack([o[:plane], back]), jnp.stack([back, o[:plane]]))
        product = jnp.dot(ordered.reshape(px, channels), low[10 * C :], preferred_element_type=F32)
        return hid + product + bias

    ua = gather_call(n, 4, u.reshape(canvases, plane, channels))
    o, dup, dw_att, dvec_att = attention_call(True, ua, key_ids, query_ids, offsets, dz, vec, low)
    first_output = attention_output(o, hid, low, vec[10])
    du = scatter_call(n, 6, dup.reshape(n, plane, channels)).reshape(px, channels)
    norms = (mean1, inv1, mean2, inv2, mean3, inv3)
    input_grad, matrix_grad, dvec = resnet_backward_call(
        n, dims, 7, cot, du, hid, y1, x, norms, s1, s2, pick, spread, div, masks, vec, top, low, dw_att)
    vector_grad = jnp.concatenate([dvec, dvec_att], axis=0)
    new_params, new_first, new_second, *new_small, new_whole = step_call(
        columns, n, 9, matrix_grad.reshape((columns, half, 2) + params.shape), params, first_moment,
        second_moment, vector_grad, wide_vectors, padded(vector_first), padded(vector_second))
    new_whole = new_whole.reshape(-1, channels)
    new_top, new_low = new_whole[: 11 * C], new_whole[11 * C :]
    new_vec = rounded_vectors(new_small[0])
    hid2, u2 = resnet_forward_call(
        n, dims, False, x, pick, spread, cnt, mean1, inv1, masks, new_vec, new_top, new_low)
    ua2 = gather_call(n, 5, u2.reshape(canvases, plane, channels))
    (o2,) = attention_call(False, ua2, key_ids, query_ids, offsets, dz, new_vec, new_low)
    second_output = attention_output(o2, hid2, new_low, new_vec[10])
    return (
        *(a.reshape(shape) for a in (hid, first_output, second_output, input_grad)),
        new_params,
        new_first,
        new_second,
        *(a[:count] for a in new_small),
    )


def solution(mesh):
    spatial = P(CANVAS, HEIGHT, None, None)
    owned = P((CANVAS, HEIGHT), None)
    return jax.shard_map(
        functools.partial(body, mesh.shape[CANVAS], mesh.shape[HEIGHT]),
        mesh=mesh,
        in_specs=(spatial, P(CANVAS, HEIGHT, None), owned, P(), owned, owned, P(), P(), spatial),
        out_specs=(spatial, spatial, spatial, spatial, owned, owned, owned, P(), P(), P()),
        check_vma=False,
    )
```
